32 devices in a mesh: rep: 2 (over y), fsdp: 16 (over z, x, core).
Axes of the slice: x: 2, y: 2, z: 4, core: 2. Of those that a mesh axis runs over, the one named last changes fastest.
Arguments:
- tokens: bfloat16 [32, 1024, 1024], P(('rep', 'fsdp')), may hold values from -6 to 6
- norm_gain: float32 [1024], replicated, may hold values from 0.25 to 1.75
- in_weight: bfloat16 [1024, 4384], P('fsdp'), may hold values from -0.1875 to 0.1875
- conv_weight: float32 [4, 2304], replicated, may hold values from -3 to 3
- conv_bias: float32 [2304], replicated, may hold values from -0.5 to 0.5
- step_bias: float32 [32], replicated, may hold values from -7 to -1
- decay_log: float32 [32], replicated, may hold values from -1 to 2.5
- skip_gain: float32 [32], replicated, may hold values from 0.5 to 1.5
- out_gain: float32 [2048], replicated, may hold values from 0.25 to 1.75
- out_weight: bfloat16 [2048, 1024], P('fsdp'), may hold values from -0.125 to 0.125
- cotangent: bfloat16 [32, 1024, 1024], P(('rep', 'fsdp')), may hold values from -6 to 6
- teacher: bfloat16 [32, 1024, 1024], P(('rep', 'fsdp')), may hold values from -6 to 6
- segment: int32 [32, 1024], P(('rep', 'fsdp')), may hold values from 0 to 3, never falling along the last dimension, each value on 1 to 512 neighbouring positions
- valid_mask: int32 [32, 1024], P(('rep', 'fsdp')), may hold values from 0 to 1, as said below
Outputs:
- output: bfloat16 [32, 1024, 1024], P(('rep', 'fsdp'))
- loss_value: float32 [], replicated
- grad_tokens: bfloat16 [32, 1024, 1024], P(('rep', 'fsdp'))
- grad_norm_gain: float32 [1024], replicated
- grad_in_weight: float32 [1024, 4384], P('fsdp')
- grad_conv_weight: float32 [4, 2304], replicated
- grad_conv_bias: float32 [2304], replicated
- grad_step_bias: float32 [32], replicated
- grad_decay_log: float32 [32], replicated
- grad_skip_gain: float32 [32], replicated
- grad_out_gain: float32 [2048], replicated
- grad_out_weight: float32 [2048, 1024], P('fsdp')
The draws below stay inside these ranges and needn't reach their ends.
Inputs may be any that keep to these rules, and one draw needn't show every extreme that they name: `segment`: within each sequence the number is 0 at the start and never falls; each document has 1 to 512 positions, one has exactly that many. `valid_mask`: each sequence has 1 on a leading run of 341 positions or more and 0 after it.
All inputs are finite; a program needn't handle non-finite values.
Results may differ from the reference program's by a relative error of at most 0.0078.
Values may be sent and summed in bfloat16 or wider, within the bound.
A program may use at most 320 MiB of HBM per device.

```python
import math
import jax
import jax.numpy as jnp
import numpy as np
from jax import lax

D = 1024
HEADS = 32
CONV = 4
STRETCH = 256
DOCS = 4
LEN = 1024
SEQS = 32
INNER = 2048
XBC = 2304
PROJ = 4384
LOSS_WEIGHT = 4194304


def draw_valid_mask(key, part):
    row_index = jnp.arange(SEQS)
    half_rows = max(SEQS // 2, 2)
    position = row_index % half_rows
    base_length = LEN // 3 + position * (2 * LEN // 3) // (half_rows - 1)
    jitter = jax.random.randint(key, (SEQS,), 0, LEN // 16 + 1)
    live_length = jnp.minimum(base_length + jitter, LEN)
    return (jnp.arange(LEN)[None, :] < live_length[:, None]).astype(jnp.int32)


def steps_of(key, dims, cuts, smallest, high):
    level, own = 1.0, jax.random.fold_in(key, 6)
    for axis_at, blocks in cuts:
        steps = jnp.exp(jax.random.uniform(jax.random.fold_in(own, axis_at), (blocks,), jnp.float32, smallest / len(cuts), high / len(cuts)))
        level = level * jnp.repeat(steps, dims[axis_at] // blocks).reshape([-1 if axis == axis_at else 1 for axis in range(len(dims))])
    return level


def length_profile(count, total, limit, lean):
    portions = [(1 << 20) // math.isqrt(grade ** lean) + 1 for grade in range(2, count + 1)]
    spare, given = total - limit - (count - 1), [1] * (count - 1)
    while spare > 0:
        free = [i for i in range(count - 1) if given[i] < limit]
        whole, budget = sum([portions[i] for i in free]), spare
        for i in free:
            more = min(limit - given[i], max(1, budget * portions[i] // whole), spare)
            given[i] = given[i] + more
            spare = spare - more
    return np.array([limit] + given)


def uneven_parts(own_key, amount, total, reach, lean):
    if amount == 2:
        one = jax.random.randint(own_key, (), max(1, total - reach), min(reach, total - 1) + 1)
        return jnp.stack([one, total - one])
    tallies = jnp.asarray(length_profile(amount, total, reach, lean), jnp.int32)
    twos = (amount - 1) // 2
    giver, sink = tallies[1:1 + 2 * twos:2], tallies[2:2 + 2 * twos:2]
    room = jnp.minimum(giver - 1, reach - sink)
    moved = jax.random.randint(jax.random.fold_in(own_key, 1), (twos,), 0, 1 << 20) % (room + 1)
    tallies = tallies.at[1:1 + 2 * twos:2].set(giver - moved).at[2:2 + 2 * twos:2].set(sink + moved)
    return tallies[jax.random.permutation(jax.random.fold_in(own_key, 2), amount)]


def gaussian(rng, shape, deviation, reach, cuts=(), kind=jnp.bfloat16):
    level = steps_of(rng, shape, cuts, -0.22, 0.18) if cuts else 1.0
    values = jax.random.normal(rng, shape, jnp.float32) * deviation * level
    return jnp.minimum(jnp.maximum(values, -reach), reach).astype(kind)


def setup_inputs(seed: int = 0) -> dict:
    key_list = jax.random.split(jax.random.key(seed), 15)
    return {
        "tokens": gaussian(key_list[0], (SEQS, LEN, D), 1.0, 6.0, ((0, 32),)),
        "norm_gain": jnp.clip(1.0 + 0.15 * jax.random.normal(key_list[1], (D,), jnp.float32), 0.25, 1.75),
        "in_weight": gaussian(key_list[2], (D, PROJ), D ** -0.5, 0.1875, ((0, 16),)),
        "conv_weight": gaussian(key_list[3], (CONV, XBC), CONV ** -0.5, 3.0, (), jnp.float32),
        "conv_bias": jnp.clip(jax.random.uniform(key_list[4], (XBC,), jnp.float32, -0.5, 0.5), -0.5, 0.5),
        "step_bias": jnp.clip(jax.random.uniform(key_list[5], (HEADS,), jnp.float32, -7.0, -1.0), -7.0, -1.0),
        "decay_log": jnp.clip(jax.random.uniform(key_list[6], (HEADS,), jnp.float32, -1.0, 2.5), -1.0, 2.5),
        "skip_gain": jnp.clip(jax.random.uniform(key_list[7], (HEADS,), jnp.float32, 0.5, 1.5), 0.5, 1.5),
        "out_gain": jnp.clip(1.0 + 0.15 * jax.random.normal(key_list[8], (INNER,), jnp.float32), 0.25, 1.75),
        "out_weight": gaussian(key_list[9], (INNER, D), INNER ** -0.5, 0.125, ((0, 16),)),
        "cotangent": gaussian(key_list[10], (SEQS, LEN, D), 1.0, 6.0, ((0, 32),)),
        "teacher": gaussian(key_list[11], (SEQS, LEN, D), 1.0, 6.0, ((0, 32),)),
        "segment": jax.vmap(lambda own: jnp.searchsorted(jnp.cumsum(uneven_parts(own, DOCS, LEN, LEN // 2, 0)), jnp.arange(LEN), side="right"))(jax.random.split(key_list[12], SEQS)).reshape((SEQS, LEN)).astype(jnp.int32),
        "valid_mask": draw_valid_mask(jax.random.fold_in(key_list[14], 71), 0),
    }


epsilon = 1e-05

@jax.custom_vjp
def low(v):
    return lax.optimization_barrier(v.astype(jnp.bfloat16)).astype(jnp.float32)

@jax.custom_vjp
def low_back(v):
    return v

def low_keep(v):
    return (low(v), None)

def low_pass(kept, grad):
    return (grad,)

def back_keep(v):
    return (v, None)

def back_low(kept, grad):
    return (low(grad),)
low.defvjp(low_keep, low_pass)
low_back.defvjp(back_keep, back_low)

def prenorm(values, gain_vector):
    return values * lax.rsqrt(lax.optimization_barrier(jnp.mean(values * values, axis=1, keepdims=True)) + epsilon) * gain_vector[None, :]

def convolve(conv_in, segment, conv_weight, conv_bias):
    tap_count = conv_weight.shape[0]
    summed = conv_bias[None, :] + conv_weight[0][None, :] * conv_in
    for offset in range(1, tap_count):
        delayed = jnp.concatenate([jnp.zeros((offset, conv_in.shape[1]), conv_in.dtype), conv_in[:-offset]], axis=0)
        same_doc = jnp.concatenate([jnp.zeros((offset,), conv_in.dtype), (segment[offset:] == segment[:-offset]).astype(conv_in.dtype)], axis=0)
        summed = summed + conv_weight[offset][None, :] * delayed * same_doc[:, None]
    return jax.nn.silu(summed)

def block_step(carried, block_data):
    state_in, last_doc, decay_rate = carried
    x_heads, step_size, inputs_b, outputs_c, doc_ids = block_data
    highest = lax.Precision.HIGHEST
    kind = step_size.dtype
    decay_sum = jnp.cumsum(step_size * decay_rate[None, :], axis=0)
    positions = jnp.arange(doc_ids.shape[0])
    causal = (positions[:, None] >= positions[None, :]) & (doc_ids[:, None] == doc_ids[None, :])
    spread = decay_sum[:, None, :] - decay_sum[None, :, :]
    weights = jnp.exp(jnp.where(causal[:, :, None], spread, 0.0)) * causal[:, :, None].astype(kind)
    scores = jnp.dot(outputs_c, inputs_b.T, precision=highest)
    mixing = scores[:, :, None] * weights * step_size[None, :, :]
    within_block = jnp.einsum('ijh,jhp->ihp', mixing, x_heads, precision=highest)
    keep_prev = (doc_ids == last_doc).astype(kind)
    from_state = jnp.einsum('in,hpn->ihp', outputs_c, state_in, precision=highest) * (jnp.exp(decay_sum) * keep_prev[:, None])[:, :, None]
    end_doc = doc_ids[-1]
    to_end = jnp.exp(decay_sum[-1][None, :] - decay_sum) * (doc_ids == end_doc).astype(kind)[:, None] * step_size
    carry_on = jnp.exp(decay_sum[-1]) * (end_doc == last_doc).astype(kind)
    state_out = state_in * carry_on[:, None, None] + jnp.einsum('jh,jhp,jn->hpn', to_end, x_heads, inputs_b, precision=highest)
    return ((state_out, end_doc, decay_rate), within_block + from_state)

def ssd_mixer(projected, segment, conv_weight, conv_bias, step_bias, decay_log, skip_gain, out_gain):
    length = projected.shape[0]
    inner_width = out_gain.shape[0]
    head_count = step_bias.shape[0]
    conv_width = conv_weight.shape[1]
    state_width = (conv_width - inner_width) // 2
    head_width = inner_width // head_count
    block_rows = min(STRETCH, length)
    blocks = length // block_rows
    gate_part = projected[:, :inner_width]
    conv_out = convolve(projected[:, inner_width:inner_width + conv_width], segment, conv_weight, conv_bias)
    step_size = jax.nn.softplus(projected[:, inner_width + conv_width:] + step_bias[None, :])
    decay_rate = -jnp.exp(decay_log)
    x_heads = conv_out[:, :inner_width].reshape(length, head_count, head_width)
    inputs_b = conv_out[:, inner_width:inner_width + state_width]
    outputs_c = conv_out[:, inner_width + state_width:]
    block_data = (x_heads.reshape(blocks, block_rows, head_count, head_width), step_size.reshape(blocks, block_rows, head_count), inputs_b.reshape(blocks, block_rows, state_width), outputs_c.reshape(blocks, block_rows, state_width), segment.reshape(blocks, block_rows))
    start_carry = (jnp.zeros((head_count, head_width, state_width), projected.dtype), jnp.array(-1, jnp.int32), decay_rate)
    ignored, mixed_out = lax.scan(jax.checkpoint(block_step), start_carry, block_data)
    ssd_out = mixed_out.reshape(length, head_count, head_width) + skip_gain[None, :, None] * x_heads
    gated = ssd_out.reshape(length, inner_width) * jax.nn.silu(gate_part)
    return gated * lax.rsqrt(lax.optimization_barrier(jnp.mean(gated * gated, axis=1, keepdims=True)) + epsilon) * out_gain[None, :]

def reference(tokens, norm_gain, in_weight, conv_weight, conv_bias, step_bias, decay_log, skip_gain, out_gain, out_weight, cotangent, teacher, segment, valid_mask):
    highest = lax.Precision.HIGHEST
    count = jnp.sum(valid_mask.astype(jnp.float32))
    loss_divisor = count * D
    scale_loss = LOSS_WEIGHT / loss_divisor
    params = tuple((member.astype(jnp.float32) for member in (norm_gain, in_weight, conv_weight, conv_bias, step_bias, decay_log, skip_gain, out_gain, out_weight)))

    def forward(inputs, weights, target_rows, segment_row, valid_row):
        gain_first, w_inner, conv_taps, conv_shift, bias_step, log_decay, gain_skip, gain_out, w_outer = weights
        normed = low(prenorm(inputs, gain_first))
        projected = low_back(jnp.dot(normed, w_inner, precision=highest))
        mixed = low(ssd_mixer(projected, segment_row, conv_taps, conv_shift, bias_step, log_decay, gain_skip, gain_out))
        branch = low_back(jnp.dot(mixed, w_outer, precision=highest))
        result = inputs + branch
        residual_error = result - target_rows
        squares = jnp.sum(valid_row[:, None] * residual_error * residual_error)
        return (result, squares)

    def per_sequence(summed, packed):
        inputs = packed[0].astype(jnp.float32)
        cotan_rows = packed[1].astype(jnp.float32)
        target_rows = packed[2].astype(jnp.float32)
        segment_row = packed[3]
        valid_row = packed[4].astype(jnp.float32)

        def objective(values, weights):
            return forward(values, weights, target_rows, segment_row, valid_row)
        (result, squares), backward = jax.vjp(objective, inputs, params)
        grad_inputs, grad_weights = backward((valid_row[:, None] * cotan_rows, scale_loss))
        new_sum = (summed[0] + squares, jax.tree.map(lambda former, latter: former + latter, summed[1], grad_weights))
        return (new_sum, (result.astype(jnp.bfloat16), grad_inputs.astype(jnp.bfloat16)))
    start_sum = (jnp.zeros((), jnp.float32), jax.tree.map(jnp.zeros_like, params))
    (square_total, grads), (output, grad_tokens) = lax.scan(per_sequence, start_sum, (tokens, cotangent, teacher, segment, valid_mask))
    loss_value = square_total / loss_divisor
    return (output, loss_value, grad_tokens, grads[0], grads[1], grads[2], grads[3], grads[4], grads[5], grads[6], grads[7], grads[8])
```

```python
import functools

import jax
import jax.numpy as jnp
from jax import lax
from jax.experimental import pallas as pl
from jax.experimental.pallas import tpu as pltpu
from jax.sharding import PartitionSpec as P

CHUNK = 128
LANES = 128
EPS = 1e-05
F32 = jnp.float32
BF16 = jnp.bfloat16
NT = (((1,), (1,)), ((), ()))
TN = (((0,), (0,)), ((), ()))


def mm(a, b):
    return jnp.dot(a, b, preferred_element_type=F32)


def mm_nt(a, b):
    return lax.dot_general(a, b, NT, preferred_element_type=F32)


def mm_tn(a, b):
    return lax.dot_general(a, b, TN, preferred_element_type=F32)


def split2(v):
    high = v.astype(BF16)
    return high, (v - high.astype(F32)).astype(BF16)


def split3(v):
    high = v.astype(BF16)
    rest = v - high.astype(F32)
    mid = rest.astype(BF16)
    return high, mid, (rest - mid.astype(F32)).astype(BF16)


def tri_sum(tri, v):
    heads = v.shape[1]
    parts = mm(tri, jnp.concatenate(split3(v), axis=1))
    return parts[:, :heads] + parts[:, heads : 2 * heads] + parts[:, 2 * heads :]


def sigmoid(v):
    return 0.5 * jnp.tanh(0.5 * v) + 0.5


def softplus(v):
    return jnp.maximum(v, 0.0) + jnp.log1p(jnp.exp(-jnp.abs(v)))


def iota(shape, dim):
    return lax.broadcasted_iota(jnp.int32, shape, dim)


def small_terms(step_raw, step_bias, decay_rate, keep, to_end, rows):
    shifted = step_raw + step_bias
    step = softplus(shifted)
    lower = (iota((rows, rows), 0) >= iota((rows, rows), 1)).astype(BF16)
    cum = tri_sum(lower, step * decay_rate)
    last = cum[rows - 1 : rows, :]
    return shifted, step, cum, jnp.exp(cum) * keep, jnp.exp(last - cum) * to_end


def expand(e_ref, out_ref, step, from_prev, to_end):
    stacked = jnp.concatenate(
        [jnp.concatenate(split2(v), axis=1) for v in (step, from_prev, to_end)], axis=0
    )
    out_ref[...] = mm(stacked, e_ref[...])


def conv_tile(xbuf, cw_ref, cb_ref, marks, cols, rows):
    taps = cw_ref.shape[0]
    pre = cb_ref[:, cols] + cw_ref[0:1, cols] * xbuf[8 : 8 + rows, cols]
    for k in range(1, taps):
        pre = pre + (cw_ref[k : k + 1, cols] * xbuf[8 - k : 8 - k + rows, cols]) * marks[k]
    return pre


def forward_kernel(
    p_ref, prev_ref, aux_ref, seg_ref, cw_ref, cb_ref, bias_ref, rate_ref, skip_ref, gain_ref, e_ref,
    mixed_ref, y_ref, state_out_ref,
    xbuf, ex, state, xs, xdt, xe, bc, yin, gs,
    *, inner, conv_width, heads, width, per_seq,
):
    rows = p_ref.shape[0]
    n = (conv_width - inner) // 2
    tiles = inner // LANES
    conv_tiles = conv_width // LANES

    @pl.when(lax.rem(pl.program_id(0), per_seq) == 0)
    def _():
        state[...] = jnp.zeros_like(state)

    aux = aux_ref[...]
    keep, to_end_mask = aux[:, 7:8], aux[:, 8:9]
    shifted, step, cum, from_prev, to_end = small_terms(
        p_ref[:, inner + conv_width :], bias_ref[...], rate_ref[...], keep, to_end_mask, rows
    )
    expand(e_ref, ex, step, from_prev, to_end)
    cum_t = cum.T
    xbuf[0:8, :] = prev_ref[:, inner : inner + conv_width]
    xbuf[8 : 8 + rows, :] = p_ref[:, inner : inner + conv_width]
    marks = [None] + [jnp.broadcast_to(aux[:, k : k + 1], (rows, LANES)) for k in range(1, cw_ref.shape[0])]
    for c in range(conv_tiles):
        cols = slice(c * LANES, (c + 1) * LANES)
        pre = conv_tile(xbuf, cw_ref, cb_ref, marks, cols, rows)
        act = pre * sigmoid(pre)
        if c < tiles:
            xs[:, cols] = act
            scaled = act * ex[0:rows, cols]
            xdt[:, cols] = scaled.astype(BF16)
            xe[:, cols] = (scaled * ex[2 * rows : 3 * rows, cols]).astype(BF16)
        else:
            bc[:, (c - tiles) * LANES : (c - tiles + 1) * LANES] = act.astype(BF16)
    b, cc = bc[:, :n], bc[:, n:]
    causal = (iota((rows, rows), 0) >= iota((rows, rows), 1)) & (aux[:, 0:1] == seg_ref[0])
    scores = jnp.where(causal, mm_nt(cc, b), 0.0)
    state_low = state[...].astype(BF16)
    state_out_ref[...] = state_low
    yin[...] = mm(cc, state_low)
    state[...] = state[...] * ex[2 * rows - 1 : 2 * rows, :] + mm_tn(b, xe[...])
    lane = iota((1, LANES), 1)
    masks = [(lane < width).astype(BF16), (lane >= width).astype(BF16)]
    total = jnp.zeros((rows, LANES), F32)
    for c in range(tiles):
        cols = slice(c * LANES, (c + 1) * LANES)
        mixing = []
        for h in (2 * c, 2 * c + 1):
            spread = jnp.minimum(cum[:, h : h + 1] - cum_t[h : h + 1, :], 0.0)
            mixing.append((scores * jnp.exp(spread)).astype(BF16))
        x_low = xdt[:, cols]
        y = mm(
            jnp.concatenate(mixing, axis=1), jnp.concatenate([x_low * masks[0], x_low * masks[1]], axis=0)
        ) + ex[rows : 2 * rows, cols] * yin[:, cols]
        y_ref[:, cols] = y
        gate = p_ref[:, cols]
        gated = (y + skip_ref[:, cols] * xs[:, cols]) * (gate * sigmoid(gate))
        gs[:, cols] = gated
        total = total + gated * gated
    inverse = lax.rsqrt(jnp.sum(total, axis=1, keepdims=True) / inner + EPS)
    for c in range(tiles):
        cols = slice(c * LANES, (c + 1) * LANES)
        mixed_ref[:, cols] = (gs[:, cols] * inverse * gain_ref[:, cols]).astype(BF16)


def backward_kernel(
    p_ref, prev_ref, aux_ref, seg_ref, y_ref, state_ref, gm_ref,
    cw_ref, cb_ref, bias_ref, rate_ref, skip_ref, gain_ref, e_ref, et_ref,
    gp_ref, dcw_ref, dcb_ref, dgain_ref, dskip_ref, dsmall_ref,
    xbuf, ex, adj, xs, xdt, xe, bc, slope, dy, dye, dxi, dbuf, r1, r1l, r2, r3,
    *, inner, conv_width, heads, width, per_seq,
):
    rows = p_ref.shape[0]
    n = (conv_width - inner) // 2
    tiles = inner // LANES
    conv_tiles = conv_width // LANES
    taps = cw_ref.shape[0]

    @pl.when(pl.program_id(0) == 0)
    def _():
        for ref in (dcw_ref, dcb_ref, dgain_ref, dskip_ref, dsmall_ref):
            ref[...] = jnp.zeros_like(ref)

    @pl.when(lax.rem(pl.program_id(0), per_seq) == 0)
    def _():
        adj[...] = jnp.zeros_like(adj)
        dbuf[rows : rows + 8, :] = jnp.zeros((8, conv_width), F32)

    def fold(v):
        return jnp.sum(v.reshape(rows // 8, 8, v.shape[1]), axis=0)

    aux = aux_ref[...]
    keep, to_end_mask = aux[:, 7:8], aux[:, 8:9]
    rate = rate_ref[...]
    shifted, step, cum, from_prev, to_end = small_terms(
        p_ref[:, inner + conv_width :], bias_ref[...], rate, keep, to_end_mask, rows
    )
    expand(e_ref, ex, step, from_prev, to_end)
    cum_t = cum.T
    xbuf[0:8, :] = prev_ref[:, inner : inner + conv_width]
    xbuf[8 : 8 + rows, :] = p_ref[:, inner : inner + conv_width]
    marks = [None] + [jnp.broadcast_to(aux[:, k : k + 1], (rows, LANES)) for k in range(1, taps)]
    for c in range(conv_tiles):
        cols = slice(c * LANES, (c + 1) * LANES)
        pre = conv_tile(xbuf, cw_ref, cb_ref, marks, cols, rows)
        sig = sigmoid(pre)
        act = pre * sig
        slope[:, cols] = sig + act * (1.0 - sig)
        if c < tiles:
            xs[:, cols] = act
            scaled = act * ex[0:rows, cols]
            xdt[:, cols] = scaled.astype(BF16)
            xe[:, cols] = (scaled * ex[2 * rows : 3 * rows, cols]).astype(BF16)
        else:
            bc[:, (c - tiles) * LANES : (c - tiles + 1) * LANES] = act.astype(BF16)
    squares = jnp.zeros((rows, LANES), F32)
    cross = jnp.zeros((rows, LANES), F32)
    for c in range(tiles):
        cols = slice(c * LANES, (c + 1) * LANES)
        gate = p_ref[:, cols]
        gated = (y_ref[:, cols] + skip_ref[:, cols] * xs[:, cols]) * (gate * sigmoid(gate))
        squares = squares + gated * gated
        cross = cross + gm_ref[:, cols] * gain_ref[:, cols] * gated
    inverse = lax.rsqrt(jnp.sum(squares, axis=1, keepdims=True) / inner + EPS)
    mean_cross = jnp.sum(cross, axis=1, keepdims=True) / inner * inverse
    for c in range(tiles):
        cols = slice(c * LANES, (c + 1) * LANES)
        gate = p_ref[:, cols]
        sig = sigmoid(gate)
        silu = gate * sig
        x = xs[:, cols]
        y = y_ref[:, cols]
        ssd = y + skip_ref[:, cols] * x
        unit = ssd * silu * inverse
        grad_mixed = gm_ref[:, cols]
        dgain_ref[:, cols] += fold(grad_mixed * unit)
        grad_gated = inverse * (grad_mixed * gain_ref[:, cols] - unit * mean_cross)
        grad_ssd = grad_gated * silu
        gp_ref[:, cols] = (grad_gated * ssd * (sig + silu * (1.0 - sig))).astype(BF16)
        dskip_ref[:, cols] += fold(grad_ssd * x)
        low = grad_ssd.astype(BF16)
        dy[:, cols] = low
        dye[:, cols] = (grad_ssd * ex[rows : 2 * rows, cols]).astype(BF16)
        r1[:, cols] = low
    b, cc = bc[:, :n], bc[:, n:]
    state_low = state_ref[...]
    adj_low = adj[...].astype(BF16)
    carry = ex[2 * rows - 1 : 2 * rows, :]
    grad_c = mm_nt(dye[...], state_low)
    grad_b = mm_nt(xe[...], adj_low)
    dxi[...] = mm(b, adj_low)
    through = jnp.sum(adj[...] * state_low.astype(F32), axis=0, keepdims=True) * carry
    adj[...] = adj[...] * carry + mm_tn(cc, dye[...])
    causal_t = (iota((rows, rows), 0) <= iota((rows, rows), 1)) & (aux[:, 0:1] == seg_ref[0])
    scores_t = jnp.where(causal_t, mm_nt(b, cc), 0.0)
    lane = iota((1, LANES), 1)
    masks = [(lane < width).astype(BF16), (lane >= width).astype(BF16)]
    grad_scores_t = jnp.zeros((rows, rows), F32)
    for c in range(tiles):
        cols = slice(c * LANES, (c + 1) * LANES)
        x_low, dy_low = xdt[:, cols], dy[:, cols]
        grad_mix = mm_nt(jnp.concatenate([x_low * masks[0], x_low * masks[1]], axis=0), dy_low)
        mixing = []
        for i, h in enumerate((2 * c, 2 * c + 1)):
            decay = jnp.exp(jnp.minimum(cum_t[h : h + 1, :] - cum[:, h : h + 1], 0.0))
            mixing.append((scores_t * decay).astype(BF16))
            grad_scores_t = grad_scores_t + grad_mix[i * rows : (i + 1) * rows] * decay
        within = mm(
            jnp.concatenate(mixing, axis=1), jnp.concatenate([dy_low * masks[0], dy_low * masks[1]], axis=0)
        )
        x = xs[:, cols]
        across = ex[2 * rows : 3 * rows, cols] * dxi[:, cols]
        both = within + across
        grad_ssd = dy_low.astype(F32)
        x_scaled = x_low.astype(F32)
        r1[:, cols], r1l[:, cols] = split2(grad_ssd * y_ref[:, cols] - within * x_scaled)
        r2[:, cols] = (across * x_scaled).astype(BF16)
        r3[:, cols] = (both * x).astype(BF16)
        grad_x = skip_ref[:, cols] * grad_ssd + ex[0:rows, cols] * both
        dbuf[0:rows, cols] = grad_x * slope[:, cols]
    grad_scores_t = jnp.where(causal_t, grad_scores_t, 0.0).astype(BF16)
    grad_b = grad_b + mm(grad_scores_t, cc)
    grad_c = grad_c + mm_tn(grad_scores_t, b)
    dbuf[0:rows, inner : inner + n] = grad_b * slope[:, inner : inner + n]
    dbuf[0:rows, inner + n :] = grad_c * slope[:, inner + n :]
    et = et_ref[...]
    sum1 = (mm(r1[...], et) + mm(r1l[...], et))[:, :heads]
    sum2 = mm(r2[...], et)[:, :heads]
    sum3 = mm(r3[...], et)[:, :heads]
    through8 = jnp.broadcast_to(through, (8, inner))
    high, rest = split2(through8)
    const = (mm(high, et) + mm(rest, et))[0:1, :heads]
    upper = (iota((rows, rows), 0) <= iota((rows, rows), 1)).astype(BF16)
    strict = (iota((rows, rows), 0) > iota((rows, rows), 1)).astype(BF16)
    grad_log = (tri_sum(upper, sum1) + tri_sum(strict, sum2) + const) * aux[:, 1:2]
    grad_raw = (sum3 + rate * grad_log) * sigmoid(shifted)
    gp_ref[:, inner + conv_width :] = grad_raw.astype(BF16)
    dsmall_ref[0:8, :] += fold(grad_raw)
    dsmall_ref[8:16, :] += fold(step * grad_log * rate)
    marks_next = [None] + [jnp.broadcast_to(aux[:, 3 + k : 4 + k], (rows, LANES)) for k in range(1, taps)]
    for c in range(conv_tiles):
        cols = slice(c * LANES, (c + 1) * LANES)
        here = dbuf[0:rows, cols]
        out = cw_ref[0:1, cols] * here
        dcb_ref[:, cols] += fold(here)
        dcw_ref[0:8, cols] += fold(here * xbuf[8 : 8 + rows, cols])
        for k in range(1, taps):
            out = out + (cw_ref[k : k + 1, cols] * dbuf[k : k + rows, cols]) * marks_next[k]
            dcw_ref[8 * k : 8 * k + 8, cols] += fold(here * (xbuf[8 - k : 8 - k + rows, cols] * marks[k]))
        gp_ref[:, inner + c * LANES : inner + (c + 1) * LANES] = out.astype(BF16)
    dbuf[rows : rows + 8, :] = dbuf[0:8, :]


def helpers(segment, chunk):
    seqs, length = segment.shape
    blocks = length // chunk
    def same(shift):
        return (segment[:, shift:] == segment[:, :-shift]).astype(F32)
    back = [jnp.pad(same(k), ((0, 0), (k, 0))) for k in (1, 2, 3)]
    ahead = [jnp.pad(same(k), ((0, 0), (0, k))) for k in (1, 2, 3)]
    by_block = segment.reshape(seqs, blocks, chunk)
    ends = by_block[:, :, -1]
    before = jnp.pad(ends[:, :-1], ((0, 0), (1, 0)), constant_values=-1)
    keep = (by_block == before[:, :, None]).astype(F32).reshape(seqs, length)
    to_end = (by_block == ends[:, :, None]).astype(F32).reshape(seqs, length)
    docs = segment.astype(F32)
    columns = [docs, *back, *ahead, keep, to_end] + [jnp.zeros_like(docs)] * 7
    aux = jnp.stack(columns, axis=-1).reshape(seqs * length, 16)
    return aux, docs.reshape(seqs * blocks, 1, chunk)


def head_maps(heads, width):
    inner = heads * width
    owner = jnp.arange(inner) // width
    one = (jnp.arange(heads)[:, None] == owner[None, :]).astype(BF16)
    down = (owner[:, None] == jnp.arange(LANES)[None, :]).astype(BF16)
    return jnp.concatenate([one, one], axis=0), down


def full(shape):
    return pl.BlockSpec(shape, lambda i: (0,) * len(shape))


def scan_forward(p, aux, seg_rows, conv_w, conv_b, bias, rate, skip_row, gain_row, e, per_seq):
    tokens, proj = p.shape
    inner, conv_width, heads = gain_row.shape[1], conv_w.shape[1], bias.shape[1]
    n = (conv_width - inner) // 2
    r = CHUNK
    chunks = tokens // r
    return pl.pallas_call(
        functools.partial(
            forward_kernel, inner=inner, conv_width=conv_width, heads=heads, width=inner // heads, per_seq=per_seq
        ),
        grid=(chunks,),
        in_specs=[
            pl.BlockSpec((r, proj), lambda i: (i, 0)),
            pl.BlockSpec((8, proj), lambda i: (jnp.maximum(i * (r // 8) - 1, 0), 0)),
            pl.BlockSpec((r, 16), lambda i: (i, 0)),
            pl.BlockSpec((1, 1, r), lambda i: (i, 0, 0)),
            full(conv_w.shape), full(conv_b.shape), full(bias.shape), full(rate.shape),
            full(skip_row.shape), full(gain_row.shape), full(e.shape),
        ],
        out_specs=[
            pl.BlockSpec((r, inner), lambda i: (i, 0)),
            pl.BlockSpec((r, inner), lambda i: (i, 0)),
            pl.BlockSpec((n, inner), lambda i: (i, 0)),
        ],
        out_shape=[
            jax.ShapeDtypeStruct((tokens, inner), BF16),
            jax.ShapeDtypeStruct((tokens, inner), F32),
            jax.ShapeDtypeStruct((chunks * n, inner), BF16),
        ],
        scratch_shapes=[
            pltpu.VMEM((r + 8, conv_width), F32),
            pltpu.VMEM((3 * r, inner), F32),
            pltpu.VMEM((n, inner), F32),
            pltpu.VMEM((r, inner), F32),
            pltpu.VMEM((r, inner), BF16),
            pltpu.VMEM((r, inner), BF16),
            pltpu.VMEM((r, 2 * n), BF16),
            pltpu.VMEM((r, inner), F32),
            pltpu.VMEM((r, inner), F32),
        ],
        compiler_params=pltpu.CompilerParams(
            dimension_semantics=("arbitrary",), vmem_limit_bytes=48 * 2**20
        ),
        name="scan_forward",
    )(p, p, aux, seg_rows, conv_w, conv_b, bias, rate, skip_row, gain_row, e)


def scan_backward(p, aux, seg_rows, y, states, grad_mixed, conv_w, conv_b, bias, rate, skip_row, gain_row, e, et, per_seq):
    tokens, proj = p.shape
    inner, conv_width, heads = gain_row.shape[1], conv_w.shape[1], bias.shape[1]
    taps = conv_w.shape[0]
    n = (conv_width - inner) // 2
    r = CHUNK
    chunks = tokens // r
    back = lambda i: (chunks - 1 - i, 0)
    return pl.pallas_call(
        functools.partial(
            backward_kernel, inner=inner, conv_width=conv_width, heads=heads, width=inner // heads, per_seq=per_seq
        ),
        grid=(chunks,),
        in_specs=[
            pl.BlockSpec((r, proj), back),
            pl.BlockSpec((8, proj), lambda i: (jnp.maximum((chunks - 1 - i) * (r // 8) - 1, 0), 0)),
            pl.BlockSpec((r, 16), back),
            pl.BlockSpec((1, 1, r), lambda i: (chunks - 1 - i, 0, 0)),
            pl.BlockSpec((r, inner), back),
            pl.BlockSpec((n, inner), back),
            pl.BlockSpec((r, inner), back),
            full(conv_w.shape), full(conv_b.shape), full(bias.shape), full(rate.shape),
            full(skip_row.shape), full(gain_row.shape), full(e.shape), full(et.shape),
        ],
        out_specs=[
            pl.BlockSpec((r, proj), back),
            full((8 * taps, conv_width)), full((8, conv_width)), full((8, inner)), full((8, inner)), full((16, heads)),
        ],
        out_shape=[
            jax.ShapeDtypeStruct((tokens, proj), BF16),
            jax.ShapeDtypeStruct((8 * taps, conv_width), F32),
            jax.ShapeDtypeStruct((8, conv_width), F32),
            jax.ShapeDtypeStruct((8, inner), F32),
            jax.ShapeDtypeStruct((8, inner), F32),
            jax.ShapeDtypeStruct((16, heads), F32),
        ],
        scratch_shapes=[
            pltpu.VMEM((r + 8, conv_width), F32),
            pltpu.VMEM((3 * r, inner), F32),
            pltpu.VMEM((n, inner), F32),
            pltpu.VMEM((r, inner), F32),
            pltpu.VMEM((r, inner), BF16),
            pltpu.VMEM((r, inner), BF16),
            pltpu.VMEM((r, 2 * n), BF16),
            pltpu.VMEM((r, conv_width), F32),
            pltpu.VMEM((r, inner), BF16),
            pltpu.VMEM((r, inner), BF16),
            pltpu.VMEM((r, inner), F32),
            pltpu.VMEM((r + 8, conv_width), F32),
            pltpu.VMEM((r, inner), BF16),
            pltpu.VMEM((r, inner), BF16),
            pltpu.VMEM((r, inner), BF16),
            pltpu.VMEM((r, inner), BF16),
        ],
        compiler_params=pltpu.CompilerParams(
            dimension_semantics=("arbitrary",), vmem_limit_bytes=56 * 2**20
        ),
        name="scan_backward",
    )(p, p, aux, seg_rows, y, states, grad_mixed, conv_w, conv_b, bias, rate, skip_row, gain_row, e, et)


def rms_scale(values):
    return lax.rsqrt(jnp.mean(values * values, axis=1, keepdims=True) + EPS)


def on_device(
    tokens,
    norm_gain,
    in_weight,
    conv_weight,
    conv_bias,
    step_bias,
    decay_log,
    skip_gain,
    out_gain,
    out_weight,
    cotangent,
    teacher,
    segment,
    valid_mask,
):
    seqs, length, width = tokens.shape
    rows = seqs * length
    every = ("rep", "fsdp")
    devices = lax.axis_size("rep") * lax.axis_size("fsdp")
    loss_weight = float(rows * devices * width // 8)
    valid = valid_mask.reshape(rows, 1).astype(F32)
    total_count = lax.psum(jnp.sum(valid), every)
    denominator = total_count * width

    inputs = tokens.reshape(rows, width).astype(F32)
    scaled = inputs * rms_scale(inputs)
    normed = (scaled * norm_gain[None, :]).astype(BF16)
    w_in = lax.all_gather(in_weight, "fsdp", axis=0, tiled=True)
    w_out = lax.all_gather(out_weight, "fsdp", axis=0, tiled=True)
    projected = mm(normed, w_in)

    heads = step_bias.shape[0]
    head_width = out_gain.shape[0] // heads
    aux, seg_rows = helpers(segment, CHUNK)
    e, et = head_maps(heads, head_width)
    rate = -jnp.exp(decay_log)[None, :]
    skip_row = jnp.repeat(skip_gain, head_width)[None, :]
    per_seq = length // CHUNK
    params = (conv_weight, conv_bias[None, :], step_bias[None, :], rate, skip_row, out_gain[None, :])
    mixed, y, states = scan_forward(projected, aux, seg_rows, *params, e, per_seq)

    result = inputs + mm(mixed, w_out)
    error = result - teacher.reshape(rows, width).astype(F32)
    squares = jnp.sum(valid * error * error)
    cotan = cotangent.reshape(rows, width).astype(F32)
    grad_result = valid * (cotan + 2.0 * loss_weight * error / denominator)
    grad_branch = grad_result.astype(BF16)
    grad_out = mm_tn(mixed, grad_branch).astype(BF16)
    grad_mixed = mm_nt(grad_branch, w_out)
    grad_projected, dcw, dcb, dgain, dskip, dsmall = scan_backward(
        projected, aux, seg_rows, y, states, grad_mixed, *params, e, et, per_seq
    )
    grad_in = mm_tn(normed, grad_projected).astype(BF16)
    grad_normed = mm_nt(grad_projected, w_in)
    grad_scaled = grad_normed * norm_gain[None, :]
    grad_inputs = rms_scale(inputs) * (
        grad_scaled - scaled * jnp.mean(grad_scaled * scaled, axis=1, keepdims=True)
    )
    grad_tokens = (grad_result + grad_inputs).astype(BF16).reshape(tokens.shape)

    def reduce(grad):
        shard = lax.psum_scatter(grad, "fsdp", scatter_dimension=0, tiled=True)
        return lax.psum(shard, "rep").astype(F32)

    small = (
        jnp.sum(grad_normed * scaled, axis=0),
        jnp.sum(dcw.reshape(conv_weight.shape[0], 8, -1), axis=1),
        jnp.sum(dcb, axis=0),
        jnp.sum(dsmall[:8], axis=0),
        jnp.sum(dsmall[8:], axis=0),
        jnp.sum(dskip, axis=0).reshape(heads, head_width).sum(axis=1),
        jnp.sum(dgain, axis=0),
        squares,
    )
    summed = lax.psum(small, every)
    return (
        result.astype(BF16).reshape(tokens.shape),
        summed[7] / denominator,
        grad_tokens,
        summed[0],
        reduce(grad_in),
        summed[1],
        summed[2],
        summed[3],
        summed[4],
        summed[5],
        summed[6],
        reduce(grad_out),
    )


def solution(mesh):
    tokens = P(("rep", "fsdp"), None, None)
    marks = P(("rep", "fsdp"), None)
    shard = P("fsdp", None)
    return jax.shard_map(
        on_device,
        mesh=mesh,
        in_specs=(tokens, P(), shard, P(), P(), P(), P(), P(), P(), shard, tokens, tokens, marks, marks),
        out_specs=(tokens, P(), tokens, P(), shard, P(), P(), P(), P(), P(), P(), shard),
        check_vma=False,
    )
```

```python
import functools

import jax
import jax.numpy as jnp
from jax import lax
from jax.experimental import pallas as pl
from jax.experimental.pallas import tpu as pltpu
from jax.sharding import PartitionSpec as P

CHUNK = 128
LANES = 128
EPS = 1e-05
F32 = jnp.float32
BF16 = jnp.bfloat16
NT = (((1,), (1,)), ((), ()))
TN = (((0,), (0,)), ((), ()))


def mm(a, b):
    return jnp.dot(a, b, preferred_element_type=F32)


def mm_nt(a, b):
    return lax.dot_general(a, b, NT, preferred_element_type=F32)


def mm_tn(a, b):
    return lax.dot_general(a, b, TN, preferred_element_type=F32)


def split2(v):
    high = v.astype(BF16)
    return high, (v - high.astype(F32)).astype(BF16)


def split3(v):
    high = v.astype(BF16)
    rest = v - high.astype(F32)
    mid = rest.astype(BF16)
    return high, mid, (rest - mid.astype(F32)).astype(BF16)


def tri_sum(tri, v):
    heads = v.shape[1]
    parts = mm(tri, jnp.concatenate(split3(v), axis=1))
    return parts[:, :heads] + parts[:, heads : 2 * heads] + parts[:, 2 * heads :]


def sigmoid(v):
    return 0.5 * jnp.tanh(0.5 * v) + 0.5


def softplus(v):
    return jnp.maximum(v, 0.0) + jnp.log1p(jnp.exp(-jnp.abs(v)))


def iota(shape, dim):
    return lax.broadcasted_iota(jnp.int32, shape, dim)


def small_terms(step_raw, step_bias, decay_rate, keep, to_end, rows):
    shifted = step_raw + step_bias
    step = softplus(shifted)
    lower = (iota((rows, rows), 0) >= iota((rows, rows), 1)).astype(BF16)
    cum = tri_sum(lower, step * decay_rate)
    last = cum[rows - 1 : rows, :]
    return shifted, step, cum, jnp.exp(cum) * keep, jnp.exp(last - cum) * to_end


def expand(e_ref, out_ref, step, from_prev, to_end):
    stacked = jnp.concatenate(
        [jnp.concatenate(split2(v), axis=1) for v in (step, from_prev, to_end)], axis=0
    )
    out_ref[...] = mm(stacked, e_ref[...])


def conv_tile(xbuf, cw_ref, cb_ref, marks, cols, rows):
    taps = cw_ref.shape[0]
    pre = cb_ref[:, cols] + cw_ref[0:1, cols] * xbuf[8 : 8 + rows, cols]
    for k in range(1, taps):
        pre = pre + (cw_ref[k : k + 1, cols] * xbuf[8 - k : 8 - k + rows, cols]) * marks[k]
    return pre


def forward_kernel(
    p_ref, prev_ref, aux_ref, seg_ref, cw_ref, cb_ref, bias_ref, rate_ref, skip_ref, gain_ref, e_ref,
    mixed_ref, y_ref, state_out_ref,
    xbuf, ex, state, xs, xdt, xe, bc, yin, gs,
    *, inner, conv_width, heads, width, per_seq,
):
    rows = p_ref.shape[0]
    n = (conv_width - inner) // 2
    tiles = inner // LANES
    conv_tiles = conv_width // LANES

    @pl.when(lax.rem(pl.program_id(0), per_seq) == 0)
    def _():
        state[...] = jnp.zeros_like(state)

    aux = aux_ref[...]
    keep, to_end_mask = aux[:, 7:8], aux[:, 8:9]
    shifted, step, cum, from_prev, to_end = small_terms(
        p_ref[:, inner + conv_width :], bias_ref[...], rate_ref[...], keep, to_end_mask, rows
    )
    expand(e_ref, ex, step, from_prev, to_end)
    cum_t = cum.T
    xbuf[0:8, :] = prev_ref[:, inner : inner + conv_width]
    xbuf[8 : 8 + rows, :] = p_ref[:, inner : inner + conv_width]
    marks = [None] + [jnp.broadcast_to(aux[:, k : k + 1], (rows, LANES)) for k in range(1, cw_ref.shape[0])]
    for c in range(conv_tiles):
        cols = slice(c * LANES, (c + 1) * LANES)
        pre = conv_tile(xbuf, cw_ref, cb_ref, marks, cols, rows)
        act = pre * sigmoid(pre)
        if c < tiles:
            xs[:, cols] = act
            scaled = act * ex[0:rows, cols]
            xdt[:, cols] = scaled.astype(BF16)
            xe[:, cols] = (scaled * ex[2 * rows : 3 * rows, cols]).astype(BF16)
        else:
            bc[:, (c - tiles) * LANES : (c - tiles + 1) * LANES] = act.astype(BF16)
    b, cc = bc[:, :n], bc[:, n:]
    causal = (iota((rows, rows), 0) >= iota((rows, rows), 1)) & (aux[:, 0:1] == seg_ref[0])
    scores = jnp.where(causal, mm_nt(cc, b), 0.0)
    state_low = state[...].astype(BF16)
    state_out_ref[...] = state_low
    yin[...] = mm(cc, state_low)
    state[...] = state[...] * ex[2 * rows - 1 : 2 * rows, :] + mm_tn(b, xe[...])
    lane = iota((1, LANES), 1)
    masks = [(lane < width).astype(BF16), (lane >= width).astype(BF16)]
    total = jnp.zeros((rows, LANES), F32)
    for c in range(tiles):
        cols = slice(c * LANES, (c + 1) * LANES)
        mixing = []
        for h in (2 * c, 2 * c + 1):
            spread = jnp.minimum(cum[:, h : h + 1] - cum_t[h : h + 1, :], 0.0)
            mixing.append((scores * jnp.exp(spread)).astype(BF16))
        x_low = xdt[:, cols]
        y = mm(
            jnp.concatenate(mixing, axis=1), jnp.concatenate([x_low * masks[0], x_low * masks[1]], axis=0)
        ) + ex[rows : 2 * rows, cols] * yin[:, cols]
        y = y + skip_ref[:, cols] * xs[:, cols]
        y_ref[:, cols] = y
        gate = p_ref[:, cols]
        gated = y * (gate * sigmoid(gate))
        gs[:, cols] = gated
        total = total + gated * gated
    inverse = lax.rsqrt(jnp.sum(total, axis=1, keepdims=True) / inner + EPS)
    for c in range(tiles):
        cols = slice(c * LANES, (c + 1) * LANES)
        mixed_ref[:, cols] = (gs[:, cols] * inverse * gain_ref[:, cols]).astype(BF16)


def helpers(segment, chunk):
    seqs, length = segment.shape
    blocks = length // chunk
    def same(shift):
        return (segment[:, shift:] == segment[:, :-shift]).astype(F32)
    back = [jnp.pad(same(k), ((0, 0), (k, 0))) for k in (1, 2, 3)]
    ahead = [jnp.pad(same(k), ((0, 0), (0, k))) for k in (1, 2, 3)]
    by_block = segment.reshape(seqs, blocks, chunk)
    ends = by_block[:, :, -1]
    before = jnp.pad(ends[:, :-1], ((0, 0), (1, 0)), constant_values=-1)
    keep = (by_block == before[:, :, None]).astype(F32).reshape(seqs, length)
    to_end = (by_block == ends[:, :, None]).astype(F32).reshape(seqs, length)
    docs = segment.astype(F32)
    columns = [docs, *back, *ahead, keep, to_end] + [jnp.zeros_like(docs)] * 7
    aux = jnp.stack(columns, axis=-1).reshape(seqs * length, 16)
    return aux, docs.reshape(seqs * blocks, 1, chunk)


def head_maps(heads, width):
    inner = heads * width
    owner = jnp.arange(inner) // width
    one = (jnp.arange(heads)[:, None] == owner[None, :]).astype(BF16)
    down = (owner[:, None] == jnp.arange(LANES)[None, :]).astype(BF16)
    return jnp.concatenate([one, one], axis=0), down


def full(shape):
    return pl.BlockSpec(shape, lambda i: (0,) * len(shape))


def scan_forward(p, aux, seg_rows, conv_w, conv_b, bias, rate, skip_row, gain_row, e, per_seq):
    tokens, proj = p.shape
    inner, conv_width, heads = gain_row.shape[1], conv_w.shape[1], bias.shape[1]
    n = (conv_width - inner) // 2
    r = CHUNK
    chunks = tokens // r
    return pl.pallas_call(
        functools.partial(
            forward_kernel, inner=inner, conv_width=conv_width, heads=heads, width=inner // heads, per_seq=per_seq
        ),
        grid=(chunks,),
        in_specs=[
            pl.BlockSpec((r, proj), lambda i: (i, 0)),
            pl.BlockSpec((8, proj), lambda i: (jnp.maximum(i * (r // 8) - 1, 0), 0)),
            pl.BlockSpec((r, 16), lambda i: (i, 0)),
            pl.BlockSpec((1, 1, r), lambda i: (i, 0, 0)),
            full(conv_w.shape), full(conv_b.shape), full(bias.shape), full(rate.shape),
            full(skip_row.shape), full(gain_row.shape), full(e.shape),
        ],
        out_specs=[
            pl.BlockSpec((r, inner), lambda i: (i, 0)),
            pl.BlockSpec((r, inner), lambda i: (i, 0)),
            pl.BlockSpec((n, inner), lambda i: (i, 0)),
        ],
        out_shape=[
            jax.ShapeDtypeStruct((tokens, inner), BF16),
            jax.ShapeDtypeStruct((tokens, inner), F32),
            jax.ShapeDtypeStruct((chunks * n, inner), BF16),
        ],
        scratch_shapes=[
            pltpu.VMEM((r + 8, conv_width), F32),
            pltpu.VMEM((3 * r, inner), F32),
            pltpu.VMEM((n, inner), F32),
            pltpu.VMEM((r, inner), F32),
            pltpu.VMEM((r, inner), BF16),
            pltpu.VMEM((r, inner), BF16),
            pltpu.VMEM((r, 2 * n), BF16),
            pltpu.VMEM((r, inner), F32),
            pltpu.VMEM((r, inner), F32),
        ],
        compiler_params=pltpu.CompilerParams(
            dimension_semantics=("arbitrary",), vmem_limit_bytes=48 * 2**20
        ),
        name="scan_forward",
    )(p, p, aux, seg_rows, conv_w, conv_b, bias, rate, skip_row, gain_row, e)


def gate_kernel(gate_ref, ssd_ref, gm_ref, gain_ref, dy_ref, dz_ref, dgain_ref):
    rows, inner = gate_ref.shape

    @pl.when(pl.program_id(0) == 0)
    def _():
        dgain_ref[...] = jnp.zeros_like(dgain_ref)

    squares = jnp.zeros((rows, LANES), F32)
    cross = jnp.zeros((rows, LANES), F32)
    for c in range(inner // LANES):
        cols = slice(c * LANES, (c + 1) * LANES)
        gate = gate_ref[:, cols]
        gated = ssd_ref[:, cols] * (gate * sigmoid(gate))
        squares = squares + gated * gated
        cross = cross + gm_ref[:, cols] * gain_ref[:, cols] * gated
    inverse = lax.rsqrt(jnp.sum(squares, axis=1, keepdims=True) / inner + EPS)
    mean_cross = jnp.sum(cross, axis=1, keepdims=True) / inner * inverse
    for c in range(inner // LANES):
        cols = slice(c * LANES, (c + 1) * LANES)
        gate = gate_ref[:, cols]
        sig = sigmoid(gate)
        silu = gate * sig
        ssd = ssd_ref[:, cols]
        unit = ssd * silu * inverse
        grad_mixed = gm_ref[:, cols]
        dgain_ref[:, cols] += jnp.sum((grad_mixed * unit).reshape(rows // 8, 8, LANES), axis=0)
        grad_gated = inverse * (grad_mixed * gain_ref[:, cols] - unit * mean_cross)
        dy_ref[:, cols] = (grad_gated * silu).astype(BF16)
        dz_ref[:, cols] = (grad_gated * ssd * (sig + silu * (1.0 - sig))).astype(BF16)


def gate_back(p, ssd, gm, gain_row):
    tokens, inner = ssd.shape
    r = CHUNK
    block = pl.BlockSpec((r, inner), lambda i: (i, 0))
    return pl.pallas_call(
        gate_kernel,
        grid=(tokens // r,),
        in_specs=[block, block, block, full(gain_row.shape)],
        out_specs=[block, block, full((8, inner))],
        out_shape=[
            jax.ShapeDtypeStruct((tokens, inner), BF16),
            jax.ShapeDtypeStruct((tokens, inner), BF16),
            jax.ShapeDtypeStruct((8, inner), F32),
        ],
        compiler_params=pltpu.CompilerParams(dimension_semantics=("arbitrary",), vmem_limit_bytes=32 * 2**20),
        name="gate_backward",
    )(p, ssd, gm, gain_row)


MESH = pl.DeviceIdType.MESH


class Spot:
    def __init__(self, levels):
        self.rep, self.at = lax.axis_index("rep"), lax.axis_index("fsdp")
        self.core, self.side, self.level = self.at % 2, (self.at // 2) % 2, self.at // 4
        self.levels = levels
        self.sibling = (self.rep, self.at + 1 - 2 * self.core)
        self.across = (self.rep, self.at + 2 - 4 * self.side)
        self.twin = (1 - self.rep, self.at)

    def far(self, step):
        return (self.rep, ((self.level + step) % self.levels) * 4 + self.at % 4)

    def greet(self):
        barrier = pltpu.get_barrier_semaphore()
        partners = [self.sibling, self.across, self.twin] + [self.far(d) for d in range(1, self.levels)]
        for one in partners:
            pl.semaphore_signal(barrier, inc=1, device_id=one, device_id_type=MESH)
        pl.semaphore_wait(barrier, len(partners))


def send(src, dst, send_sem, recv_sem, device):
    return pltpu.make_async_remote_copy(
        src_ref=src, dst_ref=dst, send_sem=send_sem, recv_sem=recv_sem, device_id=device, device_id_type=MESH
    )


class Unit:
    def __init__(self, spot, whole, own, from_core, from_side, from_level, mine, from_twin, sems, local, write):
        self.spot, self.whole, self.own, self.local, self.write = spot, whole, own, local, write
        self.from_core, self.from_side, self.from_level = from_core, from_side, from_level
        self.mine, self.from_twin = mine, from_twin
        self.sems = sems

    @property
    def c0(self):
        return pltpu.make_async_copy(self.whole.at[:, :, self.spot.core], self.own, self.sems.at[6])

    @property
    def c1(self):
        spot, sems = self.spot, self.sems
        return send(self.whole.at[:, :, 1 - spot.core], self.from_core, sems.at[0], sems.at[1], spot.sibling)

    @property
    def c2(self):
        spot, sems = self.spot, self.sems
        return send(self.own.at[:, 1 - spot.side], self.from_side, sems.at[2], sems.at[3], spot.across)

    @property
    def c3(self):
        spot, sems = self.spot, self.sems
        return [
            send(
                self.from_side.at[(spot.level + d) % spot.levels], self.from_level.at[d - 1],
                sems.at[5 + 2 * d], sems.at[6 + 2 * d], spot.far(d),
            )
            for d in range(1, spot.levels)
        ]

    @property
    def c4(self):
        spot, sems = self.spot, self.sems
        return send(self.mine, self.from_twin, sems.at[4], sems.at[5], spot.twin)

    def stage(self, number):
        spot, levels = self.spot, self.spot.levels
        if number == 1:
            self.c1.start()
            self.c0.start()
        elif number == 2:
            self.c0.wait()
            self.c1.wait()

            def add(i, carry):
                for side in range(2):
                    self.own[i, side] = (
                        self.own[i, side].astype(F32) + self.from_core[i, side].astype(F32)
                    ).astype(BF16)
                return carry

            lax.fori_loop(0, levels, add, 0)
            self.c2.start()
        elif number == 3:
            self.c2.wait()

            def add(i, carry):
                self.from_side[i] = (
                    self.from_side[i].astype(F32) + self.own[i, spot.side].astype(F32)
                ).astype(BF16)
                return carry

            lax.fori_loop(0, levels, add, 0)
            for copy in self.c3:
                copy.start()
        elif number == 4:
            for copy in self.c3:
                copy.wait()
            total = self.from_side[spot.level].astype(F32)
            for d in range(levels - 1):
                total = total + self.from_level[d].astype(F32)
            self.mine[...] = total.astype(BF16)
            self.c4.start()
        else:
            self.c4.wait()
            self.write(self.mine[...].astype(F32) + self.from_twin[...].astype(F32))


GROUPS = 4
BACKGROUND_STARTS = (0, 2, 5, 7, 11, 13, 18, 21)


def back_kernel(
    px_ref, prev_ref, ssd_ref, dy_ref, state_ref,
    tail_ref, aux_ref, seg_ref, cw_ref, cb_ref, bias_ref, rate_ref, skip_ref, e_ref, et_ref,
    ngain_ref, dgain_ref, square_ref,
    normed_t_hbm, wx_hbm, gn_hbm, tokens_hbm, gb_hbm, ggate_hbm, gout_hbm,
    gi_ref, go_ref, gt_ref, small_ref,
    xbuf, ex, adj, xs, xdt, xe, bc, slope, dye, dxi, dbuf, r1, r1l, r2, r3,
    tbuf, consts, stacks, raws, cums, scores, dscores, gbs, gcs, sums, tslope, gp, gpt, accum, taccum,
    normed_t, wx, gn, tokens, gb,
    own, part, part_t, own_t, from_core, from_core_t, from_side, from_side_t, from_level, from_level_t,
    mine, mine_t, twin, twin_t, sm, smr, smz, sems, small_sems, load_sems,
    *, inner, heads, width, levels, seq_chunks,
):
    group, turn = pl.program_id(0), pl.program_id(1)
    step = group * seq_chunks + turn
    chunk = seq_chunks - 1 - turn
    rows, cols_g = px_ref.shape
    n = bc.shape[2] // 2
    tiles = cols_g // LANES
    per_group = cols_g // width
    taps = cw_ref.shape[0]
    tail_cols = tail_ref.shape[1]
    conv_tail = 2 * n
    here = pl.ds(pl.multiple_of(chunk * rows, rows), rows)
    spot = Spot(levels)
    gcol = pl.multiple_of(group * cols_g, cols_g)
    rows_f = mine.shape[1]

    def loads():
        pairs = ((normed_t_hbm, normed_t), (wx_hbm, wx), (gn_hbm, gn), (tokens_hbm, tokens), (gb_hbm, gb))
        return [pltpu.make_async_copy(a, b, load_sems.at[i]) for i, (a, b) in enumerate(pairs)]

    units = []

    def writer(ref, row, col, wide):
        def write(v):
            ref[row : row + rows_f, col : col + wide] = v[:, :wide]
        return write

    for u in range(GROUPS * 2):
        if u < GROUPS:
            hbm = gout_hbm.at[:, :, :, pl.ds((u // 2) * rows_f, rows_f), pl.ds((u % 2) * cols_g, cols_g)]
            write = writer(go_ref, (u // 2) * rows_f, (u % 2) * cols_g, cols_g)
        else:
            hbm = ggate_hbm.at[:, :, :, :, pl.ds((u - GROUPS) * cols_g, cols_g)]
            write = writer(gi_ref, 0, (u - GROUPS) * cols_g, cols_g)
        units.append((u, hbm, own.at[u], write))
    for g in range(GROUPS):
        u = 2 * GROUPS + g
        units.append((u, part.at[g % 2], own.at[u], writer(gi_ref, 0, inner + g * cols_g, cols_g)))
    units = [
        Unit(
            spot, whole, mine_half, from_core.at[u], from_side.at[u], from_level.at[u], mine.at[u], twin.at[u],
            sems.at[u], True, write,
        )
        for u, whole, mine_half, write in units
    ]
    tail_wide = gi_ref.shape[1] - 2 * inner
    tail_unit = Unit(
        spot, part_t, own_t, from_core_t, from_side_t, from_level_t, mine_t, twin_t, sems.at[3 * GROUPS], True,
        writer(gi_ref, 0, 2 * inner, tail_wide),
    )

    events = {}
    last_step = GROUPS * seq_chunks - 1
    late = []
    plan = [(s * seq_chunks // 8, units[u]) for u, s in enumerate(BACKGROUND_STARTS)]
    plan += [((g + 1) * seq_chunks, units[2 * GROUPS + g]) for g in range(GROUPS - 1)]
    for begin, unit in plan:
        for number, delay in ((1, 0), (2, 1), (3, 4), (4, 7), (5, 8)):
            events.setdefault(min(begin + delay, last_step), []).append((unit, number))

    @pl.when(step == 0)
    def _():
        for copy in loads():
            copy.start()
        spot.greet()
        accum[...] = jnp.zeros_like(accum)
        taccum[...] = jnp.zeros_like(taccum)
        cums[...] = jnp.zeros_like(cums)

    for at, happen in sorted(events.items()):
        if at == last_step:
            late += happen
            continue

        @pl.when(step == at)
        def _(happen=happen):
            for unit, number in sorted(happen, key=lambda pair: -pair[1]):
                unit.stage(number)

    def fold(v):
        return jnp.sum(v.reshape(rows // 8, 8, v.shape[1]), axis=0)

    aux = aux_ref[here, :]
    marks = [None] + [jnp.broadcast_to(aux[:, k : k + 1], (rows, LANES)) for k in range(1, taps)]
    marks_next = [None] + [jnp.broadcast_to(aux[:, 3 + k : 4 + k], (rows, LANES)) for k in range(1, taps)]
    lower = iota((rows, rows), 0) >= iota((rows, rows), 1)
    upper = iota((rows, rows), 0) <= iota((rows, rows), 1)
    rate = rate_ref[...]

    def conv_pre(buffer, cols, wcols):
        pre = cb_ref[:, wcols] + cw_ref[0:1, wcols] * buffer[8 : 8 + rows, cols]
        for k in range(1, taps):
            pre = pre + (cw_ref[k : k + 1, wcols] * buffer[8 - k : 8 - k + rows, cols]) * marks[k]
        return pre

    def conv_back(buffer, cols, wcols, acc, acc_cols):
        grad = buffer[0:rows, cols]
        out = cw_ref[0:1, wcols] * grad
        acc[8 * taps : 8 * taps + 8, acc_cols] += fold(grad)
        acc[0:8, acc_cols] += fold(grad * xbuf[8 : 8 + rows, cols])
        for k in range(1, taps):
            out = out + (cw_ref[k : k + 1, wcols] * buffer[k : k + rows, cols]) * marks_next[k]
            acc[8 * k : 8 * k + 8, acc_cols] += fold(grad * (xbuf[8 - k : 8 - k + rows, cols] * marks[k]))
        return out

    def fill_tail():
        xbuf[8 : 8 + rows, 0:conv_tail] = tail_ref[here, 0:conv_tail]
        before = pl.ds(pl.multiple_of(jnp.maximum(chunk * rows - 8, 0), 8), 8)
        xbuf[0:8, 0:conv_tail] = tail_ref[before, 0:conv_tail]

    @pl.when(group == 0)
    def _():
        shifted, step_size, cum, from_prev, to_end = small_terms(
            tail_ref[here, conv_tail : conv_tail + heads], bias_ref[...], rate, aux[:, 7:8], aux[:, 8:9], rows
        )
        raws[here, 0:heads] = shifted
        raws[here, heads : 2 * heads] = step_size
        cums[chunk, :, 0:heads] = cum
        stacks[chunk] = jnp.concatenate(
            [jnp.concatenate(split2(v), axis=1) for v in (step_size, from_prev, to_end)], axis=0
        )
        fill_tail()
        for c in range(conv_tail // LANES):
            cols = slice(c * LANES, (c + 1) * LANES)
            pre = conv_pre(xbuf, cols, slice(inner + c * LANES, inner + (c + 1) * LANES))
            sig = sigmoid(pre)
            act = pre * sig
            tslope[here, cols] = sig + act * (1.0 - sig)
            bc[chunk, :, cols] = act.astype(BF16)
        same = upper & (aux[:, 0:1] == seg_ref[chunk])
        scores[chunk] = jnp.where(same, mm_nt(bc[chunk, :, 0:n], bc[chunk, :, n:]), 0.0)
        dscores[chunk] = jnp.zeros((rows, rows), F32)
        gbs[here, :] = jnp.zeros((rows, n), F32)
        gcs[here, :] = jnp.zeros((rows, n), F32)
        consts[chunk] = jnp.zeros((8, LANES), F32)
        for i in range(3):
            sums[i, here, :] = jnp.zeros((rows, LANES), F32)

    @pl.when(turn == 0)
    def _():
        adj[...] = jnp.zeros_like(adj)
        dbuf[rows : rows + 8, :] = jnp.zeros((8, cols_g), F32)

    ex[...] = mm(stacks[chunk], e_ref[:, pl.ds(gcol, cols_g)])
    head0 = group * per_group
    pick = (iota((LANES, LANES), 0) == iota((LANES, LANES), 1) + head0).astype(BF16)
    cum_all = cums[chunk]
    moved = [mm(v, pick) for v in split3(cum_all)]
    cum = moved[0] + moved[1] + moved[2]
    cum_t = cum.T
    xbuf[0:8, :] = prev_ref[...]
    xbuf[8 : 8 + rows, :] = px_ref[...]
    for c in range(tiles):
        cols = slice(c * LANES, (c + 1) * LANES)
        wcols = pl.ds(gcol + c * LANES, LANES)
        pre = conv_pre(xbuf, cols, wcols)
        sig = sigmoid(pre)
        act = pre * sig
        slope[:, cols] = sig + act * (1.0 - sig)
        xs[:, cols] = act
        scaled = act * ex[0:rows, cols]
        xdt[:, cols] = scaled.astype(BF16)
        xe[:, cols] = (scaled * ex[2 * rows : 3 * rows, cols]).astype(BF16)
        dye[:, cols] = (dy_ref[:, cols].astype(F32) * ex[rows : 2 * rows, cols]).astype(BF16)
    b, cc = bc[chunk, :, 0:n], bc[chunk, :, n:]
    state_low = state_ref[...]
    adj_low = adj[...].astype(BF16)
    carry = ex[2 * rows - 1 : 2 * rows, :]
    gcs[here, :] += mm_nt(dye[...], state_low)
    gbs[here, :] += mm_nt(xe[...], adj_low)
    dxi[...] = mm(b, adj_low)
    through = jnp.sum(adj[...] * state_low.astype(F32), axis=0, keepdims=True) * carry
    adj[...] = adj[...] * carry + mm_tn(cc, dye[...])
    scores_t = scores[chunk]
    lane = iota((1, LANES), 1)
    masks = [(lane < width).astype(BF16), (lane >= width).astype(BF16)]
    grad_scores_t = jnp.zeros((rows, rows), F32)
    for c in range(tiles):
        cols = slice(c * LANES, (c + 1) * LANES)
        acols = pl.ds(gcol + c * LANES, LANES)
        x_low, dy_low = xdt[:, cols], dy_ref[:, cols]
        grad_mix = mm_nt(jnp.concatenate([x_low * masks[0], x_low * masks[1]], axis=0), dy_low)
        mixing = []
        for i, h in enumerate((2 * c, 2 * c + 1)):
            decay = jnp.exp(jnp.minimum(cum_t[h : h + 1, :] - cum[:, h : h + 1], 0.0))
            mixing.append((scores_t * decay).astype(BF16))
            grad_scores_t = grad_scores_t + grad_mix[i * rows : (i + 1) * rows] * decay
        within = mm(
            jnp.concatenate(mixing, axis=1), jnp.concatenate([dy_low * masks[0], dy_low * masks[1]], axis=0)
        )
        x = xs[:, cols]
        skip = skip_ref[:, acols]
        across = ex[2 * rows : 3 * rows, cols] * dxi[:, cols]
        both = within + across
        grad_ssd = dy_low.astype(F32)
        x_scaled = x_low.astype(F32)
        r1[:, cols], r1l[:, cols] = split2(grad_ssd * (ssd_ref[:, cols] - skip * x) - within * x_scaled)
        r2[:, cols] = (across * x_scaled).astype(BF16)
        r3[:, cols] = (both * x).astype(BF16)
        accum[8 * taps + 8 : 8 * taps + 16, acols] += fold(grad_ssd * x)
        grad_x = skip * grad_ssd + ex[0:rows, cols] * both
        dbuf[0:rows, cols] = grad_x * slope[:, cols]
    dscores[chunk] += grad_scores_t
    et = et_ref[pl.ds(gcol, cols_g), :]
    sums[0, here, :] += mm(r1[...], et) + mm(r1l[...], et)
    sums[1, here, :] += mm(r2[...], et)
    sums[2, here, :] += mm(r3[...], et)
    high, rest = split2(jnp.broadcast_to(through, (8, cols_g)))
    consts[chunk] += mm(high, et) + mm(rest, et)
    for c in range(tiles):
        cols = slice(c * LANES, (c + 1) * LANES)
        acols = pl.ds(gcol + c * LANES, LANES)
        gp[here, cols] = conv_back(dbuf, cols, acols, accum, acols).astype(BF16)
    dbuf[rows : rows + 8, :] = dbuf[0:8, :]

    @pl.when(group == GROUPS - 1)
    def _():
        same = upper & (aux[:, 0:1] == seg_ref[chunk])
        grad_scores = jnp.where(same, dscores[chunk], 0.0).astype(BF16)
        grad_b = gbs[here, :] + mm(grad_scores, cc)
        grad_c = gcs[here, :] + mm_tn(grad_scores, b)
        fill_tail()

        @pl.when(turn == 0)
        def _():
            tbuf[rows : rows + 8, :] = jnp.zeros((8, 2 * n), F32)

        tbuf[0:rows, 0:n] = grad_b * tslope[here, 0:n]
        tbuf[0:rows, n : 2 * n] = grad_c * tslope[here, n : 2 * n]
        for c in range(conv_tail // LANES):
            cols = slice(c * LANES, (c + 1) * LANES)
            gpt[here, cols] = conv_back(
                tbuf, cols, slice(inner + c * LANES, inner + (c + 1) * LANES), taccum, cols
            ).astype(BF16)
        tbuf[rows : rows + 8, :] = tbuf[0:8, :]
        shifted = raws[here, 0:heads]
        step_size = raws[here, heads : 2 * heads]
        const = consts[chunk, 0:1, 0:heads]
        grad_log = (
            tri_sum(upper.astype(BF16), sums[0, here, 0:heads])
            + tri_sum((iota((rows, rows), 0) > iota((rows, rows), 1)).astype(BF16), sums[1, here, 0:heads])
            + const
        ) * aux[:, 1:2]
        grad_raw = (sums[2, here, 0:heads] + rate * grad_log) * sigmoid(shifted)
        gpt[here, conv_tail:] = jnp.concatenate(
            [grad_raw, jnp.zeros((rows, tail_cols - conv_tail - heads), F32)], axis=1
        ).astype(BF16)
        small = 8 * taps + 8
        taccum[small : small + 8, 0:heads] += fold(grad_raw)
        taccum[small : small + 8, LANES : LANES + heads] += fold(step_size * grad_log * rate)

    def weight_grad(low, out):
        def one(i, carry):
            block = pl.ds(pl.multiple_of(i * 4 * rows_f, 4 * rows_f), 4 * rows_f)
            v = mm(normed_t[block, :], low[...]).astype(BF16)
            for side in range(2):
                for core in range(2):
                    at = (2 * side + core) * rows_f
                    out[i, side, core] = v[at : at + rows_f]
            return carry

        lax.fori_loop(0, levels, one, 0)

    def input_grad(low, weights):
        def one(i, carry):
            block = pl.ds(pl.multiple_of(i * 256, 256), 256)
            gn[block, :] += mm_nt(low[block, :], weights[...])
            return carry

        lax.fori_loop(0, gn.shape[0] // 256, one, 0)

    for g in range(GROUPS - 1):

        @pl.when(step == (g + 1) * seq_chunks - 1)
        def _(g=g):
            if g == 0:
                for copy in loads():
                    copy.wait()
            weight_grad(gp, part.at[g % 2])
            input_grad(gp, wx.at[:, g * cols_g : (g + 1) * cols_g])

    @pl.when(step == last_step)
    def _():
        for unit, number in sorted(late, key=lambda pair: pair[1]):
            unit.stage(number)
        last = units[3 * GROUPS - 1]
        weight_grad(gpt, part_t)
        tail_unit.stage(1)
        weight_grad(gp, part.at[(GROUPS - 1) % 2])
        last.stage(1)
        input_grad(gpt, wx.at[:, inner : inner + tail_cols])
        tail_unit.stage(2)
        input_grad(gp, wx.at[:, (GROUPS - 1) * cols_g : GROUPS * cols_g])
        last.stage(2)
        d = gn.shape[1]
        ngain = ngain_ref[...]

        def block_norm(i, total):
            block = pl.ds(pl.multiple_of(i * 64, 64), 64)
            v = tokens[block, :].astype(F32)
            rinv = lax.rsqrt(jnp.sum(v * v, axis=1, keepdims=True) / d + EPS)
            scaled = v * rinv
            grad = gn[block, :]
            total = total + jnp.sum((grad * scaled).reshape(8, 8, d), axis=0)
            grad = grad * ngain
            mean = jnp.sum(grad * scaled, axis=1, keepdims=True) / d
            gb[block, :] = (gb[block, :].astype(F32) + rinv * (grad - scaled * mean)).astype(BF16)
            return total

        dnorm = lax.fori_loop(0, gn.shape[0] // 64, block_norm, jnp.zeros((8, d), F32))
        leave = pltpu.make_async_copy(gb, gt_ref, load_sems.at[5])
        leave.start()

        def one_row(v):
            return jnp.sum(v, axis=0, keepdims=True)

        local = sm.at[0]
        local[...] = jnp.zeros(local.shape, F32)
        for k in range(taps + 1):
            local[k : k + 1, 0:inner] = one_row(accum[8 * k : 8 * k + 8, :])
            local[k : k + 1, inner : inner + conv_tail] = one_row(taccum[8 * k : 8 * k + 8, 0:conv_tail])
        local[5:6, 0:inner] = one_row(dgain_ref[...])
        local[6:7, 0:inner] = one_row(accum[8 * taps + 8 : 8 * taps + 16, :])
        local[7:8, 0:d] = one_row(dnorm)
        small = 8 * taps + 8
        local[7:8, d : d + conv_tail] = one_row(taccum[small : small + 8, 0:conv_tail])
        local[7:8, d + conv_tail : d + conv_tail + LANES] = one_row(square_ref[...])
        exchange = [
            send(sm.at[i], smr.at[i], small_sems.at[2 * i], small_sems.at[2 * i + 1], device)
            for i, device in enumerate((spot.sibling, spot.across, spot.twin))
        ]
        spread = [
            send(sm.at[3], smz.at[spot.level], small_sems.at[4 + 2 * d], small_sems.at[5 + 2 * d], spot.far(d))
            for d in range(1, levels)
        ]

        def fold_small(i):
            exchange[i].wait()
            sm[i + 1] = sm[i] + smr[i]

        exchange[0].start()
        tail_unit.stage(3)
        fold_small(0)
        exchange[1].start()
        last.stage(3)
        fold_small(1)
        exchange[2].start()
        tail_unit.stage(4)
        fold_small(2)
        for copy in spread:
            copy.start()
        smz[spot.level] = sm[3]
        last.stage(4)
        tail_unit.stage(5)
        for copy in spread:
            copy.wait()
        total = smz[0]
        for i in range(1, levels):
            total = total + smz[i]
        small_ref[...] = total
        last.stage(5)
        leave.wait()


def back(
    px, px_block, tail, ssd, dy, states, aux, seg_rows, conv_w, conv_b, bias, rate, skip_row, e, et,
    norm_gain, dgain, squares, normed_t, wx, gn, tokens, gb, ggate, gout, proj,
):
    length, inner = ssd.shape
    heads = bias.shape[1]
    levels, rows_f = ggate.shape[0], ggate.shape[3]
    taps = conv_w.shape[0]
    n = (conv_w.shape[1] - inner) // 2
    r = CHUNK
    chunks = length // r
    wide = inner // GROUPS
    tcols = tail.shape[1]
    d = normed_t.shape[0]
    small_cols = inner + tcols
    units = 3 * GROUPS
    back_at = lambda off: lambda g, c: (chunks - 1 - c, g + off)
    whole = lambda a: pl.BlockSpec(a.shape, lambda g, c: (0,) * a.ndim, pipeline_mode=pl.Buffered(1))
    anywhere = pl.BlockSpec(memory_space=pl.ANY)
    vm = pltpu.VMEM
    out = lambda s: pl.BlockSpec(s, lambda g, c: (0,) * len(s))
    return pl.pallas_call(
        functools.partial(
            back_kernel, inner=inner, heads=heads, width=inner // heads, levels=levels, seq_chunks=chunks
        ),
        grid=(GROUPS, chunks),
        in_specs=[
            pl.BlockSpec((r, wide), back_at(px_block)),
            pl.BlockSpec((8, wide), lambda g, c: (jnp.maximum((chunks - 1 - c) * (r // 8) - 1, 0), g + px_block)),
            pl.BlockSpec((r, wide), back_at(0)),
            pl.BlockSpec((r, wide), back_at(0)),
            pl.BlockSpec((n, wide), back_at(0)),
            *[whole(a) for a in (tail, aux, seg_rows, conv_w, conv_b, bias, rate, skip_row, e, et, norm_gain, dgain, squares)],
            *[anywhere] * 7,
        ],
        out_specs=[out((rows_f, proj)), out((2 * rows_f, d)), anywhere, out((8, small_cols))],
        out_shape=[
            jax.ShapeDtypeStruct((rows_f, proj), F32),
            jax.ShapeDtypeStruct((2 * rows_f, d), F32),
            jax.ShapeDtypeStruct((length, d), BF16),
            jax.ShapeDtypeStruct((8, small_cols), F32),
        ],
        scratch_shapes=[
            vm((r + 8, wide), F32), vm((3 * r, wide), F32), vm((n, wide), F32), vm((r, wide), F32),
            vm((r, wide), BF16), vm((r, wide), BF16), vm((chunks, r, 2 * n), BF16), vm((r, wide), F32),
            vm((r, wide), BF16), vm((r, wide), F32), vm((r + 8, wide), F32),
            vm((r, wide), BF16), vm((r, wide), BF16), vm((r, wide), BF16), vm((r, wide), BF16),
            vm((r + 8, 2 * n), F32), vm((chunks, 8, LANES), F32),
            vm((chunks, 3 * r, 2 * heads), BF16), vm((length, LANES), F32), vm((chunks, r, LANES), F32),
            vm((chunks, r, r), F32), vm((chunks, r, r), F32), vm((length, n), F32), vm((length, n), F32),
            vm((3, length, LANES), F32), vm((length, 2 * n), F32), vm((length, wide), BF16), vm((length, tcols), BF16),
            vm((8 * taps + 16, inner), F32), vm((8 * taps + 16, 2 * n), F32),
            vm(normed_t.shape, BF16), vm(wx.shape, BF16), vm(gn.shape, F32), vm(tokens.shape, BF16), vm(gb.shape, BF16),
            vm((units, levels, 2, rows_f, wide), BF16), vm((2, levels, 2, 2, rows_f, wide), BF16),
            vm((levels, 2, 2, rows_f, tcols), BF16), vm((levels, 2, rows_f, tcols), BF16),
            vm((units, levels, 2, rows_f, wide), BF16), vm((levels, 2, rows_f, tcols), BF16),
            vm((units, levels, rows_f, wide), BF16), vm((levels, rows_f, tcols), BF16),
            vm((units, levels - 1, rows_f, wide), BF16), vm((levels - 1, rows_f, tcols), BF16),
            vm((units, rows_f, wide), BF16), vm((rows_f, tcols), BF16),
            vm((units, rows_f, wide), BF16), vm((rows_f, tcols), BF16),
            vm((4, 8, small_cols), F32), vm((3, 8, small_cols), F32), vm((levels, 8, small_cols), F32),
            pltpu.SemaphoreType.DMA((units + 1, 5 + 2 * levels)),
            pltpu.SemaphoreType.DMA((4 + 2 * levels,)),
            pltpu.SemaphoreType.DMA((6,)),
        ],
        compiler_params=pltpu.CompilerParams(
            dimension_semantics=("arbitrary", "arbitrary"), vmem_limit_bytes=60 * 2**20,
            collective_id=1, has_side_effects=True,
        ),
        name="scan_backward",
    )(
        px, px, ssd, dy, states, tail, aux, seg_rows, conv_w, conv_b, bias, rate, skip_row, e, et,
        norm_gain, dgain, squares, normed_t, wx, gn, tokens, gb, ggate, gout,
    )


def rms_scale(values):
    return lax.rsqrt(jnp.mean(values * values, axis=1, keepdims=True) + EPS)


def on_device(
    tokens,
    norm_gain,
    in_weight,
    conv_weight,
    conv_bias,
    step_bias,
    decay_log,
    skip_gain,
    out_gain,
    out_weight,
    cotangent,
    teacher,
    segment,
    valid_mask,
):
    seqs, length, width = tokens.shape
    rows = seqs * length
    every = ("rep", "fsdp")
    shards = lax.axis_size("fsdp")
    devices = lax.axis_size("rep") * shards
    loss_weight = float(rows * devices * width // 8)
    valid = valid_mask.reshape(rows, 1).astype(F32)
    total_count = lax.psum(jnp.sum(valid), every)
    denominator = total_count * width

    flat = tokens.reshape(rows, width)
    inputs = flat.astype(F32)
    normed = (inputs * rms_scale(inputs) * norm_gain[None, :]).astype(BF16)
    w_in = lax.all_gather(in_weight, "fsdp", axis=0, tiled=True)
    w_out = lax.all_gather(out_weight, "fsdp", axis=0, tiled=True)
    projected = mm(normed, w_in)

    heads = step_bias.shape[0]
    inner = out_gain.shape[0]
    head_width = inner // heads
    aux, seg_rows = helpers(segment, CHUNK)
    e, et = head_maps(heads, head_width)
    rate = -jnp.exp(decay_log)[None, :]
    skip_row = jnp.repeat(skip_gain, head_width)[None, :]
    per_seq = length // CHUNK
    params = (conv_weight, conv_bias[None, :], step_bias[None, :], rate, skip_row)
    gain_row = out_gain[None, :]
    mixed, ssd, states = scan_forward(projected, aux, seg_rows, *params, gain_row, e, per_seq)

    result = inputs + mm(mixed, w_out)
    error = result - teacher.reshape(rows, width).astype(F32)
    squares = jnp.sum((valid * error * error).reshape(rows, width // LANES, LANES), axis=(0, 1))
    cotan = cotangent.reshape(rows, width).astype(F32)
    grad_result = valid * (cotan + 2.0 * loss_weight * error / denominator)
    grad_branch = grad_result.astype(BF16)
    grad_out = mm_tn(mixed, grad_branch).astype(BF16)
    grad_mixed = mm_nt(grad_branch, w_out)
    dy, dz, dgain = gate_back(projected, ssd, grad_mixed, gain_row)
    grad_gate = mm_tn(normed, dz).astype(BF16)
    gn = mm_nt(dz, w_in[:, :inner])
    levels = shards // 4
    tail_at = 2 * inner
    tail_pad = -(in_weight.shape[1] - tail_at) % LANES
    tail = jnp.pad(projected[:, tail_at:], ((0, 0), (0, tail_pad)))
    wx = jnp.pad(w_in[:, inner:], ((0, 0), (0, tail_pad)))
    squares8 = jnp.pad(squares[None, :], ((0, 7), (0, 0)))
    grad_in, grad_out, grad_tokens, small = back(
        projected, inner // (inner // GROUPS), tail, ssd, dy, states, aux, seg_rows, *params, e, et,
        norm_gain[None, :], dgain, squares8, normed.T, wx, gn, flat, grad_branch,
        grad_gate.reshape(levels, 2, 2, width // shards, inner),
        grad_out.reshape(levels, 2, 2, inner // shards, width), in_weight.shape[1],
    )
    taps, conv_width = conv_weight.shape
    extra = small[7, width:]
    loss = jnp.sum(extra[2 * LANES : 3 * LANES]) / denominator
    return (
        result.astype(BF16).reshape(tokens.shape),
        loss,
        grad_tokens.reshape(tokens.shape),
        small[7, :width],
        grad_in,
        small[:taps, :conv_width],
        small[taps, :conv_width],
        extra[:heads],
        extra[LANES : LANES + heads],
        small[6, :inner].reshape(heads, head_width).sum(axis=1),
        small[5, :inner],
        grad_out,
    )


def solution(mesh):
    tokens = P(("rep", "fsdp"), None, None)
    marks = P(("rep", "fsdp"), None)
    shard = P("fsdp", None)
    return jax.shard_map(
        on_device,
        mesh=mesh,
        in_specs=(tokens, P(), shard, P(), P(), P(), P(), P(), P(), shard, tokens, tokens, marks, marks),
        out_specs=(tokens, P(), tokens, P(), shard, P(), P(), P(), P(), P(), P(), shard),
        check_vma=False,
    )
```

```python
import functools

import jax
import jax.numpy as jnp
from jax import lax
from jax.experimental import pallas as pl
from jax.experimental.pallas import tpu as pltpu
from jax.sharding import PartitionSpec as P

CHUNK = 128
LANES = 128
EPS = 1e-05
F32 = jnp.float32
BF16 = jnp.bfloat16
NT = (((1,), (1,)), ((), ()))
TN = (((0,), (0,)), ((), ()))


def mm(a, b):
    return jnp.dot(a, b, preferred_element_type=F32)


def mm_nt(a, b):
    return lax.dot_general(a, b, NT, preferred_element_type=F32)


def mm_tn(a, b):
    return lax.dot_general(a, b, TN, preferred_element_type=F32)


def split2(v):
    high = v.astype(BF16)
    return high, (v - high.astype(F32)).astype(BF16)


def split3(v):
    high = v.astype(BF16)
    rest = v - high.astype(F32)
    mid = rest.astype(BF16)
    return high, mid, (rest - mid.astype(F32)).astype(BF16)


def tri_sum(tri, v):
    heads = v.shape[1]
    parts = mm(tri, jnp.concatenate(split3(v), axis=1))
    return parts[:, :heads] + parts[:, heads : 2 * heads] + parts[:, 2 * heads :]


def sigmoid(v):
    return 0.5 * jnp.tanh(0.5 * v) + 0.5


def softplus(v):
    return jnp.maximum(v, 0.0) + jnp.log1p(jnp.exp(-jnp.abs(v)))


def iota(shape, dim):
    return lax.broadcasted_iota(jnp.int32, shape, dim)


def small_terms(step_raw, step_bias, decay_rate, keep, to_end, rows):
    shifted = step_raw + step_bias
    step = softplus(shifted)
    lower = (iota((rows, rows), 0) >= iota((rows, rows), 1)).astype(BF16)
    cum = tri_sum(lower, step * decay_rate)
    last = cum[rows - 1 : rows, :]
    return shifted, step, cum, jnp.exp(cum) * keep, jnp.exp(last - cum) * to_end


def expand(e_ref, out_ref, step, from_prev, to_end):
    stacked = jnp.concatenate(
        [jnp.concatenate(split2(v), axis=1) for v in (step, from_prev, to_end)], axis=0
    )
    out_ref[...] = mm(stacked, e_ref[...])


def helpers(segment, valid, chunk):
    seqs, length = segment.shape
    blocks = length // chunk
    def same(shift):
        return (segment[:, shift:] == segment[:, :-shift]).astype(F32)
    back = [jnp.pad(same(k), ((0, 0), (k, 0))) for k in (1, 2, 3)]
    ahead = [jnp.pad(same(k), ((0, 0), (0, k))) for k in (1, 2, 3)]
    by_block = segment.reshape(seqs, blocks, chunk)
    ends = by_block[:, :, -1]
    before = jnp.pad(ends[:, :-1], ((0, 0), (1, 0)), constant_values=-1)
    keep = (by_block == before[:, :, None]).astype(F32).reshape(seqs, length)
    to_end = (by_block == ends[:, :, None]).astype(F32).reshape(seqs, length)
    docs = segment.astype(F32)
    columns = [docs, *back, *ahead, keep, to_end, valid] + [jnp.zeros_like(docs)] * 6
    aux = jnp.stack(columns, axis=-1).reshape(seqs * length, 16)
    return aux, docs.reshape(seqs * blocks, 1, chunk)


def head_maps(heads, width):
    inner = heads * width
    owner = jnp.arange(inner) // width
    one = (jnp.arange(heads)[:, None] == owner[None, :]).astype(BF16)
    down = (owner[:, None] == jnp.arange(LANES)[None, :]).astype(BF16)
    return jnp.concatenate([one, one], axis=0), down


def full(shape):
    return pl.BlockSpec(shape, lambda i: (0,) * len(shape))


MESH = pl.DeviceIdType.MESH


class Spot:
    def __init__(self, levels):
        self.rep, self.at = lax.axis_index("rep"), lax.axis_index("fsdp")
        self.core, self.side, self.level = self.at % 2, (self.at // 2) % 2, self.at // 4
        self.levels = levels
        self.sibling = (self.rep, self.at + 1 - 2 * self.core)
        self.across = (self.rep, self.at + 2 - 4 * self.side)
        self.twin = (1 - self.rep, self.at)

    def far(self, step):
        return (self.rep, ((self.level + step) % self.levels) * 4 + self.at % 4)

    def greet(self):
        barrier = pltpu.get_barrier_semaphore()
        partners = [self.sibling, self.across, self.twin] + [self.far(d) for d in range(1, self.levels)]
        for one in partners:
            pl.semaphore_signal(barrier, inc=1, device_id=one, device_id_type=MESH)
        pl.semaphore_wait(barrier, len(partners))


def send(src, dst, send_sem, recv_sem, device):
    return pltpu.make_async_remote_copy(
        src_ref=src, dst_ref=dst, send_sem=send_sem, recv_sem=recv_sem, device_id=device, device_id_type=MESH
    )


class Unit:
    def __init__(self, spot, whole, own, from_core, from_side, from_level, mine, from_twin, sems, local, write):
        self.spot, self.whole, self.own, self.local, self.write = spot, whole, own, local, write
        self.from_core, self.from_side, self.from_level = from_core, from_side, from_level
        self.mine, self.from_twin = mine, from_twin
        self.sems = sems

    @property
    def c0(self):
        return pltpu.make_async_copy(self.whole.at[:, :, self.spot.core], self.own, self.sems.at[6])

    @property
    def c1(self):
        spot, sems = self.spot, self.sems
        return send(self.whole.at[:, :, 1 - spot.core], self.from_core, sems.at[0], sems.at[1], spot.sibling)

    @property
    def c2(self):
        spot, sems = self.spot, self.sems
        return send(self.own.at[:, 1 - spot.side], self.from_side, sems.at[2], sems.at[3], spot.across)

    @property
    def c3(self):
        spot, sems = self.spot, self.sems
        return [
            send(
                self.from_side.at[(spot.level + d) % spot.levels], self.from_level.at[d - 1],
                sems.at[5 + 2 * d], sems.at[6 + 2 * d], spot.far(d),
            )
            for d in range(1, spot.levels)
        ]

    @property
    def c4(self):
        spot, sems = self.spot, self.sems
        return send(self.mine, self.from_twin, sems.at[4], sems.at[5], spot.twin)

    def stage(self, number):
        spot, levels = self.spot, self.spot.levels
        if number == 1:
            self.c1.start()
            self.c0.start()
        elif number == 2:
            self.c0.wait()
            self.c1.wait()

            def add(i, carry):
                for side in range(2):
                    self.own[i, side] = (
                        self.own[i, side].astype(F32) + self.from_core[i, side].astype(F32)
                    ).astype(BF16)
                return carry

            lax.fori_loop(0, levels, add, 0)
            self.c2.start()
        elif number == 3:
            self.c2.wait()

            def add(i, carry):
                self.from_side[i] = (
                    self.from_side[i].astype(F32) + self.own[i, spot.side].astype(F32)
                ).astype(BF16)
                return carry

            lax.fori_loop(0, levels, add, 0)
            for copy in self.c3:
                copy.start()
        elif number == 4:
            for copy in self.c3:
                copy.wait()
            total = self.from_side[spot.level].astype(F32)
            for d in range(levels - 1):
                total = total + self.from_level[d].astype(F32)
            self.mine[...] = total.astype(BF16)
            self.c4.start()
        else:
            self.c4.wait()
            self.write(self.mine[...].astype(F32) + self.from_twin[...].astype(F32))


GROUPS = 4
BACKGROUND_STARTS = (0, 2, 5, 7, 11, 13, 18, 21)


def back_kernel(
    px_ref, prev_ref, ssd_ref, dy_ref, state_ref,
    tail_ref, aux_ref, seg_ref, cw_ref, cb_ref, bias_ref, rate_ref, skip_ref, e_ref, et_ref,
    ngain_ref, dgain_ref, square_ref,
    normed_t_hbm, wx_hbm, wt_hbm, gn_hbm, tokens_hbm, gb_hbm, ggate_hbm, gout_hbm,
    gi_ref, go_ref, gt_ref, small_ref,
    xbuf, ex, adj, xs, xdt, xe, bc, slope, dye, dxi, dbuf, r1, r1l, r2, r3,
    tbuf, consts, stacks, raws, cums, scores, dscores, gbs, gcs, sums, tslope, gp, gpt, accum, taccum,
    normed_t, wx, wt, gn, tokens, gb,
    own, part, part_t, own_t, from_core, from_core_t, from_side, from_side_t, from_level, from_level_t,
    mine, mine_t, twin, twin_t, sm, smr, smz, sems, small_sems, load_sems,
    *, inner, heads, width, levels, seq_chunks,
):
    group, turn = pl.program_id(0), pl.program_id(1)
    step = group * seq_chunks + turn
    chunk = seq_chunks - 1 - turn
    rows, cols_g = px_ref.shape
    n = bc.shape[2] // 2
    tiles = cols_g // LANES
    per_group = cols_g // width
    taps = cw_ref.shape[0]
    tail_cols = tail_ref.shape[1]
    conv_tail = 2 * n
    here = pl.ds(pl.multiple_of(chunk * rows, rows), rows)
    spot = Spot(levels)
    gcol = pl.multiple_of(group * cols_g, cols_g)
    rows_f = mine.shape[1]

    def loads():
        pairs = ((normed_t_hbm, normed_t), (wx_hbm, wx), (wt_hbm, wt), (gn_hbm, gn), (tokens_hbm, tokens), (gb_hbm, gb))
        return [pltpu.make_async_copy(a, b, load_sems.at[i]) for i, (a, b) in enumerate(pairs)]

    units = []

    def writer(ref, row, col, wide):
        def write(v):
            ref[row : row + rows_f, col : col + wide] = v[:, :wide]
        return write

    for u in range(GROUPS * 2):
        if u < GROUPS:
            hbm = gout_hbm.at[:, :, :, pl.ds((u // 2) * rows_f, rows_f), pl.ds((u % 2) * cols_g, cols_g)]
            write = writer(go_ref, (u // 2) * rows_f, (u % 2) * cols_g, cols_g)
        else:
            hbm = ggate_hbm.at[:, :, :, :, pl.ds((u - GROUPS) * cols_g, cols_g)]
            write = writer(gi_ref, 0, (u - GROUPS) * cols_g, cols_g)
        units.append((u, hbm, own.at[u], write))
    for g in range(GROUPS):
        u = 2 * GROUPS + g
        units.append((u, part.at[g % 2], own.at[u], writer(gi_ref, 0, inner + g * cols_g, cols_g)))
    units = [
        Unit(
            spot, whole, mine_half, from_core.at[u], from_side.at[u], from_level.at[u], mine.at[u], twin.at[u],
            sems.at[u], True, write,
        )
        for u, whole, mine_half, write in units
    ]
    tail_wide = gi_ref.shape[1] - 2 * inner
    tail_unit = Unit(
        spot, part_t, own_t, from_core_t, from_side_t, from_level_t, mine_t, twin_t, sems.at[3 * GROUPS], True,
        writer(gi_ref, 0, 2 * inner, tail_wide),
    )

    events = {}
    last_step = GROUPS * seq_chunks - 1
    late = []
    plan = [(s * seq_chunks // 8, units[u]) for u, s in enumerate(BACKGROUND_STARTS)]
    plan += [((g + 1) * seq_chunks, units[2 * GROUPS + g]) for g in range(GROUPS - 1)]
    for begin, unit in plan:
        for number, delay in ((1, 0), (2, 1), (3, 4), (4, 7), (5, 8)):
            events.setdefault(min(begin + delay, last_step), []).append((unit, number))

    @pl.when(step == 0)
    def _():
        for copy in loads():
            copy.start()
        spot.greet()
        accum[...] = jnp.zeros_like(accum)
        taccum[...] = jnp.zeros_like(taccum)
        cums[...] = jnp.zeros_like(cums)

    for at, happen in sorted(events.items()):
        if at == last_step:
            late += happen
            continue

        @pl.when(step == at)
        def _(happen=happen):
            for unit, number in sorted(happen, key=lambda pair: -pair[1]):
                unit.stage(number)

    def fold(v):
        return jnp.sum(v.reshape(rows // 8, 8, v.shape[1]), axis=0)

    aux = aux_ref[here, :]
    marks = [None] + [jnp.broadcast_to(aux[:, k : k + 1], (rows, LANES)) for k in range(1, taps)]
    marks_next = [None] + [jnp.broadcast_to(aux[:, 3 + k : 4 + k], (rows, LANES)) for k in range(1, taps)]
    lower = iota((rows, rows), 0) >= iota((rows, rows), 1)
    upper = iota((rows, rows), 0) <= iota((rows, rows), 1)
    rate = rate_ref[...]

    def conv_pre(buffer, cols, wcols):
        pre = cb_ref[:, wcols] + cw_ref[0:1, wcols] * buffer[8 : 8 + rows, cols]
        for k in range(1, taps):
            pre = pre + (cw_ref[k : k + 1, wcols] * buffer[8 - k : 8 - k + rows, cols]) * marks[k]
        return pre

    def conv_back(buffer, cols, wcols, acc, acc_cols):
        grad = buffer[0:rows, cols]
        out = cw_ref[0:1, wcols] * grad
        acc[8 * taps : 8 * taps + 8, acc_cols] += fold(grad)
        acc[0:8, acc_cols] += fold(grad * xbuf[8 : 8 + rows, cols])
        for k in range(1, taps):
            out = out + (cw_ref[k : k + 1, wcols] * buffer[k : k + rows, cols]) * marks_next[k]
            acc[8 * k : 8 * k + 8, acc_cols] += fold(grad * (xbuf[8 - k : 8 - k + rows, cols] * marks[k]))
        return out

    def fill_tail():
        xbuf[8 : 8 + rows, 0:conv_tail] = tail_ref[here, 0:conv_tail]
        before = pl.ds(pl.multiple_of(jnp.maximum(chunk * rows - 8, 0), 8), 8)
        xbuf[0:8, 0:conv_tail] = tail_ref[before, 0:conv_tail]

    @pl.when(group == 0)
    def _():
        shifted, step_size, cum, from_prev, to_end = small_terms(
            tail_ref[here, conv_tail : conv_tail + heads], bias_ref[...], rate, aux[:, 7:8], aux[:, 8:9], rows
        )
        raws[here, 0:heads] = shifted
        raws[here, heads : 2 * heads] = step_size
        cums[chunk, :, 0:heads] = cum
        stacks[chunk] = jnp.concatenate(
            [jnp.concatenate(split2(v), axis=1) for v in (step_size, from_prev, to_end)], axis=0
        )
        fill_tail()
        for c in range(conv_tail // LANES):
            cols = slice(c * LANES, (c + 1) * LANES)
            pre = conv_pre(xbuf, cols, slice(inner + c * LANES, inner + (c + 1) * LANES))
            sig = sigmoid(pre)
            act = pre * sig
            tslope[here, cols] = sig + act * (1.0 - sig)
            bc[chunk, :, cols] = act.astype(BF16)
        same = upper & (aux[:, 0:1] == seg_ref[chunk])
        scores[chunk] = jnp.where(same, mm_nt(bc[chunk, :, 0:n], bc[chunk, :, n:]), 0.0)
        dscores[chunk] = jnp.zeros((rows, rows), F32)
        gbs[here, :] = jnp.zeros((rows, n), F32)
        gcs[here, :] = jnp.zeros((rows, n), F32)
        consts[chunk] = jnp.zeros((8, LANES), F32)
        for i in range(3):
            sums[i, here, :] = jnp.zeros((rows, LANES), F32)

    @pl.when(turn == 0)
    def _():
        adj[...] = jnp.zeros_like(adj)
        dbuf[rows : rows + 8, :] = jnp.zeros((8, cols_g), F32)

    ex[...] = mm(stacks[chunk], e_ref[:, pl.ds(gcol, cols_g)])
    head0 = group * per_group
    pick = (iota((LANES, LANES), 0) == iota((LANES, LANES), 1) + head0).astype(BF16)
    cum_all = cums[chunk]
    moved = [mm(v, pick) for v in split3(cum_all)]
    cum = moved[0] + moved[1] + moved[2]
    cum_t = cum.T
    xbuf[0:8, :] = prev_ref[...]
    xbuf[8 : 8 + rows, :] = px_ref[...]
    for c in range(tiles):
        cols = slice(c * LANES, (c + 1) * LANES)
        wcols = pl.ds(gcol + c * LANES, LANES)
        pre = conv_pre(xbuf, cols, wcols)
        sig = sigmoid(pre)
        act = pre * sig
        slope[:, cols] = sig + act * (1.0 - sig)
        xs[:, cols] = act
        scaled = act * ex[0:rows, cols]
        xdt[:, cols] = scaled.astype(BF16)
        xe[:, cols] = (scaled * ex[2 * rows : 3 * rows, cols]).astype(BF16)
        dye[:, cols] = (dy_ref[:, cols].astype(F32) * ex[rows : 2 * rows, cols]).astype(BF16)
    b, cc = bc[chunk, :, 0:n], bc[chunk, :, n:]
    state_low = state_ref[...]
    adj_low = adj[...].astype(BF16)
    carry = ex[2 * rows - 1 : 2 * rows, :]
    gcs[here, :] += mm_nt(dye[...], state_low)
    gbs[here, :] += mm_nt(xe[...], adj_low)
    dxi[...] = mm(b, adj_low)
    through = jnp.sum(adj[...] * state_low.astype(F32), axis=0, keepdims=True) * carry
    adj[...] = adj[...] * carry + mm_tn(cc, dye[...])
    scores_t = scores[chunk]
    lane = iota((1, LANES), 1)
    masks = [(lane < width).astype(BF16), (lane >= width).astype(BF16)]
    grad_scores_t = jnp.zeros((rows, rows), F32)
    for c in range(tiles):
        cols = slice(c * LANES, (c + 1) * LANES)
        acols = pl.ds(gcol + c * LANES, LANES)
        x_low, dy_low = xdt[:, cols], dy_ref[:, cols]
        grad_mix = mm_nt(jnp.concatenate([x_low * masks[0], x_low * masks[1]], axis=0), dy_low)
        mixing = []
        for i, h in enumerate((2 * c, 2 * c + 1)):
            decay = jnp.exp(jnp.minimum(cum_t[h : h + 1, :] - cum[:, h : h + 1], 0.0))
            mixing.append((scores_t * decay).astype(BF16))
            grad_scores_t = grad_scores_t + grad_mix[i * rows : (i + 1) * rows] * decay
        within = mm(
            jnp.concatenate(mixing, axis=1), jnp.concatenate([dy_low * masks[0], dy_low * masks[1]], axis=0)
        )
        x = xs[:, cols]
        skip = skip_ref[:, acols]
        across = ex[2 * rows : 3 * rows, cols] * dxi[:, cols]
        both = within + across
        grad_ssd = dy_low.astype(F32)
        x_scaled = x_low.astype(F32)
        r1[:, cols], r1l[:, cols] = split2(grad_ssd * (ssd_ref[:, cols] - skip * x) - within * x_scaled)
        r2[:, cols] = (across * x_scaled).astype(BF16)
        r3[:, cols] = (both * x).astype(BF16)
        accum[8 * taps + 8 : 8 * taps + 16, acols] += fold(grad_ssd * x)
        grad_x = skip * grad_ssd + ex[0:rows, cols] * both
        dbuf[0:rows, cols] = grad_x * slope[:, cols]
    dscores[chunk] += grad_scores_t
    et = et_ref[pl.ds(gcol, cols_g), :]
    sums[0, here, :] += mm(r1[...], et) + mm(r1l[...], et)
    sums[1, here, :] += mm(r2[...], et)
    sums[2, here, :] += mm(r3[...], et)
    high, rest = split2(jnp.broadcast_to(through, (8, cols_g)))
    consts[chunk] += mm(high, et) + mm(rest, et)
    for c in range(tiles):
        cols = slice(c * LANES, (c + 1) * LANES)
        acols = pl.ds(gcol + c * LANES, LANES)
        gp[here, cols] = conv_back(dbuf, cols, acols, accum, acols).astype(BF16)
    dbuf[rows : rows + 8, :] = dbuf[0:8, :]

    @pl.when(group == GROUPS - 1)
    def _():
        same = upper & (aux[:, 0:1] == seg_ref[chunk])
        grad_scores = jnp.where(same, dscores[chunk], 0.0).astype(BF16)
        grad_b = gbs[here, :] + mm(grad_scores, cc)
        grad_c = gcs[here, :] + mm_tn(grad_scores, b)
        fill_tail()

        @pl.when(turn == 0)
        def _():
            tbuf[rows : rows + 8, :] = jnp.zeros((8, 2 * n), F32)

        tbuf[0:rows, 0:n] = grad_b * tslope[here, 0:n]
        tbuf[0:rows, n : 2 * n] = grad_c * tslope[here, n : 2 * n]
        for c in range(conv_tail // LANES):
            cols = slice(c * LANES, (c + 1) * LANES)
            gpt[here, cols] = conv_back(
                tbuf, cols, slice(inner + c * LANES, inner + (c + 1) * LANES), taccum, cols
            ).astype(BF16)
        tbuf[rows : rows + 8, :] = tbuf[0:8, :]
        shifted = raws[here, 0:heads]
        step_size = raws[here, heads : 2 * heads]
        const = consts[chunk, 0:1, 0:heads]
        grad_log = (
            tri_sum(upper.astype(BF16), sums[0, here, 0:heads])
            + tri_sum((iota((rows, rows), 0) > iota((rows, rows), 1)).astype(BF16), sums[1, here, 0:heads])
            + const
        ) * aux[:, 1:2]
        grad_raw = (sums[2, here, 0:heads] + rate * grad_log) * sigmoid(shifted)
        gpt[here, conv_tail:] = jnp.concatenate(
            [grad_raw, jnp.zeros((rows, tail_cols - conv_tail - heads), F32)], axis=1
        ).astype(BF16)
        small = 8 * taps + 8
        taccum[small : small + 8, 0:heads] += fold(grad_raw)
        taccum[small : small + 8, LANES : LANES + heads] += fold(step_size * grad_log * rate)

    def weight_grad(low, out):
        def one(i, carry):
            block = pl.ds(pl.multiple_of(i * 4 * rows_f, 4 * rows_f), 4 * rows_f)
            v = mm(normed_t[block, :], low[...]).astype(BF16)
            for side in range(2):
                for core in range(2):
                    at = (2 * side + core) * rows_f
                    out[i, side, core] = v[at : at + rows_f]
            return carry

        lax.fori_loop(0, levels, one, 0)

    def input_grad(low, weights):
        def one(i, carry):
            block = pl.ds(pl.multiple_of(i * 256, 256), 256)
            gn[block, :] += mm_nt(low[block, :], weights[...])
            return carry

        lax.fori_loop(0, gn.shape[0] // 256, one, 0)

    for g in range(GROUPS - 1):

        @pl.when(step == (g + 1) * seq_chunks - 1)
        def _(g=g):
            if g == 0:
                for copy in loads():
                    copy.wait()
            weight_grad(gp, part.at[g % 2])
            input_grad(gp, wx.at[:, g * cols_g : (g + 1) * cols_g])

    @pl.when(step == last_step)
    def _():
        for unit, number in sorted(late, key=lambda pair: pair[1]):
            unit.stage(number)
        last = units[3 * GROUPS - 1]
        weight_grad(gpt, part_t)
        tail_unit.stage(1)
        weight_grad(gp, part.at[(GROUPS - 1) % 2])
        last.stage(1)
        input_grad(gpt, wt)
        tail_unit.stage(2)
        input_grad(gp, wx.at[:, (GROUPS - 1) * cols_g : GROUPS * cols_g])
        last.stage(2)
        d = gn.shape[1]
        ngain = ngain_ref[...]

        def block_norm(i, total):
            block = pl.ds(pl.multiple_of(i * 64, 64), 64)
            v = tokens[block, :].astype(F32)
            rinv = lax.rsqrt(jnp.sum(v * v, axis=1, keepdims=True) / d + EPS)
            scaled = v * rinv
            grad = gn[block, :]
            total = total + jnp.sum((grad * scaled).reshape(8, 8, d), axis=0)
            grad = grad * ngain
            mean = jnp.sum(grad * scaled, axis=1, keepdims=True) / d
            gb[block, :] = (gb[block, :].astype(F32) + rinv * (grad - scaled * mean)).astype(BF16)
            return total

        dnorm = lax.fori_loop(0, gn.shape[0] // 64, block_norm, jnp.zeros((8, d), F32))
        leave = pltpu.make_async_copy(gb, gt_ref, load_sems.at[6])
        leave.start()

        def one_row(v):
            return jnp.sum(v, axis=0, keepdims=True)

        local = sm.at[0]
        local[...] = jnp.zeros(local.shape, F32)
        for k in range(taps + 1):
            local[k : k + 1, 0:inner] = one_row(accum[8 * k : 8 * k + 8, :])
            local[k : k + 1, inner : inner + conv_tail] = one_row(taccum[8 * k : 8 * k + 8, 0:conv_tail])
        local[5:6, 0:inner] = one_row(dgain_ref[...])
        local[6:7, 0:inner] = one_row(accum[8 * taps + 8 : 8 * taps + 16, :])
        local[7:8, 0:d] = one_row(dnorm)
        small = 8 * taps + 8
        local[7:8, d : d + conv_tail] = one_row(taccum[small : small + 8, 0:conv_tail])
        local[7:8, d + conv_tail : d + conv_tail + LANES] = one_row(square_ref[...])
        exchange = [
            send(sm.at[i], smr.at[i], small_sems.at[2 * i], small_sems.at[2 * i + 1], device)
            for i, device in enumerate((spot.sibling, spot.across, spot.twin))
        ]
        spread = [
            send(sm.at[3], smz.at[spot.level], small_sems.at[4 + 2 * d], small_sems.at[5 + 2 * d], spot.far(d))
            for d in range(1, levels)
        ]

        def fold_small(i):
            exchange[i].wait()
            sm[i + 1] = sm[i] + smr[i]

        exchange[0].start()
        tail_unit.stage(3)
        fold_small(0)
        exchange[1].start()
        last.stage(3)
        fold_small(1)
        exchange[2].start()
        tail_unit.stage(4)
        fold_small(2)
        for copy in spread:
            copy.start()
        smz[spot.level] = sm[3]
        last.stage(4)
        tail_unit.stage(5)
        for copy in spread:
            copy.wait()
        total = smz[0]
        for i in range(1, levels):
            total = total + smz[i]
        small_ref[...] = total
        last.stage(5)
        leave.wait()


def back(
    px, px_block, tail, ssd, dy, states, aux, seg_rows, conv_w, conv_b, bias, rate, skip_row, e, et,
    norm_gain, dgain, squares, normed_t, wx, wt, gn, tokens, gb, ggate, gout, proj,
):
    length, inner = ssd.shape
    heads = bias.shape[1]
    levels, rows_f = ggate.shape[0], ggate.shape[3]
    taps = conv_w.shape[0]
    n = (conv_w.shape[1] - inner) // 2
    r = CHUNK
    chunks = length // r
    wide = inner // GROUPS
    tcols = tail.shape[1]
    d = normed_t.shape[0]
    small_cols = inner + tcols
    units = 3 * GROUPS
    back_at = lambda off: lambda g, c: (chunks - 1 - c, g + off)
    whole = lambda a: pl.BlockSpec(a.shape, lambda g, c: (0,) * a.ndim, pipeline_mode=pl.Buffered(1))
    anywhere = pl.BlockSpec(memory_space=pl.ANY)
    vm = pltpu.VMEM
    out = lambda s: pl.BlockSpec(s, lambda g, c: (0,) * len(s))
    return pl.pallas_call(
        functools.partial(
            back_kernel, inner=inner, heads=heads, width=inner // heads, levels=levels, seq_chunks=chunks
        ),
        grid=(GROUPS, chunks),
        in_specs=[
            pl.BlockSpec((r, wide), back_at(px_block)),
            pl.BlockSpec((8, wide), lambda g, c: (jnp.maximum((chunks - 1 - c) * (r // 8) - 1, 0), g + px_block)),
            pl.BlockSpec((r, wide), back_at(0)),
            pl.BlockSpec((r, wide), back_at(0)),
            pl.BlockSpec((n, wide), back_at(0)),
            *[whole(a) for a in (tail, aux, seg_rows, conv_w, conv_b, bias, rate, skip_row, e, et, norm_gain, dgain, squares)],
            *[anywhere] * 8,
        ],
        out_specs=[out((rows_f, proj)), out((2 * rows_f, d)), anywhere, out((8, small_cols))],
        out_shape=[
            jax.ShapeDtypeStruct((rows_f, proj), F32),
            jax.ShapeDtypeStruct((2 * rows_f, d), F32),
            jax.ShapeDtypeStruct((length, d), BF16),
            jax.ShapeDtypeStruct((8, small_cols), F32),
        ],
        scratch_shapes=[
            vm((r + 8, wide), F32), vm((3 * r, wide), F32), vm((n, wide), F32), vm((r, wide), F32),
            vm((r, wide), BF16), vm((r, wide), BF16), vm((chunks, r, 2 * n), BF16), vm((r, wide), F32),
            vm((r, wide), BF16), vm((r, wide), F32), vm((r + 8, wide), F32),
            vm((r, wide), BF16), vm((r, wide), BF16), vm((r, wide), BF16), vm((r, wide), BF16),
            vm((r + 8, 2 * n), F32), vm((chunks, 8, LANES), F32),
            vm((chunks, 3 * r, 2 * heads), BF16), vm((length, LANES), F32), vm((chunks, r, LANES), F32),
            vm((chunks, r, r), F32), vm((chunks, r, r), F32), vm((length, n), F32), vm((length, n), F32),
            vm((3, length, LANES), F32), vm((length, 2 * n), F32), vm((length, wide), BF16), vm((length, tcols), BF16),
            vm((8 * taps + 16, inner), F32), vm((8 * taps + 16, 2 * n), F32),
            vm(normed_t.shape, BF16), vm(wx.shape, BF16), vm(wt.shape, BF16), vm(gn.shape, F32), vm(tokens.shape, BF16), vm(gb.shape, BF16),
            vm((units, levels, 2, rows_f, wide), BF16), vm((2, levels, 2, 2, rows_f, wide), BF16),
            vm((levels, 2, 2, rows_f, tcols), BF16), vm((levels, 2, rows_f, tcols), BF16),
            vm((units, levels, 2, rows_f, wide), BF16), vm((levels, 2, rows_f, tcols), BF16),
            vm((units, levels, rows_f, wide), BF16), vm((levels, rows_f, tcols), BF16),
            vm((units, levels - 1, rows_f, wide), BF16), vm((levels - 1, rows_f, tcols), BF16),
            vm((units, rows_f, wide), BF16), vm((rows_f, tcols), BF16),
            vm((units, rows_f, wide), BF16), vm((rows_f, tcols), BF16),
            vm((4, 8, small_cols), F32), vm((3, 8, small_cols), F32), vm((levels, 8, small_cols), F32),
            pltpu.SemaphoreType.DMA((units + 1, 5 + 2 * levels)),
            pltpu.SemaphoreType.DMA((4 + 2 * levels,)),
            pltpu.SemaphoreType.DMA((7,)),
        ],
        compiler_params=pltpu.CompilerParams(
            dimension_semantics=("arbitrary", "arbitrary"), vmem_limit_bytes=60 * 2**20,
            collective_id=1, has_side_effects=True,
        ),
        name="scan_backward",
    )(
        px, px, ssd, dy, states, tail, aux, seg_rows, conv_w, conv_b, bias, rate, skip_row, e, et,
        norm_gain, dgain, squares, normed_t, wx, wt, gn, tokens, gb, ggate, gout,
    )


class Load:
    def __init__(self, spot, shard, whole, sems, split):
        self.spot, self.shard, self.whole, self.sems, self.split = spot, shard, whole, sems, split

    def part(self, ref):
        if not self.split:
            return ref
        half = ref.shape[-1] // 2
        cols = pl.ds(pl.multiple_of(self.spot.rep * half, half), half)
        return ref.at[(slice(None),) * (len(ref.shape) - 1) + (cols,)]

    @property
    def a0(self):
        spot = self.spot
        here = self.whole.at[spot.level, spot.side, spot.core]
        return pltpu.make_async_copy(self.part(self.shard), self.part(here), self.sems.at[0])

    @property
    def a(self):
        spot, sems = self.spot, self.sems
        here = self.whole.at[spot.level, spot.side, spot.core]
        return [
            send(self.part(self.shard), self.part(here), sems.at[5 + 2 * d], sems.at[6 + 2 * d], spot.far(d))
            for d in range(1, spot.levels)
        ]

    @property
    def b(self):
        spot, sems = self.spot, self.sems
        if self.split:
            block = self.part(self.whole.at[:, spot.side, spot.core])
        else:
            half = spot.levels // 2
            block = self.whole.at[pl.ds(spot.rep * half, half), spot.side, spot.core]
        return send(block, block, sems.at[1], sems.at[2], spot.across)

    @property
    def c(self):
        spot, sems = self.spot, self.sems
        if self.split:
            block = self.part(self.whole.at[:, :, spot.core])
        else:
            half = spot.levels // 2
            block = self.whole.at[pl.ds(spot.rep * half, half), 1 - spot.side, spot.core]
        return send(block, block, sems.at[3], sems.at[4], spot.twin)

    @property
    def d(self):
        spot, sems = self.spot, self.sems
        block = self.whole.at[:, :, spot.core]
        last = 5 + 2 * spot.levels
        return send(block, block, sems.at[last], sems.at[last + 1], spot.sibling)

    def stage(self, number):
        if number == 1:
            self.a0.start()
            for copy in self.a:
                copy.start()
        elif number == 2:
            self.a0.wait()
            for copy in self.a:
                copy.wait()
            self.b.start()
        elif number == 3:
            self.b.wait()
            self.c.start()
        elif number == 4:
            self.c.wait()
            self.d.start()
        else:
            self.d.wait()


LOAD_STEPS = (5, 8, 12)


def first_kernel(
    cotan_ref, teacher_ref,
    tokens_hbm, ngain_ref, aux_ref, seg_ref, count_ref, cw_ref, cb_ref, bias_ref, rate_ref, skip_ref, gain_ref, e_ref,
    in_hbm, tail_hbm, out_hbm,
    px_ref, ssd_ref, state_out_ref, tail_out, normed_out, normed_t_out, wx_out, wtail_out,
    output_ref, gb_ref, mixed_ref, dy_ref, dz_ref, gn_ref, dgain_ref, small_ref,
    tokens, normed, normed_t, wx, wg, wo, weight_tail, tail, pbuf, ssd_all, gates, gateds, gms, results, inverses,
    ex, state, xs, xdt, xe, bc, yin, cums, scores, stacks,
    counts, countr, countz, sems, count_sems, copy_sems, leave_sems,
    *, inner, heads, width, levels, seq_chunks, loss_weight,
):
    step = pl.program_id(0)
    group, chunk = step // seq_chunks, step % seq_chunks
    rows, cols_g = px_ref.shape
    n = bc.shape[2] // 2
    tiles = cols_g // LANES
    per_group = cols_g // width
    taps = cw_ref.shape[0]
    rows_f = in_hbm.shape[0]
    tail_cols = tail.shape[1]
    conv_tail = 2 * n
    length, d_model = tokens.shape
    spot = Spot(levels)
    here = pl.ds(pl.multiple_of(chunk * rows, rows), rows)
    gcol = pl.multiple_of(group * cols_g, cols_g)
    last_step = GROUPS * seq_chunks - 1

    tail_load = Load(spot, tail_hbm, weight_tail, sems.at[0], False)
    loads = []
    for k in range(2 * GROUPS):
        cols = pl.ds((k % GROUPS) * cols_g, cols_g)
        shard = in_hbm.at[:, pl.ds((inner if k < GROUPS else 0) + (k % GROUPS) * cols_g, cols_g)]
        loads.append((shard, (wx if k < GROUPS else wg).at[:, :, :, :, cols]))
    for k in range(GROUPS):
        cols = pl.ds(k * (d_model // GROUPS), d_model // GROUPS)
        loads.append((out_hbm.at[:, cols], wo.at[:, :, :, :, cols]))
    loads = [Load(spot, shard, whole, sems.at[1 + k], k % 2 == 1) for k, (shard, whole) in enumerate(loads)]
    leaves = [
        (wx, wx_out), (weight_tail, wtail_out), (normed, normed_out), (normed_t, normed_t_out), (tail.at[8:], tail_out)
    ]

    def leave(k):
        return pltpu.make_async_copy(*leaves[k], leave_sems.at[k])

    exchange = lambda i: send(
        counts.at[i], countr.at[i], count_sems.at[2 * i], count_sems.at[2 * i + 1],
        (spot.sibling, spot.across, spot.twin)[i],
    )
    spread = lambda d: send(
        counts.at[3], countz.at[spot.level], count_sems.at[4 + 2 * d], count_sems.at[5 + 2 * d], spot.far(d)
    )

    def marks_of(aux):
        return [None] + [jnp.broadcast_to(aux[:, k : k + 1], (rows, LANES)) for k in range(1, taps)]

    def conv(buffer, at, cols, wcols, marks):
        block = buffer[pl.ds(at, rows + 8), cols]
        pre = cb_ref[:, wcols] + cw_ref[0:1, wcols] * block[8:]
        for k in range(1, taps):
            pre = pre + (cw_ref[k : k + 1, wcols] * block[8 - k : 8 - k + rows]) * marks[k]
        return pre * sigmoid(pre)

    def project(weight, out, cols):
        for i in range(length // 256):
            out[8 + i * 256 : 8 + (i + 1) * 256, :] = mm(normed[i * 256 : (i + 1) * 256, :], weight[:, cols])

    @pl.when(step == 0)
    def _():
        fetch = pltpu.make_async_copy(tokens_hbm, tokens, copy_sems.at[0])
        fetch.start()
        counts[0] = count_ref[...]
        spot.greet()
        tail_load.stage(1)
        exchange(0).start()
        loads[0].stage(1)
        loads[1].stage(1)
        fetch.wait()

        def norm(i, carry):
            block = pl.ds(pl.multiple_of(i * 64, 64), 64)
            v = tokens[block, :].astype(F32)
            v = v * lax.rsqrt(jnp.sum(v * v, axis=1, keepdims=True) / d_model + EPS)
            normed[block, :] = (v * ngain_ref[...]).astype(BF16)
            return carry

        lax.fori_loop(0, length // 64, norm, 0)
        tail[0:8, :] = jnp.zeros((8, tail_cols), F32)
        pbuf[0:8, :] = jnp.zeros((8, cols_g), F32)
        tail_load.stage(2)
        exchange(0).wait()
        counts[1] = counts[0] + countr[0]
        exchange(1).start()
        for i in range(length // 256):
            block = slice(i * 256, (i + 1) * 256)
            normed_t[:, block] = normed[block, :].T
        leave(2).start()
        leave(3).start()
        tail_load.stage(3)
        exchange(1).wait()
        counts[2] = counts[1] + countr[1]
        exchange(2).start()
        loads[0].stage(2)
        tail_load.stage(4)
        exchange(2).wait()
        counts[3] = counts[2] + countr[2]
        for k in range(1, levels):
            spread(k).start()
        countz[spot.level] = counts[3]
        loads[0].stage(3)
        tail_load.stage(5)
        leave(1).start()
        project(weight_tail.reshape(d_model, tail_cols), tail, slice(0, tail_cols))
        leave(4).start()
        loads[0].stage(4)
        for k in range(1, levels):
            spread(k).wait()
        total = countz[0]
        for k in range(1, levels):
            total = total + countz[k]
        counts[4] = total
        cums[...] = jnp.zeros_like(cums)

        def shared(i, carry):
            at = pl.ds(pl.multiple_of(i * rows, rows), rows)
            aux = aux_ref[at, :]
            marks = marks_of(aux)
            start = pl.multiple_of(i * rows, rows)
            raw = tail[pl.ds(start + 8, rows), conv_tail : conv_tail + heads]
            shifted, size, cum, from_prev, to_end = small_terms(
                raw, bias_ref[...], rate_ref[...], aux[:, 7:8], aux[:, 8:9], rows
            )
            cums[i, :, 0:heads] = cum
            stacks[i] = jnp.concatenate(
                [jnp.concatenate(split2(v), axis=1) for v in (size, from_prev, to_end)], axis=0
            )
            for c in range(conv_tail // LANES):
                cols = slice(c * LANES, (c + 1) * LANES)
                act = conv(tail, start, cols, slice(inner + c * LANES, inner + (c + 1) * LANES), marks)
                bc[i, :, cols] = act.astype(BF16)
            causal = (iota((rows, rows), 0) >= iota((rows, rows), 1)) & (aux[:, 0:1] == seg_ref[i])
            scores[i] = jnp.where(causal, mm_nt(bc[i, :, n:], bc[i, :, 0:n]), 0.0)
            return carry

        lax.fori_loop(0, seq_chunks, shared, 0)

    scan_steps = GROUPS * seq_chunks
    events = {}
    for k in range(1, 3 * GROUPS):
        begin = max(0, (k - 2) * 3 * seq_chunks // 8)
        times = [begin, *[begin + 1 + delay * seq_chunks // 8 for delay in LOAD_STEPS]]
        if k == 1:
            times = [None, 1, seq_chunks // 2, seq_chunks - 1]
        need = min(k * seq_chunks, scan_steps)
        for number, when in enumerate(times):
            if when is not None:
                events.setdefault(min(when, need), []).append((k, number + 1))
        if k < 2 * GROUPS:
            events.setdefault(need, []).append((k, 5))
    late = sorted(events.pop(scan_steps), key=lambda pair: (pair[1] + pair[0], pair[0]))
    for at, happen in sorted(events.items()):

        @pl.when(step == at)
        def _(happen=sorted(happen, key=lambda pair: (pair[0], pair[1]))):
            for k, number in happen:
                loads[k].stage(number)

    @pl.when(step == scan_steps)
    def _():
        leave(0).start()
        for k, number in late:
            loads[k].stage(number)

    for g in range(GROUPS):

        @pl.when(step == g * seq_chunks)
        def _(g=g):
            if g == 0:
                loads[0].stage(5)
            project(wx.reshape(d_model, inner), pbuf, slice(g * cols_g, (g + 1) * cols_g))

    @pl.when(step < scan_steps)
    def _():
        @pl.when(chunk == 0)
        def _():
            state[...] = jnp.zeros_like(state)

        aux = aux_ref[here, :]
        marks = marks_of(aux)
        ex[...] = mm(stacks[chunk], e_ref[:, pl.ds(gcol, cols_g)])
        head0 = group * per_group
        pick = (iota((LANES, LANES), 0) == iota((LANES, LANES), 1) + head0).astype(BF16)
        moved = [mm(v, pick) for v in split3(cums[chunk])]
        cum = moved[0] + moved[1] + moved[2]
        cum_t = cum.T
        start = pl.multiple_of(chunk * rows, rows)
        px_ref[...] = pbuf[pl.ds(start + 8, rows), :]
        for c in range(tiles):
            cols = slice(c * LANES, (c + 1) * LANES)
            act = conv(pbuf, start, cols, pl.ds(gcol + c * LANES, LANES), marks)
            xs[:, cols] = act
            scaled = act * ex[0:rows, cols]
            xdt[:, cols] = scaled.astype(BF16)
            xe[:, cols] = (scaled * ex[2 * rows : 3 * rows, cols]).astype(BF16)
        b, cc = bc[chunk, :, 0:n], bc[chunk, :, n:]
        state_low = state[...].astype(BF16)
        state_out_ref[...] = state_low
        yin[...] = mm(cc, state_low)
        state[...] = state[...] * ex[2 * rows - 1 : 2 * rows, :] + mm_tn(b, xe[...])
        score = scores[chunk]
        lane = iota((1, LANES), 1)
        masks = [(lane < width).astype(BF16), (lane >= width).astype(BF16)]
        for c in range(tiles):
            cols = slice(c * LANES, (c + 1) * LANES)
            mixing = []
            for h in (2 * c, 2 * c + 1):
                spread_h = jnp.minimum(cum[:, h : h + 1] - cum_t[h : h + 1, :], 0.0)
                mixing.append((score * jnp.exp(spread_h)).astype(BF16))
            x_low = xdt[:, cols]
            y = mm(
                jnp.concatenate(mixing, axis=1), jnp.concatenate([x_low * masks[0], x_low * masks[1]], axis=0)
            ) + ex[rows : 2 * rows, cols] * yin[:, cols]
            acols = pl.ds(gcol + c * LANES, LANES)
            y = y + skip_ref[:, acols] * xs[:, cols]
            ssd_ref[:, cols] = y
            ssd_all[here, acols] = y

    @pl.when(step >= scan_steps)
    def _():
        turn = step - scan_steps
        block_rows = gates.shape[0]
        base = pl.multiple_of(turn * block_rows, block_rows)
        flat_gate = wg.reshape(d_model, inner)
        flat_out = wo.reshape(inner, d_model)
        sub = 64
        own_rows = normed[pl.ds(base, block_rows), :]
        for k in range(GROUPS):
            cols = slice(k * cols_g, (k + 1) * cols_g)
            gates[:, cols] = mm(own_rows, flat_gate[:, cols])

        @pl.when(turn == 0)
        def _():
            dgain_ref[...] = jnp.zeros_like(dgain_ref)
            small_ref[...] = jnp.zeros_like(small_ref)
            for k in range(2 * GROUPS, 3 * GROUPS):
                loads[k].stage(5)

        def norm_of(i):
            at = pl.ds(pl.multiple_of(i * sub, sub), sub)
            return at, pl.ds(pl.multiple_of(base + i * sub, sub), sub)

        def forward_part(i, carry):
            at, full_at = norm_of(i)
            squares = jnp.zeros((sub, LANES), F32)
            for c in range(inner // LANES):
                cols = slice(c * LANES, (c + 1) * LANES)
                gate = gates[at, cols]
                gated = ssd_all[full_at, cols] * (gate * sigmoid(gate))
                gateds[at, cols] = gated
                squares = squares + gated * gated
            inverse = lax.rsqrt(jnp.sum(squares, axis=1, keepdims=True) / inner + EPS)
            for c in range(inner // LANES):
                cols = slice(c * LANES, (c + 1) * LANES)
                unit = gateds[at, cols] * inverse
                gateds[at, cols] = unit
                mixed_ref[at, cols] = (unit * gain_ref[:, cols]).astype(BF16)
            inverses[at, :] = jnp.broadcast_to(inverse, (sub, LANES))
            return carry

        lax.fori_loop(0, block_rows // sub, forward_part, 0)
        results[...] = mm(mixed_ref[...], flat_out[...])
        scale = 2.0 * loss_weight / (counts[4, 0:1, :] * d_model)

        def loss_part(i, carry):
            at, full_at = norm_of(i)
            valid = jnp.broadcast_to(aux_ref[full_at, 9:10], (sub, LANES))
            squares = jnp.zeros((8, LANES), F32)
            for c in range(d_model // LANES):
                cols = slice(c * LANES, (c + 1) * LANES)
                result = tokens[full_at, cols].astype(F32) + results[at, cols]
                output_ref[at, cols] = result.astype(BF16)
                error = result - teacher_ref[at, cols].astype(F32)
                squares = squares + jnp.sum((valid * error * error).reshape(sub // 8, 8, LANES), axis=0)
                gb_ref[at, cols] = (valid * (cotan_ref[at, cols].astype(F32) + scale * error)).astype(BF16)
            small_ref[0:8, :] += squares
            return carry

        lax.fori_loop(0, block_rows // sub, loss_part, 0)
        small_ref[8:16, :] = counts[4]
        grads = gb_ref[...]
        for k in range(GROUPS):
            cols = slice(k * cols_g, (k + 1) * cols_g)
            gms[:, cols] = mm_nt(grads, flat_out[cols, :])

        def backward_part(i, carry):
            at, full_at = norm_of(i)
            cross = jnp.zeros((sub, LANES), F32)
            for c in range(inner // LANES):
                cols = slice(c * LANES, (c + 1) * LANES)
                cross = cross + gms[at, cols] * gain_ref[:, cols] * gateds[at, cols]
            inverse = inverses[at, :]
            mean_cross = jnp.sum(cross, axis=1, keepdims=True) / inner
            for c in range(inner // LANES):
                cols = slice(c * LANES, (c + 1) * LANES)
                gate = gates[at, cols]
                sig = sigmoid(gate)
                silu = gate * sig
                unit = gateds[at, cols]
                grad_mixed = gms[at, cols]
                dgain_ref[:, cols] += jnp.sum((grad_mixed * unit).reshape(sub // 8, 8, LANES), axis=0)
                grad_gated = inverse * (grad_mixed * gain_ref[:, cols] - unit * mean_cross)
                dy_ref[at, cols] = (grad_gated * silu).astype(BF16)
                dz_ref[at, cols] = (
                    grad_gated * ssd_all[full_at, cols] * (sig + silu * (1.0 - sig))
                ).astype(BF16)
            return carry

        lax.fori_loop(0, block_rows // sub, backward_part, 0)
        gn_ref[...] = mm_nt(dz_ref[...], flat_gate[...])

        @pl.when(turn == length // block_rows - 1)
        def _():
            for k in range(len(leaves)):
                leave(k).wait()


def first(
    tokens, norm_gain, aux, seg_rows, count, conv_w, conv_b, bias, rate, skip_row, gain_row, e,
    cotangent, teacher, w_in, w_tail, w_out, levels, loss_weight,
):
    length, d = tokens.shape
    heads, inner = bias.shape[1], skip_row.shape[1]
    rows_f = w_in.shape[0]
    n = (conv_w.shape[1] - inner) // 2
    r = CHUNK
    chunks = length // r
    wide = inner // GROUPS
    tcols = w_tail.shape[1]
    units = 3 * GROUPS
    tall = 256
    scan_steps = GROUPS * chunks

    def scan_block(s):
        s = jnp.minimum(s, scan_steps - 1)
        return s % chunks, s // chunks

    block = lambda h: pl.BlockSpec((h, wide), scan_block)
    late = lambda w: pl.BlockSpec((tall, w), lambda s: (jnp.maximum(s - scan_steps, 0), 0))
    whole = lambda a: pl.BlockSpec(a.shape, lambda s: (0,) * a.ndim, pipeline_mode=pl.Buffered(1))
    fixed = lambda *dims: pl.BlockSpec(dims, lambda s: (0,) * len(dims))
    anywhere = pl.BlockSpec(memory_space=pl.ANY)
    vm = pltpu.VMEM
    shape = jax.ShapeDtypeStruct
    wide_shape = (levels, 2, 2, rows_f, inner)
    return pl.pallas_call(
        functools.partial(
            first_kernel, inner=inner, heads=heads, width=inner // heads, levels=levels, seq_chunks=chunks,
            loss_weight=loss_weight,
        ),
        grid=(scan_steps + length // tall,),
        in_specs=[
            late(d), late(d), anywhere,
            *[whole(a) for a in (norm_gain, aux, seg_rows, count, conv_w, conv_b, bias, rate, skip_row, gain_row, e)],
            anywhere, anywhere, anywhere,
        ],
        out_specs=[
            block(r), block(r), block(n), *[anywhere] * 5,
            late(d), late(d), late(inner), late(inner), late(inner), late(d), fixed(8, inner), fixed(16, LANES),
        ],
        out_shape=[
            shape((length, inner), F32), shape((length, inner), F32), shape((chunks * n, inner), BF16),
            shape((length, tcols), F32), shape((length, d), BF16), shape((d, length), BF16),
            shape(wide_shape, BF16), shape((levels, 2, 2, rows_f, tcols), BF16),
            shape((length, d), BF16), shape((length, d), BF16), shape((length, inner), BF16),
            shape((length, inner), BF16), shape((length, inner), BF16), shape((length, d), F32),
            shape((8, inner), F32), shape((16, LANES), F32),
        ],
        scratch_shapes=[
            vm((length, d), BF16), vm((length, d), BF16), vm((d, length), BF16),
            vm(wide_shape, BF16), vm(wide_shape, BF16), vm((levels, 2, 2, 2 * rows_f, d), BF16),
            vm((levels, 2, 2, rows_f, tcols), BF16),
            vm((length + 8, tcols), F32), vm((length + 8, wide), F32), vm((length, inner), F32),
            vm((tall, inner), F32), vm((tall, inner), F32), vm((tall, inner), F32), vm((tall, d), F32),
            vm((tall, LANES), F32),
            vm((3 * r, wide), F32), vm((n, wide), F32), vm((r, wide), F32), vm((r, wide), BF16), vm((r, wide), BF16),
            vm((chunks, r, 2 * n), BF16), vm((r, wide), F32), vm((chunks, r, LANES), F32), vm((chunks, r, r), F32),
            vm((chunks, 3 * r, 2 * heads), BF16),
            vm((5, 8, LANES), F32), vm((3, 8, LANES), F32), vm((levels, 8, LANES), F32),
            pltpu.SemaphoreType.DMA((units + 1, 7 + 2 * levels)),
            pltpu.SemaphoreType.DMA((4 + 2 * levels,)),
            pltpu.SemaphoreType.DMA((1,)),
            pltpu.SemaphoreType.DMA((5,)),
        ],
        compiler_params=pltpu.CompilerParams(
            dimension_semantics=("arbitrary",), vmem_limit_bytes=60 * 2**20,
            collective_id=2, has_side_effects=True,
        ),
        name="scan_forward",
    )(
        cotangent, teacher, tokens, norm_gain, aux, seg_rows, count, conv_w, conv_b, bias, rate, skip_row, gain_row, e,
        w_in, w_tail, w_out,
    )


def on_device(
    tokens,
    norm_gain,
    in_weight,
    conv_weight,
    conv_bias,
    step_bias,
    decay_log,
    skip_gain,
    out_gain,
    out_weight,
    cotangent,
    teacher,
    segment,
    valid_mask,
):
    seqs, length, width = tokens.shape
    rows = seqs * length
    shards = lax.axis_size("fsdp")
    devices = lax.axis_size("rep") * shards
    levels = shards // 4
    loss_weight = float(rows * devices * width // 8)
    valid = valid_mask.astype(F32)
    heads = step_bias.shape[0]
    inner = out_gain.shape[0]
    head_width = inner // heads
    aux, seg_rows = helpers(segment, valid, CHUNK)
    e, et = head_maps(heads, head_width)
    rate = -jnp.exp(decay_log)[None, :]
    skip_row = jnp.repeat(skip_gain, head_width)[None, :]
    params = (conv_weight, conv_bias[None, :], step_bias[None, :], rate, skip_row)
    tail_at = 2 * inner
    tail_pad = -(in_weight.shape[1] - tail_at) % LANES
    in_tail = jnp.pad(in_weight[:, tail_at:], ((0, 0), (0, tail_pad)))
    count = jnp.broadcast_to(jnp.sum(valid), (8, LANES))
    flat, cotan, target = (v.reshape(rows, width) for v in (tokens, cotangent, teacher))
    (
        px, ssd, states, tail, normed, normed_t, wx, wt, output, grad_branch, mixed, dy, dz, gn, dgain, sums
    ) = first(
        flat, norm_gain[None, :], aux, seg_rows, count, *params, out_gain[None, :], e, cotan, target,
        in_weight, in_tail, out_weight, levels, loss_weight,
    )
    wx, wt = (w.reshape(-1, w.shape[-1]) for w in (wx, wt))
    denominator = sums[8, 0] * width
    grad_out = mm_tn(mixed, grad_branch).astype(BF16)
    grad_gate = mm(normed_t, dz).astype(BF16)
    grad_in, grad_out, grad_tokens, small = back(
        px, 0, tail, ssd, dy, states, aux, seg_rows, *params, e, et,
        norm_gain[None, :], dgain, sums[:8], normed_t, wx, wt, gn, flat, grad_branch,
        grad_gate.reshape(levels, 2, 2, width // shards, inner),
        grad_out.reshape(levels, 2, 2, inner // shards, width), in_weight.shape[1],
    )
    taps, conv_width = conv_weight.shape
    extra = small[7, width:]
    loss = jnp.sum(extra[2 * LANES : 3 * LANES]) / denominator
    return (
        output.reshape(tokens.shape),
        loss,
        grad_tokens.reshape(tokens.shape),
        small[7, :width],
        grad_in,
        small[:taps, :conv_width],
        small[taps, :conv_width],
        extra[:heads],
        extra[LANES : LANES + heads],
        small[6, :inner].reshape(heads, head_width).sum(axis=1),
        small[5, :inner],
        grad_out,
    )


def solution(mesh):
    tokens = P(("rep", "fsdp"), None, None)
    marks = P(("rep", "fsdp"), None)
    shard = P("fsdp", None)
    return jax.shard_map(
        on_device,
        mesh=mesh,
        in_specs=(tokens, P(), shard, P(), P(), P(), P(), P(), P(), shard, tokens, tokens, marks, marks),
        out_specs=(tokens, P(), tokens, P(), shard, P(), P(), P(), P(), P(), P(), shard),
        check_vma=False,
    )
```

```python
import functools

import jax
import jax.numpy as jnp
from jax import lax
from jax.experimental import pallas as pl
from jax.experimental.pallas import tpu as pltpu
from jax.sharding import PartitionSpec as P

CHUNK = 128
LANES = 128
EPS = 1e-05
F32 = jnp.float32
BF16 = jnp.bfloat16
NT = (((1,), (1,)), ((), ()))
TN = (((0,), (0,)), ((), ()))


def mm(a, b):
    return jnp.dot(a, b, preferred_element_type=F32)


def mm_nt(a, b):
    return lax.dot_general(a, b, NT, preferred_element_type=F32)


def mm_tn(a, b):
    return lax.dot_general(a, b, TN, preferred_element_type=F32)


def split2(v):
    high = v.astype(BF16)
    return high, (v - high.astype(F32)).astype(BF16)


def split3(v):
    high = v.astype(BF16)
    rest = v - high.astype(F32)
    mid = rest.astype(BF16)
    return high, mid, (rest - mid.astype(F32)).astype(BF16)


def tri_sum(tri, v):
    heads = v.shape[1]
    parts = mm(tri, jnp.concatenate(split3(v), axis=1))
    return parts[:, :heads] + parts[:, heads : 2 * heads] + parts[:, 2 * heads :]


def sum_tri(v, tri):
    heads = v.shape[0]
    parts = mm(jnp.concatenate(split3(v), axis=0), tri)
    return parts[:heads] + parts[heads : 2 * heads] + parts[2 * heads :]


def sigmoid(v):
    return 0.5 * jnp.tanh(0.5 * v) + 0.5


def softplus(v):
    return jnp.maximum(v, 0.0) + jnp.log1p(jnp.exp(-jnp.abs(v)))


def iota(shape, dim):
    return lax.broadcasted_iota(jnp.int32, shape, dim)


def small_terms(step_raw, step_bias, decay_rate, keep, to_end, rows):
    shifted = step_raw + step_bias
    step = softplus(shifted)
    lower = (iota((rows, rows), 0) >= iota((rows, rows), 1)).astype(BF16)
    cum = tri_sum(lower, step * decay_rate)
    last = cum[rows - 1 : rows, :]
    return shifted, step, cum, jnp.exp(cum) * keep, jnp.exp(last - cum) * to_end


def expand(e_ref, out_ref, step, from_prev, to_end):
    stacked = jnp.concatenate(
        [jnp.concatenate(split2(v), axis=1) for v in (step, from_prev, to_end)], axis=0
    )
    out_ref[...] = mm(stacked, e_ref[...])


def full(shape):
    return pl.BlockSpec(shape, lambda i: (0,) * len(shape))


def prepare_kernel(
    segment_ref, valid_ref, bias_ref, log_ref, skip_ref, cb_ref, ngain_ref, gain_ref, weight_ref,
    aux_ref, rows_ref, count_ref, bias_out, rate_out, rate_t_out, skip_out, cb_out, ngain_out, gain_out, e_out, tail_out,
    *, tail_cols,
):
    length = segment_ref.shape[1]
    heads = bias_ref.shape[0]
    inner = gain_ref.shape[0]
    width = inner // heads
    docs = segment_ref[...].astype(F32)
    valid = valid_ref[...].astype(F32)
    place = iota((8, length), 1)
    wide = jnp.broadcast_to(docs, (8, length))
    marks = []
    for k in (1, 2, 3):
        marks.append(jnp.where((wide == pltpu.roll(wide, k, 1)) & (place >= k), 1.0, 0.0)[0:1])
    for k in (1, 2, 3):
        marks.append(jnp.where((wide == pltpu.roll(wide, length - k, 1)) & (place < length - k), 1.0, 0.0)[0:1])
    for c in range(length // CHUNK):
        cols = slice(c * CHUNK, (c + 1) * CHUNK)
        own = docs[:, cols]
        last = docs[:, (c + 1) * CHUNK - 1 : (c + 1) * CHUNK]
        keep = jnp.zeros_like(own)
        if c:
            keep = jnp.where(own == docs[:, c * CHUNK - 1 : c * CHUNK], 1.0, 0.0)
        stacked = [own, *[v[:, cols] for v in marks], keep, jnp.where(own == last, 1.0, 0.0), valid[:, cols]]
        stacked.append(jnp.zeros((LANES - len(stacked), CHUNK), F32))
        aux_ref[cols, :] = jnp.concatenate(stacked, axis=0).T[:, 0:16]
        rows_ref[c] = own
    count_ref[...] = jnp.broadcast_to(jnp.sum(valid, axis=1, keepdims=True), count_ref.shape)
    bias_out[...] = bias_ref[...].reshape(1, heads)
    rate = -jnp.exp(log_ref[...].reshape(1, heads))
    rate_out[...] = rate
    spare = jnp.concatenate([rate, jnp.zeros((1, LANES - heads), F32)], axis=1)
    rate_t_out[...] = jnp.broadcast_to(spare, (LANES, LANES)).T[0:heads, 0:1]
    e = (iota((2 * heads, inner), 0) % heads == iota((2 * heads, inner), 1) // width).astype(BF16)
    e_out[...] = e
    skip = jnp.broadcast_to(skip_ref[...].reshape(1, heads), (16, heads))
    parts = [mm(v, e[0:heads]) for v in split3(skip)]
    skip_out[...] = (parts[0] + parts[1] + parts[2])[0:1]
    cb_out[...] = cb_ref[...].reshape(1, cb_ref.shape[0])
    ngain_out[...] = ngain_ref[...].reshape(1, ngain_ref.shape[0])
    gain_out[...] = gain_ref[...].reshape(1, inner)
    rows_f = weight_ref.shape[0]
    tail_out[...] = jnp.concatenate(
        [weight_ref[:, 0:tail_cols], jnp.zeros((rows_f, tail_out.shape[1] - tail_cols), BF16)], axis=1
    )


def prepare(segment, valid_mask, step_bias, decay_log, skip_gain, conv_bias, norm_gain, out_gain, in_weight):
    length = segment.shape[1]
    heads, inner = step_bias.shape[0], out_gain.shape[0]
    rows_f, proj = in_weight.shape
    tail_cols = proj - 2 * inner
    tail_wide = -(-tail_cols // LANES) * LANES
    shape = jax.ShapeDtypeStruct
    small = (segment, valid_mask, step_bias, decay_log, skip_gain, conv_bias, norm_gain, out_gain)
    outs = [
        shape((length, 16), F32), shape((length // CHUNK, 1, CHUNK), F32), shape((8, LANES), F32),
        shape((1, heads), F32), shape((1, heads), F32), shape((heads, 1), F32), shape((1, inner), F32),
        shape((1, conv_bias.shape[0]), F32), shape((1, norm_gain.shape[0]), F32), shape((1, inner), F32),
        shape((2 * heads, inner), BF16), shape((rows_f, tail_wide), BF16),
    ]
    block = 512
    return pl.pallas_call(
        functools.partial(prepare_kernel, tail_cols=tail_cols),
        grid=(1,),
        in_specs=[*[full(a.shape) for a in small], pl.BlockSpec((rows_f, block), lambda i: (0, 2 * inner // block))],
        out_specs=[full(o.shape) for o in outs],
        out_shape=outs,
        name="prepare",
    )(*small, in_weight)


def finish_kernel(
    gi_ref, go_ref, gt_ref, output_ref, small_ref, dng_ref, sums_ref, e_ref,
    out_final, loss_ref, gt_final, ngain_ref, gi_final, cw_ref, cb_ref, bias_ref, log_ref, skip_ref, gain_ref, go_final,
    gi, go, gt, output, sems,
):
    trios = ((gt_ref, gt, gt_final), (output_ref, output, out_final), (gi_ref, gi, gi_final), (go_ref, go, go_final))
    fetches = [pltpu.make_async_copy(a, b, sems.at[i]) for i, (a, b, c) in enumerate(trios)]
    stores = [pltpu.make_async_copy(b, c, sems.at[4 + i]) for i, (a, b, c) in enumerate(trios)]
    for copy in fetches:
        copy.start()
    for fetched, stored in zip(fetches, stores):
        fetched.wait()
        stored.start()
    taps, conv_width = cw_ref.shape
    heads, inner = bias_ref.shape[0], gain_ref.shape[0]
    d = dng_ref.shape[0] * LANES
    cw_ref[...] = small_ref[0:taps, 0:conv_width]
    cb_ref[...] = small_ref[taps : taps + 1, 0:conv_width].reshape(conv_width)
    gain_ref[...] = small_ref[5:6, 0:inner].reshape(inner)
    bias_ref[...] = small_ref[7:8, 0:heads].reshape(heads)
    log_ref[...] = small_ref[7:8, LANES : LANES + heads].reshape(heads)
    squares = jnp.sum(small_ref[7:8, 2 * LANES : 3 * LANES], axis=1, keepdims=True)
    loss_ref[...] = squares / (sums_ref[8:9, 0:1] * d)
    by_head = jnp.zeros((16, 2 * heads), F32)
    for v in split3(jnp.broadcast_to(small_ref[6:7, 0:inner], (16, inner))):
        by_head = by_head + mm_nt(v, e_ref[...])
    skip_ref[...] = by_head[0:1, 0:heads].reshape(heads)
    ngain_ref[...] = dng_ref[...].reshape(d)
    for copy in stores:
        copy.wait()


def finish(gi, go, gt, output, small, dng, sums, e, taps, conv_width, heads, inner):
    shape = jax.ShapeDtypeStruct
    anywhere = pl.BlockSpec(memory_space=pl.ANY)
    outs = [
        shape(output.shape, BF16), shape((1, 1), F32), shape(gt.shape, BF16), shape((dng.size,), F32),
        shape(gi.shape, F32), shape((taps, conv_width), F32), shape((conv_width,), F32), shape((heads,), F32),
        shape((heads,), F32), shape((heads,), F32), shape((inner,), F32), shape(go.shape, F32),
    ]
    far = (0, 2, 4, 11)
    return pl.pallas_call(
        finish_kernel,
        grid=(1,),
        in_specs=[*[anywhere] * 4, *[full(a.shape) for a in (small, dng, sums, e)]],
        out_specs=[anywhere if i in far else full(o.shape) for i, o in enumerate(outs)],
        out_shape=outs,
        scratch_shapes=[
            *[pltpu.VMEM(a.shape, a.dtype) for a in (gi, go, gt, output)], pltpu.SemaphoreType.DMA((8,)),
        ],
        compiler_params=pltpu.CompilerParams(vmem_limit_bytes=60 * 2**20),
        name="finish",
    )(gi, go, gt, output, small, dng, sums, e)


MESH = pl.DeviceIdType.MESH


class Spot:
    def __init__(self, levels):
        self.rep, self.at = lax.axis_index("rep"), lax.axis_index("fsdp")
        self.core, self.side, self.level = self.at % 2, (self.at // 2) % 2, self.at // 4
        self.levels = levels
        self.sibling = (self.rep, self.at + 1 - 2 * self.core)
        self.across = (self.rep, self.at + 2 - 4 * self.side)
        self.twin = (1 - self.rep, self.at)

    def far(self, step):
        return (self.rep, ((self.level + step) % self.levels) * 4 + self.at % 4)

    def corner(self, j):
        flip = lambda v, bit: 1 - v if j & bit else v
        return (flip(self.rep, 4), self.level * 4 + flip(self.side, 2) * 2 + flip(self.core, 1))

    def greet(self, corners=False):
        barrier = pltpu.get_barrier_semaphore()
        near = [self.corner(j) for j in range(1, 8)] if corners else [self.sibling, self.across, self.twin]
        partners = near + [self.far(d) for d in range(1, self.levels)]
        for one in partners:
            pl.semaphore_signal(barrier, inc=1, device_id=one, device_id_type=MESH)
        pl.semaphore_wait(barrier, len(partners))


def send(src, dst, send_sem, recv_sem, device):
    return pltpu.make_async_remote_copy(
        src_ref=src, dst_ref=dst, send_sem=send_sem, recv_sem=recv_sem, device_id=device, device_id_type=MESH
    )


class Split:
    def __init__(self, spot, whole, own, from_core, half, from_side, from_level, mine, from_twin, sems, write):
        self.spot, self.whole, self.own, self.write = spot, whole, own, write
        self.from_core, self.half, self.from_side, self.from_level = from_core, half, from_side, from_level
        self.mine, self.from_twin, self.sems = mine, from_twin, sems
        self.cols = half.shape[-1]

    def columns(self, rep):
        return pl.ds(pl.multiple_of(rep * self.cols, self.cols), self.cols)

    @property
    def c0(self):
        return pltpu.make_async_copy(self.whole.at[:, :, self.spot.core], self.own, self.sems.at[6])

    @property
    def c1(self):
        spot, sems = self.spot, self.sems
        return send(self.whole.at[:, :, 1 - spot.core], self.from_core, sems.at[0], sems.at[1], spot.sibling)

    @property
    def c2(self):
        spot, sems = self.spot, self.sems
        block = self.own.at[:, :, :, self.columns(1 - spot.rep)]
        return send(block, self.half, sems.at[2], sems.at[3], spot.twin)

    @property
    def c3(self):
        spot, sems = self.spot, self.sems
        last = 5 + 2 * spot.levels
        return send(self.half.at[:, 1 - spot.side], self.from_side, sems.at[last], sems.at[last + 1], spot.across)

    @property
    def c4(self):
        spot, sems = self.spot, self.sems
        return [
            send(
                self.from_side.at[(spot.level + d) % spot.levels], self.from_level.at[d - 1],
                sems.at[5 + 2 * d], sems.at[6 + 2 * d], spot.far(d),
            )
            for d in range(1, spot.levels)
        ]

    @property
    def c5(self):
        spot, sems = self.spot, self.sems
        return send(self.mine, self.from_twin, sems.at[4], sems.at[5], spot.twin)

    def stage(self, number):
        spot, levels = self.spot, self.spot.levels
        if number == 1:
            self.c1.start()
            self.c0.start()
        elif number == 2:
            self.c0.wait()
            self.c1.wait()

            def add(i, carry):
                for side in range(2):
                    self.own[i, side] = self.own[i, side] + self.from_core[i, side]
                return carry

            lax.fori_loop(0, levels, add, 0)
            self.c2.start()
        elif number == 3:
            self.c2.wait()
            columns = self.columns(spot.rep)

            def add(i, carry):
                for side in range(2):
                    self.half[i, side] = self.half[i, side] + self.own[i, side, :, columns]
                return carry

            lax.fori_loop(0, levels, add, 0)
            self.c3.start()
        elif number == 4:
            self.c3.wait()

            def add(i, carry):
                self.from_side[i] = self.from_side[i] + self.half[i, spot.side]
                return carry

            lax.fori_loop(0, levels, add, 0)
            for copy in self.c4:
                copy.start()
        elif number == 5:
            for copy in self.c4:
                copy.wait()
            total = self.from_side[spot.level].astype(F32)
            for d in range(levels - 1):
                total = total + self.from_level[d].astype(F32)
            self.mine[...] = total.astype(BF16)
            self.c5.start()
        else:
            self.c5.wait()
            self.write(self.mine[...].astype(F32), self.columns(spot.rep))
            self.write(self.from_twin[...].astype(F32), self.columns(1 - spot.rep))


class Unit:
    def __init__(self, spot, whole, own, from_core, from_side, from_level, mine, from_twin, sems, write):
        self.spot, self.whole, self.own, self.write = spot, whole, own, write
        self.from_core, self.from_side, self.from_level = from_core, from_side, from_level
        self.mine, self.from_twin = mine, from_twin
        self.sems = sems

    @property
    def c0(self):
        return pltpu.make_async_copy(self.whole.at[:, :, self.spot.core], self.own, self.sems.at[6])

    @property
    def c1(self):
        spot, sems = self.spot, self.sems
        return send(self.whole.at[:, :, 1 - spot.core], self.from_core, sems.at[0], sems.at[1], spot.sibling)

    @property
    def c2(self):
        spot, sems = self.spot, self.sems
        return send(self.own.at[:, 1 - spot.side], self.from_side, sems.at[2], sems.at[3], spot.across)

    @property
    def c3(self):
        spot, sems = self.spot, self.sems
        return [
            send(
                self.from_side.at[(spot.level + d) % spot.levels], self.from_level.at[d - 1],
                sems.at[5 + 2 * d], sems.at[6 + 2 * d], spot.far(d),
            )
            for d in range(1, spot.levels)
        ]

    @property
    def c4(self):
        spot, sems = self.spot, self.sems
        return send(self.mine, self.from_twin, sems.at[4], sems.at[5], spot.twin)

    def stage(self, number):
        spot, levels = self.spot, self.spot.levels
        if number == 1:
            self.c1.start()
            self.c0.start()
        elif number == 2:
            self.c0.wait()
            self.c1.wait()

            def add(i, carry):
                for side in range(2):
                    self.own[i, side] = self.own[i, side] + self.from_core[i, side]
                return carry

            lax.fori_loop(0, levels, add, 0)
            self.c2.start()
        elif number == 3:
            self.c2.wait()

            def add(i, carry):
                self.from_side[i] = self.from_side[i] + self.own[i, spot.side]
                return carry

            lax.fori_loop(0, levels, add, 0)
            for copy in self.c3:
                copy.start()
        elif number == 4:
            for copy in self.c3:
                copy.wait()
            total = self.from_side[spot.level].astype(F32)
            for d in range(levels - 1):
                total = total + self.from_level[d].astype(F32)
            self.mine[...] = total.astype(BF16)
            self.c4.start()
        else:
            self.c4.wait()
            self.write(self.mine[...].astype(F32) + self.from_twin[...].astype(F32))


GROUPS = 4
STARTS = (0, 2, 4, 6, 8, 11, 13, 16, 18, 20, 24)
UNIT_DELAYS = (0, 1, 5, 9, 11)
SPLIT_DELAYS = (0, 1, 5, 8, 11, 13)


def back_kernel(
    px_ref, prev_ref, y_ref, dy_ref, state_ref,
    tail_ref, aux_ref, seg_ref, cw_ref, cb_ref, bias_ref, rate_ref, skip_ref, e_ref, rate_t_ref,
    ngain_ref, dgain_ref, square_ref,
    normed_t_hbm, wx_hbm, wt_hbm, gn_hbm, tokens_hbm, gb_hbm, ggate_hbm, gout_hbm,
    gi_ref, go_ref, gt_ref, small_ref, dng_ref,
    xbuf, ex, adj, xs, xdt, xe, bc, slope, dye, dxi, dbuf, r1, r1l, r2, r3,
    tbuf, consts, stacks, raws, cums, cum_ts, ones, steps, scores, dscores, gbs, gcs, sums, tslope, gp, gpt, accum, taccum,
    normed_t, wx, wt, gn, tokens, gb,
    own, part, part_t, own_t, from_core, from_core_t, from_side, from_side_t, from_level, from_level_t,
    mine, mine_t, twin, twin_t, half, half_side, half_level, half_mine, half_twin, local, sm, smr, smz, gain_out, gain_near, gain_sum, gain_far, sems, small_sems, gain_sems, load_sems,
    *, inner, heads, width, levels, seq_chunks,
):
    group, turn = pl.program_id(0), pl.program_id(1)
    step = group * seq_chunks + turn
    chunk = seq_chunks - 1 - turn
    rows, cols_g = px_ref.shape
    n = bc.shape[2] // 2
    tiles = cols_g // LANES
    per_group = cols_g // width
    taps = cw_ref.shape[0]
    tail_cols = tail_ref.shape[1]
    conv_tail = 2 * n
    here = pl.ds(pl.multiple_of(chunk * rows, rows), rows)
    spot = Spot(levels)
    gcol = pl.multiple_of(group * cols_g, cols_g)
    rows_f = mine.shape[1]

    def loads():
        pairs = ((normed_t_hbm, normed_t), (wx_hbm, wx), (wt_hbm, wt), (gn_hbm, gn), (tokens_hbm, tokens), (gb_hbm, gb))
        return [pltpu.make_async_copy(a, b, load_sems.at[i]) for i, (a, b) in enumerate(pairs)]

    def writer(ref, row, col, wide):
        def write(v, columns=None):
            if columns is None:
                ref[row : row + rows_f, col : col + wide] = v[:, :wide]
            else:
                at = pl.multiple_of(col + columns.start, LANES)
                ref[row : row + rows_f, pl.ds(at, columns.size)] = v
        return write

    sources = []
    for u in range(GROUPS):
        hbm = gout_hbm.at[:, :, :, pl.ds((u // 2) * rows_f, rows_f), pl.ds((u % 2) * cols_g, cols_g)]
        sources.append((hbm, writer(go_ref, (u // 2) * rows_f, (u % 2) * cols_g, cols_g)))
    for u in range(GROUPS):
        hbm = ggate_hbm.at[:, :, :, :, pl.ds(u * cols_g, cols_g)]
        sources.append((hbm, writer(gi_ref, 0, u * cols_g, cols_g)))
    for g in range(GROUPS):
        sources.append((part.at[g % 2], writer(gi_ref, 0, inner + g * cols_g, cols_g)))
    order = [0, 1, 2, 3, 8, 4, 5, 9, 6, 7, 10, 11]
    units = []
    for i, u in enumerate(order):
        k = i // 2
        whole, write = sources[u]
        if i % 2:
            units.append(
                Split(
                    spot, whole, own.at[u], from_core.at[u], half.at[k], half_side.at[k], half_level.at[k],
                    half_mine.at[k], half_twin.at[k], sems.at[u], write,
                )
            )
        else:
            units.append(
                Unit(
                    spot, whole, own.at[u], from_core.at[u], from_side.at[k], from_level.at[k], mine.at[k], twin.at[k],
                    sems.at[u], write,
                )
            )
    tail_wide = gi_ref.shape[1] - 2 * inner
    tail_unit = Unit(
        spot, part_t, own_t, from_core_t, from_side_t, from_level_t, mine_t, twin_t, sems.at[3 * GROUPS],
        writer(gi_ref, 0, 2 * inner, tail_wide),
    )

    events = {}
    last_step = GROUPS * seq_chunks - 1
    late = []
    for i, (begin, unit) in enumerate(zip(STARTS, units)):
        begin = begin * seq_chunks // 8
        for number, delay in enumerate(SPLIT_DELAYS if i % 2 else UNIT_DELAYS):
            events.setdefault(min(begin + delay, last_step), []).append((unit, number + 1))

    @pl.when(step == 0)
    def _():
        for copy in loads():
            copy.start()
        spot.greet(corners=True)
        accum[...] = jnp.zeros_like(accum)
        taccum[...] = jnp.zeros_like(taccum)
        steps[...] = jnp.zeros_like(steps)
        ones[...] = (iota(ones.shape, 0) == iota(ones.shape, 1) // width).astype(BF16)

    for at, happen in sorted(events.items()):
        if at == last_step:
            late += happen
            continue

        @pl.when(step == at)
        def _(happen=happen):
            for unit, number in sorted(happen, key=lambda pair: -pair[1]):
                unit.stage(number)

    def fold(v):
        return jnp.sum(v.reshape(v.shape[0] // 8, 8, v.shape[1]), axis=0)

    aux = aux_ref[here, :]
    marks = [None] + [jnp.broadcast_to(aux[:, k : k + 1], (rows, LANES)) for k in range(1, taps)]
    marks_next = [None] + [jnp.broadcast_to(aux[:, 3 + k : 4 + k], (rows, LANES)) for k in range(1, taps)]
    lower = iota((rows, rows), 0) >= iota((rows, rows), 1)
    upper = iota((rows, rows), 0) <= iota((rows, rows), 1)
    rate = rate_ref[...]

    def conv_pre(buffer, cols, wcols):
        pre = cb_ref[:, wcols] + cw_ref[0:1, wcols] * buffer[8 : 8 + rows, cols]
        for k in range(1, taps):
            pre = pre + (cw_ref[k : k + 1, wcols] * buffer[8 - k : 8 - k + rows, cols]) * marks[k]
        return pre

    def conv_back(buffer, cols, wcols, acc, acc_cols):
        outs = []
        adds = [jnp.zeros((8, LANES), F32) for _ in range(taps + 1)]
        for at in range(0, rows, 64):
            inputs = xbuf[8 + at : 72 + at, cols]
            for k in range(taps):
                grad = buffer[at + k : at + k + 64, cols]
                if k == 0:
                    out = cw_ref[0:1, wcols] * grad
                    adds[taps] = adds[taps] + fold(grad)
                else:
                    grad = grad * marks_next[k][at : at + 64]
                    out = out + cw_ref[k : k + 1, wcols] * grad
                adds[k] = adds[k] + fold(grad * inputs)
            outs.append(out)
        for k in range(taps + 1):
            acc[8 * k : 8 * k + 8, acc_cols] += adds[k]
        return jnp.concatenate(outs, axis=0)

    def fill_tail():
        xbuf[8 : 8 + rows, 0:conv_tail] = tail_ref[here, 0:conv_tail]
        before = pl.ds(pl.multiple_of(jnp.maximum(chunk * rows - 8, 0), 8), 8)
        xbuf[0:8, 0:conv_tail] = tail_ref[before, 0:conv_tail]

    @pl.when(group == 0)
    def _():
        shifted, step_size, cum, from_prev, to_end = small_terms(
            tail_ref[here, conv_tail : conv_tail + heads], bias_ref[...], rate, aux[:, 7:8], aux[:, 8:9], rows
        )
        turned = jnp.concatenate([shifted, step_size, cum, jnp.zeros((rows, LANES - 3 * heads), F32)], axis=1).T
        raws[chunk] = turned[0 : 2 * heads]
        cum_ts[chunk] = turned[2 * heads : 3 * heads]
        for g in range(GROUPS):
            cums[g, here, 0:per_group] = cum[:, g * per_group : (g + 1) * per_group]
        stacks[chunk] = jnp.concatenate(
            [jnp.concatenate(split2(v), axis=1) for v in (step_size, from_prev, to_end)], axis=0
        )
        fill_tail()
        for c in range(conv_tail // LANES):
            cols = slice(c * LANES, (c + 1) * LANES)
            pre = conv_pre(xbuf, cols, slice(inner + c * LANES, inner + (c + 1) * LANES))
            sig = sigmoid(pre)
            act = pre * sig
            tslope[here, cols] = sig + act * (1.0 - sig)
            bc[chunk, :, cols] = act.astype(BF16)
        same = upper & (aux[:, 0:1] == seg_ref[chunk])
        scores[chunk] = jnp.where(same, mm_nt(bc[chunk, :, 0:n], bc[chunk, :, n:]), 0.0)
        dscores[chunk] = jnp.zeros((rows, rows), F32)
        gbs[here, :] = jnp.zeros((rows, n), F32)
        gcs[here, :] = jnp.zeros((rows, n), F32)

    @pl.when(turn == 0)
    def _():
        adj[...] = jnp.zeros_like(adj)
        dbuf[rows : rows + 8, :] = jnp.zeros((8, cols_g), F32)

    ex[...] = mm(stacks[chunk], e_ref[:, pl.ds(gcol, cols_g)])
    own_heads = pl.ds(pl.multiple_of(group * per_group, per_group), per_group)
    cum = cums[group, here, :]
    cum_t = cum_ts[chunk, own_heads, :]
    xbuf[0:8, :] = prev_ref[...]
    xbuf[8 : 8 + rows, :] = px_ref[...]
    for c in range(tiles):
        cols = slice(c * LANES, (c + 1) * LANES)
        wcols = pl.ds(gcol + c * LANES, LANES)
        pre = conv_pre(xbuf, cols, wcols)
        sig = sigmoid(pre)
        act = pre * sig
        slope[:, cols] = sig + act * (1.0 - sig)
        xs[:, cols] = act
        scaled = act * ex[0:rows, cols]
        xdt[:, cols] = scaled.astype(BF16)
        xe[:, cols] = (scaled * ex[2 * rows : 3 * rows, cols]).astype(BF16)
        dye[:, cols] = (dy_ref[:, cols].astype(F32) * ex[rows : 2 * rows, cols]).astype(BF16)
    b, cc = bc[chunk, :, 0:n], bc[chunk, :, n:]
    state_low = state_ref[...]
    adj_low = adj[...].astype(BF16)
    carry = ex[2 * rows - 1 : 2 * rows, :]
    gcs[here, :] += mm_nt(dye[...], state_low)
    gbs[here, :] += mm_nt(xe[...], adj_low)
    dxi[...] = mm(b, adj_low)
    through = jnp.sum(adj[...] * state_low.astype(F32), axis=0, keepdims=True) * carry
    adj[...] = adj[...] * carry + mm_tn(cc, dye[...])
    scores_t = scores[chunk]
    lane = iota((1, LANES), 1)
    masks = [(lane < width).astype(BF16), (lane >= width).astype(BF16)]
    grad_scores_t = jnp.zeros((rows, rows), F32)
    for c in range(tiles):
        cols = slice(c * LANES, (c + 1) * LANES)
        acols = pl.ds(gcol + c * LANES, LANES)
        x_low, dy_low = xdt[:, cols], dy_ref[:, cols]
        grad_mix = mm_nt(jnp.concatenate([x_low * masks[0], x_low * masks[1]], axis=0), dy_low)
        mixing = []
        for i, h in enumerate((2 * c, 2 * c + 1)):
            decay = jnp.exp(jnp.minimum(cum_t[h : h + 1, :] - cum[:, h : h + 1], 0.0))
            mixing.append((scores_t * decay).astype(BF16))
            grad_scores_t = grad_scores_t + grad_mix[i * rows : (i + 1) * rows] * decay
        within = mm(
            jnp.concatenate(mixing, axis=1), jnp.concatenate([dy_low * masks[0], dy_low * masks[1]], axis=0)
        )
        x = xs[:, cols]
        skip = skip_ref[:, acols]
        across = ex[2 * rows : 3 * rows, cols] * dxi[:, cols]
        both = within + across
        grad_ssd = dy_low.astype(F32)
        x_scaled = x_low.astype(F32)
        r1[:, cols], r1l[:, cols] = split2(grad_ssd * y_ref[:, cols] - within * x_scaled)
        r2[:, cols] = (across * x_scaled).astype(BF16)
        r3[:, cols] = (both * x).astype(BF16)
        accum[8 * taps + 8 : 8 * taps + 16, acols] += fold(grad_ssd * x)
        grad_x = skip * grad_ssd + ex[0:rows, cols] * both
        dbuf[0:rows, cols] = grad_x * slope[:, cols]
    dscores[chunk] += grad_scores_t
    by_head = ones[...]
    sums[0, chunk, own_heads, :] = (mm_nt(by_head, r1[...]) + mm_nt(by_head, r1l[...]))[0:per_group]
    sums[1, chunk, own_heads, :] = mm_nt(by_head, r2[...])[0:per_group]
    sums[2, chunk, own_heads, :] = mm_nt(by_head, r3[...])[0:per_group]
    high, rest = split2(jnp.broadcast_to(through, (16, cols_g)))
    const = (mm_nt(by_head, high) + mm_nt(by_head, rest))[0:per_group, 0:1]
    consts[chunk, own_heads, :] = jnp.broadcast_to(const, (per_group, LANES))
    for c in range(tiles):
        cols = slice(c * LANES, (c + 1) * LANES)
        acols = pl.ds(gcol + c * LANES, LANES)
        gp[here, cols] = conv_back(dbuf, cols, acols, accum, acols).astype(BF16)
    dbuf[rows : rows + 8, :] = dbuf[0:8, :]

    @pl.when(group == GROUPS - 1)
    def _():
        same = upper & (aux[:, 0:1] == seg_ref[chunk])
        grad_scores = jnp.where(same, dscores[chunk], 0.0).astype(BF16)
        grad_b = gbs[here, :] + mm(grad_scores, cc)
        grad_c = gcs[here, :] + mm_tn(grad_scores, b)
        fill_tail()

        @pl.when(turn == 0)
        def _():
            tbuf[rows : rows + 8, :] = jnp.zeros((8, 2 * n), F32)

        tbuf[0:rows, 0:n] = grad_b * tslope[here, 0:n]
        tbuf[0:rows, n : 2 * n] = grad_c * tslope[here, n : 2 * n]
        for c in range(conv_tail // LANES):
            cols = slice(c * LANES, (c + 1) * LANES)
            gpt[here, cols] = conv_back(
                tbuf, cols, slice(inner + c * LANES, inner + (c + 1) * LANES), taccum, cols
            ).astype(BF16)
        tbuf[rows : rows + 8, :] = tbuf[0:8, :]
        shifted, step_size = raws[chunk, 0:heads, :], raws[chunk, heads : 2 * heads, :]
        turned_aux = jnp.concatenate([aux, jnp.zeros((rows, LANES - aux.shape[1]), F32)], axis=1).T
        grad_log = (
            sum_tri(sums[0, chunk], lower.astype(BF16))
            + sum_tri(sums[1, chunk], (iota((rows, rows), 0) < iota((rows, rows), 1)).astype(BF16))
            + consts[chunk]
        ) * turned_aux[1:2, :]
        rate_t = jnp.broadcast_to(rate_t_ref[...], (heads, rows))
        grad_raw = (sums[2, chunk] + rate_t * grad_log) * sigmoid(shifted)
        gpt[here, conv_tail:] = (
            jnp.concatenate([grad_raw, jnp.zeros((tail_cols - conv_tail - heads, rows), F32)], axis=0).T
        ).astype(BF16)
        steps[0] += grad_raw
        steps[1] += step_size * grad_log * rate_t

    def weight_grad(low, out):
        flat = out.reshape(normed_t.shape[0], low.shape[1])
        for k in range(0, low.shape[1], 256):
            cols = slice(k, min(k + 256, low.shape[1]))
            flat[:, cols] = mm(normed_t[...], low[:, cols]).astype(BF16)

    def input_grad(low, weights):
        for k in range(gn.shape[1] // 256):
            cols = slice(k * 256, (k + 1) * 256)
            gn[:, cols] += mm_nt(low[...], weights[cols, :])

    for g in range(GROUPS - 1):

        @pl.when(step == (g + 1) * seq_chunks - 1)
        def _(g=g):
            if g == 0:
                for copy in loads():
                    copy.wait()
            weight_grad(gp, part.at[g % 2])
            input_grad(gp, wx.at[:, g * cols_g : (g + 1) * cols_g])

    @pl.when(step == last_step)
    def _():
        d = gn.shape[1]
        half_cols = sm.shape[2]

        def half_of(core):
            return pl.ds(pl.multiple_of(core * half_cols, half_cols), half_cols)

        def exchange(i):
            src = (local.at[:, half_of(1 - spot.core)], sm.at[0], sm.at[1], sm.at[3])[i]
            device = (spot.sibling, spot.across, spot.twin, spot.sibling)[i]
            return send(src, smr.at[i], small_sems.at[2 * i], small_sems.at[2 * i + 1], device)

        spread = lambda k: send(
            sm.at[2], smz.at[spot.level], small_sems.at[6 + 2 * k], small_sems.at[7 + 2 * k], spot.far(k)
        )

        def one_row(v):
            return jnp.sum(v, axis=0, keepdims=True)

        def fold_small(i):
            exchange(i).wait()
            sm[i] = (local[:, half_of(spot.core)] if i == 0 else sm[i - 1]) + smr[i]

        local[...] = jnp.zeros(local.shape, F32)
        for k in range(taps + 1):
            local[k : k + 1, 0:inner] = one_row(accum[8 * k : 8 * k + 8, :])
            local[k : k + 1, inner : inner + conv_tail] = one_row(taccum[8 * k : 8 * k + 8, 0:conv_tail])
        local[5:6, 0:inner] = one_row(dgain_ref[...])
        local[6:7, 0:inner] = one_row(accum[8 * taps + 8 : 8 * taps + 16, :])
        for i in range(2):
            turned = jnp.concatenate([steps[i], jnp.zeros((LANES - heads, LANES), F32)], axis=0).T
            local[7:8, i * LANES : (i + 1) * LANES] = one_row(turned)
        local[7:8, 2 * LANES : 3 * LANES] = one_row(square_ref[...])
        exchange(0).start()
        for unit, number in sorted(late, key=lambda pair: pair[1]):
            unit.stage(number)
        last = units[-1]
        weight_grad(gpt, part_t)
        tail_unit.stage(1)
        fold_small(0)
        exchange(1).start()
        weight_grad(gp, part.at[(GROUPS - 1) % 2])
        last.stage(1)
        tail_unit.stage(2)
        fold_small(1)
        exchange(2).start()
        input_grad(gpt, wt)
        last.stage(2)
        fold_small(2)
        for k in range(1, levels):
            spread(k).start()
        smz[spot.level] = sm[2]
        input_grad(gp, wx.at[:, (GROUPS - 1) * cols_g : GROUPS * cols_g])
        tail_unit.stage(3)
        ngain = ngain_ref[...]

        def block_norm(i, total):
            block = pl.ds(pl.multiple_of(i * 64, 64), 64)
            v = tokens[block, :].astype(F32)
            rinv = lax.rsqrt(jnp.sum(v * v, axis=1, keepdims=True) / d + EPS)
            scaled = v * rinv
            grad = gn[block, :]
            total = total + jnp.sum((grad * scaled).reshape(8, 8, d), axis=0)
            grad = grad * ngain
            mean = jnp.sum(grad * scaled, axis=1, keepdims=True) / d
            gb[block, :] = (gb[block, :].astype(F32) + rinv * (grad - scaled * mean)).astype(BF16)
            return total

        blocks = gn.shape[0] // 64
        dnorm = lax.fori_loop(0, blocks // 2, block_norm, jnp.zeros((8, d), F32))
        last.stage(3)
        dnorm = lax.fori_loop(blocks // 2, blocks, block_norm, dnorm)
        leave = pltpu.make_async_copy(gb, gt_ref, load_sems.at[6])
        leave.start()
        dnorm = one_row(dnorm)
        place = spot.rep * 4 + spot.side * 2 + spot.core
        for k in range(d // LANES):
            gain_out[k : k + 1, :] = dnorm[:, k * LANES : (k + 1) * LANES]
        near = lambda k: send(
            gain_out, gain_near.at[place], gain_sems.at[2 * k - 2], gain_sems.at[2 * k - 1], spot.corner(k)
        )
        beyond = lambda k: send(
            gain_sum, gain_far.at[spot.level], gain_sems.at[12 + 2 * k], gain_sems.at[13 + 2 * k], spot.far(k)
        )
        for k in range(1, 8):
            near(k).start()
        gain_near[place] = gain_out[...]
        last.stage(4)
        for k in range(1, levels):
            spread(k).wait()
        total = smz[0]
        for k in range(1, levels):
            total = total + smz[k]
        sm[3] = total
        exchange(3).start()
        for k in range(1, 8):
            near(k).wait()
        total = gain_near[0]
        for k in range(1, 8):
            total = total + gain_near[k]
        gain_sum[...] = total
        for k in range(1, levels):
            beyond(k).start()
        gain_far[spot.level] = gain_sum[...]
        tail_unit.stage(4)
        last.stage(5)
        for k in range(1, levels):
            beyond(k).wait()
        total = gain_far[0]
        for k in range(1, levels):
            total = total + gain_far[k]
        dng_ref[...] = total
        exchange(3).wait()
        small_ref[:, half_of(spot.core)] = sm[3]
        small_ref[:, half_of(1 - spot.core)] = smr[3]
        tail_unit.stage(5)
        last.stage(6)
        leave.wait()


def back(
    px, px_block, tail, y, dy, states, aux, seg_rows, conv_w, conv_b, bias, rate, skip_row, e, rate_t,
    norm_gain, dgain, squares, normed_t, wx, wt, gn, tokens, gb, ggate, gout, proj,
):
    length, inner = y.shape
    heads = bias.shape[1]
    levels, rows_f = ggate.shape[0], ggate.shape[3]
    taps = conv_w.shape[0]
    n = (conv_w.shape[1] - inner) // 2
    r = CHUNK
    chunks = length // r
    wide = inner // GROUPS
    tcols = tail.shape[1]
    d = normed_t.shape[0]
    small_cols = inner + tcols + LANES
    units = 3 * GROUPS
    back_at = lambda off: lambda g, c: (chunks - 1 - c, g + off)
    whole = lambda a: pl.BlockSpec(a.shape, lambda g, c: (0,) * a.ndim, pipeline_mode=pl.Buffered(1))
    anywhere = pl.BlockSpec(memory_space=pl.ANY)
    vm = pltpu.VMEM
    out = lambda s: pl.BlockSpec(s, lambda g, c: (0,) * len(s))
    return pl.pallas_call(
        functools.partial(
            back_kernel, inner=inner, heads=heads, width=inner // heads, levels=levels, seq_chunks=chunks
        ),
        grid=(GROUPS, chunks),
        in_specs=[
            pl.BlockSpec((r, wide), back_at(px_block)),
            pl.BlockSpec((8, wide), lambda g, c: (jnp.maximum((chunks - 1 - c) * (r // 8) - 1, 0), g + px_block)),
            pl.BlockSpec((r, wide), back_at(0)),
            pl.BlockSpec((r, wide), back_at(0)),
            pl.BlockSpec((n, wide), back_at(0)),
            *[whole(a) for a in (tail, aux, seg_rows, conv_w, conv_b, bias, rate, skip_row, e, rate_t, norm_gain, dgain, squares)],
            *[anywhere] * 8,
        ],
        out_specs=[out((rows_f, proj)), out((2 * rows_f, d)), anywhere, out((8, small_cols)), out((d // LANES, LANES))],
        out_shape=[
            jax.ShapeDtypeStruct((rows_f, proj), F32),
            jax.ShapeDtypeStruct((2 * rows_f, d), F32),
            jax.ShapeDtypeStruct((length, d), BF16),
            jax.ShapeDtypeStruct((8, small_cols), F32),
            jax.ShapeDtypeStruct((d // LANES, LANES), F32),
        ],
        scratch_shapes=[
            vm((r + 8, wide), F32), vm((3 * r, wide), F32), vm((n, wide), F32), vm((r, wide), F32),
            vm((r, wide), BF16), vm((r, wide), BF16), vm((chunks, r, 2 * n), BF16), vm((r, wide), F32),
            vm((r, wide), BF16), vm((r, wide), F32), vm((r + 8, wide), F32),
            vm((r, wide), BF16), vm((r, wide), BF16), vm((r, wide), BF16), vm((r, wide), BF16),
            vm((r + 8, 2 * n), F32), vm((chunks, heads, LANES), F32),
            vm((chunks, 3 * r, 2 * heads), BF16), vm((chunks, 2 * heads, r), F32), vm((GROUPS, length, LANES), F32),
            vm((chunks, heads, r), F32), vm((16, wide), BF16), vm((2, heads, r), F32),
            vm((chunks, r, r), F32), vm((chunks, r, r), F32), vm((length, n), F32), vm((length, n), F32),
            vm((3, chunks, heads, r), F32), vm((length, 2 * n), F32), vm((length, wide), BF16), vm((length, tcols), BF16),
            vm((8 * taps + 16, inner), F32), vm((8 * taps + 8, 2 * n), F32),
            vm(normed_t.shape, BF16), vm(wx.shape, BF16), vm(wt.shape, BF16), vm(gn.shape, F32), vm(tokens.shape, BF16), vm(gb.shape, BF16),
            vm((units, levels, 2, rows_f, wide), BF16), vm((2, levels, 2, 2, rows_f, wide), BF16),
            vm((levels, 2, 2, rows_f, tcols), BF16), vm((levels, 2, rows_f, tcols), BF16),
            vm((units, levels, 2, rows_f, wide), BF16), vm((levels, 2, rows_f, tcols), BF16),
            vm((units // 2, levels, rows_f, wide), BF16), vm((levels, rows_f, tcols), BF16),
            vm((units // 2, levels - 1, rows_f, wide), BF16), vm((levels - 1, rows_f, tcols), BF16),
            vm((units // 2, rows_f, wide), BF16), vm((rows_f, tcols), BF16),
            vm((units // 2, rows_f, wide), BF16), vm((rows_f, tcols), BF16),
            vm((units // 2, levels, 2, rows_f, wide // 2), BF16), vm((units // 2, levels, rows_f, wide // 2), BF16),
            vm((units // 2, levels - 1, rows_f, wide // 2), BF16),
            vm((units // 2, rows_f, wide // 2), BF16), vm((units // 2, rows_f, wide // 2), BF16),
            vm((8, small_cols), F32), vm((4, 8, small_cols // 2), F32), vm((4, 8, small_cols // 2), F32),
            vm((levels, 8, small_cols // 2), F32),
            vm((d // LANES, LANES), F32), vm((8, d // LANES, LANES), F32), vm((d // LANES, LANES), F32),
            vm((levels, d // LANES, LANES), F32),
            pltpu.SemaphoreType.DMA((units + 1, 7 + 2 * levels)),
            pltpu.SemaphoreType.DMA((6 + 2 * levels,)),
            pltpu.SemaphoreType.DMA((12 + 2 * levels,)),
            pltpu.SemaphoreType.DMA((7,)),
        ],
        compiler_params=pltpu.CompilerParams(
            dimension_semantics=("arbitrary", "arbitrary"), vmem_limit_bytes=60 * 2**20,
            collective_id=1, has_side_effects=True,
        ),
        name="scan_backward",
    )(
        px, px, y, dy, states, tail, aux, seg_rows, conv_w, conv_b, bias, rate, skip_row, e, rate_t,
        norm_gain, dgain, squares, normed_t, wx, wt, gn, tokens, gb, ggate, gout,
    )


class Load:
    def __init__(self, spot, shard, whole, sems, split):
        self.spot, self.shard, self.whole, self.sems, self.split = spot, shard, whole, sems, split

    def part(self, ref):
        if not self.split:
            return ref
        half = ref.shape[-1] // 2
        cols = pl.ds(pl.multiple_of(self.spot.rep * half, half), half)
        return ref.at[(slice(None),) * (len(ref.shape) - 1) + (cols,)]

    @property
    def a0(self):
        spot = self.spot
        here = self.whole.at[spot.level, spot.side, spot.core]
        return pltpu.make_async_copy(self.part(self.shard), self.part(here), self.sems.at[0])

    @property
    def a(self):
        spot, sems = self.spot, self.sems
        here = self.whole.at[spot.level, spot.side, spot.core]
        return [
            send(self.part(self.shard), self.part(here), sems.at[5 + 2 * d], sems.at[6 + 2 * d], spot.far(d))
            for d in range(1, spot.levels)
        ]

    @property
    def b(self):
        spot, sems = self.spot, self.sems
        if self.split:
            block = self.part(self.whole.at[:, spot.side, spot.core])
        else:
            half = spot.levels // 2
            block = self.whole.at[pl.ds(spot.rep * half, half), spot.side, spot.core]
        return send(block, block, sems.at[1], sems.at[2], spot.across)

    @property
    def c(self):
        spot, sems = self.spot, self.sems
        if self.split:
            block = self.part(self.whole.at[:, :, spot.core])
        else:
            half = spot.levels // 2
            block = self.whole.at[pl.ds(spot.rep * half, half), 1 - spot.side, spot.core]
        return send(block, block, sems.at[3], sems.at[4], spot.twin)

    @property
    def d(self):
        spot, sems = self.spot, self.sems
        block = self.whole.at[:, :, spot.core]
        last = 5 + 2 * spot.levels
        return send(block, block, sems.at[last], sems.at[last + 1], spot.sibling)

    def stage(self, number):
        if number == 1:
            self.a0.start()
            for copy in self.a:
                copy.start()
        elif number == 2:
            self.a0.wait()
            for copy in self.a:
                copy.wait()
            self.b.start()
        elif number == 3:
            self.b.wait()
            self.c.start()
        elif number == 4:
            self.c.wait()
            self.d.start()
        else:
            self.d.wait()


LOAD_STEPS = (5, 8, 12)


def first_kernel(
    cotan_ref, teacher_ref,
    tokens_hbm, ngain_ref, aux_ref, seg_ref, count_ref, cw_ref, cb_ref, bias_ref, rate_ref, skip_ref, gain_ref, e_ref,
    in_hbm, tail_hbm, out_hbm,
    px_ref, ssd_ref, state_out_ref, tail_out, normed_out, normed_t_out, wx_out, wtail_out,
    output_ref, gb_ref, mixed_ref, dy_ref, dz_ref, gn_ref, dgain_ref, small_ref,
    tokens, normed, normed_t, wx, wg, wo, weight_tail, tail, pbuf, ssd_all, gates, gateds, gms, results, inverses,
    ex, state, xs, xdt, xe, bc, yin, cums, scores, stacks,
    counts, countr, countz, sems, count_sems, copy_sems, leave_sems,
    *, inner, heads, width, levels, seq_chunks, loss_weight,
):
    step = pl.program_id(0)
    group, chunk = step // seq_chunks, step % seq_chunks
    rows, cols_g = px_ref.shape
    n = bc.shape[2] // 2
    tiles = cols_g // LANES
    per_group = cols_g // width
    taps = cw_ref.shape[0]
    rows_f = in_hbm.shape[0]
    tail_cols = tail.shape[1]
    conv_tail = 2 * n
    length, d_model = tokens.shape
    spot = Spot(levels)
    here = pl.ds(pl.multiple_of(chunk * rows, rows), rows)
    gcol = pl.multiple_of(group * cols_g, cols_g)
    last_step = GROUPS * seq_chunks - 1

    tail_load = Load(spot, tail_hbm, weight_tail, sems.at[0], False)
    loads = []
    for k in range(2 * GROUPS):
        cols = pl.ds((k % GROUPS) * cols_g, cols_g)
        shard = in_hbm.at[:, pl.ds((inner if k < GROUPS else 0) + (k % GROUPS) * cols_g, cols_g)]
        loads.append((shard, (wx if k < GROUPS else wg).at[:, :, :, :, cols]))
    for k in range(GROUPS):
        cols = pl.ds(k * (d_model // GROUPS), d_model // GROUPS)
        loads.append((out_hbm.at[:, cols], wo.at[:, :, :, :, cols]))
    loads = [Load(spot, shard, whole, sems.at[1 + k], k % 2 == 1) for k, (shard, whole) in enumerate(loads)]
    leaves = [
        (wx, wx_out), (weight_tail, wtail_out), (normed, normed_out), (normed_t, normed_t_out), (tail.at[8:], tail_out)
    ]

    def leave(k):
        return pltpu.make_async_copy(*leaves[k], leave_sems.at[k])

    exchange = lambda i: send(
        counts.at[i], countr.at[i], count_sems.at[2 * i], count_sems.at[2 * i + 1],
        (spot.sibling, spot.across, spot.twin)[i],
    )
    spread = lambda d: send(
        counts.at[3], countz.at[spot.level], count_sems.at[4 + 2 * d], count_sems.at[5 + 2 * d], spot.far(d)
    )

    def marks_of(aux):
        return [None] + [jnp.broadcast_to(aux[:, k : k + 1], (rows, LANES)) for k in range(1, taps)]

    def conv(buffer, at, cols, wcols, marks):
        block = buffer[pl.ds(at, rows + 8), cols]
        pre = cb_ref[:, wcols] + cw_ref[0:1, wcols] * block[8:]
        for k in range(1, taps):
            pre = pre + (cw_ref[k : k + 1, wcols] * block[8 - k : 8 - k + rows]) * marks[k]
        return pre * sigmoid(pre)

    def project(weight, out, cols):
        for i in range(length // 256):
            out[8 + i * 256 : 8 + (i + 1) * 256, :] = mm(normed[i * 256 : (i + 1) * 256, :], weight[:, cols])

    @pl.when(step == 0)
    def _():
        fetch = pltpu.make_async_copy(tokens_hbm, tokens, copy_sems.at[0])
        fetch.start()
        counts[0] = count_ref[...]
        spot.greet()
        tail_load.stage(1)
        exchange(0).start()
        loads[0].stage(1)
        loads[1].stage(1)
        fetch.wait()

        def norm(i, carry):
            block = pl.ds(pl.multiple_of(i * 64, 64), 64)
            v = tokens[block, :].astype(F32)
            v = v * lax.rsqrt(jnp.sum(v * v, axis=1, keepdims=True) / d_model + EPS)
            normed[block, :] = (v * ngain_ref[...]).astype(BF16)
            return carry

        lax.fori_loop(0, length // 64, norm, 0)
        def turn_rows(blocks):
            for i in blocks:
                block = slice(i * 256, (i + 1) * 256)
                normed_t[:, block] = normed[block, :].T

        def shared(i, carry):
            at = pl.ds(pl.multiple_of(i * rows, rows), rows)
            aux = aux_ref[at, :]
            marks = marks_of(aux)
            start = pl.multiple_of(i * rows, rows)
            raw = tail[pl.ds(start + 8, rows), conv_tail : conv_tail + heads]
            shifted, size, cum, from_prev, to_end = small_terms(
                raw, bias_ref[...], rate_ref[...], aux[:, 7:8], aux[:, 8:9], rows
            )
            cums[i, :, 0:heads] = cum
            stacks[i] = jnp.concatenate(
                [jnp.concatenate(split2(v), axis=1) for v in (size, from_prev, to_end)], axis=0
            )
            for c in range(conv_tail // LANES):
                cols = slice(c * LANES, (c + 1) * LANES)
                act = conv(tail, start, cols, slice(inner + c * LANES, inner + (c + 1) * LANES), marks)
                bc[i, :, cols] = act.astype(BF16)
            causal = (iota((rows, rows), 0) >= iota((rows, rows), 1)) & (aux[:, 0:1] == seg_ref[i])
            scores[i] = jnp.where(causal, mm_nt(bc[i, :, n:], bc[i, :, 0:n]), 0.0)
            return carry

        tail[0:8, :] = jnp.zeros((8, tail_cols), F32)
        pbuf[0:8, :] = jnp.zeros((8, cols_g), F32)
        cums[...] = jnp.zeros_like(cums)
        tail_load.stage(2)
        exchange(0).wait()
        counts[1] = counts[0] + countr[0]
        exchange(1).start()
        blocks = length // 256
        turn_rows(range(blocks // 2))
        tail_load.stage(3)
        exchange(1).wait()
        counts[2] = counts[1] + countr[1]
        exchange(2).start()
        turn_rows(range(blocks // 2, blocks))
        leave(2).start()
        leave(3).start()
        tail_load.stage(4)
        loads[0].stage(2)
        exchange(2).wait()
        counts[3] = counts[2] + countr[2]
        for k in range(1, levels):
            spread(k).start()
        countz[spot.level] = counts[3]
        tail_load.stage(5)
        leave(1).start()
        project(weight_tail.reshape(d_model, tail_cols), tail, slice(0, tail_cols))
        leave(4).start()
        loads[0].stage(3)
        lax.fori_loop(0, seq_chunks // 2, shared, 0)
        loads[0].stage(4)
        loads[1].stage(2)
        lax.fori_loop(seq_chunks // 2, seq_chunks, shared, 0)
        for k in range(1, levels):
            spread(k).wait()
        total = countz[0]
        for k in range(1, levels):
            total = total + countz[k]
        counts[4] = total

    scan_steps = GROUPS * seq_chunks
    events = {}
    for k in range(1, 3 * GROUPS):
        begin = max(0, (k - 2) * 3 * seq_chunks // 8)
        times = [begin, *[begin + 1 + delay * seq_chunks // 8 for delay in LOAD_STEPS]]
        if k == 1:
            times = [None, None, seq_chunks // 4, 5 * seq_chunks // 8]
        need = min(k * seq_chunks, scan_steps)
        for number, when in enumerate(times):
            if when is not None:
                events.setdefault(min(when, need), []).append((k, number + 1))
        if k < 2 * GROUPS:
            events.setdefault(need, []).append((k, 5))
    late = sorted(events.pop(scan_steps), key=lambda pair: (pair[1] + pair[0], pair[0]))
    for at, happen in sorted(events.items()):

        @pl.when(step == at)
        def _(happen=sorted(happen, key=lambda pair: (pair[0], pair[1]))):
            for k, number in happen:
                loads[k].stage(number)

    @pl.when(step == scan_steps)
    def _():
        leave(0).start()
        for k, number in late:
            loads[k].stage(number)

    for g in range(GROUPS):

        @pl.when(step == g * seq_chunks)
        def _(g=g):
            if g == 0:
                loads[0].stage(5)
            project(wx.reshape(d_model, inner), pbuf, slice(g * cols_g, (g + 1) * cols_g))

    @pl.when(step < scan_steps)
    def _():
        @pl.when(chunk == 0)
        def _():
            state[...] = jnp.zeros_like(state)

        aux = aux_ref[here, :]
        marks = marks_of(aux)
        ex[...] = mm(stacks[chunk], e_ref[:, pl.ds(gcol, cols_g)])
        head0 = group * per_group
        pick = (iota((LANES, LANES), 0) == iota((LANES, LANES), 1) + head0).astype(BF16)
        moved = [mm(v, pick) for v in split3(cums[chunk])]
        cum = moved[0] + moved[1] + moved[2]
        cum_t = cum.T
        start = pl.multiple_of(chunk * rows, rows)
        px_ref[...] = pbuf[pl.ds(start + 8, rows), :]
        for c in range(tiles):
            cols = slice(c * LANES, (c + 1) * LANES)
            act = conv(pbuf, start, cols, pl.ds(gcol + c * LANES, LANES), marks)
            xs[:, cols] = act
            scaled = act * ex[0:rows, cols]
            xdt[:, cols] = scaled.astype(BF16)
            xe[:, cols] = (scaled * ex[2 * rows : 3 * rows, cols]).astype(BF16)
        b, cc = bc[chunk, :, 0:n], bc[chunk, :, n:]
        state_low = state[...].astype(BF16)
        state_out_ref[...] = state_low
        yin[...] = mm(cc, state_low)
        state[...] = state[...] * ex[2 * rows - 1 : 2 * rows, :] + mm_tn(b, xe[...])
        score = scores[chunk]
        lane = iota((1, LANES), 1)
        masks = [(lane < width).astype(BF16), (lane >= width).astype(BF16)]
        for c in range(tiles):
            cols = slice(c * LANES, (c + 1) * LANES)
            mixing = []
            for h in (2 * c, 2 * c + 1):
                spread_h = jnp.minimum(cum[:, h : h + 1] - cum_t[h : h + 1, :], 0.0)
                mixing.append((score * jnp.exp(spread_h)).astype(BF16))
            x_low = xdt[:, cols]
            y = mm(
                jnp.concatenate(mixing, axis=1), jnp.concatenate([x_low * masks[0], x_low * masks[1]], axis=0)
            ) + ex[rows : 2 * rows, cols] * yin[:, cols]
            acols = pl.ds(gcol + c * LANES, LANES)
            ssd_ref[:, cols] = y
            ssd_all[here, acols] = y + skip_ref[:, acols] * xs[:, cols]

    @pl.when(step >= scan_steps)
    def _():
        turn = step - scan_steps
        block_rows = gates.shape[0]
        base = pl.multiple_of(turn * block_rows, block_rows)
        flat_gate = wg.reshape(d_model, inner)
        flat_out = wo.reshape(inner, d_model)
        sub = 64
        own_rows = normed[pl.ds(base, block_rows), :]
        for k in range(GROUPS):
            cols = slice(k * cols_g, (k + 1) * cols_g)
            gates[:, cols] = mm(own_rows, flat_gate[:, cols])

        @pl.when(turn == 0)
        def _():
            dgain_ref[...] = jnp.zeros_like(dgain_ref)
            small_ref[...] = jnp.zeros_like(small_ref)
            for k in range(2 * GROUPS, 3 * GROUPS):
                loads[k].stage(5)

        def norm_of(i):
            at = pl.ds(pl.multiple_of(i * sub, sub), sub)
            return at, pl.ds(pl.multiple_of(base + i * sub, sub), sub)

        def forward_part(i, carry):
            at, full_at = norm_of(i)
            squares = jnp.zeros((sub, LANES), F32)
            for c in range(inner // LANES):
                cols = slice(c * LANES, (c + 1) * LANES)
                gate = gates[at, cols]
                gated = ssd_all[full_at, cols] * (gate * sigmoid(gate))
                gateds[at, cols] = gated
                squares = squares + gated * gated
            inverse = lax.rsqrt(jnp.sum(squares, axis=1, keepdims=True) / inner + EPS)
            for c in range(inner // LANES):
                cols = slice(c * LANES, (c + 1) * LANES)
                unit = gateds[at, cols] * inverse
                gateds[at, cols] = unit
                mixed_ref[at, cols] = (unit * gain_ref[:, cols]).astype(BF16)
            inverses[at, :] = jnp.broadcast_to(inverse, (sub, LANES))
            return carry

        lax.fori_loop(0, block_rows // sub, forward_part, 0)
        results[...] = mm(mixed_ref[...], flat_out[...])
        scale = 2.0 * loss_weight / (counts[4, 0:1, :] * d_model)

        def loss_part(i, carry):
            at, full_at = norm_of(i)
            valid = jnp.broadcast_to(aux_ref[full_at, 9:10], (sub, LANES))
            squares = jnp.zeros((8, LANES), F32)
            for c in range(d_model // LANES):
                cols = slice(c * LANES, (c + 1) * LANES)
                result = tokens[full_at, cols].astype(F32) + results[at, cols]
                output_ref[at, cols] = result.astype(BF16)
                error = result - teacher_ref[at, cols].astype(F32)
                squares = squares + jnp.sum((valid * error * error).reshape(sub // 8, 8, LANES), axis=0)
                gb_ref[at, cols] = (valid * (cotan_ref[at, cols].astype(F32) + scale * error)).astype(BF16)
            small_ref[0:8, :] += squares
            return carry

        lax.fori_loop(0, block_rows // sub, loss_part, 0)
        small_ref[8:16, :] = counts[4]
        grads = gb_ref[...]
        for k in range(GROUPS):
            cols = slice(k * cols_g, (k + 1) * cols_g)
            gms[:, cols] = mm_nt(grads, flat_out[cols, :])

        def backward_part(i, carry):
            at, full_at = norm_of(i)
            cross = jnp.zeros((sub, LANES), F32)
            for c in range(inner // LANES):
                cols = slice(c * LANES, (c + 1) * LANES)
                cross = cross + gms[at, cols] * gain_ref[:, cols] * gateds[at, cols]
            inverse = inverses[at, :]
            mean_cross = jnp.sum(cross, axis=1, keepdims=True) / inner
            for c in range(inner // LANES):
                cols = slice(c * LANES, (c + 1) * LANES)
                gate = gates[at, cols]
                sig = sigmoid(gate)
                silu = gate * sig
                unit = gateds[at, cols]
                grad_mixed = gms[at, cols]
                dgain_ref[:, cols] += jnp.sum((grad_mixed * unit).reshape(sub // 8, 8, LANES), axis=0)
                grad_gated = inverse * (grad_mixed * gain_ref[:, cols] - unit * mean_cross)
                dy_ref[at, cols] = (grad_gated * silu).astype(BF16)
                dz_ref[at, cols] = (
                    grad_gated * ssd_all[full_at, cols] * (sig + silu * (1.0 - sig))
                ).astype(BF16)
            return carry

        lax.fori_loop(0, block_rows // sub, backward_part, 0)
        gn_ref[...] = mm_nt(dz_ref[...], flat_gate[...])

        @pl.when(turn == length // block_rows - 1)
        def _():
            for k in range(len(leaves)):
                leave(k).wait()


def first(
    tokens, norm_gain, aux, seg_rows, count, conv_w, conv_b, bias, rate, skip_row, gain_row, e,
    cotangent, teacher, w_in, w_tail, w_out, levels, loss_weight,
):
    length, d = tokens.shape
    heads, inner = bias.shape[1], skip_row.shape[1]
    rows_f = w_in.shape[0]
    n = (conv_w.shape[1] - inner) // 2
    r = CHUNK
    chunks = length // r
    wide = inner // GROUPS
    tcols = w_tail.shape[1]
    units = 3 * GROUPS
    tall = 256
    scan_steps = GROUPS * chunks

    def scan_block(s):
        s = jnp.minimum(s, scan_steps - 1)
        return s % chunks, s // chunks

    block = lambda h: pl.BlockSpec((h, wide), scan_block)
    late = lambda w: pl.BlockSpec((tall, w), lambda s: (jnp.maximum(s - scan_steps, 0), 0))
    whole = lambda a: pl.BlockSpec(a.shape, lambda s: (0,) * a.ndim, pipeline_mode=pl.Buffered(1))
    fixed = lambda *dims: pl.BlockSpec(dims, lambda s: (0,) * len(dims))
    anywhere = pl.BlockSpec(memory_space=pl.ANY)
    vm = pltpu.VMEM
    shape = jax.ShapeDtypeStruct
    wide_shape = (levels, 2, 2, rows_f, inner)
    return pl.pallas_call(
        functools.partial(
            first_kernel, inner=inner, heads=heads, width=inner // heads, levels=levels, seq_chunks=chunks,
            loss_weight=loss_weight,
        ),
        grid=(scan_steps + length // tall,),
        in_specs=[
            late(d), late(d), anywhere,
            *[whole(a) for a in (norm_gain, aux, seg_rows, count, conv_w, conv_b, bias, rate, skip_row, gain_row, e)],
            anywhere, anywhere, anywhere,
        ],
        out_specs=[
            block(r), block(r), block(n), *[anywhere] * 5,
            late(d), late(d), late(inner), late(inner), late(inner), late(d), fixed(8, inner), fixed(16, LANES),
        ],
        out_shape=[
            shape((length, inner), F32), shape((length, inner), F32), shape((chunks * n, inner), BF16),
            shape((length, tcols), F32), shape((length, d), BF16), shape((d, length), BF16),
            shape(wide_shape, BF16), shape((levels, 2, 2, rows_f, tcols), BF16),
            shape((length, d), BF16), shape((length, d), BF16), shape((length, inner), BF16),
            shape((length, inner), BF16), shape((length, inner), BF16), shape((length, d), F32),
            shape((8, inner), F32), shape((16, LANES), F32),
        ],
        scratch_shapes=[
            vm((length, d), BF16), vm((length, d), BF16), vm((d, length), BF16),
            vm(wide_shape, BF16), vm(wide_shape, BF16), vm((levels, 2, 2, 2 * rows_f, d), BF16),
            vm((levels, 2, 2, rows_f, tcols), BF16),
            vm((length + 8, tcols), F32), vm((length + 8, wide), F32), vm((length, inner), F32),
            vm((tall, inner), F32), vm((tall, inner), F32), vm((tall, inner), F32), vm((tall, d), F32),
            vm((tall, LANES), F32),
            vm((3 * r, wide), F32), vm((n, wide), F32), vm((r, wide), F32), vm((r, wide), BF16), vm((r, wide), BF16),
            vm((chunks, r, 2 * n), BF16), vm((r, wide), F32), vm((chunks, r, LANES), F32), vm((chunks, r, r), F32),
            vm((chunks, 3 * r, 2 * heads), BF16),
            vm((5, 8, LANES), F32), vm((3, 8, LANES), F32), vm((levels, 8, LANES), F32),
            pltpu.SemaphoreType.DMA((units + 1, 7 + 2 * levels)),
            pltpu.SemaphoreType.DMA((4 + 2 * levels,)),
            pltpu.SemaphoreType.DMA((1,)),
            pltpu.SemaphoreType.DMA((5,)),
        ],
        compiler_params=pltpu.CompilerParams(
            dimension_semantics=("arbitrary",), vmem_limit_bytes=60 * 2**20,
            collective_id=2, has_side_effects=True,
        ),
        name="scan_forward",
    )(
        cotangent, teacher, tokens, norm_gain, aux, seg_rows, count, conv_w, conv_b, bias, rate, skip_row, gain_row, e,
        w_in, w_tail, w_out,
    )


def on_device(
    tokens,
    norm_gain,
    in_weight,
    conv_weight,
    conv_bias,
    step_bias,
    decay_log,
    skip_gain,
    out_gain,
    out_weight,
    cotangent,
    teacher,
    segment,
    valid_mask,
):
    seqs, length, width = tokens.shape
    rows = seqs * length
    shards = lax.axis_size("fsdp")
    devices = lax.axis_size("rep") * shards
    levels = shards // 4
    loss_weight = float(rows * devices * width // 8)
    heads, inner = step_bias.shape[0], out_gain.shape[0]
    aux, seg_rows, count, bias, rate, rate_t, skip_row, conv_row, ngain_row, gain_row, e, in_tail = prepare(
        segment, valid_mask, step_bias, decay_log, skip_gain, conv_bias, norm_gain, out_gain, in_weight
    )
    params = (conv_weight, conv_row, bias, rate, skip_row)
    flat, cotan, target = (v.reshape(rows, width) for v in (tokens, cotangent, teacher))
    (
        px, y, states, tail, normed, normed_t, wx, wt, output, grad_branch, mixed, dy, dz, gn, dgain, sums
    ) = first(
        flat, ngain_row, aux, seg_rows, count, *params, gain_row, e, cotan, target,
        in_weight, in_tail, out_weight, levels, loss_weight,
    )
    wx, wt = (w.reshape(-1, w.shape[-1]) for w in (wx, wt))
    grad_out = mm_tn(mixed, grad_branch).astype(BF16)
    grad_gate = mm(normed_t, dz).astype(BF16)
    grad_in, grad_out, grad_tokens, small, norm_sum = back(
        px, 0, tail, y, dy, states, aux, seg_rows, *params, e, rate_t,
        ngain_row, dgain, sums[:8], normed_t, wx, wt, gn, flat, grad_branch,
        grad_gate.reshape(levels, 2, 2, width // shards, inner),
        grad_out.reshape(levels, 2, 2, inner // shards, width), in_weight.shape[1],
    )
    outs = finish(
        grad_in, grad_out, grad_tokens, output, small, norm_sum, sums, e, *conv_weight.shape, heads, inner
    )
    return (
        outs[0].reshape(tokens.shape), outs[1].reshape(()), outs[2].reshape(tokens.shape), *outs[3:]
    )


def solution(mesh):
    tokens = P(("rep", "fsdp"), None, None)
    marks = P(("rep", "fsdp"), None)
    shard = P("fsdp", None)
    return jax.shard_map(
        on_device,
        mesh=mesh,
        in_specs=(tokens, P(), shard, P(), P(), P(), P(), P(), P(), shard, tokens, tokens, marks, marks),
        out_specs=(tokens, P(), tokens, P(), shard, P(), P(), P(), P(), P(), P(), shard),
        check_vma=False,
    )
```

```python
import functools

import jax
import jax.numpy as jnp
from jax import lax
from jax.experimental import pallas as pl
from jax.experimental.pallas import tpu as pltpu
from jax.sharding import PartitionSpec as P

CHUNK = 128
LANES = 128
EPS = 1e-05
F32 = jnp.float32
BF16 = jnp.bfloat16
NT = (((1,), (1,)), ((), ()))
TN = (((0,), (0,)), ((), ()))


def mm(a, b):
    return jnp.dot(a, b, preferred_element_type=F32)


def mm_nt(a, b):
    return lax.dot_general(a, b, NT, preferred_element_type=F32)


def mm_tn(a, b):
    return lax.dot_general(a, b, TN, preferred_element_type=F32)


def split2(v):
    high = v.astype(BF16)
    return high, (v - high.astype(F32)).astype(BF16)


def split3(v):
    high = v.astype(BF16)
    rest = v - high.astype(F32)
    mid = rest.astype(BF16)
    return high, mid, (rest - mid.astype(F32)).astype(BF16)


def tri_sum(tri, v):
    heads = v.shape[1]
    parts = mm(tri, jnp.concatenate(split3(v), axis=1))
    return parts[:, :heads] + parts[:, heads : 2 * heads] + parts[:, 2 * heads :]


def sum_tri(v, tri):
    heads = v.shape[0]
    parts = mm(jnp.concatenate(split3(v), axis=0), tri)
    return parts[:heads] + parts[heads : 2 * heads] + parts[2 * heads :]


def sigmoid(v):
    return 0.5 * jnp.tanh(0.5 * v) + 0.5


def softplus(v):
    return jnp.maximum(v, 0.0) + jnp.log1p(jnp.exp(-jnp.abs(v)))


def iota(shape, dim):
    return lax.broadcasted_iota(jnp.int32, shape, dim)


def small_terms(step_raw, step_bias, decay_rate, keep, to_end, rows):
    shifted = step_raw + step_bias
    step = softplus(shifted)
    lower = (iota((rows, rows), 0) >= iota((rows, rows), 1)).astype(BF16)
    cum = tri_sum(lower, step * decay_rate)
    last = cum[rows - 1 : rows, :]
    return shifted, step, cum, jnp.exp(cum) * keep, jnp.exp(last - cum) * to_end


def expand(e_ref, out_ref, step, from_prev, to_end):
    stacked = jnp.concatenate(
        [jnp.concatenate(split2(v), axis=1) for v in (step, from_prev, to_end)], axis=0
    )
    out_ref[...] = mm(stacked, e_ref[...])


def full(shape):
    return pl.BlockSpec(shape, lambda i: (0,) * len(shape))


def prepare_kernel(
    segment_ref, valid_ref, bias_ref, log_ref, skip_ref, cb_ref, ngain_ref, gain_ref, weight_ref,
    aux_ref, rows_ref, count_ref, bias_out, rate_out, rate_t_out, skip_out, cb_out, ngain_out, gain_out, e_out, tail_out,
    *, tail_cols,
):
    length = segment_ref.shape[1]
    heads = bias_ref.shape[0]
    inner = gain_ref.shape[0]
    width = inner // heads
    docs = segment_ref[...].astype(F32)
    valid = valid_ref[...].astype(F32)
    place = iota((8, length), 1)
    wide = jnp.broadcast_to(docs, (8, length))
    marks = []
    for k in (1, 2, 3):
        marks.append(jnp.where((wide == pltpu.roll(wide, k, 1)) & (place >= k), 1.0, 0.0)[0:1])
    for k in (1, 2, 3):
        marks.append(jnp.where((wide == pltpu.roll(wide, length - k, 1)) & (place < length - k), 1.0, 0.0)[0:1])
    for c in range(length // CHUNK):
        cols = slice(c * CHUNK, (c + 1) * CHUNK)
        own = docs[:, cols]
        last = docs[:, (c + 1) * CHUNK - 1 : (c + 1) * CHUNK]
        keep = jnp.zeros_like(own)
        if c:
            keep = jnp.where(own == docs[:, c * CHUNK - 1 : c * CHUNK], 1.0, 0.0)
        stacked = [own, *[v[:, cols] for v in marks], keep, jnp.where(own == last, 1.0, 0.0), valid[:, cols]]
        stacked.append(jnp.zeros((LANES - len(stacked), CHUNK), F32))
        aux_ref[cols, :] = jnp.concatenate(stacked, axis=0).T[:, 0:16]
        rows_ref[c] = own
    count_ref[...] = jnp.broadcast_to(jnp.sum(valid, axis=1, keepdims=True), count_ref.shape)
    bias_out[...] = bias_ref[...].reshape(1, heads)
    rate = -jnp.exp(log_ref[...].reshape(1, heads))
    rate_out[...] = rate
    spare = jnp.concatenate([rate, jnp.zeros((1, LANES - heads), F32)], axis=1)
    rate_t_out[...] = jnp.broadcast_to(spare, (LANES, LANES)).T[0:heads, 0:1]
    e = (iota((2 * heads, inner), 0) % heads == iota((2 * heads, inner), 1) // width).astype(BF16)
    e_out[...] = e
    skip = jnp.broadcast_to(skip_ref[...].reshape(1, heads), (16, heads))
    parts = [mm(v, e[0:heads]) for v in split3(skip)]
    skip_out[...] = (parts[0] + parts[1] + parts[2])[0:1]
    cb_out[...] = cb_ref[...].reshape(1, cb_ref.shape[0])
    ngain_out[...] = ngain_ref[...].reshape(1, ngain_ref.shape[0])
    gain_out[...] = gain_ref[...].reshape(1, inner)
    rows_f = weight_ref.shape[0]
    tail_out[...] = jnp.concatenate(
        [weight_ref[:, 0:tail_cols], jnp.zeros((rows_f, tail_out.shape[1] - tail_cols), BF16)], axis=1
    )


def prepare(segment, valid_mask, step_bias, decay_log, skip_gain, conv_bias, norm_gain, out_gain, in_weight):
    length = segment.shape[1]
    heads, inner = step_bias.shape[0], out_gain.shape[0]
    rows_f, proj = in_weight.shape
    tail_cols = proj - 2 * inner
    tail_wide = -(-tail_cols // LANES) * LANES
    shape = jax.ShapeDtypeStruct
    small = (segment, valid_mask, step_bias, decay_log, skip_gain, conv_bias, norm_gain, out_gain)
    outs = [
        shape((length, 16), F32), shape((length // CHUNK, 1, CHUNK), F32), shape((8, LANES), F32),
        shape((1, heads), F32), shape((1, heads), F32), shape((heads, 1), F32), shape((1, inner), F32),
        shape((1, conv_bias.shape[0]), F32), shape((1, norm_gain.shape[0]), F32), shape((1, inner), F32),
        shape((2 * heads, inner), BF16), shape((rows_f, tail_wide), BF16),
    ]
    block = 512
    return pl.pallas_call(
        functools.partial(prepare_kernel, tail_cols=tail_cols),
        grid=(1,),
        in_specs=[*[full(a.shape) for a in small], pl.BlockSpec((rows_f, block), lambda i: (0, 2 * inner // block))],
        out_specs=[full(o.shape) for o in outs],
        out_shape=outs,
        name="prepare",
    )(*small, in_weight)


def finish_kernel(
    gi_ref, go_ref, gt_ref, output_ref, small_ref, dng_ref, sums_ref, e_ref,
    out_final, loss_ref, gt_final, ngain_ref, gi_final, cw_ref, cb_ref, bias_ref, log_ref, skip_ref, gain_ref, go_final,
    gi, go, gt, output, sems,
):
    trios = ((gt_ref, gt, gt_final), (output_ref, output, out_final), (gi_ref, gi, gi_final), (go_ref, go, go_final))
    fetches = [pltpu.make_async_copy(a, b, sems.at[i]) for i, (a, b, c) in enumerate(trios)]
    stores = [pltpu.make_async_copy(b, c, sems.at[4 + i]) for i, (a, b, c) in enumerate(trios)]
    for copy in fetches:
        copy.start()
    for fetched, stored in zip(fetches, stores):
        fetched.wait()
        stored.start()
    taps, conv_width = cw_ref.shape
    heads, inner = bias_ref.shape[0], gain_ref.shape[0]
    d = dng_ref.shape[0] * LANES
    cw_ref[...] = small_ref[0:taps, 0:conv_width]
    cb_ref[...] = small_ref[taps : taps + 1, 0:conv_width].reshape(conv_width)
    gain_ref[...] = small_ref[5:6, 0:inner].reshape(inner)
    bias_ref[...] = small_ref[7:8, 0:heads].reshape(heads)
    log_ref[...] = small_ref[7:8, LANES : LANES + heads].reshape(heads)
    squares = jnp.sum(small_ref[7:8, 2 * LANES : 3 * LANES], axis=1, keepdims=True)
    loss_ref[...] = squares / (sums_ref[8:9, 0:1] * d)
    by_head = jnp.zeros((16, 2 * heads), F32)
    for v in split3(jnp.broadcast_to(small_ref[6:7, 0:inner], (16, inner))):
        by_head = by_head + mm_nt(v, e_ref[...])
    skip_ref[...] = by_head[0:1, 0:heads].reshape(heads)
    ngain_ref[...] = dng_ref[...].reshape(d)
    for copy in stores:
        copy.wait()


def finish(gi, go, gt, output, small, dng, sums, e, taps, conv_width, heads, inner):
    shape = jax.ShapeDtypeStruct
    anywhere = pl.BlockSpec(memory_space=pl.ANY)
    outs = [
        shape(output.shape, BF16), shape((1, 1), F32), shape(gt.shape, BF16), shape((dng.size,), F32),
        shape(gi.shape, F32), shape((taps, conv_width), F32), shape((conv_width,), F32), shape((heads,), F32),
        shape((heads,), F32), shape((heads,), F32), shape((inner,), F32), shape(go.shape, F32),
    ]
    far = (0, 2, 4, 11)
    return pl.pallas_call(
        finish_kernel,
        grid=(1,),
        in_specs=[*[anywhere] * 4, *[full(a.shape) for a in (small, dng, sums, e)]],
        out_specs=[anywhere if i in far else full(o.shape) for i, o in enumerate(outs)],
        out_shape=outs,
        scratch_shapes=[
            *[pltpu.VMEM(a.shape, a.dtype) for a in (gi, go, gt, output)], pltpu.SemaphoreType.DMA((8,)),
        ],
        compiler_params=pltpu.CompilerParams(vmem_limit_bytes=60 * 2**20),
        name="finish",
    )(gi, go, gt, output, small, dng, sums, e)


MESH = pl.DeviceIdType.MESH


class Spot:
    def __init__(self, levels):
        self.rep, self.at = lax.axis_index("rep"), lax.axis_index("fsdp")
        self.core, self.side, self.level = self.at % 2, (self.at // 2) % 2, self.at // 4
        self.levels = levels
        self.sibling = (self.rep, self.at + 1 - 2 * self.core)
        self.across = (self.rep, self.at + 2 - 4 * self.side)
        self.twin = (1 - self.rep, self.at)

    def far(self, step):
        return (self.rep, ((self.level + step) % self.levels) * 4 + self.at % 4)

    def corner(self, j):
        flip = lambda v, bit: 1 - v if j & bit else v
        return (flip(self.rep, 4), self.level * 4 + flip(self.side, 2) * 2 + flip(self.core, 1))

    def greet(self, corners=False):
        barrier = pltpu.get_barrier_semaphore()
        near = [self.corner(j) for j in range(1, 8)] if corners else [self.sibling, self.across, self.twin]
        partners = near + [self.far(d) for d in range(1, self.levels)]
        for one in partners:
            pl.semaphore_signal(barrier, inc=1, device_id=one, device_id_type=MESH)
        pl.semaphore_wait(barrier, len(partners))


def send(src, dst, send_sem, recv_sem, device):
    return pltpu.make_async_remote_copy(
        src_ref=src, dst_ref=dst, send_sem=send_sem, recv_sem=recv_sem, device_id=device, device_id_type=MESH
    )


class Split:
    def __init__(self, spot, whole, own, from_core, half, from_side, from_level, mine, from_twin, sems, write):
        self.spot, self.whole, self.own, self.write = spot, whole, own, write
        self.from_core, self.half, self.from_side, self.from_level = from_core, half, from_side, from_level
        self.mine, self.from_twin, self.sems = mine, from_twin, sems
        self.cols = half.shape[-1]

    def columns(self, rep):
        return pl.ds(pl.multiple_of(rep * self.cols, self.cols), self.cols)

    @property
    def c0(self):
        return pltpu.make_async_copy(self.whole.at[:, :, self.spot.core], self.own, self.sems.at[6])

    @property
    def c1(self):
        spot, sems = self.spot, self.sems
        return send(self.whole.at[:, :, 1 - spot.core], self.from_core, sems.at[0], sems.at[1], spot.sibling)

    @property
    def c2(self):
        spot, sems = self.spot, self.sems
        block = self.own.at[:, :, :, self.columns(1 - spot.rep)]
        return send(block, self.half, sems.at[2], sems.at[3], spot.twin)

    @property
    def c3(self):
        spot, sems = self.spot, self.sems
        last = 5 + 2 * spot.levels
        return send(self.half.at[:, 1 - spot.side], self.from_side, sems.at[last], sems.at[last + 1], spot.across)

    @property
    def c4(self):
        spot, sems = self.spot, self.sems
        return [
            send(
                self.from_side.at[(spot.level + d) % spot.levels], self.from_level.at[d - 1],
                sems.at[5 + 2 * d], sems.at[6 + 2 * d], spot.far(d),
            )
            for d in range(1, spot.levels)
        ]

    @property
    def c5(self):
        spot, sems = self.spot, self.sems
        return send(self.mine, self.from_twin, sems.at[4], sems.at[5], spot.twin)

    def stage(self, number):
        spot, levels = self.spot, self.spot.levels
        if number == 1:
            self.c1.start()
            self.c0.start()
        elif number == 2:
            self.c0.wait()
            self.c1.wait()

            def add(i, carry):
                for side in range(2):
                    self.own[i, side] = self.own[i, side] + self.from_core[i, side]
                return carry

            lax.fori_loop(0, levels, add, 0)
            self.c2.start()
        elif number == 3:
            self.c2.wait()
            columns = self.columns(spot.rep)

            def add(i, carry):
                for side in range(2):
                    self.half[i, side] = self.half[i, side] + self.own[i, side, :, columns]
                return carry

            lax.fori_loop(0, levels, add, 0)
            self.c3.start()
        elif number == 4:
            self.c3.wait()

            def add(i, carry):
                self.from_side[i] = self.from_side[i] + self.half[i, spot.side]
                return carry

            lax.fori_loop(0, levels, add, 0)
            for copy in self.c4:
                copy.start()
        elif number == 5:
            for copy in self.c4:
                copy.wait()
            total = self.from_side[spot.level].astype(F32)
            for d in range(levels - 1):
                total = total + self.from_level[d].astype(F32)
            self.mine[...] = total.astype(BF16)
            self.c5.start()
        else:
            self.c5.wait()
            self.write(self.mine[...].astype(F32), self.columns(spot.rep))
            self.write(self.from_twin[...].astype(F32), self.columns(1 - spot.rep))


class Unit:
    def __init__(self, spot, whole, own, from_core, from_side, from_level, mine, from_twin, sems, write):
        self.spot, self.whole, self.own, self.write = spot, whole, own, write
        self.from_core, self.from_side, self.from_level = from_core, from_side, from_level
        self.mine, self.from_twin = mine, from_twin
        self.sems = sems

    @property
    def c0(self):
        return pltpu.make_async_copy(self.whole.at[:, :, self.spot.core], self.own, self.sems.at[6])

    @property
    def c1(self):
        spot, sems = self.spot, self.sems
        return send(self.whole.at[:, :, 1 - spot.core], self.from_core, sems.at[0], sems.at[1], spot.sibling)

    @property
    def c2(self):
        spot, sems = self.spot, self.sems
        return send(self.own.at[:, 1 - spot.side], self.from_side, sems.at[2], sems.at[3], spot.across)

    @property
    def c3(self):
        spot, sems = self.spot, self.sems
        return [
            send(
                self.from_side.at[(spot.level + d) % spot.levels], self.from_level.at[d - 1],
                sems.at[5 + 2 * d], sems.at[6 + 2 * d], spot.far(d),
            )
            for d in range(1, spot.levels)
        ]

    @property
    def c4(self):
        spot, sems = self.spot, self.sems
        return send(self.mine, self.from_twin, sems.at[4], sems.at[5], spot.twin)

    def stage(self, number):
        spot, levels = self.spot, self.spot.levels
        if number == 1:
            self.c1.start()
            self.c0.start()
        elif number == 2:
            self.c0.wait()
            self.c1.wait()

            def add(i, carry):
                for side in range(2):
                    self.own[i, side] = self.own[i, side] + self.from_core[i, side]
                return carry

            lax.fori_loop(0, levels, add, 0)
            self.c2.start()
        elif number == 3:
            self.c2.wait()

            def add(i, carry):
                self.from_side[i] = self.from_side[i] + self.own[i, spot.side]
                return carry

            lax.fori_loop(0, levels, add, 0)
            for copy in self.c3:
                copy.start()
        elif number == 4:
            for copy in self.c3:
                copy.wait()
            total = self.from_side[spot.level].astype(F32)
            for d in range(levels - 1):
                total = total + self.from_level[d].astype(F32)
            self.mine[...] = total.astype(BF16)
            self.c4.start()
        else:
            self.c4.wait()
            self.write(self.mine[...].astype(F32) + self.from_twin[...].astype(F32))


GROUPS = 4
STARTS = (0, 2, 4, 6, 8, 11, 13, 16, 18, 20, 24)
UNIT_DELAYS = (0, 1, 5, 9, 11)
SPLIT_DELAYS = (0, 1, 5, 8, 11, 13)


def back_kernel(
    px_ref, prev_ref, y_ref, dy_ref, state_ref,
    tail_ref, aux_ref, seg_ref, cw_ref, cb_ref, bias_ref, rate_ref, skip_ref, e_ref, rate_t_ref,
    ngain_ref, dgain_ref, square_ref,
    normed_t_hbm, wx_hbm, wt_hbm, gn_hbm, tokens_hbm, gb_hbm, ggate_hbm, gout_hbm,
    gi_ref, go_ref, gt_ref, small_ref, dng_ref,
    xbuf, ex, adj, xs, xdt, xe, bc, slope, dye, dxi, dbuf, r1, r1l, r2, r3,
    tbuf, consts, stacks, raws, cums, cum_ts, ones, steps, scores, dscores, gbs, gcs, sums, tslope, gp, gpt, accum, taccum,
    normed_t, wx, wt, gn, tokens, gb,
    own, part, part_t, own_t, from_core, from_core_t, from_side, from_side_t, from_level, from_level_t,
    mine, mine_t, twin, twin_t, half, half_side, half_level, half_mine, half_twin, local, sm, smr, smz, gain_out, gain_near, gain_sum, gain_far, sems, small_sems, gain_sems, load_sems,
    *, inner, heads, width, levels, seq_chunks,
):
    group, turn = pl.program_id(0), pl.program_id(1)
    step = group * seq_chunks + turn
    chunk = seq_chunks - 1 - turn
    rows, cols_g = px_ref.shape
    n = bc.shape[2] // 2
    tiles = cols_g // LANES
    per_group = cols_g // width
    taps = cw_ref.shape[0]
    tail_cols = tail_ref.shape[1]
    conv_tail = 2 * n
    here = pl.ds(pl.multiple_of(chunk * rows, rows), rows)
    spot = Spot(levels)
    gcol = pl.multiple_of(group * cols_g, cols_g)
    rows_f = mine.shape[1]

    def loads():
        pairs = ((normed_t_hbm, normed_t), (wx_hbm, wx), (wt_hbm, wt), (gn_hbm, gn), (tokens_hbm, tokens), (gb_hbm, gb))
        return [pltpu.make_async_copy(a, b, load_sems.at[i]) for i, (a, b) in enumerate(pairs)]

    def writer(ref, row, col, wide):
        def write(v, columns=None):
            if columns is None:
                ref[row : row + rows_f, col : col + wide] = v[:, :wide]
            else:
                at = pl.multiple_of(col + columns.start, LANES)
                ref[row : row + rows_f, pl.ds(at, columns.size)] = v
        return write

    sources = []
    for u in range(GROUPS):
        hbm = gout_hbm.at[:, :, :, pl.ds((u // 2) * rows_f, rows_f), pl.ds((u % 2) * cols_g, cols_g)]
        sources.append((hbm, writer(go_ref, (u // 2) * rows_f, (u % 2) * cols_g, cols_g)))
    for u in range(GROUPS):
        hbm = ggate_hbm.at[:, :, :, :, pl.ds(u * cols_g, cols_g)]
        sources.append((hbm, writer(gi_ref, 0, u * cols_g, cols_g)))
    for g in range(GROUPS):
        sources.append((part.at[g % 2], writer(gi_ref, 0, inner + g * cols_g, cols_g)))
    order = [0, 1, 2, 3, 8, 4, 5, 9, 6, 7, 10, 11]
    units = []
    for i, u in enumerate(order):
        k = i // 2
        whole, write = sources[u]
        if i % 2:
            units.append(
                Split(
                    spot, whole, own.at[u], from_core.at[u], half.at[k], half_side.at[k], half_level.at[k],
                    half_mine.at[k], half_twin.at[k], sems.at[u], write,
                )
            )
        else:
            units.append(
                Unit(
                    spot, whole, own.at[u], from_core.at[u], from_side.at[k], from_level.at[k], mine.at[k], twin.at[k],
                    sems.at[u], write,
                )
            )
    tail_wide = gi_ref.shape[1] - 2 * inner
    tail_unit = Unit(
        spot, part_t, own_t, from_core_t, from_side_t, from_level_t, mine_t, twin_t, sems.at[3 * GROUPS],
        writer(gi_ref, 0, 2 * inner, tail_wide),
    )

    events = {}
    last_step = GROUPS * seq_chunks - 1
    late = []
    for i, (begin, unit) in enumerate(zip(STARTS, units)):
        begin = begin * seq_chunks // 8
        for number, delay in enumerate(SPLIT_DELAYS if i % 2 else UNIT_DELAYS):
            events.setdefault(min(begin + delay, last_step), []).append((unit, number + 1))

    @pl.when(step == 0)
    def _():
        for copy in loads():
            copy.start()
        spot.greet(corners=True)
        accum[...] = jnp.zeros_like(accum)
        taccum[...] = jnp.zeros_like(taccum)
        steps[...] = jnp.zeros_like(steps)
        ones[...] = (iota(ones.shape, 0) == iota(ones.shape, 1) // width).astype(BF16)

    for at, happen in sorted(events.items()):
        if at == last_step:
            late += happen
            continue

        @pl.when(step == at)
        def _(happen=happen):
            for unit, number in sorted(happen, key=lambda pair: -pair[1]):
                unit.stage(number)

    def fold(v):
        return jnp.sum(v.reshape(v.shape[0] // 8, 8, v.shape[1]), axis=0)

    aux = aux_ref[here, :]
    marks = [None] + [jnp.broadcast_to(aux[:, k : k + 1], (rows, LANES)) for k in range(1, taps)]
    marks_next = [None] + [jnp.broadcast_to(aux[:, 3 + k : 4 + k], (rows, LANES)) for k in range(1, taps)]
    lower = iota((rows, rows), 0) >= iota((rows, rows), 1)
    upper = iota((rows, rows), 0) <= iota((rows, rows), 1)
    rate = rate_ref[...]

    def conv_pre(buffer, cols, wcols):
        pre = cb_ref[:, wcols] + cw_ref[0:1, wcols] * buffer[8 : 8 + rows, cols]
        for k in range(1, taps):
            pre = pre + (cw_ref[k : k + 1, wcols] * buffer[8 - k : 8 - k + rows, cols]) * marks[k]
        return pre

    def conv_back(buffer, cols, wcols, acc, acc_cols):
        outs = []
        adds = [jnp.zeros((8, LANES), F32) for _ in range(taps + 1)]
        for at in range(0, rows, 64):
            inputs = xbuf[8 + at : 72 + at, cols]
            for k in range(taps):
                grad = buffer[at + k : at + k + 64, cols]
                if k == 0:
                    out = cw_ref[0:1, wcols] * grad
                    adds[taps] = adds[taps] + fold(grad)
                else:
                    grad = grad * marks_next[k][at : at + 64]
                    out = out + cw_ref[k : k + 1, wcols] * grad
                adds[k] = adds[k] + fold(grad * inputs)
            outs.append(out)
        for k in range(taps + 1):
            acc[8 * k : 8 * k + 8, acc_cols] += adds[k]
        return jnp.concatenate(outs, axis=0)

    def fill_tail():
        xbuf[8 : 8 + rows, 0:conv_tail] = tail_ref[here, 0:conv_tail]
        before = pl.ds(pl.multiple_of(jnp.maximum(chunk * rows - 8, 0), 8), 8)
        xbuf[0:8, 0:conv_tail] = tail_ref[before, 0:conv_tail]

    @pl.when(group == 0)
    def _():
        shifted, step_size, cum, from_prev, to_end = small_terms(
            tail_ref[here, conv_tail : conv_tail + heads], bias_ref[...], rate, aux[:, 7:8], aux[:, 8:9], rows
        )
        turned = jnp.concatenate([shifted, step_size, cum, jnp.zeros((rows, LANES - 3 * heads), F32)], axis=1).T
        raws[chunk] = turned[0 : 2 * heads]
        cum_ts[chunk] = turned[2 * heads : 3 * heads]
        for g in range(GROUPS):
            cums[g, here, 0:per_group] = cum[:, g * per_group : (g + 1) * per_group]
        stacks[chunk] = jnp.concatenate(
            [jnp.concatenate(split2(v), axis=1) for v in (step_size, from_prev, to_end)], axis=0
        )
        fill_tail()
        for c in range(conv_tail // LANES):
            cols = slice(c * LANES, (c + 1) * LANES)
            pre = conv_pre(xbuf, cols, slice(inner + c * LANES, inner + (c + 1) * LANES))
            sig = sigmoid(pre)
            act = pre * sig
            tslope[here, cols] = sig + act * (1.0 - sig)
            bc[chunk, :, cols] = act.astype(BF16)
        same = upper & (aux[:, 0:1] == seg_ref[chunk])
        scores[chunk] = jnp.where(same, mm_nt(bc[chunk, :, 0:n], bc[chunk, :, n:]), 0.0)
        dscores[chunk] = jnp.zeros((rows, rows), F32)
        gbs[here, :] = jnp.zeros((rows, n), F32)
        gcs[here, :] = jnp.zeros((rows, n), F32)

    @pl.when(turn == 0)
    def _():
        adj[...] = jnp.zeros_like(adj)
        dbuf[rows : rows + 8, :] = jnp.zeros((8, cols_g), F32)

    ex[...] = mm(stacks[chunk], e_ref[:, pl.ds(gcol, cols_g)])
    own_heads = pl.ds(pl.multiple_of(group * per_group, per_group), per_group)
    cum = cums[group, here, :]
    cum_t = cum_ts[chunk, own_heads, :]
    xbuf[0:8, :] = prev_ref[...]
    xbuf[8 : 8 + rows, :] = px_ref[...]
    for c in range(tiles):
        cols = slice(c * LANES, (c + 1) * LANES)
        wcols = pl.ds(gcol + c * LANES, LANES)
        pre = conv_pre(xbuf, cols, wcols)
        sig = sigmoid(pre)
        act = pre * sig
        slope[:, cols] = sig + act * (1.0 - sig)
        xs[:, cols] = act
        scaled = act * ex[0:rows, cols]
        xdt[:, cols] = scaled.astype(BF16)
        xe[:, cols] = (scaled * ex[2 * rows : 3 * rows, cols]).astype(BF16)
        dye[:, cols] = (dy_ref[:, cols].astype(F32) * ex[rows : 2 * rows, cols]).astype(BF16)
    b, cc = bc[chunk, :, 0:n], bc[chunk, :, n:]
    state_low = state_ref[...]
    adj_low = adj[...].astype(BF16)
    carry = ex[2 * rows - 1 : 2 * rows, :]
    gcs[here, :] += mm_nt(dye[...], state_low)
    gbs[here, :] += mm_nt(xe[...], adj_low)
    dxi[...] = mm(b, adj_low)
    through = jnp.sum(adj[...] * state_low.astype(F32), axis=0, keepdims=True) * carry
    adj[...] = adj[...] * carry + mm_tn(cc, dye[...])
    scores_t = scores[chunk]
    lane = iota((1, LANES), 1)
    masks = [(lane < width).astype(BF16), (lane >= width).astype(BF16)]
    grad_scores_t = jnp.zeros((rows, rows), F32)
    for c in range(tiles):
        cols = slice(c * LANES, (c + 1) * LANES)
        acols = pl.ds(gcol + c * LANES, LANES)
        x_low, dy_low = xdt[:, cols], dy_ref[:, cols]
        grad_mix = mm_nt(jnp.concatenate([x_low * masks[0], x_low * masks[1]], axis=0), dy_low)
        mixing = []
        for i, h in enumerate((2 * c, 2 * c + 1)):
            decay = jnp.exp(jnp.minimum(cum_t[h : h + 1, :] - cum[:, h : h + 1], 0.0))
            mixing.append((scores_t * decay).astype(BF16))
            grad_scores_t = grad_scores_t + grad_mix[i * rows : (i + 1) * rows] * decay
        within = mm(
            jnp.concatenate(mixing, axis=1), jnp.concatenate([dy_low * masks[0], dy_low * masks[1]], axis=0)
        )
        x = xs[:, cols]
        skip = skip_ref[:, acols]
        across = ex[2 * rows : 3 * rows, cols] * dxi[:, cols]
        both = within + across
        grad_ssd = dy_low.astype(F32)
        x_scaled = x_low.astype(F32)
        r1[:, cols], r1l[:, cols] = split2(grad_ssd * y_ref[:, cols] - within * x_scaled)
        r2[:, cols] = (across * x_scaled).astype(BF16)
        r3[:, cols] = (both * x).astype(BF16)
        accum[8 * taps + 8 : 8 * taps + 16, acols] += fold(grad_ssd * x)
        grad_x = skip * grad_ssd + ex[0:rows, cols] * both
        dbuf[0:rows, cols] = grad_x * slope[:, cols]
    dscores[chunk] += grad_scores_t
    by_head = ones[...]
    sums[0, chunk, own_heads, :] = (mm_nt(by_head, r1[...]) + mm_nt(by_head, r1l[...]))[0:per_group]
    sums[1, chunk, own_heads, :] = mm_nt(by_head, r2[...])[0:per_group]
    sums[2, chunk, own_heads, :] = mm_nt(by_head, r3[...])[0:per_group]
    high, rest = split2(jnp.broadcast_to(through, (16, cols_g)))
    const = (mm_nt(by_head, high) + mm_nt(by_head, rest))[0:per_group, 0:1]
    consts[chunk, own_heads, :] = jnp.broadcast_to(const, (per_group, LANES))
    for c in range(tiles):
        cols = slice(c * LANES, (c + 1) * LANES)
        acols = pl.ds(gcol + c * LANES, LANES)
        gp[here, cols] = conv_back(dbuf, cols, acols, accum, acols).astype(BF16)
    dbuf[rows : rows + 8, :] = dbuf[0:8, :]

    @pl.when(group == GROUPS - 1)
    def _():
        same = upper & (aux[:, 0:1] == seg_ref[chunk])
        grad_scores = jnp.where(same, dscores[chunk], 0.0).astype(BF16)
        grad_b = gbs[here, :] + mm(grad_scores, cc)
        grad_c = gcs[here, :] + mm_tn(grad_scores, b)
        fill_tail()

        @pl.when(turn == 0)
        def _():
            tbuf[rows : rows + 8, :] = jnp.zeros((8, 2 * n), F32)

        tbuf[0:rows, 0:n] = grad_b * tslope[here, 0:n]
        tbuf[0:rows, n : 2 * n] = grad_c * tslope[here, n : 2 * n]
        for c in range(conv_tail // LANES):
            cols = slice(c * LANES, (c + 1) * LANES)
            gpt[here, cols] = conv_back(
                tbuf, cols, slice(inner + c * LANES, inner + (c + 1) * LANES), taccum, cols
            ).astype(BF16)
        tbuf[rows : rows + 8, :] = tbuf[0:8, :]
        shifted, step_size = raws[chunk, 0:heads, :], raws[chunk, heads : 2 * heads, :]
        turned_aux = jnp.concatenate([aux, jnp.zeros((rows, LANES - aux.shape[1]), F32)], axis=1).T
        grad_log = (
            sum_tri(sums[0, chunk], lower.astype(BF16))
            + sum_tri(sums[1, chunk], (iota((rows, rows), 0) < iota((rows, rows), 1)).astype(BF16))
            + consts[chunk]
        ) * turned_aux[1:2, :]
        rate_t = jnp.broadcast_to(rate_t_ref[...], (heads, rows))
        grad_raw = (sums[2, chunk] + rate_t * grad_log) * sigmoid(shifted)
        gpt[here, conv_tail:] = (
            jnp.concatenate([grad_raw, jnp.zeros((tail_cols - conv_tail - heads, rows), F32)], axis=0).T
        ).astype(BF16)
        steps[0] += grad_raw
        steps[1] += step_size * grad_log * rate_t

    def weight_grad(low, out):
        flat = out.reshape(normed_t.shape[0], low.shape[1])
        for k in range(0, low.shape[1], 256):
            cols = slice(k, min(k + 256, low.shape[1]))
            flat[:, cols] = mm(normed_t[...], low[:, cols]).astype(BF16)

    def input_grad(low, weights):
        for k in range(gn.shape[1] // 256):
            cols = slice(k * 256, (k + 1) * 256)
            gn[:, cols] += mm_nt(low[...], weights[cols, :])

    for g in range(GROUPS - 1):

        @pl.when(step == (g + 1) * seq_chunks - 1)
        def _(g=g):
            if g == 0:
                for copy in loads():
                    copy.wait()
            weight_grad(gp, part.at[g % 2])
            input_grad(gp, wx.at[:, g * cols_g : (g + 1) * cols_g])

    @pl.when(step == last_step)
    def _():
        d = gn.shape[1]
        half_cols = sm.shape[2]

        def half_of(core):
            return pl.ds(pl.multiple_of(core * half_cols, half_cols), half_cols)

        def exchange(i):
            src = (local.at[:, half_of(1 - spot.core)], sm.at[0], sm.at[1], sm.at[3])[i]
            device = (spot.sibling, spot.across, spot.twin, spot.sibling)[i]
            return send(src, smr.at[i], small_sems.at[2 * i], small_sems.at[2 * i + 1], device)

        spread = lambda k: send(
            sm.at[2], smz.at[spot.level], small_sems.at[6 + 2 * k], small_sems.at[7 + 2 * k], spot.far(k)
        )

        def one_row(v):
            return jnp.sum(v, axis=0, keepdims=True)

        def fold_small(i):
            exchange(i).wait()
            sm[i] = (local[:, half_of(spot.core)] if i == 0 else sm[i - 1]) + smr[i]

        local[...] = jnp.zeros(local.shape, F32)
        for k in range(taps + 1):
            local[k : k + 1, 0:inner] = one_row(accum[8 * k : 8 * k + 8, :])
            local[k : k + 1, inner : inner + conv_tail] = one_row(taccum[8 * k : 8 * k + 8, 0:conv_tail])
        local[5:6, 0:inner] = one_row(dgain_ref[...])
        local[6:7, 0:inner] = one_row(accum[8 * taps + 8 : 8 * taps + 16, :])
        for i in range(2):
            turned = jnp.concatenate([steps[i], jnp.zeros((LANES - heads, LANES), F32)], axis=0).T
            local[7:8, i * LANES : (i + 1) * LANES] = one_row(turned)
        local[7:8, 2 * LANES : 3 * LANES] = one_row(square_ref[...])
        exchange(0).start()
        for unit, number in sorted(late, key=lambda pair: pair[1]):
            unit.stage(number)
        last = units[-1]
        weight_grad(gpt, part_t)
        tail_unit.stage(1)
        fold_small(0)
        exchange(1).start()
        weight_grad(gp, part.at[(GROUPS - 1) % 2])
        last.stage(1)
        tail_unit.stage(2)
        fold_small(1)
        exchange(2).start()
        input_grad(gpt, wt)
        last.stage(2)
        fold_small(2)
        for k in range(1, levels):
            spread(k).start()
        smz[spot.level] = sm[2]
        input_grad(gp, wx.at[:, (GROUPS - 1) * cols_g : GROUPS * cols_g])
        tail_unit.stage(3)
        ngain = ngain_ref[...]

        def block_norm(i, total):
            block = pl.ds(pl.multiple_of(i * 64, 64), 64)
            v = tokens[block, :].astype(F32)
            rinv = lax.rsqrt(jnp.sum(v * v, axis=1, keepdims=True) / d + EPS)
            scaled = v * rinv
            grad = gn[block, :]
            total = total + jnp.sum((grad * scaled).reshape(8, 8, d), axis=0)
            grad = grad * ngain
            mean = jnp.sum(grad * scaled, axis=1, keepdims=True) / d
            gb[block, :] = (gb[block, :].astype(F32) + rinv * (grad - scaled * mean)).astype(BF16)
            return total

        blocks = gn.shape[0] // 64
        dnorm = lax.fori_loop(0, blocks // 2, block_norm, jnp.zeros((8, d), F32))
        last.stage(3)
        dnorm = lax.fori_loop(blocks // 2, blocks, block_norm, dnorm)
        leave = pltpu.make_async_copy(gb, gt_ref, load_sems.at[6])
        leave.start()
        dnorm = one_row(dnorm)
        place = spot.rep * 4 + spot.side * 2 + spot.core
        for k in range(d // LANES):
            gain_out[k : k + 1, :] = dnorm[:, k * LANES : (k + 1) * LANES]
        near = lambda k: send(
            gain_out, gain_near.at[place], gain_sems.at[2 * k - 2], gain_sems.at[2 * k - 1], spot.corner(k)
        )
        beyond = lambda k: send(
            gain_sum, gain_far.at[spot.level], gain_sems.at[12 + 2 * k], gain_sems.at[13 + 2 * k], spot.far(k)
        )
        for k in range(1, 8):
            near(k).start()
        gain_near[place] = gain_out[...]
        last.stage(4)
        for k in range(1, levels):
            spread(k).wait()
        total = smz[0]
        for k in range(1, levels):
            total = total + smz[k]
        sm[3] = total
        exchange(3).start()
        for k in range(1, 8):
            near(k).wait()
        total = gain_near[0]
        for k in range(1, 8):
            total = total + gain_near[k]
        gain_sum[...] = total
        for k in range(1, levels):
            beyond(k).start()
        gain_far[spot.level] = gain_sum[...]
        tail_unit.stage(4)
        last.stage(5)
        for k in range(1, levels):
            beyond(k).wait()
        total = gain_far[0]
        for k in range(1, levels):
            total = total + gain_far[k]
        dng_ref[...] = total
        exchange(3).wait()
        small_ref[:, half_of(spot.core)] = sm[3]
        small_ref[:, half_of(1 - spot.core)] = smr[3]
        tail_unit.stage(5)
        last.stage(6)
        leave.wait()


def back(
    px, px_block, tail, y, dy, states, aux, seg_rows, conv_w, conv_b, bias, rate, skip_row, e, rate_t,
    norm_gain, dgain, squares, normed_t, wx, wt, gn, tokens, gb, ggate, gout, proj,
):
    length, inner = y.shape
    heads = bias.shape[1]
    levels, rows_f = ggate.shape[0], ggate.shape[3]
    taps = conv_w.shape[0]
    n = (conv_w.shape[1] - inner) // 2
    r = CHUNK
    chunks = length // r
    wide = inner // GROUPS
    tcols = tail.shape[1]
    d = normed_t.shape[0]
    small_cols = inner + tcols + LANES
    units = 3 * GROUPS
    back_at = lambda off: lambda g, c: (chunks - 1 - c, g + off)
    whole = lambda a: pl.BlockSpec(a.shape, lambda g, c: (0,) * a.ndim, pipeline_mode=pl.Buffered(1))
    anywhere = pl.BlockSpec(memory_space=pl.ANY)
    vm = pltpu.VMEM
    out = lambda s: pl.BlockSpec(s, lambda g, c: (0,) * len(s))
    return pl.pallas_call(
        functools.partial(
            back_kernel, inner=inner, heads=heads, width=inner // heads, levels=levels, seq_chunks=chunks
        ),
        grid=(GROUPS, chunks),
        in_specs=[
            pl.BlockSpec((r, wide), back_at(px_block)),
            pl.BlockSpec((8, wide), lambda g, c: (jnp.maximum((chunks - 1 - c) * (r // 8) - 1, 0), g + px_block)),
            pl.BlockSpec((r, wide), back_at(0)),
            pl.BlockSpec((r, wide), back_at(0)),
            pl.BlockSpec((n, wide), back_at(0)),
            *[whole(a) for a in (tail, aux, seg_rows, conv_w, conv_b, bias, rate, skip_row, e, rate_t, norm_gain, dgain, squares)],
            *[anywhere] * 8,
        ],
        out_specs=[out((rows_f, proj)), out((2 * rows_f, d)), anywhere, out((8, small_cols)), out((d // LANES, LANES))],
        out_shape=[
            jax.ShapeDtypeStruct((rows_f, proj), F32),
            jax.ShapeDtypeStruct((2 * rows_f, d), F32),
            jax.ShapeDtypeStruct((length, d), BF16),
            jax.ShapeDtypeStruct((8, small_cols), F32),
            jax.ShapeDtypeStruct((d // LANES, LANES), F32),
        ],
        scratch_shapes=[
            vm((r + 8, wide), F32), vm((3 * r, wide), F32), vm((n, wide), F32), vm((r, wide), F32),
            vm((r, wide), BF16), vm((r, wide), BF16), vm((chunks, r, 2 * n), BF16), vm((r, wide), F32),
            vm((r, wide), BF16), vm((r, wide), F32), vm((r + 8, wide), F32),
            vm((r, wide), BF16), vm((r, wide), BF16), vm((r, wide), BF16), vm((r, wide), BF16),
            vm((r + 8, 2 * n), F32), vm((chunks, heads, LANES), F32),
            vm((chunks, 3 * r, 2 * heads), BF16), vm((chunks, 2 * heads, r), F32), vm((GROUPS, length, LANES), F32),
            vm((chunks, heads, r), F32), vm((16, wide), BF16), vm((2, heads, r), F32),
            vm((chunks, r, r), F32), vm((chunks, r, r), F32), vm((length, n), F32), vm((length, n), F32),
            vm((3, chunks, heads, r), F32), vm((length, 2 * n), F32), vm((length, wide), BF16), vm((length, tcols), BF16),
            vm((8 * taps + 16, inner), F32), vm((8 * taps + 8, 2 * n), F32),
            vm(normed_t.shape, BF16), vm(wx.shape, BF16), vm(wt.shape, BF16), vm(gn.shape, F32), vm(tokens.shape, BF16), vm(gb.shape, BF16),
            vm((units, levels, 2, rows_f, wide), BF16), vm((2, levels, 2, 2, rows_f, wide), BF16),
            vm((levels, 2, 2, rows_f, tcols), BF16), vm((levels, 2, rows_f, tcols), BF16),
            vm((units, levels, 2, rows_f, wide), BF16), vm((levels, 2, rows_f, tcols), BF16),
            vm((units // 2, levels, rows_f, wide), BF16), vm((levels, rows_f, tcols), BF16),
            vm((units // 2, levels - 1, rows_f, wide), BF16), vm((levels - 1, rows_f, tcols), BF16),
            vm((units // 2, rows_f, wide), BF16), vm((rows_f, tcols), BF16),
            vm((units // 2, rows_f, wide), BF16), vm((rows_f, tcols), BF16),
            vm((units // 2, levels, 2, rows_f, wide // 2), BF16), vm((units // 2, levels, rows_f, wide // 2), BF16),
            vm((units // 2, levels - 1, rows_f, wide // 2), BF16),
            vm((units // 2, rows_f, wide // 2), BF16), vm((units // 2, rows_f, wide // 2), BF16),
            vm((8, small_cols), F32), vm((4, 8, small_cols // 2), F32), vm((4, 8, small_cols // 2), F32),
            vm((levels, 8, small_cols // 2), F32),
            vm((d // LANES, LANES), F32), vm((8, d // LANES, LANES), F32), vm((d // LANES, LANES), F32),
            vm((levels, d // LANES, LANES), F32),
            pltpu.SemaphoreType.DMA((units + 1, 7 + 2 * levels)),
            pltpu.SemaphoreType.DMA((6 + 2 * levels,)),
            pltpu.SemaphoreType.DMA((12 + 2 * levels,)),
            pltpu.SemaphoreType.DMA((7,)),
        ],
        compiler_params=pltpu.CompilerParams(
            dimension_semantics=("arbitrary", "arbitrary"), vmem_limit_bytes=60 * 2**20,
            collective_id=1, has_side_effects=True,
        ),
        name="scan_backward",
    )(
        px, px, y, dy, states, tail, aux, seg_rows, conv_w, conv_b, bias, rate, skip_row, e, rate_t,
        norm_gain, dgain, squares, normed_t, wx, wt, gn, tokens, gb, ggate, gout,
    )


class Load:
    def __init__(self, spot, shard, whole, sems, split):
        self.spot, self.shard, self.whole, self.sems, self.split = spot, shard, whole, sems, split

    def part(self, ref):
        if not self.split:
            return ref
        half = ref.shape[-1] // 2
        cols = pl.ds(pl.multiple_of(self.spot.rep * half, half), half)
        return ref.at[(slice(None),) * (len(ref.shape) - 1) + (cols,)]

    @property
    def a0(self):
        spot = self.spot
        here = self.whole.at[spot.level, spot.side, spot.core]
        return pltpu.make_async_copy(self.part(self.shard), self.part(here), self.sems.at[0])

    @property
    def a(self):
        spot, sems = self.spot, self.sems
        here = self.whole.at[spot.level, spot.side, spot.core]
        return [
            send(self.part(self.shard), self.part(here), sems.at[5 + 2 * d], sems.at[6 + 2 * d], spot.far(d))
            for d in range(1, spot.levels)
        ]

    @property
    def b(self):
        spot, sems = self.spot, self.sems
        if self.split:
            block = self.part(self.whole.at[:, spot.side, spot.core])
        else:
            half = spot.levels // 2
            block = self.whole.at[pl.ds(spot.rep * half, half), spot.side, spot.core]
        return send(block, block, sems.at[1], sems.at[2], spot.across)

    @property
    def c(self):
        spot, sems = self.spot, self.sems
        if self.split:
            block = self.part(self.whole.at[:, :, spot.core])
        else:
            half = spot.levels // 2
            block = self.whole.at[pl.ds(spot.rep * half, half), 1 - spot.side, spot.core]
        return send(block, block, sems.at[3], sems.at[4], spot.twin)

    @property
    def d(self):
        spot, sems = self.spot, self.sems
        block = self.whole.at[:, :, spot.core]
        last = 5 + 2 * spot.levels
        return send(block, block, sems.at[last], sems.at[last + 1], spot.sibling)

    def stage(self, number):
        if number == 1:
            self.a0.start()
            for copy in self.a:
                copy.start()
        elif number == 2:
            self.a0.wait()
            for copy in self.a:
                copy.wait()
            self.b.start()
        elif number == 3:
            self.b.wait()
            self.c.start()
        elif number == 4:
            self.c.wait()
            self.d.start()
        else:
            self.d.wait()


LOAD_STEPS = (5, 8, 14)


def first_kernel(
    cotan_ref, teacher_ref,
    tokens_hbm, ngain_ref, aux_ref, seg_ref, count_ref, cw_ref, cb_ref, bias_ref, rate_ref, skip_ref, gain_ref, e_ref,
    in_hbm, tail_hbm, out_hbm,
    px_ref, ssd_ref, state_out_ref, tail_out, normed_out, normed_t_out, wx_out, wtail_out,
    output_ref, gb_ref, mixed_ref, dy_ref, dz_ref, gn_ref, dgain_ref, small_ref,
    tokens, normed, normed_t, wx, wg, wo, weight_tail, tail, pbuf, ssd_all, gates, gms, inverses,
    ex, state, xs, xdt, xe, bc, yin, cums, scores, stacks,
    counts, countr, countz, sems, count_sems, copy_sems, leave_sems,
    *, inner, heads, width, levels, seq_chunks, loss_weight,
):
    step = pl.program_id(0)
    group, chunk = step // seq_chunks, step % seq_chunks
    rows, cols_g = px_ref.shape
    n = bc.shape[2] // 2
    tiles = cols_g // LANES
    per_group = cols_g // width
    taps = cw_ref.shape[0]
    rows_f = in_hbm.shape[0]
    tail_cols = tail.shape[1]
    conv_tail = 2 * n
    length, d_model = tokens.shape
    spot = Spot(levels)
    here = pl.ds(pl.multiple_of(chunk * rows, rows), rows)
    gcol = pl.multiple_of(group * cols_g, cols_g)
    last_step = GROUPS * seq_chunks - 1

    tail_load = Load(spot, tail_hbm, weight_tail, sems.at[0], False)
    loads = []
    for k in range(2 * GROUPS):
        cols = pl.ds((k % GROUPS) * cols_g, cols_g)
        shard = in_hbm.at[:, pl.ds((inner if k < GROUPS else 0) + (k % GROUPS) * cols_g, cols_g)]
        loads.append((shard, (wx if k < GROUPS else wg).at[:, :, :, :, cols]))
    for k in range(GROUPS):
        cols = pl.ds(k * (d_model // GROUPS), d_model // GROUPS)
        loads.append((out_hbm.at[:, cols], wo.at[:, :, :, :, cols]))
    loads = [Load(spot, shard, whole, sems.at[1 + k], k > 2 and k % 2 == 1) for k, (shard, whole) in enumerate(loads)]
    leaves = [
        (wx, wx_out), (weight_tail, wtail_out), (normed, normed_out), (normed_t, normed_t_out), (tail.at[8:], tail_out)
    ]

    def leave(k):
        return pltpu.make_async_copy(*leaves[k], leave_sems.at[k])

    exchange = lambda i: send(
        counts.at[i], countr.at[i], count_sems.at[2 * i], count_sems.at[2 * i + 1],
        (spot.sibling, spot.across, spot.twin)[i],
    )
    spread = lambda d: send(
        counts.at[3], countz.at[spot.level], count_sems.at[4 + 2 * d], count_sems.at[5 + 2 * d], spot.far(d)
    )

    def marks_of(aux):
        return [None] + [jnp.broadcast_to(aux[:, k : k + 1], (rows, LANES)) for k in range(1, taps)]

    def conv(buffer, at, cols, wcols, marks):
        block = buffer[pl.ds(at, rows + 8), cols]
        pre = cb_ref[:, wcols] + cw_ref[0:1, wcols] * block[8:]
        for k in range(1, taps):
            pre = pre + (cw_ref[k : k + 1, wcols] * block[8 - k : 8 - k + rows]) * marks[k]
        return pre * sigmoid(pre)

    def project(weight, out, cols):
        for i in range(length // 256):
            out[8 + i * 256 : 8 + (i + 1) * 256, :] = mm(normed[i * 256 : (i + 1) * 256, :], weight[:, cols])

    @pl.when(step == 0)
    def _():
        fetch = pltpu.make_async_copy(tokens_hbm, tokens, copy_sems.at[0])
        fetch.start()
        counts[0] = count_ref[...]
        spot.greet()
        tail_load.stage(1)
        exchange(0).start()
        loads[0].stage(1)
        loads[1].stage(1)
        fetch.wait()

        def norm(i, carry):
            block = pl.ds(pl.multiple_of(i * 64, 64), 64)
            v = tokens[block, :].astype(F32)
            v = v * lax.rsqrt(jnp.sum(v * v, axis=1, keepdims=True) / d_model + EPS)
            normed[block, :] = (v * ngain_ref[...]).astype(BF16)
            return carry

        lax.fori_loop(0, length // 64, norm, 0)
        def turn_rows(blocks):
            for i in blocks:
                block = slice(i * 256, (i + 1) * 256)
                normed_t[:, block] = normed[block, :].T

        def shared(i, carry):
            at = pl.ds(pl.multiple_of(i * rows, rows), rows)
            aux = aux_ref[at, :]
            marks = marks_of(aux)
            start = pl.multiple_of(i * rows, rows)
            raw = tail[pl.ds(start + 8, rows), conv_tail : conv_tail + heads]
            shifted, size, cum, from_prev, to_end = small_terms(
                raw, bias_ref[...], rate_ref[...], aux[:, 7:8], aux[:, 8:9], rows
            )
            cums[i, :, 0:heads] = cum
            stacks[i] = jnp.concatenate(
                [jnp.concatenate(split2(v), axis=1) for v in (size, from_prev, to_end)], axis=0
            )
            for c in range(conv_tail // LANES):
                cols = slice(c * LANES, (c + 1) * LANES)
                act = conv(tail, start, cols, slice(inner + c * LANES, inner + (c + 1) * LANES), marks)
                bc[i, :, cols] = act.astype(BF16)
            causal = (iota((rows, rows), 0) >= iota((rows, rows), 1)) & (aux[:, 0:1] == seg_ref[i])
            scores[i] = jnp.where(causal, mm_nt(bc[i, :, n:], bc[i, :, 0:n]), 0.0)
            return carry

        tail[0:8, :] = jnp.zeros((8, tail_cols), F32)
        pbuf[0:8, :] = jnp.zeros((8, cols_g), F32)
        cums[...] = jnp.zeros_like(cums)
        tail_load.stage(2)
        blocks = length // 256
        turn_rows(range(blocks // 2))
        tail_load.stage(3)
        turn_rows(range(blocks // 2, blocks))
        leave(2).start()
        leave(3).start()
        tail_load.stage(4)
        loads[0].stage(2)
        tail_load.stage(5)
        leave(1).start()
        project(weight_tail.reshape(d_model, tail_cols), tail, slice(0, tail_cols))
        leave(4).start()
        loads[0].stage(3)
        lax.fori_loop(0, seq_chunks // 2, shared, 0)
        loads[0].stage(4)
        loads[1].stage(2)
        lax.fori_loop(seq_chunks // 2, seq_chunks, shared, 0)

    scan_steps = GROUPS * seq_chunks
    events = {}
    for k in range(1, 3 * GROUPS):
        begin = max(0, (k - 2) * 3 * seq_chunks // 8)
        times = [begin, *[begin + 1 + delay * seq_chunks // 8 for delay in LOAD_STEPS]]
        if k == 1:
            times = [None, None, seq_chunks // 4, 5 * seq_chunks // 8]
        need = min(k * seq_chunks, scan_steps)
        for number, when in enumerate(times):
            if when is not None:
                events.setdefault(min(when, need), []).append((k, number + 1))
        if k < 2 * GROUPS:
            events.setdefault(need, []).append((k, 5))
    late = sorted(events.pop(scan_steps), key=lambda pair: (pair[1] + pair[0], pair[0]))
    for at, happen in sorted(events.items()):

        @pl.when(step == at)
        def _(happen=sorted(happen, key=lambda pair: (pair[0], pair[1]))):
            for k, number in happen:
                loads[k].stage(number)

    @pl.when(step == scan_steps)
    def _():
        leave(0).start()
        rest = list(late)
        flat_gate = wg.reshape(d_model, inner)
        for k in range(GROUPS):
            while True:
                one = rest.pop(0)
                loads[one[0]].stage(one[1])
                if one == (GROUPS + k, 5):
                    break
            cols = slice(k * cols_g, (k + 1) * cols_g)
            gates[:, cols] = mm(normed[...], flat_gate[:, cols])

        def gate_norm(i, carry):
            at = pl.ds(pl.multiple_of(i * 64, 64), 64)
            squares = jnp.zeros((64, LANES), F32)
            for c in range(inner // LANES):
                cols = slice(c * LANES, (c + 1) * LANES)
                gate = gates[at, cols]
                gated = ssd_all[at, cols] * (gate * sigmoid(gate))
                squares = squares + gated * gated
            inverse = lax.rsqrt(jnp.sum(squares, axis=1, keepdims=True) / inner + EPS)
            inverses[at, :] = jnp.broadcast_to(inverse, (64, LANES))
            return carry

        parts = 4
        blocks = length // 64
        share = -(-len(rest) // parts)
        for i in range(parts):
            for k, number in rest[i * share : (i + 1) * share]:
                loads[k].stage(number)
            lax.fori_loop(i * blocks // parts, (i + 1) * blocks // parts, gate_norm, 0)
        for k in range(2 * GROUPS, 3 * GROUPS):
            loads[k].stage(5)

    for i in range(4):

        @pl.when(step == (1 + i) * seq_chunks // 2 + 1)
        def _(i=i):
            if i < 3:
                exchange(i).wait()
                counts[i + 1] = counts[i] + countr[i]
            if i < 2:
                exchange(i + 1).start()
            elif i == 2:
                for k in range(1, levels):
                    spread(k).start()
                countz[spot.level] = counts[3]
            else:
                for k in range(1, levels):
                    spread(k).wait()
                total = countz[0]
                for k in range(1, levels):
                    total = total + countz[k]
                counts[4] = total

    for g in range(GROUPS):

        @pl.when(step == g * seq_chunks)
        def _(g=g):
            if g == 0:
                loads[0].stage(5)
            project(wx.reshape(d_model, inner), pbuf, slice(g * cols_g, (g + 1) * cols_g))

    @pl.when(step < scan_steps)
    def _():
        @pl.when(chunk == 0)
        def _():
            state[...] = jnp.zeros_like(state)

        aux = aux_ref[here, :]
        marks = marks_of(aux)
        ex[...] = mm(stacks[chunk], e_ref[:, pl.ds(gcol, cols_g)])
        head0 = group * per_group
        pick = (iota((LANES, LANES), 0) == iota((LANES, LANES), 1) + head0).astype(BF16)
        moved = [mm(v, pick) for v in split3(cums[chunk])]
        cum = moved[0] + moved[1] + moved[2]
        cum_t = cum.T
        start = pl.multiple_of(chunk * rows, rows)
        px_ref[...] = pbuf[pl.ds(start + 8, rows), :]
        for c in range(tiles):
            cols = slice(c * LANES, (c + 1) * LANES)
            act = conv(pbuf, start, cols, pl.ds(gcol + c * LANES, LANES), marks)
            xs[:, cols] = act
            scaled = act * ex[0:rows, cols]
            xdt[:, cols] = scaled.astype(BF16)
            xe[:, cols] = (scaled * ex[2 * rows : 3 * rows, cols]).astype(BF16)
        b, cc = bc[chunk, :, 0:n], bc[chunk, :, n:]
        state_low = state[...].astype(BF16)
        state_out_ref[...] = state_low
        yin[...] = mm(cc, state_low)
        state[...] = state[...] * ex[2 * rows - 1 : 2 * rows, :] + mm_tn(b, xe[...])
        score = scores[chunk]
        lane = iota((1, LANES), 1)
        masks = [(lane < width).astype(BF16), (lane >= width).astype(BF16)]
        for c in range(tiles):
            cols = slice(c * LANES, (c + 1) * LANES)
            mixing = []
            for h in (2 * c, 2 * c + 1):
                spread_h = jnp.minimum(cum[:, h : h + 1] - cum_t[h : h + 1, :], 0.0)
                mixing.append((score * jnp.exp(spread_h)).astype(BF16))
            x_low = xdt[:, cols]
            y = mm(
                jnp.concatenate(mixing, axis=1), jnp.concatenate([x_low * masks[0], x_low * masks[1]], axis=0)
            ) + ex[rows : 2 * rows, cols] * yin[:, cols]
            acols = pl.ds(gcol + c * LANES, LANES)
            ssd_ref[:, cols] = y
            ssd_all[here, acols] = y + skip_ref[:, acols] * xs[:, cols]

    @pl.when(step >= scan_steps)
    def _():
        turn = step - scan_steps
        block_rows = gms.shape[0]
        base = pl.multiple_of(turn * block_rows, block_rows)
        flat_gate = wg.reshape(d_model, inner)
        flat_out = wo.reshape(inner, d_model)
        sub = 64

        @pl.when(turn == 0)
        def _():
            dgain_ref[...] = jnp.zeros_like(dgain_ref)
            small_ref[...] = jnp.zeros_like(small_ref)

        def norm_of(i):
            at = pl.ds(pl.multiple_of(i * sub, sub), sub)
            return at, pl.ds(pl.multiple_of(base + i * sub, sub), sub)

        def forward_part(i, carry):
            at, full_at = norm_of(i)
            inverse = inverses[full_at, :]
            for c in range(inner // LANES):
                cols = slice(c * LANES, (c + 1) * LANES)
                gate = gates[full_at, cols]
                unit = ssd_all[full_at, cols] * (gate * sigmoid(gate)) * inverse
                mixed_ref[at, cols] = (unit * gain_ref[:, cols]).astype(BF16)
            return carry

        lax.fori_loop(0, block_rows // sub, forward_part, 0)
        results = gms.at[:, 0:d_model]
        results[...] = mm(mixed_ref[...], flat_out[...])
        scale = 2.0 * loss_weight / (counts[4, 0:1, :] * d_model)

        def loss_part(i, carry):
            at, full_at = norm_of(i)
            valid = jnp.broadcast_to(aux_ref[full_at, 9:10], (sub, LANES))
            squares = jnp.zeros((8, LANES), F32)
            for c in range(d_model // LANES):
                cols = slice(c * LANES, (c + 1) * LANES)
                result = tokens[full_at, cols].astype(F32) + results[at, cols]
                output_ref[at, cols] = result.astype(BF16)
                error = result - teacher_ref[at, cols].astype(F32)
                squares = squares + jnp.sum((valid * error * error).reshape(sub // 8, 8, LANES), axis=0)
                gb_ref[at, cols] = (valid * (cotan_ref[at, cols].astype(F32) + scale * error)).astype(BF16)
            small_ref[0:8, :] += squares
            return carry

        lax.fori_loop(0, block_rows // sub, loss_part, 0)
        small_ref[8:16, :] = counts[4]
        grads = gb_ref[...]
        for k in range(GROUPS):
            cols = slice(k * cols_g, (k + 1) * cols_g)
            gms[:, cols] = mm_nt(grads, flat_out[cols, :])

        def backward_part(i, carry):
            at, full_at = norm_of(i)
            cross = jnp.zeros((sub, LANES), F32)
            for c in range(inner // LANES):
                cols = slice(c * LANES, (c + 1) * LANES)
                cross = cross + gms[at, cols] * mixed_ref[at, cols].astype(F32)
            inverse = inverses[full_at, :]
            mean_cross = jnp.sum(cross, axis=1, keepdims=True) / inner
            for c in range(inner // LANES):
                cols = slice(c * LANES, (c + 1) * LANES)
                gate = gates[full_at, cols]
                sig = sigmoid(gate)
                silu = gate * sig
                ssd = ssd_all[full_at, cols]
                unit = ssd * silu * inverse
                grad_mixed = gms[at, cols]
                dgain_ref[:, cols] += jnp.sum((grad_mixed * unit).reshape(sub // 8, 8, LANES), axis=0)
                grad_gated = inverse * (grad_mixed * gain_ref[:, cols] - unit * mean_cross)
                dy_ref[at, cols] = (grad_gated * silu).astype(BF16)
                dz_ref[at, cols] = (
                    grad_gated * ssd * (sig + silu * (1.0 - sig))
                ).astype(BF16)
            return carry

        lax.fori_loop(0, block_rows // sub, backward_part, 0)
        gn_ref[...] = mm_nt(dz_ref[...], flat_gate[...])

        @pl.when(turn == length // block_rows - 1)
        def _():
            for k in range(len(leaves)):
                leave(k).wait()


def first(
    tokens, norm_gain, aux, seg_rows, count, conv_w, conv_b, bias, rate, skip_row, gain_row, e,
    cotangent, teacher, w_in, w_tail, w_out, levels, loss_weight,
):
    length, d = tokens.shape
    heads, inner = bias.shape[1], skip_row.shape[1]
    rows_f = w_in.shape[0]
    n = (conv_w.shape[1] - inner) // 2
    r = CHUNK
    chunks = length // r
    wide = inner // GROUPS
    tcols = w_tail.shape[1]
    units = 3 * GROUPS
    tall = 256
    scan_steps = GROUPS * chunks

    def scan_block(s):
        s = jnp.minimum(s, scan_steps - 1)
        return s % chunks, s // chunks

    block = lambda h: pl.BlockSpec((h, wide), scan_block)
    late = lambda w, deep=2: pl.BlockSpec(
        (tall, w), lambda s: (jnp.maximum(s - scan_steps, 0), 0), pipeline_mode=pl.Buffered(deep)
    )
    whole = lambda a: pl.BlockSpec(a.shape, lambda s: (0,) * a.ndim, pipeline_mode=pl.Buffered(1))
    fixed = lambda *dims: pl.BlockSpec(dims, lambda s: (0,) * len(dims))
    anywhere = pl.BlockSpec(memory_space=pl.ANY)
    vm = pltpu.VMEM
    shape = jax.ShapeDtypeStruct
    wide_shape = (levels, 2, 2, rows_f, inner)
    return pl.pallas_call(
        functools.partial(
            first_kernel, inner=inner, heads=heads, width=inner // heads, levels=levels, seq_chunks=chunks,
            loss_weight=loss_weight,
        ),
        grid=(scan_steps + length // tall,),
        in_specs=[
            late(d), late(d), anywhere,
            *[whole(a) for a in (norm_gain, aux, seg_rows, count, conv_w, conv_b, bias, rate, skip_row, gain_row, e)],
            anywhere, anywhere, anywhere,
        ],
        out_specs=[
            block(r), block(r), block(n), *[anywhere] * 5,
            late(d), late(d), late(inner), late(inner), late(inner), late(d), fixed(8, inner), fixed(16, LANES),
        ],
        out_shape=[
            shape((length, inner), F32), shape((length, inner), F32), shape((chunks * n, inner), BF16),
            shape((length, tcols), F32), shape((length, d), BF16), shape((d, length), BF16),
            shape(wide_shape, BF16), shape((levels, 2, 2, rows_f, tcols), BF16),
            shape((length, d), BF16), shape((length, d), BF16), shape((length, inner), BF16),
            shape((length, inner), BF16), shape((length, inner), BF16), shape((length, d), F32),
            shape((8, inner), F32), shape((16, LANES), F32),
        ],
        scratch_shapes=[
            vm((length, d), BF16), vm((length, d), BF16), vm((d, length), BF16),
            vm(wide_shape, BF16), vm(wide_shape, BF16), vm((levels, 2, 2, 2 * rows_f, d), BF16),
            vm((levels, 2, 2, rows_f, tcols), BF16),
            vm((length + 8, tcols), F32), vm((length + 8, wide), F32), vm((length, inner), F32),
            vm((length, inner), F32), vm((tall, inner), F32), vm((length, LANES), F32),
            vm((3 * r, wide), F32), vm((n, wide), F32), vm((r, wide), F32), vm((r, wide), BF16), vm((r, wide), BF16),
            vm((chunks, r, 2 * n), BF16), vm((r, wide), F32), vm((chunks, r, LANES), F32), vm((chunks, r, r), F32),
            vm((chunks, 3 * r, 2 * heads), BF16),
            vm((5, 8, LANES), F32), vm((3, 8, LANES), F32), vm((levels, 8, LANES), F32),
            pltpu.SemaphoreType.DMA((units + 1, 7 + 2 * levels)),
            pltpu.SemaphoreType.DMA((4 + 2 * levels,)),
            pltpu.SemaphoreType.DMA((1,)),
            pltpu.SemaphoreType.DMA((5,)),
        ],
        compiler_params=pltpu.CompilerParams(
            dimension_semantics=("arbitrary",), vmem_limit_bytes=60 * 2**20,
            collective_id=2, has_side_effects=True,
        ),
        name="scan_forward",
    )(
        cotangent, teacher, tokens, norm_gain, aux, seg_rows, count, conv_w, conv_b, bias, rate, skip_row, gain_row, e,
        w_in, w_tail, w_out,
    )


def on_device(
    tokens,
    norm_gain,
    in_weight,
    conv_weight,
    conv_bias,
    step_bias,
    decay_log,
    skip_gain,
    out_gain,
    out_weight,
    cotangent,
    teacher,
    segment,
    valid_mask,
):
    seqs, length, width = tokens.shape
    rows = seqs * length
    shards = lax.axis_size("fsdp")
    devices = lax.axis_size("rep") * shards
    levels = shards // 4
    loss_weight = float(rows * devices * width // 8)
    heads, inner = step_bias.shape[0], out_gain.shape[0]
    aux, seg_rows, count, bias, rate, rate_t, skip_row, conv_row, ngain_row, gain_row, e, in_tail = prepare(
        segment, valid_mask, step_bias, decay_log, skip_gain, conv_bias, norm_gain, out_gain, in_weight
    )
    params = (conv_weight, conv_row, bias, rate, skip_row)
    flat, cotan, target = (v.reshape(rows, width) for v in (tokens, cotangent, teacher))
    (
        px, y, states, tail, normed, normed_t, wx, wt, output, grad_branch, mixed, dy, dz, gn, dgain, sums
    ) = first(
        flat, ngain_row, aux, seg_rows, count, *params, gain_row, e, cotan, target,
        in_weight, in_tail, out_weight, levels, loss_weight,
    )
    wx, wt = (w.reshape(-1, w.shape[-1]) for w in (wx, wt))
    grad_out = mm_tn(mixed, grad_branch).astype(BF16)
    grad_gate = mm(normed_t, dz).astype(BF16)
    grad_in, grad_out, grad_tokens, small, norm_sum = back(
        px, 0, tail, y, dy, states, aux, seg_rows, *params, e, rate_t,
        ngain_row, dgain, sums[:8], normed_t, wx, wt, gn, flat, grad_branch,
        grad_gate.reshape(levels, 2, 2, width // shards, inner),
        grad_out.reshape(levels, 2, 2, inner // shards, width), in_weight.shape[1],
    )
    outs = finish(
        grad_in, grad_out, grad_tokens, output, small, norm_sum, sums, e, *conv_weight.shape, heads, inner
    )
    return (
        outs[0].reshape(tokens.shape), outs[1].reshape(()), outs[2].reshape(tokens.shape), *outs[3:]
    )


def solution(mesh):
    tokens = P(("rep", "fsdp"), None, None)
    marks = P(("rep", "fsdp"), None)
    shard = P("fsdp", None)
    return jax.shard_map(
        on_device,
        mesh=mesh,
        in_specs=(tokens, P(), shard, P(), P(), P(), P(), P(), P(), shard, tokens, tokens, marks, marks),
        out_specs=(tokens, P(), tokens, P(), shard, P(), P(), P(), P(), P(), P(), shard),
        check_vma=False,
    )
```

```python
import functools

import jax
import jax.numpy as jnp
from jax import lax
from jax.experimental import pallas as pl
from jax.experimental.pallas import tpu as pltpu
from jax.sharding import PartitionSpec as P

CHUNK = 128
LANES = 128
EPS = 1e-05
F32 = jnp.float32
BF16 = jnp.bfloat16
NT = (((1,), (1,)), ((), ()))
TN = (((0,), (0,)), ((), ()))


def mm(a, b):
    return jnp.dot(a, b, preferred_element_type=F32)


def mm_nt(a, b):
    return lax.dot_general(a, b, NT, preferred_element_type=F32)


def mm_tn(a, b):
    return lax.dot_general(a, b, TN, preferred_element_type=F32)


def split2(v):
    high = v.astype(BF16)
    return high, (v - high.astype(F32)).astype(BF16)


def split3(v):
    high = v.astype(BF16)
    rest = v - high.astype(F32)
    mid = rest.astype(BF16)
    return high, mid, (rest - mid.astype(F32)).astype(BF16)


def tri_sum(tri, v):
    heads = v.shape[1]
    parts = mm(tri, jnp.concatenate(split3(v), axis=1))
    return parts[:, :heads] + parts[:, heads : 2 * heads] + parts[:, 2 * heads :]


def sum_tri(v, tri):
    heads = v.shape[0]
    parts = mm(jnp.concatenate(split3(v), axis=0), tri)
    return parts[:heads] + parts[heads : 2 * heads] + parts[2 * heads :]


def sigmoid(v):
    return 0.5 * jnp.tanh(0.5 * v) + 0.5


def softplus(v):
    return jnp.maximum(v, 0.0) + jnp.log1p(jnp.exp(-jnp.abs(v)))


def iota(shape, dim):
    return lax.broadcasted_iota(jnp.int32, shape, dim)


def small_terms(step_raw, step_bias, decay_rate, keep, to_end, rows):
    shifted = step_raw + step_bias
    step = softplus(shifted)
    lower = (iota((rows, rows), 0) >= iota((rows, rows), 1)).astype(BF16)
    cum = tri_sum(lower, step * decay_rate)
    last = cum[rows - 1 : rows, :]
    return shifted, step, cum, jnp.exp(cum) * keep, jnp.exp(last - cum) * to_end


def expand(e_ref, out_ref, step, from_prev, to_end):
    stacked = jnp.concatenate(
        [jnp.concatenate(split2(v), axis=1) for v in (step, from_prev, to_end)], axis=0
    )
    out_ref[...] = mm(stacked, e_ref[...])


def full(shape):
    return pl.BlockSpec(shape, lambda i: (0,) * len(shape))


def prepare_kernel(
    segment_ref, valid_ref, bias_ref, log_ref, skip_ref, cb_ref, ngain_ref, gain_ref, weight_ref,
    aux_ref, rows_ref, count_ref, bias_out, rate_out, rate_t_out, skip_out, cb_out, ngain_out, gain_out, e_out, tail_out,
    *, tail_cols,
):
    length = segment_ref.shape[1]
    heads = bias_ref.shape[0]
    inner = gain_ref.shape[0]
    width = inner // heads
    docs = segment_ref[...].astype(F32)
    valid = valid_ref[...].astype(F32)
    place = iota((8, length), 1)
    wide = jnp.broadcast_to(docs, (8, length))
    marks = []
    for k in (1, 2, 3):
        marks.append(jnp.where((wide == pltpu.roll(wide, k, 1)) & (place >= k), 1.0, 0.0)[0:1])
    for k in (1, 2, 3):
        marks.append(jnp.where((wide == pltpu.roll(wide, length - k, 1)) & (place < length - k), 1.0, 0.0)[0:1])
    for c in range(length // CHUNK):
        cols = slice(c * CHUNK, (c + 1) * CHUNK)
        own = docs[:, cols]
        last = docs[:, (c + 1) * CHUNK - 1 : (c + 1) * CHUNK]
        keep = jnp.zeros_like(own)
        if c:
            keep = jnp.where(own == docs[:, c * CHUNK - 1 : c * CHUNK], 1.0, 0.0)
        stacked = [own, *[v[:, cols] for v in marks], keep, jnp.where(own == last, 1.0, 0.0), valid[:, cols]]
        stacked.append(jnp.zeros((LANES - len(stacked), CHUNK), F32))
        aux_ref[cols, :] = jnp.concatenate(stacked, axis=0).T[:, 0:16]
        rows_ref[c] = own
    count_ref[...] = jnp.broadcast_to(jnp.sum(valid, axis=1, keepdims=True), count_ref.shape)
    bias_out[...] = bias_ref[...].reshape(1, heads)
    rate = -jnp.exp(log_ref[...].reshape(1, heads))
    rate_out[...] = rate
    spare = jnp.concatenate([rate, jnp.zeros((1, LANES - heads), F32)], axis=1)
    rate_t_out[...] = jnp.broadcast_to(spare, (LANES, LANES)).T[0:heads, 0:1]
    e = (iota((2 * heads, inner), 0) % heads == iota((2 * heads, inner), 1) // width).astype(BF16)
    e_out[...] = e
    skip = jnp.broadcast_to(skip_ref[...].reshape(1, heads), (16, heads))
    parts = [mm(v, e[0:heads]) for v in split3(skip)]
    skip_out[...] = (parts[0] + parts[1] + parts[2])[0:1]
    cb_out[...] = cb_ref[...].reshape(1, cb_ref.shape[0])
    ngain_out[...] = ngain_ref[...].reshape(1, ngain_ref.shape[0])
    gain_out[...] = gain_ref[...].reshape(1, inner)
    rows_f = weight_ref.shape[0]
    tail_out[...] = jnp.concatenate(
        [weight_ref[:, 0:tail_cols], jnp.zeros((rows_f, tail_out.shape[1] - tail_cols), BF16)], axis=1
    )


def prepare(segment, valid_mask, step_bias, decay_log, skip_gain, conv_bias, norm_gain, out_gain, in_weight):
    length = segment.shape[1]
    heads, inner = step_bias.shape[0], out_gain.shape[0]
    rows_f, proj = in_weight.shape
    tail_cols = proj - 2 * inner
    tail_wide = -(-tail_cols // LANES) * LANES
    shape = jax.ShapeDtypeStruct
    small = (segment, valid_mask, step_bias, decay_log, skip_gain, conv_bias, norm_gain, out_gain)
    outs = [
        shape((length, 16), F32), shape((length // CHUNK, 1, CHUNK), F32), shape((8, LANES), F32),
        shape((1, heads), F32), shape((1, heads), F32), shape((heads, 1), F32), shape((1, inner), F32),
        shape((1, conv_bias.shape[0]), F32), shape((1, norm_gain.shape[0]), F32), shape((1, inner), F32),
        shape((2 * heads, inner), BF16), shape((rows_f, tail_wide), BF16),
    ]
    block = 512
    return pl.pallas_call(
        functools.partial(prepare_kernel, tail_cols=tail_cols),
        grid=(1,),
        in_specs=[*[full(a.shape) for a in small], pl.BlockSpec((rows_f, block), lambda i: (0, 2 * inner // block))],
        out_specs=[full(o.shape) for o in outs],
        out_shape=outs,
        name="prepare",
    )(*small, in_weight)


def finish_kernel(
    gi_ref, go_ref, gt_ref, output_ref, small_ref, dng_ref, sums_ref, e_ref,
    out_final, loss_ref, gt_final, ngain_ref, gi_final, cw_ref, cb_ref, bias_ref, log_ref, skip_ref, gain_ref, go_final,
    gi, go, gt, output, sems,
):
    trios = ((gt_ref, gt, gt_final), (output_ref, output, out_final), (gi_ref, gi, gi_final), (go_ref, go, go_final))
    fetches = [pltpu.make_async_copy(a, b, sems.at[i]) for i, (a, b, c) in enumerate(trios)]
    stores = [pltpu.make_async_copy(b, c, sems.at[4 + i]) for i, (a, b, c) in enumerate(trios)]
    for copy in fetches:
        copy.start()
    for fetched, stored in zip(fetches, stores):
        fetched.wait()
        stored.start()
    taps, conv_width = cw_ref.shape
    heads, inner = bias_ref.shape[0], gain_ref.shape[0]
    d = dng_ref.shape[0] * LANES
    cw_ref[...] = small_ref[0:taps, 0:conv_width]
    cb_ref[...] = small_ref[taps : taps + 1, 0:conv_width].reshape(conv_width)
    gain_ref[...] = small_ref[5:6, 0:inner].reshape(inner)
    bias_ref[...] = small_ref[7:8, 0:heads].reshape(heads)
    log_ref[...] = small_ref[7:8, LANES : LANES + heads].reshape(heads)
    squares = jnp.sum(small_ref[7:8, 2 * LANES : 3 * LANES], axis=1, keepdims=True)
    loss_ref[...] = squares / (sums_ref[8:9, 0:1] * d)
    by_head = jnp.zeros((16, 2 * heads), F32)
    for v in split3(jnp.broadcast_to(small_ref[6:7, 0:inner], (16, inner))):
        by_head = by_head + mm_nt(v, e_ref[...])
    skip_ref[...] = by_head[0:1, 0:heads].reshape(heads)
    ngain_ref[...] = dng_ref[...].reshape(d)
    for copy in stores:
        copy.wait()


def finish(gi, go, gt, output, small, dng, sums, e, taps, conv_width, heads, inner):
    shape = jax.ShapeDtypeStruct
    anywhere = pl.BlockSpec(memory_space=pl.ANY)
    outs = [
        shape(output.shape, BF16), shape((1, 1), F32), shape(gt.shape, BF16), shape((dng.size,), F32),
        shape(gi.shape, F32), shape((taps, conv_width), F32), shape((conv_width,), F32), shape((heads,), F32),
        shape((heads,), F32), shape((heads,), F32), shape((inner,), F32), shape(go.shape, F32),
    ]
    far = (0, 2, 4, 11)
    return pl.pallas_call(
        finish_kernel,
        grid=(1,),
        in_specs=[*[anywhere] * 4, *[full(a.shape) for a in (small, dng, sums, e)]],
        out_specs=[anywhere if i in far else full(o.shape) for i, o in enumerate(outs)],
        out_shape=outs,
        scratch_shapes=[
            *[pltpu.VMEM(a.shape, a.dtype) for a in (gi, go, gt, output)], pltpu.SemaphoreType.DMA((8,)),
        ],
        compiler_params=pltpu.CompilerParams(vmem_limit_bytes=60 * 2**20),
        name="finish",
    )(gi, go, gt, output, small, dng, sums, e)


MESH = pl.DeviceIdType.MESH


class Spot:
    def __init__(self, levels):
        self.rep, self.at = lax.axis_index("rep"), lax.axis_index("fsdp")
        self.core, self.side, self.level = self.at % 2, (self.at // 2) % 2, self.at // 4
        self.levels = levels
        self.sibling = (self.rep, self.at + 1 - 2 * self.core)
        self.across = (self.rep, self.at + 2 - 4 * self.side)
        self.twin = (1 - self.rep, self.at)

    def far(self, step):
        return (self.rep, ((self.level + step) % self.levels) * 4 + self.at % 4)

    def corner(self, j):
        flip = lambda v, bit: 1 - v if j & bit else v
        return (flip(self.rep, 4), self.level * 4 + flip(self.side, 2) * 2 + flip(self.core, 1))

    def greet(self, corners=False):
        barrier = pltpu.get_barrier_semaphore()
        near = [self.corner(j) for j in range(1, 8)] if corners else [self.sibling, self.across, self.twin]
        partners = near + [self.far(d) for d in range(1, self.levels)]
        for one in partners:
            pl.semaphore_signal(barrier, inc=1, device_id=one, device_id_type=MESH)
        pl.semaphore_wait(barrier, len(partners))


def send(src, dst, send_sem, recv_sem, device):
    return pltpu.make_async_remote_copy(
        src_ref=src, dst_ref=dst, send_sem=send_sem, recv_sem=recv_sem, device_id=device, device_id_type=MESH
    )


class Split:
    def __init__(self, spot, whole, own, from_core, half, from_side, from_level, mine, from_twin, sems, write):
        self.spot, self.whole, self.own, self.write = spot, whole, own, write
        self.from_core, self.half, self.from_side, self.from_level = from_core, half, from_side, from_level
        self.mine, self.from_twin, self.sems = mine, from_twin, sems
        self.cols = half.shape[-1]

    def columns(self, rep):
        return pl.ds(pl.multiple_of(rep * self.cols, self.cols), self.cols)

    @property
    def c0(self):
        return pltpu.make_async_copy(self.whole.at[:, :, self.spot.core], self.own, self.sems.at[6])

    @property
    def c1(self):
        spot, sems = self.spot, self.sems
        return send(self.whole.at[:, :, 1 - spot.core], self.from_core, sems.at[0], sems.at[1], spot.sibling)

    @property
    def c2(self):
        spot, sems = self.spot, self.sems
        block = self.own.at[:, :, :, self.columns(1 - spot.rep)]
        return send(block, self.half, sems.at[2], sems.at[3], spot.twin)

    @property
    def c3(self):
        spot, sems = self.spot, self.sems
        last = 5 + 2 * spot.levels
        return send(self.half.at[:, 1 - spot.side], self.from_side, sems.at[last], sems.at[last + 1], spot.across)

    @property
    def c4(self):
        spot, sems = self.spot, self.sems
        return [
            send(
                self.from_side.at[(spot.level + d) % spot.levels], self.from_level.at[d - 1],
                sems.at[5 + 2 * d], sems.at[6 + 2 * d], spot.far(d),
            )
            for d in range(1, spot.levels)
        ]

    @property
    def c5(self):
        spot, sems = self.spot, self.sems
        return send(self.mine, self.from_twin, sems.at[4], sems.at[5], spot.twin)

    def stage(self, number):
        spot, levels = self.spot, self.spot.levels
        if number == 1:
            self.c1.start()
            self.c0.start()
        elif number == 2:
            self.c0.wait()
            self.c1.wait()

            def add(i, carry):
                for side in range(2):
                    self.own[i, side] = self.own[i, side] + self.from_core[i, side]
                return carry

            lax.fori_loop(0, levels, add, 0)
            self.c2.start()
        elif number == 3:
            self.c2.wait()
            columns = self.columns(spot.rep)

            def add(i, carry):
                for side in range(2):
                    self.half[i, side] = self.half[i, side] + self.own[i, side, :, columns]
                return carry

            lax.fori_loop(0, levels, add, 0)
            self.c3.start()
        elif number == 4:
            self.c3.wait()

            def add(i, carry):
                self.from_side[i] = self.from_side[i] + self.half[i, spot.side]
                return carry

            lax.fori_loop(0, levels, add, 0)
            for copy in self.c4:
                copy.start()
        elif number == 5:
            for copy in self.c4:
                copy.wait()
            total = self.from_side[spot.level].astype(F32)
            for d in range(levels - 1):
                total = total + self.from_level[d].astype(F32)
            self.mine[...] = total.astype(BF16)
            self.c5.start()
        else:
            self.c5.wait()
            self.write(self.mine[...].astype(F32), self.columns(spot.rep))
            self.write(self.from_twin[...].astype(F32), self.columns(1 - spot.rep))


class Unit:
    def __init__(self, spot, whole, own, from_core, from_side, from_level, mine, from_twin, sems, write):
        self.spot, self.whole, self.own, self.write = spot, whole, own, write
        self.from_core, self.from_side, self.from_level = from_core, from_side, from_level
        self.mine, self.from_twin = mine, from_twin
        self.sems = sems

    @property
    def c0(self):
        return pltpu.make_async_copy(self.whole.at[:, :, self.spot.core], self.own, self.sems.at[6])

    @property
    def c1(self):
        spot, sems = self.spot, self.sems
        return send(self.whole.at[:, :, 1 - spot.core], self.from_core, sems.at[0], sems.at[1], spot.sibling)

    @property
    def c2(self):
        spot, sems = self.spot, self.sems
        return send(self.own.at[:, 1 - spot.side], self.from_side, sems.at[2], sems.at[3], spot.across)

    @property
    def c3(self):
        spot, sems = self.spot, self.sems
        return [
            send(
                self.from_side.at[(spot.level + d) % spot.levels], self.from_level.at[d - 1],
                sems.at[5 + 2 * d], sems.at[6 + 2 * d], spot.far(d),
            )
            for d in range(1, spot.levels)
        ]

    @property
    def c4(self):
        spot, sems = self.spot, self.sems
        return send(self.mine, self.from_twin, sems.at[4], sems.at[5], spot.twin)

    def stage(self, number):
        spot, levels = self.spot, self.spot.levels
        if number == 1:
            self.c1.start()
            self.c0.start()
        elif number == 2:
            self.c0.wait()
            self.c1.wait()

            def add(i, carry):
                for side in range(2):
                    self.own[i, side] = self.own[i, side] + self.from_core[i, side]
                return carry

            lax.fori_loop(0, levels, add, 0)
            self.c2.start()
        elif number == 3:
            self.c2.wait()

            def add(i, carry):
                self.from_side[i] = self.from_side[i] + self.own[i, spot.side]
                return carry

            lax.fori_loop(0, levels, add, 0)
            for copy in self.c3:
                copy.start()
        elif number == 4:
            for copy in self.c3:
                copy.wait()
            total = self.from_side[spot.level].astype(F32)
            for d in range(levels - 1):
                total = total + self.from_level[d].astype(F32)
            self.mine[...] = total.astype(BF16)
            self.c4.start()
        else:
            self.c4.wait()
            self.write(self.mine[...].astype(F32) + self.from_twin[...].astype(F32))


GROUPS = 4
STARTS = (0, 2, 4, 6, 8, 11, 13, 16, 18, 20, 24)
UNIT_DELAYS = (0, 2, 6, 10, 12)
SPLIT_DELAYS = (0, 2, 6, 9, 12, 14)


def back_kernel(
    px_ref, prev_ref, y_ref, dy_ref, state_ref,
    tail_ref, aux_ref, seg_ref, cw_ref, cb_ref, bias_ref, rate_ref, skip_ref, e_ref, rate_t_ref,
    ngain_ref, dgain_ref, square_ref,
    normed_t_hbm, wx_hbm, wt_hbm, gn_hbm, tokens_hbm, gb_hbm, ggate_hbm, gout_hbm,
    gi_ref, go_ref, gt_ref, small_ref, dng_ref,
    xbuf, ex, adj, xs, xdt, xe, bc, slope, dye, dxi, dbuf, r1, r1l, r2, r3,
    tbuf, consts, stacks, raws, cums, cum_ts, ones, steps, scores, dscores, gbs, gcs, sums, tslope, gp, gpt, accum, taccum,
    normed_t, wx, wt, gn, tokens, gb,
    own, part, part_t, own_t, from_core, from_core_t, from_side, from_side_t, from_level, from_level_t,
    mine, mine_t, twin, twin_t, half, half_side, half_level, half_mine, half_twin, local, sm, smr, smz, gain_out, gain_near, gain_sum, gain_far, sems, small_sems, gain_sems, load_sems,
    *, inner, heads, width, levels, seq_chunks,
):
    group, turn = pl.program_id(0), pl.program_id(1)
    step = group * seq_chunks + turn
    chunk = seq_chunks - 1 - turn
    rows, cols_g = px_ref.shape
    n = bc.shape[2] // 2
    tiles = cols_g // LANES
    per_group = cols_g // width
    taps = cw_ref.shape[0]
    tail_cols = tail_ref.shape[1]
    conv_tail = 2 * n
    here = pl.ds(pl.multiple_of(chunk * rows, rows), rows)
    spot = Spot(levels)
    gcol = pl.multiple_of(group * cols_g, cols_g)
    rows_f = mine.shape[1]

    def loads():
        pairs = ((normed_t_hbm, normed_t), (wx_hbm, wx), (wt_hbm, wt), (gn_hbm, gn), (tokens_hbm, tokens), (gb_hbm, gb))
        return [pltpu.make_async_copy(a, b, load_sems.at[i]) for i, (a, b) in enumerate(pairs)]

    def writer(ref, row, col, wide):
        def write(v, columns=None):
            if columns is None:
                ref[row : row + rows_f, col : col + wide] = v[:, :wide]
            else:
                at = pl.multiple_of(col + columns.start, LANES)
                ref[row : row + rows_f, pl.ds(at, columns.size)] = v
        return write

    sources = []
    for u in range(GROUPS):
        hbm = gout_hbm.at[:, :, :, pl.ds((u // 2) * rows_f, rows_f), pl.ds((u % 2) * cols_g, cols_g)]
        sources.append((hbm, writer(go_ref, (u // 2) * rows_f, (u % 2) * cols_g, cols_g)))
    for u in range(GROUPS):
        hbm = ggate_hbm.at[:, :, :, :, pl.ds(u * cols_g, cols_g)]
        sources.append((hbm, writer(gi_ref, 0, u * cols_g, cols_g)))
    for g in range(GROUPS):
        sources.append((part.at[g % 2], writer(gi_ref, 0, inner + g * cols_g, cols_g)))
    order = [0, 1, 2, 3, 8, 4, 5, 9, 6, 7, 10, 11]
    units = []
    for i, u in enumerate(order):
        k = i // 2
        whole, write = sources[u]
        if i % 2:
            units.append(
                Split(
                    spot, whole, own.at[u], from_core.at[u], half.at[k], half_side.at[k], half_level.at[k],
                    half_mine.at[k], half_twin.at[k], sems.at[u], write,
                )
            )
        else:
            units.append(
                Unit(
                    spot, whole, own.at[u], from_core.at[u], from_side.at[k], from_level.at[k], mine.at[k], twin.at[k],
                    sems.at[u], write,
                )
            )
    tail_wide = gi_ref.shape[1] - 2 * inner
    tail_unit = Unit(
        spot, part_t, own_t, from_core_t, from_side_t, from_level_t, mine_t, twin_t, sems.at[3 * GROUPS],
        writer(gi_ref, 0, 2 * inner, tail_wide),
    )

    events = {}
    last_step = GROUPS * seq_chunks - 1
    late = []
    for i, (begin, unit) in enumerate(zip(STARTS, units)):
        begin = begin * seq_chunks // 8
        for number, delay in enumerate(SPLIT_DELAYS if i % 2 else UNIT_DELAYS):
            events.setdefault(min(begin + delay, last_step), []).append((unit, number + 1))

    @pl.when(step == 0)
    def _():
        for copy in loads():
            copy.start()
        spot.greet(corners=True)
        accum[...] = jnp.zeros_like(accum)
        taccum[...] = jnp.zeros_like(taccum)
        steps[...] = jnp.zeros_like(steps)
        ones[...] = (iota(ones.shape, 0) == iota(ones.shape, 1) // width).astype(BF16)

    for at, happen in sorted(events.items()):
        if at == last_step:
            late += happen
            continue

        @pl.when(step == at)
        def _(happen=happen):
            for unit, number in sorted(happen, key=lambda pair: -pair[1]):
                unit.stage(number)

    def fold(v):
        return jnp.sum(v.reshape(v.shape[0] // 8, 8, v.shape[1]), axis=0)

    aux = aux_ref[here, :]
    marks = [None] + [jnp.broadcast_to(aux[:, k : k + 1], (rows, LANES)) for k in range(1, taps)]
    marks_next = [None] + [jnp.broadcast_to(aux[:, 3 + k : 4 + k], (rows, LANES)) for k in range(1, taps)]
    lower = iota((rows, rows), 0) >= iota((rows, rows), 1)
    upper = iota((rows, rows), 0) <= iota((rows, rows), 1)
    rate = rate_ref[...]

    def conv_pre(buffer, cols, wcols):
        pre = cb_ref[:, wcols] + cw_ref[0:1, wcols] * buffer[8 : 8 + rows, cols]
        for k in range(1, taps):
            pre = pre + (cw_ref[k : k + 1, wcols] * buffer[8 - k : 8 - k + rows, cols]) * marks[k]
        return pre

    def conv_back(buffer, cols, wcols, acc, acc_cols):
        outs = []
        adds = [jnp.zeros((8, LANES), F32) for _ in range(taps + 1)]
        for at in range(0, rows, 64):
            inputs = xbuf[8 + at : 72 + at, cols]
            for k in range(taps):
                grad = buffer[at + k : at + k + 64, cols]
                if k == 0:
                    out = cw_ref[0:1, wcols] * grad
                    adds[taps] = adds[taps] + fold(grad)
                else:
                    grad = grad * marks_next[k][at : at + 64]
                    out = out + cw_ref[k : k + 1, wcols] * grad
                adds[k] = adds[k] + fold(grad * inputs)
            outs.append(out)
        for k in range(taps + 1):
            acc[8 * k : 8 * k + 8, acc_cols] += adds[k]
        return jnp.concatenate(outs, axis=0)

    def fill_tail():
        xbuf[8 : 8 + rows, 0:conv_tail] = tail_ref[here, 0:conv_tail]
        before = pl.ds(pl.multiple_of(jnp.maximum(chunk * rows - 8, 0), 8), 8)
        xbuf[0:8, 0:conv_tail] = tail_ref[before, 0:conv_tail]

    @pl.when(group == 0)
    def _():
        shifted, step_size, cum, from_prev, to_end = small_terms(
            tail_ref[here, conv_tail : conv_tail + heads], bias_ref[...], rate, aux[:, 7:8], aux[:, 8:9], rows
        )
        turned = jnp.concatenate([shifted, step_size, cum, jnp.zeros((rows, LANES - 3 * heads), F32)], axis=1).T
        raws[chunk] = turned[0 : 2 * heads]
        cum_ts[chunk] = turned[2 * heads : 3 * heads]
        for g in range(GROUPS):
            cums[g, here, 0:per_group] = cum[:, g * per_group : (g + 1) * per_group]
        stacks[chunk] = jnp.concatenate(
            [jnp.concatenate(split2(v), axis=1) for v in (step_size, from_prev, to_end)], axis=0
        )
        fill_tail()
        for c in range(conv_tail // LANES):
            cols = slice(c * LANES, (c + 1) * LANES)
            pre = conv_pre(xbuf, cols, slice(inner + c * LANES, inner + (c + 1) * LANES))
            sig = sigmoid(pre)
            act = pre * sig
            tslope[here, cols] = sig + act * (1.0 - sig)
            bc[chunk, :, cols] = act.astype(BF16)
        same = upper & (aux[:, 0:1] == seg_ref[chunk])
        scores[chunk] = jnp.where(same, mm_nt(bc[chunk, :, 0:n], bc[chunk, :, n:]), 0.0)
        dscores[chunk] = jnp.zeros((rows, rows), F32)
        gbs[here, :] = jnp.zeros((rows, n), F32)
        gcs[here, :] = jnp.zeros((rows, n), F32)

    @pl.when(turn == 0)
    def _():
        adj[...] = jnp.zeros_like(adj)
        dbuf[rows : rows + 8, :] = jnp.zeros((8, cols_g), F32)

    ex[...] = mm(stacks[chunk], e_ref[:, pl.ds(gcol, cols_g)])
    own_heads = pl.ds(pl.multiple_of(group * per_group, per_group), per_group)
    cum = cums[group, here, :]
    cum_t = cum_ts[chunk, own_heads, :]
    xbuf[0:8, :] = prev_ref[...]
    xbuf[8 : 8 + rows, :] = px_ref[...]
    for c in range(tiles):
        cols = slice(c * LANES, (c + 1) * LANES)
        wcols = pl.ds(gcol + c * LANES, LANES)
        for at in range(0, rows, 64):
            part_rows = slice(at, at + 64)
            pre = cb_ref[:, wcols] + cw_ref[0:1, wcols] * xbuf[8 + at : 72 + at, cols]
            for k in range(1, taps):
                shifted = xbuf[8 + at - k : 72 + at - k, cols]
                pre = pre + (cw_ref[k : k + 1, wcols] * shifted) * marks[k][part_rows]
            sig = sigmoid(pre)
            act = pre * sig
            slope[part_rows, cols] = sig + act * (1.0 - sig)
            xs[part_rows, cols] = act
            scaled = act * ex[part_rows, cols]
            xdt[part_rows, cols] = scaled.astype(BF16)
            xe[part_rows, cols] = (scaled * ex[2 * rows + at : 2 * rows + at + 64, cols]).astype(BF16)
            dye[part_rows, cols] = (
                dy_ref[part_rows, cols].astype(F32) * ex[rows + at : rows + at + 64, cols]
            ).astype(BF16)
    b, cc = bc[chunk, :, 0:n], bc[chunk, :, n:]
    state_low = state_ref[...]
    adj_low = adj[...].astype(BF16)
    carry = ex[2 * rows - 1 : 2 * rows, :]
    gcs[here, :] += mm_nt(dye[...], state_low)
    gbs[here, :] += mm_nt(xe[...], adj_low)
    dxi[...] = mm(b, adj_low)
    through = jnp.sum(adj[...] * state_low.astype(F32), axis=0, keepdims=True) * carry
    adj[...] = adj[...] * carry + mm_tn(cc, dye[...])
    scores_t = scores[chunk]
    lane = iota((1, LANES), 1)
    masks = [(lane < width).astype(BF16), (lane >= width).astype(BF16)]
    grad_scores_t = jnp.zeros((rows, rows), F32)
    for c in range(tiles):
        cols = slice(c * LANES, (c + 1) * LANES)
        acols = pl.ds(gcol + c * LANES, LANES)
        x_low, dy_low = xdt[:, cols], dy_ref[:, cols]
        grad_mix = mm_nt(jnp.concatenate([x_low * masks[0], x_low * masks[1]], axis=0), dy_low)
        mixing = []
        for i, h in enumerate((2 * c, 2 * c + 1)):
            decay = jnp.exp(jnp.minimum(cum_t[h : h + 1, :] - cum[:, h : h + 1], 0.0))
            mixing.append((scores_t * decay).astype(BF16))
            grad_scores_t = grad_scores_t + grad_mix[i * rows : (i + 1) * rows] * decay
        within = mm(
            jnp.concatenate(mixing, axis=1), jnp.concatenate([dy_low * masks[0], dy_low * masks[1]], axis=0)
        )
        x = xs[:, cols]
        skip = skip_ref[:, acols]
        across = ex[2 * rows : 3 * rows, cols] * dxi[:, cols]
        both = within + across
        grad_ssd = dy_low.astype(F32)
        x_scaled = x_low.astype(F32)
        r1[:, cols], r1l[:, cols] = split2(grad_ssd * y_ref[:, cols] - within * x_scaled)
        r2[:, cols] = (across * x_scaled).astype(BF16)
        r3[:, cols] = (both * x).astype(BF16)
        accum[8 * taps + 8 : 8 * taps + 16, acols] += fold(grad_ssd * x)
        grad_x = skip * grad_ssd + ex[0:rows, cols] * both
        dbuf[0:rows, cols] = grad_x * slope[:, cols]
    dscores[chunk] += grad_scores_t
    by_head = ones[...]
    sums[0, chunk, own_heads, :] = (mm_nt(by_head, r1[...]) + mm_nt(by_head, r1l[...]))[0:per_group]
    sums[1, chunk, own_heads, :] = mm_nt(by_head, r2[...])[0:per_group]
    sums[2, chunk, own_heads, :] = mm_nt(by_head, r3[...])[0:per_group]
    high, rest = split2(jnp.broadcast_to(through, (16, cols_g)))
    const = (mm_nt(by_head, high) + mm_nt(by_head, rest))[0:per_group, 0:1]
    consts[chunk, own_heads, :] = jnp.broadcast_to(const, (per_group, LANES))
    for c in range(tiles):
        cols = slice(c * LANES, (c + 1) * LANES)
        acols = pl.ds(gcol + c * LANES, LANES)
        gp[here, cols] = conv_back(dbuf, cols, acols, accum, acols).astype(BF16)
    dbuf[rows : rows + 8, :] = dbuf[0:8, :]

    @pl.when(group == GROUPS - 1)
    def _():
        same = upper & (aux[:, 0:1] == seg_ref[chunk])
        grad_scores = jnp.where(same, dscores[chunk], 0.0).astype(BF16)
        grad_b = gbs[here, :] + mm(grad_scores, cc)
        grad_c = gcs[here, :] + mm_tn(grad_scores, b)
        fill_tail()

        @pl.when(turn == 0)
        def _():
            tbuf[rows : rows + 8, :] = jnp.zeros((8, 2 * n), F32)

        tbuf[0:rows, 0:n] = grad_b * tslope[here, 0:n]
        tbuf[0:rows, n : 2 * n] = grad_c * tslope[here, n : 2 * n]
        for c in range(conv_tail // LANES):
            cols = slice(c * LANES, (c + 1) * LANES)
            gpt[here, cols] = conv_back(
                tbuf, cols, slice(inner + c * LANES, inner + (c + 1) * LANES), taccum, cols
            ).astype(BF16)
        tbuf[rows : rows + 8, :] = tbuf[0:8, :]
        shifted, step_size = raws[chunk, 0:heads, :], raws[chunk, heads : 2 * heads, :]
        turned_aux = jnp.concatenate([aux, jnp.zeros((rows, LANES - aux.shape[1]), F32)], axis=1).T
        grad_log = (
            sum_tri(sums[0, chunk], lower.astype(BF16))
            + sum_tri(sums[1, chunk], (iota((rows, rows), 0) < iota((rows, rows), 1)).astype(BF16))
            + consts[chunk]
        ) * turned_aux[1:2, :]
        rate_t = jnp.broadcast_to(rate_t_ref[...], (heads, rows))
        grad_raw = (sums[2, chunk] + rate_t * grad_log) * sigmoid(shifted)
        gpt[here, conv_tail:] = (
            jnp.concatenate([grad_raw, jnp.zeros((tail_cols - conv_tail - heads, rows), F32)], axis=0).T
        ).astype(BF16)
        steps[0] += grad_raw
        steps[1] += step_size * grad_log * rate_t

    def weight_grad(low, out):
        flat = out.reshape(normed_t.shape[0], low.shape[1])
        for k in range(0, low.shape[1], 256):
            cols = slice(k, min(k + 256, low.shape[1]))
            flat[:, cols] = mm(normed_t[...], low[:, cols]).astype(BF16)

    def input_grad(low, weights):
        for k in range(gn.shape[1] // 256):
            cols = slice(k * 256, (k + 1) * 256)
            gn[:, cols] += mm_nt(low[...], weights[cols, :])

    for g in range(GROUPS - 1):

        @pl.when(step == (g + 1) * seq_chunks - 1)
        def _(g=g):
            if g == 0:
                for copy in loads():
                    copy.wait()
            weight_grad(gp, part.at[g % 2])
            input_grad(gp, wx.at[:, g * cols_g : (g + 1) * cols_g])

    @pl.when(step == last_step)
    def _():
        d = gn.shape[1]
        half_cols = sm.shape[2]

        def half_of(core):
            return pl.ds(pl.multiple_of(core * half_cols, half_cols), half_cols)

        def exchange(i):
            src = (local.at[:, half_of(1 - spot.core)], sm.at[0], sm.at[1], sm.at[3])[i]
            device = (spot.sibling, spot.across, spot.twin, spot.sibling)[i]
            return send(src, smr.at[i], small_sems.at[2 * i], small_sems.at[2 * i + 1], device)

        spread = lambda k: send(
            sm.at[2], smz.at[spot.level], small_sems.at[6 + 2 * k], small_sems.at[7 + 2 * k], spot.far(k)
        )

        def one_row(v):
            return jnp.sum(v, axis=0, keepdims=True)

        def fold_small(i):
            exchange(i).wait()
            sm[i] = (local[:, half_of(spot.core)] if i == 0 else sm[i - 1]) + smr[i]

        local[...] = jnp.zeros(local.shape, F32)
        for k in range(taps + 1):
            local[k : k + 1, 0:inner] = one_row(accum[8 * k : 8 * k + 8, :])
            local[k : k + 1, inner : inner + conv_tail] = one_row(taccum[8 * k : 8 * k + 8, 0:conv_tail])
        local[5:6, 0:inner] = one_row(dgain_ref[...])
        local[6:7, 0:inner] = one_row(accum[8 * taps + 8 : 8 * taps + 16, :])
        for i in range(2):
            turned = jnp.concatenate([steps[i], jnp.zeros((LANES - heads, LANES), F32)], axis=0).T
            local[7:8, i * LANES : (i + 1) * LANES] = one_row(turned)
        local[7:8, 2 * LANES : 3 * LANES] = one_row(square_ref[...])
        exchange(0).start()
        for unit, number in sorted(late, key=lambda pair: pair[1]):
            unit.stage(number)
        last = units[-1]
        weight_grad(gpt, part_t)
        tail_unit.stage(1)
        fold_small(0)
        exchange(1).start()
        weight_grad(gp, part.at[(GROUPS - 1) % 2])
        last.stage(1)
        tail_unit.stage(2)
        fold_small(1)
        exchange(2).start()
        input_grad(gpt, wt)
        last.stage(2)
        fold_small(2)
        for k in range(1, levels):
            spread(k).start()
        smz[spot.level] = sm[2]
        input_grad(gp, wx.at[:, (GROUPS - 1) * cols_g : GROUPS * cols_g])
        tail_unit.stage(3)
        ngain = ngain_ref[...]

        def block_norm(i, total):
            block = pl.ds(pl.multiple_of(i * 64, 64), 64)
            v = tokens[block, :].astype(F32)
            rinv = lax.rsqrt(jnp.sum(v * v, axis=1, keepdims=True) / d + EPS)
            scaled = v * rinv
            grad = gn[block, :]
            total = total + jnp.sum((grad * scaled).reshape(8, 8, d), axis=0)
            grad = grad * ngain
            mean = jnp.sum(grad * scaled, axis=1, keepdims=True) / d
            gb[block, :] = (gb[block, :].astype(F32) + rinv * (grad - scaled * mean)).astype(BF16)
            return total

        blocks = gn.shape[0] // 64
        dnorm = lax.fori_loop(0, blocks // 2, block_norm, jnp.zeros((8, d), F32))
        last.stage(3)
        dnorm = lax.fori_loop(blocks // 2, blocks, block_norm, dnorm)
        leave = pltpu.make_async_copy(gb, gt_ref, load_sems.at[6])
        leave.start()
        dnorm = one_row(dnorm)
        place = spot.rep * 4 + spot.side * 2 + spot.core
        for k in range(d // LANES):
            gain_out[k : k + 1, :] = dnorm[:, k * LANES : (k + 1) * LANES]
        near = lambda k: send(
            gain_out, gain_near.at[place], gain_sems.at[2 * k - 2], gain_sems.at[2 * k - 1], spot.corner(k)
        )
        beyond = lambda k: send(
            gain_sum, gain_far.at[spot.level], gain_sems.at[12 + 2 * k], gain_sems.at[13 + 2 * k], spot.far(k)
        )
        for k in range(1, 8):
            near(k).start()
        gain_near[place] = gain_out[...]
        last.stage(4)
        for k in range(1, levels):
            spread(k).wait()
        total = smz[0]
        for k in range(1, levels):
            total = total + smz[k]
        sm[3] = total
        exchange(3).start()
        for k in range(1, 8):
            near(k).wait()
        total = gain_near[0]
        for k in range(1, 8):
            total = total + gain_near[k]
        gain_sum[...] = total
        for k in range(1, levels):
            beyond(k).start()
        gain_far[spot.level] = gain_sum[...]
        tail_unit.stage(4)
        last.stage(5)
        for k in range(1, levels):
            beyond(k).wait()
        total = gain_far[0]
        for k in range(1, levels):
            total = total + gain_far[k]
        dng_ref[...] = total
        exchange(3).wait()
        small_ref[:, half_of(spot.core)] = sm[3]
        small_ref[:, half_of(1 - spot.core)] = smr[3]
        tail_unit.stage(5)
        last.stage(6)
        leave.wait()


def back(
    px, px_block, tail, y, dy, states, aux, seg_rows, conv_w, conv_b, bias, rate, skip_row, e, rate_t,
    norm_gain, dgain, squares, normed_t, wx, wt, gn, tokens, gb, ggate, gout, proj,
):
    length, inner = y.shape
    heads = bias.shape[1]
    levels, rows_f = ggate.shape[0], ggate.shape[3]
    taps = conv_w.shape[0]
    n = (conv_w.shape[1] - inner) // 2
    r = CHUNK
    chunks = length // r
    wide = inner // GROUPS
    tcols = tail.shape[1]
    d = normed_t.shape[0]
    small_cols = inner + tcols + LANES
    units = 3 * GROUPS
    back_at = lambda off: lambda g, c: (chunks - 1 - c, g + off)
    whole = lambda a: pl.BlockSpec(a.shape, lambda g, c: (0,) * a.ndim, pipeline_mode=pl.Buffered(1))
    anywhere = pl.BlockSpec(memory_space=pl.ANY)
    vm = pltpu.VMEM
    out = lambda s: pl.BlockSpec(s, lambda g, c: (0,) * len(s))
    return pl.pallas_call(
        functools.partial(
            back_kernel, inner=inner, heads=heads, width=inner // heads, levels=levels, seq_chunks=chunks
        ),
        grid=(GROUPS, chunks),
        in_specs=[
            pl.BlockSpec((r, wide), back_at(px_block)),
            pl.BlockSpec((8, wide), lambda g, c: (jnp.maximum((chunks - 1 - c) * (r // 8) - 1, 0), g + px_block)),
            pl.BlockSpec((r, wide), back_at(0)),
            pl.BlockSpec((r, wide), back_at(0)),
            pl.BlockSpec((n, wide), back_at(0)),
            *[whole(a) for a in (tail, aux, seg_rows, conv_w, conv_b, bias, rate, skip_row, e, rate_t, norm_gain, dgain, squares)],
            *[anywhere] * 8,
        ],
        out_specs=[out((rows_f, proj)), out((2 * rows_f, d)), anywhere, out((8, small_cols)), out((d // LANES, LANES))],
        out_shape=[
            jax.ShapeDtypeStruct((rows_f, proj), F32),
            jax.ShapeDtypeStruct((2 * rows_f, d), F32),
            jax.ShapeDtypeStruct((length, d), BF16),
            jax.ShapeDtypeStruct((8, small_cols), F32),
            jax.ShapeDtypeStruct((d // LANES, LANES), F32),
        ],
        scratch_shapes=[
            vm((r + 8, wide), F32), vm((3 * r, wide), F32), vm((n, wide), F32), vm((r, wide), F32),
            vm((r, wide), BF16), vm((r, wide), BF16), vm((chunks, r, 2 * n), BF16), vm((r, wide), F32),
            vm((r, wide), BF16), vm((r, wide), F32), vm((r + 8, wide), F32),
            vm((r, wide), BF16), vm((r, wide), BF16), vm((r, wide), BF16), vm((r, wide), BF16),
            vm((r + 8, 2 * n), F32), vm((chunks, heads, LANES), F32),
            vm((chunks, 3 * r, 2 * heads), BF16), vm((chunks, 2 * heads, r), F32), vm((GROUPS, length, LANES), F32),
            vm((chunks, heads, r), F32), vm((16, wide), BF16), vm((2, heads, r), F32),
            vm((chunks, r, r), F32), vm((chunks, r, r), F32), vm((length, n), F32), vm((length, n), F32),
            vm((3, chunks, heads, r), F32), vm((length, 2 * n), F32), vm((length, wide), BF16), vm((length, tcols), BF16),
            vm((8 * taps + 16, inner), F32), vm((8 * taps + 8, 2 * n), F32),
            vm(normed_t.shape, BF16), vm(wx.shape, BF16), vm(wt.shape, BF16), vm(gn.shape, F32), vm(tokens.shape, BF16), vm(gb.shape, BF16),
            vm((units, levels, 2, rows_f, wide), BF16), vm((2, levels, 2, 2, rows_f, wide), BF16),
            vm((levels, 2, 2, rows_f, tcols), BF16), vm((levels, 2, rows_f, tcols), BF16),
            vm((units, levels, 2, rows_f, wide), BF16), vm((levels, 2, rows_f, tcols), BF16),
            vm((units // 2, levels, rows_f, wide), BF16), vm((levels, rows_f, tcols), BF16),
            vm((units // 2, levels - 1, rows_f, wide), BF16), vm((levels - 1, rows_f, tcols), BF16),
            vm((units // 2, rows_f, wide), BF16), vm((rows_f, tcols), BF16),
            vm((units // 2, rows_f, wide), BF16), vm((rows_f, tcols), BF16),
            vm((units // 2, levels, 2, rows_f, wide // 2), BF16), vm((units // 2, levels, rows_f, wide // 2), BF16),
            vm((units // 2, levels - 1, rows_f, wide // 2), BF16),
            vm((units // 2, rows_f, wide // 2), BF16), vm((units // 2, rows_f, wide // 2), BF16),
            vm((8, small_cols), F32), vm((4, 8, small_cols // 2), F32), vm((4, 8, small_cols // 2), F32),
            vm((levels, 8, small_cols // 2), F32),
            vm((d // LANES, LANES), F32), vm((8, d // LANES, LANES), F32), vm((d // LANES, LANES), F32),
            vm((levels, d // LANES, LANES), F32),
            pltpu.SemaphoreType.DMA((units + 1, 7 + 2 * levels)),
            pltpu.SemaphoreType.DMA((6 + 2 * levels,)),
            pltpu.SemaphoreType.DMA((12 + 2 * levels,)),
            pltpu.SemaphoreType.DMA((7,)),
        ],
        compiler_params=pltpu.CompilerParams(
            dimension_semantics=("arbitrary", "arbitrary"), vmem_limit_bytes=60 * 2**20,
            collective_id=1, has_side_effects=True,
        ),
        name="scan_backward",
    )(
        px, px, y, dy, states, tail, aux, seg_rows, conv_w, conv_b, bias, rate, skip_row, e, rate_t,
        norm_gain, dgain, squares, normed_t, wx, wt, gn, tokens, gb, ggate, gout,
    )


class Load:
    def __init__(self, spot, shard, whole, sems, split):
        self.spot, self.shard, self.whole, self.sems, self.split = spot, shard, whole, sems, split

    def part(self, ref):
        if not self.split:
            return ref
        half = ref.shape[-1] // 2
        cols = pl.ds(pl.multiple_of(self.spot.rep * half, half), half)
        return ref.at[(slice(None),) * (len(ref.shape) - 1) + (cols,)]

    @property
    def a0(self):
        spot = self.spot
        here = self.whole.at[spot.level, spot.side, spot.core]
        return pltpu.make_async_copy(self.part(self.shard), self.part(here), self.sems.at[0])

    @property
    def a(self):
        spot, sems = self.spot, self.sems
        here = self.whole.at[spot.level, spot.side, spot.core]
        return [
            send(self.part(self.shard), self.part(here), sems.at[5 + 2 * d], sems.at[6 + 2 * d], spot.far(d))
            for d in range(1, spot.levels)
        ]

    @property
    def b(self):
        spot, sems = self.spot, self.sems
        if self.split:
            block = self.part(self.whole.at[:, spot.side, spot.core])
        else:
            half = spot.levels // 2
            block = self.whole.at[pl.ds(spot.rep * half, half), spot.side, spot.core]
        return send(block, block, sems.at[1], sems.at[2], spot.across)

    @property
    def c(self):
        spot, sems = self.spot, self.sems
        if self.split:
            block = self.part(self.whole.at[:, :, spot.core])
        else:
            half = spot.levels // 2
            block = self.whole.at[pl.ds(spot.rep * half, half), 1 - spot.side, spot.core]
        return send(block, block, sems.at[3], sems.at[4], spot.twin)

    @property
    def d(self):
        spot, sems = self.spot, self.sems
        block = self.whole.at[:, :, spot.core]
        last = 5 + 2 * spot.levels
        return send(block, block, sems.at[last], sems.at[last + 1], spot.sibling)

    def stage(self, number):
        if number == 1:
            self.a0.start()
            for copy in self.a:
                copy.start()
        elif number == 2:
            self.a0.wait()
            for copy in self.a:
                copy.wait()
            self.b.start()
        elif number == 3:
            self.b.wait()
            self.c.start()
        elif number == 4:
            self.c.wait()
            self.d.start()
        else:
            self.d.wait()


LOAD_STEPS = (5, 8, 14)


def first_kernel(
    cotan_ref, teacher_ref,
    tokens_hbm, ngain_ref, aux_ref, seg_ref, count_ref, cw_ref, cb_ref, bias_ref, rate_ref, skip_ref, gain_ref, e_ref,
    in_hbm, tail_hbm, out_hbm,
    px_ref, ssd_ref, state_out_ref, tail_out, normed_out, normed_t_out, wx_out, wtail_out,
    output_ref, gb_ref, mixed_ref, dy_ref, dz_ref, gn_ref, dgain_ref, small_ref,
    tokens, normed, normed_t, wx, wg, wo, weight_tail, tail, pbuf, ssd_all, gates, gms, inverses,
    ex, state, xs, xdt, xe, bc, yin, cums, scores, stacks,
    counts, countr, countz, sems, count_sems, copy_sems, leave_sems,
    *, inner, heads, width, levels, seq_chunks, loss_weight,
):
    step = pl.program_id(0)
    group, chunk = step // seq_chunks, step % seq_chunks
    rows, cols_g = px_ref.shape
    n = bc.shape[2] // 2
    tiles = cols_g // LANES
    per_group = cols_g // width
    taps = cw_ref.shape[0]
    rows_f = in_hbm.shape[0]
    tail_cols = tail.shape[1]
    conv_tail = 2 * n
    length, d_model = tokens.shape
    spot = Spot(levels)
    here = pl.ds(pl.multiple_of(chunk * rows, rows), rows)
    gcol = pl.multiple_of(group * cols_g, cols_g)
    last_step = GROUPS * seq_chunks - 1

    tail_load = Load(spot, tail_hbm, weight_tail, sems.at[0], False)
    loads = []
    for k in range(2 * GROUPS):
        cols = pl.ds((k % GROUPS) * cols_g, cols_g)
        shard = in_hbm.at[:, pl.ds((inner if k < GROUPS else 0) + (k % GROUPS) * cols_g, cols_g)]
        loads.append((shard, (wx if k < GROUPS else wg).at[:, :, :, :, cols]))
    for k in range(GROUPS):
        cols = pl.ds(k * (d_model // GROUPS), d_model // GROUPS)
        loads.append((out_hbm.at[:, cols], wo.at[:, :, :, :, cols]))
    loads = [Load(spot, shard, whole, sems.at[1 + k], k > 2 and k % 2 == 1) for k, (shard, whole) in enumerate(loads)]
    leaves = [
        (wx, wx_out), (weight_tail, wtail_out), (normed, normed_out), (normed_t, normed_t_out), (tail.at[8:], tail_out)
    ]

    def leave(k):
        return pltpu.make_async_copy(*leaves[k], leave_sems.at[k])

    exchange = lambda i: send(
        counts.at[i], countr.at[i], count_sems.at[2 * i], count_sems.at[2 * i + 1],
        (spot.sibling, spot.across, spot.twin)[i],
    )
    spread = lambda d: send(
        counts.at[3], countz.at[spot.level], count_sems.at[4 + 2 * d], count_sems.at[5 + 2 * d], spot.far(d)
    )

    def marks_of(aux):
        return [None] + [jnp.broadcast_to(aux[:, k : k + 1], (rows, LANES)) for k in range(1, taps)]

    def conv(buffer, at, cols, wcols, marks):
        block = buffer[pl.ds(at, rows + 8), cols]
        pre = cb_ref[:, wcols] + cw_ref[0:1, wcols] * block[8:]
        for k in range(1, taps):
            pre = pre + (cw_ref[k : k + 1, wcols] * block[8 - k : 8 - k + rows]) * marks[k]
        return pre * sigmoid(pre)

    def project(weight, out, cols):
        for i in range(length // 256):
            out[8 + i * 256 : 8 + (i + 1) * 256, :] = mm(normed[i * 256 : (i + 1) * 256, :], weight[:, cols])

    @pl.when(step == 0)
    def _():
        fetch = pltpu.make_async_copy(tokens_hbm, tokens, copy_sems.at[0])
        fetch.start()
        counts[0] = count_ref[...]
        spot.greet()
        tail_load.stage(1)
        exchange(0).start()
        loads[0].stage(1)
        loads[1].stage(1)
        fetch.wait()

        def norm(i, carry):
            block = pl.ds(pl.multiple_of(i * 64, 64), 64)
            v = tokens[block, :].astype(F32)
            v = v * lax.rsqrt(jnp.sum(v * v, axis=1, keepdims=True) / d_model + EPS)
            normed[block, :] = (v * ngain_ref[...]).astype(BF16)
            return carry

        lax.fori_loop(0, length // 64, norm, 0)
        def turn_rows(blocks):
            for i in blocks:
                block = slice(i * 256, (i + 1) * 256)
                normed_t[:, block] = normed[block, :].T

        def shared(i, carry):
            at = pl.ds(pl.multiple_of(i * rows, rows), rows)
            aux = aux_ref[at, :]
            marks = marks_of(aux)
            start = pl.multiple_of(i * rows, rows)
            raw = tail[pl.ds(start + 8, rows), conv_tail : conv_tail + heads]
            shifted, size, cum, from_prev, to_end = small_terms(
                raw, bias_ref[...], rate_ref[...], aux[:, 7:8], aux[:, 8:9], rows
            )
            cums[i, :, 0:heads] = cum
            stacks[i] = jnp.concatenate(
                [jnp.concatenate(split2(v), axis=1) for v in (size, from_prev, to_end)], axis=0
            )
            for c in range(conv_tail // LANES):
                cols = slice(c * LANES, (c + 1) * LANES)
                act = conv(tail, start, cols, slice(inner + c * LANES, inner + (c + 1) * LANES), marks)
                bc[i, :, cols] = act.astype(BF16)
            causal = (iota((rows, rows), 0) >= iota((rows, rows), 1)) & (aux[:, 0:1] == seg_ref[i])
            scores[i] = jnp.where(causal, mm_nt(bc[i, :, n:], bc[i, :, 0:n]), 0.0)
            return carry

        tail[0:8, :] = jnp.zeros((8, tail_cols), F32)
        pbuf[0:8, :] = jnp.zeros((8, cols_g), F32)
        cums[...] = jnp.zeros_like(cums)
        tail_load.stage(2)
        blocks = length // 256
        turn_rows(range(blocks // 2))
        tail_load.stage(3)
        turn_rows(range(blocks // 2, blocks))
        leave(2).start()
        leave(3).start()
        tail_load.stage(4)
        loads[0].stage(2)
        tail_load.stage(5)
        leave(1).start()
        project(weight_tail.reshape(d_model, tail_cols), tail, slice(0, tail_cols))
        leave(4).start()
        loads[0].stage(3)
        lax.fori_loop(0, seq_chunks // 2, shared, 0)
        loads[0].stage(4)
        loads[1].stage(2)
        lax.fori_loop(seq_chunks // 2, seq_chunks, shared, 0)

    scan_steps = GROUPS * seq_chunks
    events = {}
    for k in range(1, 3 * GROUPS):
        begin = max(0, (k - 2) * 3 * seq_chunks // 8)
        times = [begin, *[begin + 1 + delay * seq_chunks // 8 for delay in LOAD_STEPS]]
        if k == 1:
            times = [None, None, seq_chunks // 4, 5 * seq_chunks // 8]
        need = min(k * seq_chunks, scan_steps)
        for number, when in enumerate(times):
            if when is not None:
                events.setdefault(min(when, need), []).append((k, number + 1))
        if k < 2 * GROUPS:
            events.setdefault(need, []).append((k, 5))
    late = sorted(events.pop(scan_steps), key=lambda pair: (pair[1] + pair[0], pair[0]))
    for at, happen in sorted(events.items()):

        @pl.when(step == at)
        def _(happen=sorted(happen, key=lambda pair: (pair[0], pair[1]))):
            for k, number in happen:
                loads[k].stage(number)

    @pl.when(step == scan_steps)
    def _():
        leave(0).start()
        rest = list(late)
        flat_gate = wg.reshape(d_model, inner)
        for k in range(GROUPS):
            while True:
                one = rest.pop(0)
                loads[one[0]].stage(one[1])
                if one == (GROUPS + k, 5):
                    break
            cols = slice(k * cols_g, (k + 1) * cols_g)
            gates[:, cols] = mm(normed[...], flat_gate[:, cols])

        def gate_norm(i, carry):
            at = pl.ds(pl.multiple_of(i * 64, 64), 64)
            squares = jnp.zeros((64, LANES), F32)
            for c in range(inner // LANES):
                cols = slice(c * LANES, (c + 1) * LANES)
                gate = gates[at, cols]
                gated = ssd_all[at, cols] * (gate * sigmoid(gate))
                squares = squares + gated * gated
            inverse = lax.rsqrt(jnp.sum(squares, axis=1, keepdims=True) / inner + EPS)
            inverses[at, :] = jnp.broadcast_to(inverse, (64, LANES))
            return carry

        parts = 4
        blocks = length // 64
        share = -(-len(rest) // parts)
        for i in range(parts):
            for k, number in rest[i * share : (i + 1) * share]:
                loads[k].stage(number)
            lax.fori_loop(i * blocks // parts, (i + 1) * blocks // parts, gate_norm, 0)
        for k in range(2 * GROUPS, 3 * GROUPS):
            loads[k].stage(5)

    for i in range(4):

        @pl.when(step == (1 + i) * seq_chunks // 2 + 1)
        def _(i=i):
            if i < 3:
                exchange(i).wait()
                counts[i + 1] = counts[i] + countr[i]
            if i < 2:
                exchange(i + 1).start()
            elif i == 2:
                for k in range(1, levels):
                    spread(k).start()
                countz[spot.level] = counts[3]
            else:
                for k in range(1, levels):
                    spread(k).wait()
                total = countz[0]
                for k in range(1, levels):
                    total = total + countz[k]
                counts[4] = total

    for g in range(GROUPS):

        @pl.when(step == g * seq_chunks)
        def _(g=g):
            if g == 0:
                loads[0].stage(5)
            project(wx.reshape(d_model, inner), pbuf, slice(g * cols_g, (g + 1) * cols_g))

    @pl.when(step < scan_steps)
    def _():
        @pl.when(chunk == 0)
        def _():
            state[...] = jnp.zeros_like(state)

        aux = aux_ref[here, :]
        marks = marks_of(aux)
        ex[...] = mm(stacks[chunk], e_ref[:, pl.ds(gcol, cols_g)])
        head0 = group * per_group
        pick = (iota((LANES, LANES), 0) == iota((LANES, LANES), 1) + head0).astype(BF16)
        moved = [mm(v, pick) for v in split3(cums[chunk])]
        cum = moved[0] + moved[1] + moved[2]
        cum_t = cum.T
        start = pl.multiple_of(chunk * rows, rows)
        px_ref[...] = pbuf[pl.ds(start + 8, rows), :]
        for c in range(tiles):
            cols = slice(c * LANES, (c + 1) * LANES)
            act = conv(pbuf, start, cols, pl.ds(gcol + c * LANES, LANES), marks)
            xs[:, cols] = act
            scaled = act * ex[0:rows, cols]
            xdt[:, cols] = scaled.astype(BF16)
            xe[:, cols] = (scaled * ex[2 * rows : 3 * rows, cols]).astype(BF16)
        b, cc = bc[chunk, :, 0:n], bc[chunk, :, n:]
        state_low = state[...].astype(BF16)
        state_out_ref[...] = state_low
        yin[...] = mm(cc, state_low)
        state[...] = state[...] * ex[2 * rows - 1 : 2 * rows, :] + mm_tn(b, xe[...])
        score = scores[chunk]
        lane = iota((1, LANES), 1)
        masks = [(lane < width).astype(BF16), (lane >= width).astype(BF16)]
        for c in range(tiles):
            cols = slice(c * LANES, (c + 1) * LANES)
            mixing = []
            for h in (2 * c, 2 * c + 1):
                spread_h = jnp.minimum(cum[:, h : h + 1] - cum_t[h : h + 1, :], 0.0)
                mixing.append((score * jnp.exp(spread_h)).astype(BF16))
            x_low = xdt[:, cols]
            y = mm(
                jnp.concatenate(mixing, axis=1), jnp.concatenate([x_low * masks[0], x_low * masks[1]], axis=0)
            ) + ex[rows : 2 * rows, cols] * yin[:, cols]
            acols = pl.ds(gcol + c * LANES, LANES)
            ssd_ref[:, cols] = y
            ssd_all[here, acols] = y + skip_ref[:, acols] * xs[:, cols]

    @pl.when(step >= scan_steps)
    def _():
        turn = step - scan_steps
        block_rows = gms.shape[0]
        base = pl.multiple_of(turn * block_rows, block_rows)
        flat_gate = wg.reshape(d_model, inner)
        flat_out = wo.reshape(inner, d_model)
        sub = 64

        @pl.when(turn == 0)
        def _():
            dgain_ref[...] = jnp.zeros_like(dgain_ref)
            small_ref[...] = jnp.zeros_like(small_ref)

        def norm_of(i):
            at = pl.ds(pl.multiple_of(i * sub, sub), sub)
            return at, pl.ds(pl.multiple_of(base + i * sub, sub), sub)

        def forward_part(i, carry):
            at, full_at = norm_of(i)
            inverse = inverses[full_at, :]
            for c in range(inner // LANES):
                cols = slice(c * LANES, (c + 1) * LANES)
                gate = gates[full_at, cols]
                unit = ssd_all[full_at, cols] * (gate * sigmoid(gate)) * inverse
                mixed_ref[at, cols] = (unit * gain_ref[:, cols]).astype(BF16)
            return carry

        lax.fori_loop(0, block_rows // sub, forward_part, 0)
        results = gms.at[:, 0:d_model]
        results[...] = mm(mixed_ref[...], flat_out[...])
        scale = 2.0 * loss_weight / (counts[4, 0:1, :] * d_model)

        def loss_part(i, carry):
            at, full_at = norm_of(i)
            valid = jnp.broadcast_to(aux_ref[full_at, 9:10], (sub, LANES))
            squares = jnp.zeros((8, LANES), F32)
            for c in range(d_model // LANES):
                cols = slice(c * LANES, (c + 1) * LANES)
                result = tokens[full_at, cols].astype(F32) + results[at, cols]
                output_ref[at, cols] = result.astype(BF16)
                error = result - teacher_ref[at, cols].astype(F32)
                squares = squares + jnp.sum((valid * error * error).reshape(sub // 8, 8, LANES), axis=0)
                gb_ref[at, cols] = (valid * (cotan_ref[at, cols].astype(F32) + scale * error)).astype(BF16)
            small_ref[0:8, :] += squares
            return carry

        lax.fori_loop(0, block_rows // sub, loss_part, 0)
        small_ref[8:16, :] = counts[4]
        grads = gb_ref[...]
        for k in range(GROUPS):
            cols = slice(k * cols_g, (k + 1) * cols_g)
            gms[:, cols] = mm_nt(grads, flat_out[cols, :])

        def backward_part(i, carry):
            at, full_at = norm_of(i)
            cross = jnp.zeros((sub, LANES), F32)
            for c in range(inner // LANES):
                cols = slice(c * LANES, (c + 1) * LANES)
                cross = cross + gms[at, cols] * mixed_ref[at, cols].astype(F32)
            inverse = inverses[full_at, :]
            mean_cross = jnp.sum(cross, axis=1, keepdims=True) / inner
            for c in range(inner // LANES):
                cols = slice(c * LANES, (c + 1) * LANES)
                gate = gates[full_at, cols]
                sig = sigmoid(gate)
                silu = gate * sig
                ssd = ssd_all[full_at, cols]
                unit = ssd * silu * inverse
                grad_mixed = gms[at, cols]
                dgain_ref[:, cols] += jnp.sum((grad_mixed * unit).reshape(sub // 8, 8, LANES), axis=0)
                grad_gated = inverse * (grad_mixed * gain_ref[:, cols] - unit * mean_cross)
                dy_ref[at, cols] = (grad_gated * silu).astype(BF16)
                dz_ref[at, cols] = (
                    grad_gated * ssd * (sig + silu * (1.0 - sig))
                ).astype(BF16)
            return carry

        lax.fori_loop(0, block_rows // sub, backward_part, 0)
        gn_ref[...] = mm_nt(dz_ref[...], flat_gate[...])

        @pl.when(turn == length // block_rows - 1)
        def _():
            for k in range(len(leaves)):
                leave(k).wait()


def first(
    tokens, norm_gain, aux, seg_rows, count, conv_w, conv_b, bias, rate, skip_row, gain_row, e,
    cotangent, teacher, w_in, w_tail, w_out, levels, loss_weight,
):
    length, d = tokens.shape
    heads, inner = bias.shape[1], skip_row.shape[1]
    rows_f = w_in.shape[0]
    n = (conv_w.shape[1] - inner) // 2
    r = CHUNK
    chunks = length // r
    wide = inner // GROUPS
    tcols = w_tail.shape[1]
    units = 3 * GROUPS
    tall = 256
    scan_steps = GROUPS * chunks

    def scan_block(s):
        s = jnp.minimum(s, scan_steps - 1)
        return s % chunks, s // chunks

    block = lambda h: pl.BlockSpec((h, wide), scan_block)
    late = lambda w, deep=2: pl.BlockSpec(
        (tall, w), lambda s: (jnp.maximum(s - scan_steps, 0), 0), pipeline_mode=pl.Buffered(deep)
    )
    whole = lambda a: pl.BlockSpec(a.shape, lambda s: (0,) * a.ndim, pipeline_mode=pl.Buffered(1))
    fixed = lambda *dims: pl.BlockSpec(dims, lambda s: (0,) * len(dims))
    anywhere = pl.BlockSpec(memory_space=pl.ANY)
    vm = pltpu.VMEM
    shape = jax.ShapeDtypeStruct
    wide_shape = (levels, 2, 2, rows_f, inner)
    return pl.pallas_call(
        functools.partial(
            first_kernel, inner=inner, heads=heads, width=inner // heads, levels=levels, seq_chunks=chunks,
            loss_weight=loss_weight,
        ),
        grid=(scan_steps + length // tall,),
        in_specs=[
            late(d), late(d), anywhere,
            *[whole(a) for a in (norm_gain, aux, seg_rows, count, conv_w, conv_b, bias, rate, skip_row, gain_row, e)],
            anywhere, anywhere, anywhere,
        ],
        out_specs=[
            block(r), block(r), block(n), *[anywhere] * 5,
            late(d), late(d), late(inner), late(inner), late(inner), late(d), fixed(8, inner), fixed(16, LANES),
        ],
        out_shape=[
            shape((length, inner), F32), shape((length, inner), F32), shape((chunks * n, inner), BF16),
            shape((length, tcols), F32), shape((length, d), BF16), shape((d, length), BF16),
            shape(wide_shape, BF16), shape((levels, 2, 2, rows_f, tcols), BF16),
            shape((length, d), BF16), shape((length, d), BF16), shape((length, inner), BF16),
            shape((length, inner), BF16), shape((length, inner), BF16), shape((length, d), F32),
            shape((8, inner), F32), shape((16, LANES), F32),
        ],
        scratch_shapes=[
            vm((length, d), BF16), vm((length, d), BF16), vm((d, length), BF16),
            vm(wide_shape, BF16), vm(wide_shape, BF16), vm((levels, 2, 2, 2 * rows_f, d), BF16),
            vm((levels, 2, 2, rows_f, tcols), BF16),
            vm((length + 8, tcols), F32), vm((length + 8, wide), F32), vm((length, inner), F32),
            vm((length, inner), F32), vm((tall, inner), F32), vm((length, LANES), F32),
            vm((3 * r, wide), F32), vm((n, wide), F32), vm((r, wide), F32), vm((r, wide), BF16), vm((r, wide), BF16),
            vm((chunks, r, 2 * n), BF16), vm((r, wide), F32), vm((chunks, r, LANES), F32), vm((chunks, r, r), F32),
            vm((chunks, 3 * r, 2 * heads), BF16),
            vm((5, 8, LANES), F32), vm((3, 8, LANES), F32), vm((levels, 8, LANES), F32),
            pltpu.SemaphoreType.DMA((units + 1, 7 + 2 * levels)),
            pltpu.SemaphoreType.DMA((4 + 2 * levels,)),
            pltpu.SemaphoreType.DMA((1,)),
            pltpu.SemaphoreType.DMA((5,)),
        ],
        compiler_params=pltpu.CompilerParams(
            dimension_semantics=("arbitrary",), vmem_limit_bytes=60 * 2**20,
            collective_id=2, has_side_effects=True,
        ),
        name="scan_forward",
    )(
        cotangent, teacher, tokens, norm_gain, aux, seg_rows, count, conv_w, conv_b, bias, rate, skip_row, gain_row, e,
        w_in, w_tail, w_out,
    )


def on_device(
    tokens,
    norm_gain,
    in_weight,
    conv_weight,
    conv_bias,
    step_bias,
    decay_log,
    skip_gain,
    out_gain,
    out_weight,
    cotangent,
    teacher,
    segment,
    valid_mask,
):
    seqs, length, width = tokens.shape
    rows = seqs * length
    shards = lax.axis_size("fsdp")
    devices = lax.axis_size("rep") * shards
    levels = shards // 4
    loss_weight = float(rows * devices * width // 8)
    heads, inner = step_bias.shape[0], out_gain.shape[0]
    aux, seg_rows, count, bias, rate, rate_t, skip_row, conv_row, ngain_row, gain_row, e, in_tail = prepare(
        segment, valid_mask, step_bias, decay_log, skip_gain, conv_bias, norm_gain, out_gain, in_weight
    )
    params = (conv_weight, conv_row, bias, rate, skip_row)
    flat, cotan, target = (v.reshape(rows, width) for v in (tokens, cotangent, teacher))
    (
        px, y, states, tail, normed, normed_t, wx, wt, output, grad_branch, mixed, dy, dz, gn, dgain, sums
    ) = first(
        flat, ngain_row, aux, seg_rows, count, *params, gain_row, e, cotan, target,
        in_weight, in_tail, out_weight, levels, loss_weight,
    )
    wx, wt = (w.reshape(-1, w.shape[-1]) for w in (wx, wt))
    grad_out = mm_tn(mixed, grad_branch).astype(BF16)
    grad_gate = mm(normed_t, dz).astype(BF16)
    grad_in, grad_out, grad_tokens, small, norm_sum = back(
        px, 0, tail, y, dy, states, aux, seg_rows, *params, e, rate_t,
        ngain_row, dgain, sums[:8], normed_t, wx, wt, gn, flat, grad_branch,
        grad_gate.reshape(levels, 2, 2, width // shards, inner),
        grad_out.reshape(levels, 2, 2, inner // shards, width), in_weight.shape[1],
    )
    outs = finish(
        grad_in, grad_out, grad_tokens, output, small, norm_sum, sums, e, *conv_weight.shape, heads, inner
    )
    return (
        outs[0].reshape(tokens.shape), outs[1].reshape(()), outs[2].reshape(tokens.shape), *outs[3:]
    )


def solution(mesh):
    tokens = P(("rep", "fsdp"), None, None)
    marks = P(("rep", "fsdp"), None)
    shard = P("fsdp", None)
    return jax.shard_map(
        on_device,
        mesh=mesh,
        in_specs=(tokens, P(), shard, P(), P(), P(), P(), P(), P(), shard, tokens, tokens, marks, marks),
        out_specs=(tokens, P(), tokens, P(), shard, P(), P(), P(), P(), P(), P(), shard),
        check_vma=False,
    )
```

```python
import functools

import jax
import jax.numpy as jnp
from jax import lax
from jax.experimental import pallas as pl
from jax.experimental.pallas import tpu as pltpu
from jax.sharding import PartitionSpec as P

CHUNK = 128
LANES = 128
EPS = 1e-05
F32 = jnp.float32
BF16 = jnp.bfloat16
NT = (((1,), (1,)), ((), ()))
TN = (((0,), (0,)), ((), ()))


def mm(a, b):
    return jnp.dot(a, b, preferred_element_type=F32)


def mm_nt(a, b):
    return lax.dot_general(a, b, NT, preferred_element_type=F32)


def mm_tn(a, b):
    return lax.dot_general(a, b, TN, preferred_element_type=F32)


def split2(v):
    high = v.astype(BF16)
    return high, (v - high.astype(F32)).astype(BF16)


def split3(v):
    high = v.astype(BF16)
    rest = v - high.astype(F32)
    mid = rest.astype(BF16)
    return high, mid, (rest - mid.astype(F32)).astype(BF16)


def tri_sum(tri, v):
    heads = v.shape[1]
    parts = mm(tri, jnp.concatenate(split3(v), axis=1))
    return parts[:, :heads] + parts[:, heads : 2 * heads] + parts[:, 2 * heads :]


def sum_tri(v, tri):
    heads = v.shape[0]
    parts = mm(jnp.concatenate(split3(v), axis=0), tri)
    return parts[:heads] + parts[heads : 2 * heads] + parts[2 * heads :]


def sigmoid(v):
    return 0.5 * jnp.tanh(0.5 * v) + 0.5


def softplus(v):
    return jnp.maximum(v, 0.0) + jnp.log1p(jnp.exp(-jnp.abs(v)))


def iota(shape, dim):
    return lax.broadcasted_iota(jnp.int32, shape, dim)


def small_terms(step_raw, step_bias, decay_rate, keep, to_end, rows):
    shifted = step_raw + step_bias
    step = softplus(shifted)
    lower = (iota((rows, rows), 0) >= iota((rows, rows), 1)).astype(BF16)
    cum = tri_sum(lower, step * decay_rate)
    last = cum[rows - 1 : rows, :]
    return shifted, step, cum, jnp.exp(cum) * keep, jnp.exp(last - cum) * to_end


def expand(e_ref, out_ref, step, from_prev, to_end):
    stacked = jnp.concatenate(
        [jnp.concatenate(split2(v), axis=1) for v in (step, from_prev, to_end)], axis=0
    )
    out_ref[...] = mm(stacked, e_ref[...])


def full(shape):
    return pl.BlockSpec(shape, lambda i: (0,) * len(shape))


def prepare_kernel(
    segment_ref, valid_ref, bias_ref, log_ref, skip_ref, cb_ref, ngain_ref, gain_ref, weight_ref,
    aux_ref, rows_ref, count_ref, bias_out, rate_out, rate_t_out, skip_out, cb_out, ngain_out, gain_out, e_out, tail_out,
    *, tail_cols,
):
    length = segment_ref.shape[1]
    heads = bias_ref.shape[0]
    inner = gain_ref.shape[0]
    width = inner // heads
    docs = segment_ref[...].astype(F32)
    valid = valid_ref[...].astype(F32)
    place = iota((8, length), 1)
    wide = jnp.broadcast_to(docs, (8, length))
    marks = []
    for k in (1, 2, 3):
        marks.append(jnp.where((wide == pltpu.roll(wide, k, 1)) & (place >= k), 1.0, 0.0)[0:1])
    for k in (1, 2, 3):
        marks.append(jnp.where((wide == pltpu.roll(wide, length - k, 1)) & (place < length - k), 1.0, 0.0)[0:1])
    for c in range(length // CHUNK):
        cols = slice(c * CHUNK, (c + 1) * CHUNK)
        own = docs[:, cols]
        last = docs[:, (c + 1) * CHUNK - 1 : (c + 1) * CHUNK]
        keep = jnp.zeros_like(own)
        if c:
            keep = jnp.where(own == docs[:, c * CHUNK - 1 : c * CHUNK], 1.0, 0.0)
        stacked = [own, *[v[:, cols] for v in marks], keep, jnp.where(own == last, 1.0, 0.0), valid[:, cols]]
        stacked.append(jnp.zeros((LANES - len(stacked), CHUNK), F32))
        aux_ref[cols, :] = jnp.concatenate(stacked, axis=0).T[:, 0:16]
        rows_ref[c] = own
    count_ref[...] = jnp.broadcast_to(jnp.sum(valid, axis=1, keepdims=True), count_ref.shape)
    bias_out[...] = bias_ref[...].reshape(1, heads)
    rate = -jnp.exp(log_ref[...].reshape(1, heads))
    rate_out[...] = rate
    spare = jnp.concatenate([rate, jnp.zeros((1, LANES - heads), F32)], axis=1)
    rate_t_out[...] = jnp.broadcast_to(spare, (LANES, LANES)).T[0:heads, 0:1]
    e = (iota((2 * heads, inner), 0) % heads == iota((2 * heads, inner), 1) // width).astype(BF16)
    e_out[...] = e
    skip = jnp.broadcast_to(skip_ref[...].reshape(1, heads), (16, heads))
    parts = [mm(v, e[0:heads]) for v in split3(skip)]
    skip_out[...] = (parts[0] + parts[1] + parts[2])[0:1]
    cb_out[...] = cb_ref[...].reshape(1, cb_ref.shape[0])
    ngain_out[...] = ngain_ref[...].reshape(1, ngain_ref.shape[0])
    gain_out[...] = gain_ref[...].reshape(1, inner)
    rows_f = weight_ref.shape[0]
    tail_out[...] = jnp.concatenate(
        [weight_ref[:, 0:tail_cols], jnp.zeros((rows_f, tail_out.shape[1] - tail_cols), BF16)], axis=1
    )


def prepare(segment, valid_mask, step_bias, decay_log, skip_gain, conv_bias, norm_gain, out_gain, in_weight):
    length = segment.shape[1]
    heads, inner = step_bias.shape[0], out_gain.shape[0]
    rows_f, proj = in_weight.shape
    tail_cols = proj - 2 * inner
    tail_wide = -(-tail_cols // LANES) * LANES
    shape = jax.ShapeDtypeStruct
    small = (segment, valid_mask, step_bias, decay_log, skip_gain, conv_bias, norm_gain, out_gain)
    outs = [
        shape((length, 16), F32), shape((length // CHUNK, 1, CHUNK), F32), shape((8, LANES), F32),
        shape((1, heads), F32), shape((1, heads), F32), shape((heads, 1), F32), shape((1, inner), F32),
        shape((1, conv_bias.shape[0]), F32), shape((1, norm_gain.shape[0]), F32), shape((1, inner), F32),
        shape((2 * heads, inner), BF16), shape((rows_f, tail_wide), BF16),
    ]
    block = 512
    return pl.pallas_call(
        functools.partial(prepare_kernel, tail_cols=tail_cols),
        grid=(1,),
        in_specs=[*[full(a.shape) for a in small], pl.BlockSpec((rows_f, block), lambda i: (0, 2 * inner // block))],
        out_specs=[full(o.shape) for o in outs],
        out_shape=outs,
        name="prepare",
    )(*small, in_weight)


def finish_kernel(
    gi_ref, go_ref, gt_ref, output_ref, small_ref, dng_ref, sums_ref, e_ref,
    out_final, loss_ref, gt_final, ngain_ref, gi_final, cw_ref, cb_ref, bias_ref, log_ref, skip_ref, gain_ref, go_final,
    gi, go, gt, output, sems,
):
    trios = ((gt_ref, gt, gt_final), (output_ref, output, out_final), (gi_ref, gi, gi_final), (go_ref, go, go_final))
    fetches = [pltpu.make_async_copy(a, b, sems.at[i]) for i, (a, b, c) in enumerate(trios)]
    stores = [pltpu.make_async_copy(b, c, sems.at[4 + i]) for i, (a, b, c) in enumerate(trios)]
    for copy in fetches:
        copy.start()
    for fetched, stored in zip(fetches, stores):
        fetched.wait()
        stored.start()
    taps, conv_width = cw_ref.shape
    heads, inner = bias_ref.shape[0], gain_ref.shape[0]
    d = dng_ref.shape[0] * LANES
    cw_ref[...] = small_ref[0:taps, 0:conv_width]
    cb_ref[...] = small_ref[taps : taps + 1, 0:conv_width].reshape(conv_width)
    gain_ref[...] = small_ref[5:6, 0:inner].reshape(inner)
    bias_ref[...] = small_ref[7:8, 0:heads].reshape(heads)
    log_ref[...] = small_ref[7:8, LANES : LANES + heads].reshape(heads)
    squares = jnp.sum(small_ref[7:8, 2 * LANES : 3 * LANES], axis=1, keepdims=True)
    loss_ref[...] = squares / (sums_ref[8:9, 0:1] * d)
    by_head = jnp.zeros((16, 2 * heads), F32)
    for v in split3(jnp.broadcast_to(small_ref[6:7, 0:inner], (16, inner))):
        by_head = by_head + mm_nt(v, e_ref[...])
    skip_ref[...] = by_head[0:1, 0:heads].reshape(heads)
    ngain_ref[...] = dng_ref[...].reshape(d)
    for copy in stores:
        copy.wait()


def finish(gi, go, gt, output, small, dng, sums, e, taps, conv_width, heads, inner):
    shape = jax.ShapeDtypeStruct
    anywhere = pl.BlockSpec(memory_space=pl.ANY)
    outs = [
        shape(output.shape, BF16), shape((1, 1), F32), shape(gt.shape, BF16), shape((dng.size,), F32),
        shape(gi.shape, F32), shape((taps, conv_width), F32), shape((conv_width,), F32), shape((heads,), F32),
        shape((heads,), F32), shape((heads,), F32), shape((inner,), F32), shape(go.shape, F32),
    ]
    far = (0, 2, 4, 11)
    return pl.pallas_call(
        finish_kernel,
        grid=(1,),
        in_specs=[*[anywhere] * 4, *[full(a.shape) for a in (small, dng, sums, e)]],
        out_specs=[anywhere if i in far else full(o.shape) for i, o in enumerate(outs)],
        out_shape=outs,
        scratch_shapes=[
            *[pltpu.VMEM(a.shape, a.dtype) for a in (gi, go, gt, output)], pltpu.SemaphoreType.DMA((8,)),
        ],
        compiler_params=pltpu.CompilerParams(vmem_limit_bytes=60 * 2**20),
        name="finish",
    )(gi, go, gt, output, small, dng, sums, e)


MESH = pl.DeviceIdType.MESH


class Spot:
    def __init__(self, levels):
        self.rep, self.at = lax.axis_index("rep"), lax.axis_index("fsdp")
        self.core, self.side, self.level = self.at % 2, (self.at // 2) % 2, self.at // 4
        self.levels = levels
        self.sibling = (self.rep, self.at + 1 - 2 * self.core)
        self.across = (self.rep, self.at + 2 - 4 * self.side)
        self.twin = (1 - self.rep, self.at)

    def far(self, step):
        return (self.rep, ((self.level + step) % self.levels) * 4 + self.at % 4)

    def corner(self, j):
        flip = lambda v, bit: 1 - v if j & bit else v
        return (flip(self.rep, 4), self.level * 4 + flip(self.side, 2) * 2 + flip(self.core, 1))

    def greet(self, corners=False):
        barrier = pltpu.get_barrier_semaphore()
        near = [self.corner(j) for j in range(1, 8)] if corners else [self.sibling, self.across, self.twin]
        partners = near + [self.far(d) for d in range(1, self.levels)]
        for one in partners:
            pl.semaphore_signal(barrier, inc=1, device_id=one, device_id_type=MESH)
        pl.semaphore_wait(barrier, len(partners))


def send(src, dst, send_sem, recv_sem, device):
    return pltpu.make_async_remote_copy(
        src_ref=src, dst_ref=dst, send_sem=send_sem, recv_sem=recv_sem, device_id=device, device_id_type=MESH
    )


class Split:
    def __init__(self, spot, whole, own, from_core, half, from_side, from_level, mine, from_twin, sems, write):
        self.spot, self.whole, self.own, self.write = spot, whole, own, write
        self.from_core, self.half, self.from_side, self.from_level = from_core, half, from_side, from_level
        self.mine, self.from_twin, self.sems = mine, from_twin, sems
        self.cols = half.shape[-1]

    def columns(self, rep):
        return pl.ds(pl.multiple_of(rep * self.cols, self.cols), self.cols)

    @property
    def c0(self):
        return pltpu.make_async_copy(self.whole.at[:, :, self.spot.core], self.own, self.sems.at[6])

    @property
    def c1(self):
        spot, sems = self.spot, self.sems
        return send(self.whole.at[:, :, 1 - spot.core], self.from_core, sems.at[0], sems.at[1], spot.sibling)

    @property
    def c2(self):
        spot, sems = self.spot, self.sems
        block = self.own.at[:, :, :, self.columns(1 - spot.rep)]
        return send(block, self.half, sems.at[2], sems.at[3], spot.twin)

    @property
    def c3(self):
        spot, sems = self.spot, self.sems
        last = 5 + 2 * spot.levels
        return send(self.half.at[:, 1 - spot.side], self.from_side, sems.at[last], sems.at[last + 1], spot.across)

    @property
    def c4(self):
        spot, sems = self.spot, self.sems
        return [
            send(
                self.from_side.at[(spot.level + d) % spot.levels], self.from_level.at[d - 1],
                sems.at[5 + 2 * d], sems.at[6 + 2 * d], spot.far(d),
            )
            for d in range(1, spot.levels)
        ]

    @property
    def c5(self):
        spot, sems = self.spot, self.sems
        return send(self.mine, self.from_twin, sems.at[4], sems.at[5], spot.twin)

    def stage(self, number):
        spot, levels = self.spot, self.spot.levels
        if number == 1:
            self.c1.start()
            self.c0.start()
        elif number == 2:
            self.c0.wait()
            self.c1.wait()

            def add(i, carry):
                for side in range(2):
                    self.own[i, side] = self.own[i, side] + self.from_core[i, side]
                return carry

            lax.fori_loop(0, levels, add, 0)
            self.c2.start()
        elif number == 3:
            self.c2.wait()
            columns = self.columns(spot.rep)

            def add(i, carry):
                for side in range(2):
                    self.half[i, side] = self.half[i, side] + self.own[i, side, :, columns]
                return carry

            lax.fori_loop(0, levels, add, 0)
            self.c3.start()
        elif number == 4:
            self.c3.wait()

            def add(i, carry):
                self.from_side[i] = self.from_side[i] + self.half[i, spot.side]
                return carry

            lax.fori_loop(0, levels, add, 0)
            for copy in self.c4:
                copy.start()
        elif number == 5:
            for copy in self.c4:
                copy.wait()
            total = self.from_side[spot.level].astype(F32)
            for d in range(levels - 1):
                total = total + self.from_level[d].astype(F32)
            self.mine[...] = total.astype(BF16)
            self.c5.start()
        else:
            self.c5.wait()
            self.write(self.mine[...].astype(F32), self.columns(spot.rep))
            self.write(self.from_twin[...].astype(F32), self.columns(1 - spot.rep))


class Unit:
    def __init__(self, spot, whole, own, from_core, from_side, from_level, mine, from_twin, sems, write):
        self.spot, self.whole, self.own, self.write = spot, whole, own, write
        self.from_core, self.from_side, self.from_level = from_core, from_side, from_level
        self.mine, self.from_twin = mine, from_twin
        self.sems = sems

    @property
    def c0(self):
        return pltpu.make_async_copy(self.whole.at[:, :, self.spot.core], self.own, self.sems.at[6])

    @property
    def c1(self):
        spot, sems = self.spot, self.sems
        return send(self.whole.at[:, :, 1 - spot.core], self.from_core, sems.at[0], sems.at[1], spot.sibling)

    @property
    def c2(self):
        spot, sems = self.spot, self.sems
        return send(self.own.at[:, 1 - spot.side], self.from_side, sems.at[2], sems.at[3], spot.across)

    @property
    def c3(self):
        spot, sems = self.spot, self.sems
        return [
            send(
                self.from_side.at[(spot.level + d) % spot.levels], self.from_level.at[d - 1],
                sems.at[5 + 2 * d], sems.at[6 + 2 * d], spot.far(d),
            )
            for d in range(1, spot.levels)
        ]

    @property
    def c4(self):
        spot, sems = self.spot, self.sems
        return send(self.mine, self.from_twin, sems.at[4], sems.at[5], spot.twin)

    def stage(self, number):
        spot, levels = self.spot, self.spot.levels
        if number == 1:
            self.c1.start()
            self.c0.start()
        elif number == 2:
            self.c0.wait()
            self.c1.wait()

            def add(i, carry):
                for side in range(2):
                    self.own[i, side] = self.own[i, side] + self.from_core[i, side]
                return carry

            lax.fori_loop(0, levels, add, 0)
            self.c2.start()
        elif number == 3:
            self.c2.wait()

            def add(i, carry):
                self.from_side[i] = self.from_side[i] + self.own[i, spot.side]
                return carry

            lax.fori_loop(0, levels, add, 0)
            for copy in self.c3:
                copy.start()
        elif number == 4:
            for copy in self.c3:
                copy.wait()
            total = self.from_side[spot.level].astype(F32)
            for d in range(levels - 1):
                total = total + self.from_level[d].astype(F32)
            self.mine[...] = total.astype(BF16)
            self.c4.start()
        else:
            self.c4.wait()
            self.write(self.mine[...].astype(F32) + self.from_twin[...].astype(F32))


GROUPS = 4
STARTS = (0, 2, 4, 6, 8, 11, 13, 16, 18, 20, 24)
UNIT_DELAYS = (0, 2, 6, 10, 12)
SPLIT_DELAYS = (0, 2, 6, 9, 12, 14)


def back_kernel(
    px_ref, prev_ref, y_ref, dy_ref, state_ref,
    tail_ref, aux_ref, seg_ref, cw_ref, cb_ref, bias_ref, rate_ref, skip_ref, e_ref, rate_t_ref,
    ngain_ref, dgain_ref, square_ref,
    normed_t_hbm, wx_hbm, wt_hbm, gn_hbm, tokens_hbm, gb_hbm, ggate_hbm, gout_hbm,
    gi_ref, go_ref, gt_ref, small_ref, dng_ref,
    xbuf, ex, adj, xs, xdt, xe, bc, slope, dye, dxi, dbuf, r1, r1l, r2, r3,
    tbuf, consts, stacks, raws, cums, cum_ts, ones, steps, scores, dscores, gbs, gcs, sums, tslope, gp, gpt, accum, taccum,
    normed_t, wx, wt, gn, tokens, gb,
    own, part, part_t, own_t, from_core, from_core_t, from_side, from_side_t, from_level, from_level_t,
    mine, mine_t, twin, twin_t, half, half_side, half_level, half_mine, half_twin, local, sm, smr, smz, gain_out, gain_near, gain_sum, gain_far, sems, small_sems, gain_sems, load_sems,
    *, inner, heads, width, levels, seq_chunks,
):
    group, turn = pl.program_id(0), pl.program_id(1)
    step = group * seq_chunks + turn
    chunk = seq_chunks - 1 - turn
    rows, cols_g = px_ref.shape
    n = bc.shape[2] // 2
    tiles = cols_g // LANES
    per_group = cols_g // width
    taps = cw_ref.shape[0]
    tail_cols = tail_ref.shape[1]
    conv_tail = 2 * n
    here = pl.ds(pl.multiple_of(chunk * rows, rows), rows)
    spot = Spot(levels)
    gcol = pl.multiple_of(group * cols_g, cols_g)
    rows_f = mine.shape[1]

    def loads():
        pairs = ((normed_t_hbm, normed_t), (wx_hbm, wx), (wt_hbm, wt), (gn_hbm, gn), (tokens_hbm, tokens), (gb_hbm, gb))
        return [pltpu.make_async_copy(a, b, load_sems.at[i]) for i, (a, b) in enumerate(pairs)]

    def writer(ref, row, col, wide):
        def write(v, columns=None):
            if columns is None:
                ref[row : row + rows_f, col : col + wide] = v[:, :wide]
            else:
                at = pl.multiple_of(col + columns.start, LANES)
                ref[row : row + rows_f, pl.ds(at, columns.size)] = v
        return write

    sources = []
    for u in range(GROUPS):
        hbm = gout_hbm.at[:, :, :, pl.ds((u // 2) * rows_f, rows_f), pl.ds((u % 2) * cols_g, cols_g)]
        sources.append((hbm, writer(go_ref, (u // 2) * rows_f, (u % 2) * cols_g, cols_g)))
    for u in range(GROUPS):
        hbm = ggate_hbm.at[:, :, :, :, pl.ds(u * cols_g, cols_g)]
        sources.append((hbm, writer(gi_ref, 0, u * cols_g, cols_g)))
    for g in range(GROUPS):
        sources.append((part.at[g % 2], writer(gi_ref, 0, inner + g * cols_g, cols_g)))
    order = [0, 1, 2, 3, 8, 4, 5, 9, 6, 7, 10, 11]
    units = []
    for i, u in enumerate(order):
        k = i // 2
        whole, write = sources[u]
        if i % 2:
            units.append(
                Split(
                    spot, whole, own.at[u], from_core.at[u], half.at[k], half_side.at[k], half_level.at[k],
                    half_mine.at[k], half_twin.at[k], sems.at[u], write,
                )
            )
        else:
            units.append(
                Unit(
                    spot, whole, own.at[u], from_core.at[u], from_side.at[k], from_level.at[k], mine.at[k], twin.at[k],
                    sems.at[u], write,
                )
            )
    tail_wide = gi_ref.shape[1] - 2 * inner
    tail_unit = Unit(
        spot, part_t, own_t, from_core_t, from_side_t, from_level_t, mine_t, twin_t, sems.at[3 * GROUPS],
        writer(gi_ref, 0, 2 * inner, tail_wide),
    )

    events = {}
    last_step = GROUPS * seq_chunks - 1
    late = []
    for i, (begin, unit) in enumerate(zip(STARTS, units)):
        begin = begin * seq_chunks // 8
        for number, delay in enumerate(SPLIT_DELAYS if i % 2 else UNIT_DELAYS):
            events.setdefault(min(begin + delay, last_step), []).append((unit, number + 1))

    @pl.when(step == 0)
    def _():
        for copy in loads():
            copy.start()
        spot.greet(corners=True)
        accum[...] = jnp.zeros_like(accum)
        taccum[...] = jnp.zeros_like(taccum)
        steps[...] = jnp.zeros_like(steps)
        ones[...] = (iota(ones.shape, 0) == iota(ones.shape, 1) // width).astype(BF16)

    for at, happen in sorted(events.items()):
        if at == last_step:
            late += happen
            continue

        @pl.when(step == at)
        def _(happen=happen):
            for unit, number in sorted(happen, key=lambda pair: -pair[1]):
                unit.stage(number)

    def fold(v):
        return jnp.sum(v.reshape(v.shape[0] // 8, 8, v.shape[1]), axis=0)

    aux = aux_ref[here, :]
    marks = [None] + [jnp.broadcast_to(aux[:, k : k + 1], (rows, LANES)) for k in range(1, taps)]
    marks_next = [None] + [jnp.broadcast_to(aux[:, 3 + k : 4 + k], (rows, LANES)) for k in range(1, taps)]
    lower = iota((rows, rows), 0) >= iota((rows, rows), 1)
    upper = iota((rows, rows), 0) <= iota((rows, rows), 1)
    rate = rate_ref[...]

    def conv_pre(buffer, cols, wcols):
        pre = cb_ref[:, wcols] + cw_ref[0:1, wcols] * buffer[8 : 8 + rows, cols]
        for k in range(1, taps):
            pre = pre + (cw_ref[k : k + 1, wcols] * buffer[8 - k : 8 - k + rows, cols]) * marks[k]
        return pre

    def conv_back(buffer, cols, wcols, acc, acc_cols):
        outs = []
        adds = [jnp.zeros((8, LANES), F32) for _ in range(taps + 1)]
        for at in range(0, rows, 64):
            inputs = xbuf[8 + at : 72 + at, cols]
            for k in range(taps):
                grad = buffer[at + k : at + k + 64, cols]
                if k == 0:
                    out = cw_ref[0:1, wcols] * grad
                    adds[taps] = adds[taps] + fold(grad)
                else:
                    grad = grad * marks_next[k][at : at + 64]
                    out = out + cw_ref[k : k + 1, wcols] * grad
                adds[k] = adds[k] + fold(grad * inputs)
            outs.append(out)
        for k in range(taps + 1):
            acc[8 * k : 8 * k + 8, acc_cols] += adds[k]
        return jnp.concatenate(outs, axis=0)

    def fill_tail():
        xbuf[8 : 8 + rows, 0:conv_tail] = tail_ref[here, 0:conv_tail]
        before = pl.ds(pl.multiple_of(jnp.maximum(chunk * rows - 8, 0), 8), 8)
        xbuf[0:8, 0:conv_tail] = tail_ref[before, 0:conv_tail]

    @pl.when(group == 0)
    def _():
        shifted, step_size, cum, from_prev, to_end = small_terms(
            tail_ref[here, conv_tail : conv_tail + heads], bias_ref[...], rate, aux[:, 7:8], aux[:, 8:9], rows
        )
        turned = jnp.concatenate([shifted, step_size, cum, jnp.zeros((rows, LANES - 3 * heads), F32)], axis=1).T
        raws[chunk] = turned[0 : 2 * heads]
        cum_ts[chunk] = turned[2 * heads : 3 * heads]
        for g in range(GROUPS):
            cums[g, here, 0:per_group] = cum[:, g * per_group : (g + 1) * per_group]
        stacks[chunk] = jnp.concatenate(
            [jnp.concatenate(split2(v), axis=1) for v in (step_size, from_prev, to_end)], axis=0
        )
        fill_tail()
        for c in range(conv_tail // LANES):
            cols = slice(c * LANES, (c + 1) * LANES)
            pre = conv_pre(xbuf, cols, slice(inner + c * LANES, inner + (c + 1) * LANES))
            sig = sigmoid(pre)
            act = pre * sig
            tslope[here, cols] = sig + act * (1.0 - sig)
            bc[chunk, :, cols] = act.astype(BF16)
        same = upper & (aux[:, 0:1] == seg_ref[chunk])
        scores[chunk] = jnp.where(same, mm_nt(bc[chunk, :, 0:n], bc[chunk, :, n:]), 0.0)
        dscores[chunk] = jnp.zeros((rows, rows), F32)
        gbs[here, :] = jnp.zeros((rows, n), F32)
        gcs[here, :] = jnp.zeros((rows, n), F32)

    @pl.when(turn == 0)
    def _():
        adj[...] = jnp.zeros_like(adj)
        dbuf[rows : rows + 8, :] = jnp.zeros((8, cols_g), F32)

    ex[...] = mm(stacks[chunk], e_ref[:, pl.ds(gcol, cols_g)])
    own_heads = pl.ds(pl.multiple_of(group * per_group, per_group), per_group)
    cum = cums[group, here, :]
    cum_t = cum_ts[chunk, own_heads, :]
    xbuf[0:8, :] = prev_ref[...]
    xbuf[8 : 8 + rows, :] = px_ref[...]
    for c in range(tiles):
        cols = slice(c * LANES, (c + 1) * LANES)
        wcols = pl.ds(gcol + c * LANES, LANES)
        for at in range(0, rows, 64):
            part_rows = slice(at, at + 64)
            pre = cb_ref[:, wcols] + cw_ref[0:1, wcols] * xbuf[8 + at : 72 + at, cols]
            for k in range(1, taps):
                shifted = xbuf[8 + at - k : 72 + at - k, cols]
                pre = pre + (cw_ref[k : k + 1, wcols] * shifted) * marks[k][part_rows]
            sig = sigmoid(pre)
            act = pre * sig
            slope[part_rows, cols] = sig + act * (1.0 - sig)
            xs[part_rows, cols] = act
            scaled = act * ex[part_rows, cols]
            xdt[part_rows, cols] = scaled.astype(BF16)
            xe[part_rows, cols] = (scaled * ex[2 * rows + at : 2 * rows + at + 64, cols]).astype(BF16)
            dye[part_rows, cols] = (
                dy_ref[part_rows, cols].astype(F32) * ex[rows + at : rows + at + 64, cols]
            ).astype(BF16)
    b, cc = bc[chunk, :, 0:n], bc[chunk, :, n:]
    state_low = state_ref[...]
    adj_low = adj[...].astype(BF16)
    carry = ex[2 * rows - 1 : 2 * rows, :]
    gcs[here, :] += mm_nt(dye[...], state_low)
    gbs[here, :] += mm_nt(xe[...], adj_low)
    dxi[...] = mm(b, adj_low)
    through = jnp.sum(adj[...] * state_low.astype(F32), axis=0, keepdims=True) * carry
    adj[...] = adj[...] * carry + mm_tn(cc, dye[...])
    scores_t = scores[chunk]
    lane = iota((1, LANES), 1)
    masks = [(lane < width).astype(BF16), (lane >= width).astype(BF16)]
    grad_scores_t = jnp.zeros((rows, rows), F32)
    for c in range(tiles):
        cols = slice(c * LANES, (c + 1) * LANES)
        acols = pl.ds(gcol + c * LANES, LANES)
        x_low, dy_low = xdt[:, cols], dy_ref[:, cols]
        grad_mix = mm_nt(jnp.concatenate([x_low * masks[0], x_low * masks[1]], axis=0), dy_low)
        mixing = []
        for i, h in enumerate((2 * c, 2 * c + 1)):
            decay = jnp.exp(jnp.minimum(cum_t[h : h + 1, :] - cum[:, h : h + 1], 0.0))
            mixing.append((scores_t * decay).astype(BF16))
            grad_scores_t = grad_scores_t + grad_mix[i * rows : (i + 1) * rows] * decay
        within = mm(
            jnp.concatenate(mixing, axis=1), jnp.concatenate([dy_low * masks[0], dy_low * masks[1]], axis=0)
        )
        x = xs[:, cols]
        skip = skip_ref[:, acols]
        across = ex[2 * rows : 3 * rows, cols] * dxi[:, cols]
        both = within + across
        grad_ssd = dy_low.astype(F32)
        x_scaled = x_low.astype(F32)
        r1[:, cols], r1l[:, cols] = split2(grad_ssd * y_ref[:, cols] - within * x_scaled)
        r2[:, cols] = (across * x_scaled).astype(BF16)
        r3[:, cols] = (both * x).astype(BF16)
        accum[8 * taps + 8 : 8 * taps + 16, acols] += fold(grad_ssd * x)
        grad_x = skip * grad_ssd + ex[0:rows, cols] * both
        dbuf[0:rows, cols] = grad_x * slope[:, cols]
    dscores[chunk] += grad_scores_t
    by_head = ones[...]
    sums[0, chunk, own_heads, :] = (mm_nt(by_head, r1[...]) + mm_nt(by_head, r1l[...]))[0:per_group]
    sums[1, chunk, own_heads, :] = mm_nt(by_head, r2[...])[0:per_group]
    sums[2, chunk, own_heads, :] = mm_nt(by_head, r3[...])[0:per_group]
    high, rest = split2(jnp.broadcast_to(through, (16, cols_g)))
    const = (mm_nt(by_head, high) + mm_nt(by_head, rest))[0:per_group, 0:1]
    consts[chunk, own_heads, :] = jnp.broadcast_to(const, (per_group, LANES))
    for c in range(tiles):
        cols = slice(c * LANES, (c + 1) * LANES)
        acols = pl.ds(gcol + c * LANES, LANES)
        gp[here, cols] = conv_back(dbuf, cols, acols, accum, acols).astype(BF16)
    dbuf[rows : rows + 8, :] = dbuf[0:8, :]

    @pl.when(group == GROUPS - 1)
    def _():
        same = upper & (aux[:, 0:1] == seg_ref[chunk])
        grad_scores = jnp.where(same, dscores[chunk], 0.0).astype(BF16)
        grad_b = gbs[here, :] + mm(grad_scores, cc)
        grad_c = gcs[here, :] + mm_tn(grad_scores, b)
        fill_tail()

        @pl.when(turn == 0)
        def _():
            tbuf[rows : rows + 8, :] = jnp.zeros((8, 2 * n), F32)

        tbuf[0:rows, 0:n] = grad_b * tslope[here, 0:n]
        tbuf[0:rows, n : 2 * n] = grad_c * tslope[here, n : 2 * n]
        for c in range(conv_tail // LANES):
            cols = slice(c * LANES, (c + 1) * LANES)
            gpt[here, cols] = conv_back(
                tbuf, cols, slice(inner + c * LANES, inner + (c + 1) * LANES), taccum, cols
            ).astype(BF16)
        tbuf[rows : rows + 8, :] = tbuf[0:8, :]
        shifted, step_size = raws[chunk, 0:heads, :], raws[chunk, heads : 2 * heads, :]
        turned_aux = jnp.concatenate([aux, jnp.zeros((rows, LANES - aux.shape[1]), F32)], axis=1).T
        grad_log = (
            sum_tri(sums[0, chunk], lower.astype(BF16))
            + sum_tri(sums[1, chunk], (iota((rows, rows), 0) < iota((rows, rows), 1)).astype(BF16))
            + consts[chunk]
        ) * turned_aux[1:2, :]
        rate_t = jnp.broadcast_to(rate_t_ref[...], (heads, rows))
        grad_raw = (sums[2, chunk] + rate_t * grad_log) * sigmoid(shifted)
        gpt[here, conv_tail:] = (
            jnp.concatenate([grad_raw, jnp.zeros((tail_cols - conv_tail - heads, rows), F32)], axis=0).T
        ).astype(BF16)
        steps[0] += grad_raw
        steps[1] += step_size * grad_log * rate_t

    def weight_grad(low, out):
        flat = out.reshape(normed_t.shape[0], low.shape[1])
        for k in range(0, low.shape[1], 256):
            cols = slice(k, min(k + 256, low.shape[1]))
            flat[:, cols] = mm(normed_t[...], low[:, cols]).astype(BF16)

    def input_grad(low, weights):
        for k in range(gn.shape[1] // 256):
            cols = slice(k * 256, (k + 1) * 256)
            gn[:, cols] += mm_nt(low[...], weights[cols, :])

    for g in range(GROUPS - 1):

        @pl.when(step == (g + 1) * seq_chunks - 1)
        def _(g=g):
            if g == 0:
                for copy in loads():
                    copy.wait()
            weight_grad(gp, part.at[g % 2])
            input_grad(gp, wx.at[:, g * cols_g : (g + 1) * cols_g])

    @pl.when(step == last_step)
    def _():
        d = gn.shape[1]
        half_cols = sm.shape[2]

        def half_of(core):
            return pl.ds(pl.multiple_of(core * half_cols, half_cols), half_cols)

        def exchange(i):
            src = (local.at[:, half_of(1 - spot.core)], sm.at[0], sm.at[1], sm.at[3])[i]
            device = (spot.sibling, spot.across, spot.twin, spot.sibling)[i]
            return send(src, smr.at[i], small_sems.at[2 * i], small_sems.at[2 * i + 1], device)

        spread = lambda k: send(
            sm.at[2], smz.at[spot.level], small_sems.at[6 + 2 * k], small_sems.at[7 + 2 * k], spot.far(k)
        )

        def one_row(v):
            return jnp.sum(v, axis=0, keepdims=True)

        def fold_small(i):
            exchange(i).wait()
            sm[i] = (local[:, half_of(spot.core)] if i == 0 else sm[i - 1]) + smr[i]

        local[...] = jnp.zeros(local.shape, F32)
        for k in range(taps + 1):
            local[k : k + 1, 0:inner] = one_row(accum[8 * k : 8 * k + 8, :])
            local[k : k + 1, inner : inner + conv_tail] = one_row(taccum[8 * k : 8 * k + 8, 0:conv_tail])
        local[5:6, 0:inner] = one_row(dgain_ref[...])
        local[6:7, 0:inner] = one_row(accum[8 * taps + 8 : 8 * taps + 16, :])
        for i in range(2):
            turned = jnp.concatenate([steps[i], jnp.zeros((LANES - heads, LANES), F32)], axis=0).T
            local[7:8, i * LANES : (i + 1) * LANES] = one_row(turned)
        local[7:8, 2 * LANES : 3 * LANES] = one_row(square_ref[...])
        exchange(0).start()
        for unit, number in sorted(late, key=lambda pair: pair[1]):
            unit.stage(number)
        last = units[-1]
        weight_grad(gpt, part_t)
        tail_unit.stage(1)
        fold_small(0)
        exchange(1).start()
        weight_grad(gp, part.at[(GROUPS - 1) % 2])
        last.stage(1)
        tail_unit.stage(2)
        fold_small(1)
        exchange(2).start()
        input_grad(gpt, wt)
        last.stage(2)
        fold_small(2)
        for k in range(1, levels):
            spread(k).start()
        smz[spot.level] = sm[2]
        input_grad(gp, wx.at[:, (GROUPS - 1) * cols_g : GROUPS * cols_g])
        tail_unit.stage(3)
        ngain = ngain_ref[...]

        def block_norm(i, total):
            block = pl.ds(pl.multiple_of(i * 64, 64), 64)
            v = tokens[block, :].astype(F32)
            rinv = lax.rsqrt(jnp.sum(v * v, axis=1, keepdims=True) / d + EPS)
            scaled = v * rinv
            grad = gn[block, :]
            total = total + jnp.sum((grad * scaled).reshape(8, 8, d), axis=0)
            grad = grad * ngain
            mean = jnp.sum(grad * scaled, axis=1, keepdims=True) / d
            gb[block, :] = (gb[block, :].astype(F32) + rinv * (grad - scaled * mean)).astype(BF16)
            return total

        blocks = gn.shape[0] // 64
        dnorm = lax.fori_loop(0, blocks // 2, block_norm, jnp.zeros((8, d), F32))
        last.stage(3)
        dnorm = lax.fori_loop(blocks // 2, blocks, block_norm, dnorm)
        leave = pltpu.make_async_copy(gb, gt_ref, load_sems.at[6])
        leave.start()
        dnorm = one_row(dnorm)
        place = spot.rep * 4 + spot.side * 2 + spot.core
        for k in range(d // LANES):
            gain_out[k : k + 1, :] = dnorm[:, k * LANES : (k + 1) * LANES]
        near = lambda k: send(
            gain_out, gain_near.at[place], gain_sems.at[2 * k - 2], gain_sems.at[2 * k - 1], spot.corner(k)
        )
        beyond = lambda k: send(
            gain_sum, gain_far.at[spot.level], gain_sems.at[12 + 2 * k], gain_sems.at[13 + 2 * k], spot.far(k)
        )
        for k in range(1, 8):
            near(k).start()
        gain_near[place] = gain_out[...]
        last.stage(4)
        for k in range(1, levels):
            spread(k).wait()
        total = smz[0]
        for k in range(1, levels):
            total = total + smz[k]
        sm[3] = total
        exchange(3).start()
        for k in range(1, 8):
            near(k).wait()
        total = gain_near[0]
        for k in range(1, 8):
            total = total + gain_near[k]
        gain_sum[...] = total
        for k in range(1, levels):
            beyond(k).start()
        gain_far[spot.level] = gain_sum[...]
        tail_unit.stage(4)
        last.stage(5)
        for k in range(1, levels):
            beyond(k).wait()
        total = gain_far[0]
        for k in range(1, levels):
            total = total + gain_far[k]
        dng_ref[...] = total
        exchange(3).wait()
        small_ref[:, half_of(spot.core)] = sm[3]
        small_ref[:, half_of(1 - spot.core)] = smr[3]
        tail_unit.stage(5)
        last.stage(6)
        leave.wait()


def back(
    px, px_block, tail, y, dy, states, aux, seg_rows, conv_w, conv_b, bias, rate, skip_row, e, rate_t,
    norm_gain, dgain, squares, normed_t, wx, wt, gn, tokens, gb, ggate, gout, proj,
):
    length, inner = y.shape
    heads = bias.shape[1]
    levels, rows_f = ggate.shape[0], ggate.shape[3]
    taps = conv_w.shape[0]
    n = (conv_w.shape[1] - inner) // 2
    r = CHUNK
    chunks = length // r
    wide = inner // GROUPS
    tcols = tail.shape[1]
    d = normed_t.shape[0]
    small_cols = inner + tcols + LANES
    units = 3 * GROUPS
    back_at = lambda off: lambda g, c: (chunks - 1 - c, g + off)
    whole = lambda a: pl.BlockSpec(a.shape, lambda g, c: (0,) * a.ndim, pipeline_mode=pl.Buffered(1))
    anywhere = pl.BlockSpec(memory_space=pl.ANY)
    vm = pltpu.VMEM
    out = lambda s: pl.BlockSpec(s, lambda g, c: (0,) * len(s))
    return pl.pallas_call(
        functools.partial(
            back_kernel, inner=inner, heads=heads, width=inner // heads, levels=levels, seq_chunks=chunks
        ),
        grid=(GROUPS, chunks),
        in_specs=[
            pl.BlockSpec((r, wide), back_at(px_block)),
            pl.BlockSpec((8, wide), lambda g, c: (jnp.maximum((chunks - 1 - c) * (r // 8) - 1, 0), g + px_block)),
            pl.BlockSpec((r, wide), back_at(0)),
            pl.BlockSpec((r, wide), back_at(0)),
            pl.BlockSpec((n, wide), back_at(0)),
            *[whole(a) for a in (tail, aux, seg_rows, conv_w, conv_b, bias, rate, skip_row, e, rate_t, norm_gain, dgain, squares)],
            *[anywhere] * 8,
        ],
        out_specs=[out((rows_f, proj)), out((2 * rows_f, d)), anywhere, out((8, small_cols)), out((d // LANES, LANES))],
        out_shape=[
            jax.ShapeDtypeStruct((rows_f, proj), F32),
            jax.ShapeDtypeStruct((2 * rows_f, d), F32),
            jax.ShapeDtypeStruct((length, d), BF16),
            jax.ShapeDtypeStruct((8, small_cols), F32),
            jax.ShapeDtypeStruct((d // LANES, LANES), F32),
        ],
        scratch_shapes=[
            vm((r + 8, wide), F32), vm((3 * r, wide), F32), vm((n, wide), F32), vm((r, wide), F32),
            vm((r, wide), BF16), vm((r, wide), BF16), vm((chunks, r, 2 * n), BF16), vm((r, wide), F32),
            vm((r, wide), BF16), vm((r, wide), F32), vm((r + 8, wide), F32),
            vm((r, wide), BF16), vm((r, wide), BF16), vm((r, wide), BF16), vm((r, wide), BF16),
            vm((r + 8, 2 * n), F32), vm((chunks, heads, LANES), F32),
            vm((chunks, 3 * r, 2 * heads), BF16), vm((chunks, 2 * heads, r), F32), vm((GROUPS, length, LANES), F32),
            vm((chunks, heads, r), F32), vm((16, wide), BF16), vm((2, heads, r), F32),
            vm((chunks, r, r), F32), vm((chunks, r, r), F32), vm((length, n), F32), vm((length, n), F32),
            vm((3, chunks, heads, r), F32), vm((length, 2 * n), F32), vm((length, wide), BF16), vm((length, tcols), BF16),
            vm((8 * taps + 16, inner), F32), vm((8 * taps + 8, 2 * n), F32),
            vm(normed_t.shape, BF16), vm(wx.shape, BF16), vm(wt.shape, BF16), vm(gn.shape, F32), vm(tokens.shape, BF16), vm(gb.shape, BF16),
            vm((units, levels, 2, rows_f, wide), BF16), vm((2, levels, 2, 2, rows_f, wide), BF16),
            vm((levels, 2, 2, rows_f, tcols), BF16), vm((levels, 2, rows_f, tcols), BF16),
            vm((units, levels, 2, rows_f, wide), BF16), vm((levels, 2, rows_f, tcols), BF16),
            vm((units // 2, levels, rows_f, wide), BF16), vm((levels, rows_f, tcols), BF16),
            vm((units // 2, levels - 1, rows_f, wide), BF16), vm((levels - 1, rows_f, tcols), BF16),
            vm((units // 2, rows_f, wide), BF16), vm((rows_f, tcols), BF16),
            vm((units // 2, rows_f, wide), BF16), vm((rows_f, tcols), BF16),
            vm((units // 2, levels, 2, rows_f, wide // 2), BF16), vm((units // 2, levels, rows_f, wide // 2), BF16),
            vm((units // 2, levels - 1, rows_f, wide // 2), BF16),
            vm((units // 2, rows_f, wide // 2), BF16), vm((units // 2, rows_f, wide // 2), BF16),
            vm((8, small_cols), F32), vm((4, 8, small_cols // 2), F32), vm((4, 8, small_cols // 2), F32),
            vm((levels, 8, small_cols // 2), F32),
            vm((d // LANES, LANES), F32), vm((8, d // LANES, LANES), F32), vm((d // LANES, LANES), F32),
            vm((levels, d // LANES, LANES), F32),
            pltpu.SemaphoreType.DMA((units + 1, 7 + 2 * levels)),
            pltpu.SemaphoreType.DMA((6 + 2 * levels,)),
            pltpu.SemaphoreType.DMA((12 + 2 * levels,)),
            pltpu.SemaphoreType.DMA((7,)),
        ],
        compiler_params=pltpu.CompilerParams(
            dimension_semantics=("arbitrary", "arbitrary"), vmem_limit_bytes=60 * 2**20,
            collective_id=1, has_side_effects=True,
        ),
        name="scan_backward",
    )(
        px, px, y, dy, states, tail, aux, seg_rows, conv_w, conv_b, bias, rate, skip_row, e, rate_t,
        norm_gain, dgain, squares, normed_t, wx, wt, gn, tokens, gb, ggate, gout,
    )


class Load:
    def __init__(self, spot, shard, whole, sems, split):
        self.spot, self.shard, self.whole, self.sems, self.split = spot, shard, whole, sems, split

    def part(self, ref):
        if not self.split:
            return ref
        half = ref.shape[-1] // 2
        cols = pl.ds(pl.multiple_of(self.spot.rep * half, half), half)
        return ref.at[(slice(None),) * (len(ref.shape) - 1) + (cols,)]

    @property
    def a0(self):
        spot = self.spot
        here = self.whole.at[spot.level, spot.side, spot.core]
        return pltpu.make_async_copy(self.part(self.shard), self.part(here), self.sems.at[0])

    @property
    def a(self):
        spot, sems = self.spot, self.sems
        here = self.whole.at[spot.level, spot.side, spot.core]
        return [
            send(self.part(self.shard), self.part(here), sems.at[5 + 2 * d], sems.at[6 + 2 * d], spot.far(d))
            for d in range(1, spot.levels)
        ]

    @property
    def b(self):
        spot, sems = self.spot, self.sems
        if self.split:
            block = self.part(self.whole.at[:, spot.side, spot.core])
        else:
            half = spot.levels // 2
            block = self.whole.at[pl.ds(spot.rep * half, half), spot.side, spot.core]
        return send(block, block, sems.at[1], sems.at[2], spot.across)

    @property
    def c(self):
        spot, sems = self.spot, self.sems
        if self.split:
            block = self.part(self.whole.at[:, :, spot.core])
        else:
            half = spot.levels // 2
            block = self.whole.at[pl.ds(spot.rep * half, half), 1 - spot.side, spot.core]
        return send(block, block, sems.at[3], sems.at[4], spot.twin)

    @property
    def d(self):
        spot, sems = self.spot, self.sems
        block = self.whole.at[:, :, spot.core]
        last = 5 + 2 * spot.levels
        return send(block, block, sems.at[last], sems.at[last + 1], spot.sibling)

    def stage(self, number):
        if number == 1:
            self.a0.start()
            for copy in self.a:
                copy.start()
        elif number == 2:
            self.a0.wait()
            for copy in self.a:
                copy.wait()
            self.b.start()
        elif number == 3:
            self.b.wait()
            self.c.start()
        elif number == 4:
            self.c.wait()
            self.d.start()
        else:
            self.d.wait()


LOAD_STEPS = (5, 8, 14)


def first_kernel(
    cotan_ref, teacher_ref,
    tokens_hbm, ngain_ref, aux_ref, seg_ref, count_ref, cw_ref, cb_ref, bias_ref, rate_ref, skip_ref, gain_ref, e_ref,
    in_hbm, tail_hbm, out_hbm,
    px_ref, ssd_ref, state_out_ref, tail_out, normed_out, normed_t_out, wx_out, wtail_out,
    output_ref, gb_ref, mixed_ref, dy_ref, dz_ref, gn_ref, dgain_ref, small_ref,
    tokens, normed, normed_t, wx, wg, wo, weight_tail, tail, pbuf, ssd_all, gates, gms, inverses,
    ex, state, xs, xdt, xe, bc, yin, cums, scores, stacks,
    counts, countr, countz, sems, count_sems, copy_sems, leave_sems,
    *, inner, heads, width, levels, seq_chunks, loss_weight,
):
    step = pl.program_id(0)
    group, chunk = step // seq_chunks, step % seq_chunks
    rows, cols_g = px_ref.shape
    n = bc.shape[2] // 2
    tiles = cols_g // LANES
    per_group = cols_g // width
    taps = cw_ref.shape[0]
    rows_f = in_hbm.shape[0]
    tail_cols = tail.shape[1]
    conv_tail = 2 * n
    length, d_model = tokens.shape
    spot = Spot(levels)
    here = pl.ds(pl.multiple_of(chunk * rows, rows), rows)
    gcol = pl.multiple_of(group * cols_g, cols_g)
    last_step = GROUPS * seq_chunks - 1

    tail_load = Load(spot, tail_hbm, weight_tail, sems.at[0], False)
    loads = []
    for k in range(2 * GROUPS):
        cols = pl.ds((k % GROUPS) * cols_g, cols_g)
        shard = in_hbm.at[:, pl.ds((inner if k < GROUPS else 0) + (k % GROUPS) * cols_g, cols_g)]
        loads.append((shard, (wx if k < GROUPS else wg).at[:, :, :, :, cols]))
    for k in range(GROUPS):
        cols = pl.ds(k * (d_model // GROUPS), d_model // GROUPS)
        loads.append((out_hbm.at[:, cols], wo.at[:, :, :, :, cols]))
    loads = [Load(spot, shard, whole, sems.at[1 + k], k > 2 and k % 2 == 1) for k, (shard, whole) in enumerate(loads)]
    leaves = [
        (wx, wx_out), (weight_tail, wtail_out), (normed, normed_out), (normed_t, normed_t_out), (tail.at[8:], tail_out)
    ]

    def leave(k):
        return pltpu.make_async_copy(*leaves[k], leave_sems.at[k])

    exchange = lambda i: send(
        counts.at[i], countr.at[i], count_sems.at[2 * i], count_sems.at[2 * i + 1],
        (spot.sibling, spot.across, spot.twin)[i],
    )
    spread = lambda d: send(
        counts.at[3], countz.at[spot.level], count_sems.at[4 + 2 * d], count_sems.at[5 + 2 * d], spot.far(d)
    )

    def marks_of(aux):
        return [None] + [jnp.broadcast_to(aux[:, k : k + 1], (rows, LANES)) for k in range(1, taps)]

    def conv(buffer, at, cols, wcols, marks):
        block = buffer[pl.ds(at, rows + 8), cols]
        pre = cb_ref[:, wcols] + cw_ref[0:1, wcols] * block[8:]
        for k in range(1, taps):
            pre = pre + (cw_ref[k : k + 1, wcols] * block[8 - k : 8 - k + rows]) * marks[k]
        return pre * sigmoid(pre)

    def project(weight, out, cols):
        for i in range(length // 256):
            out[8 + i * 256 : 8 + (i + 1) * 256, :] = mm(normed[i * 256 : (i + 1) * 256, :], weight[:, cols])

    @pl.when(step == 0)
    def _():
        fetch = pltpu.make_async_copy(tokens_hbm, tokens, copy_sems.at[0])
        fetch.start()
        counts[0] = count_ref[...]
        spot.greet()
        tail_load.stage(1)
        exchange(0).start()
        loads[0].stage(1)
        loads[1].stage(1)
        fetch.wait()

        def norm(i, carry):
            block = pl.ds(pl.multiple_of(i * 64, 64), 64)
            v = tokens[block, :].astype(F32)
            v = v * lax.rsqrt(jnp.sum(v * v, axis=1, keepdims=True) / d_model + EPS)
            normed[block, :] = (v * ngain_ref[...]).astype(BF16)
            return carry

        lax.fori_loop(0, length // 64, norm, 0)
        def turn_rows(blocks):
            for i in blocks:
                block = slice(i * 256, (i + 1) * 256)
                normed_t[:, block] = normed[block, :].T

        def shared(i, carry):
            at = pl.ds(pl.multiple_of(i * rows, rows), rows)
            aux = aux_ref[at, :]
            marks = marks_of(aux)
            start = pl.multiple_of(i * rows, rows)
            raw = tail[pl.ds(start + 8, rows), conv_tail : conv_tail + heads]
            shifted, size, cum, from_prev, to_end = small_terms(
                raw, bias_ref[...], rate_ref[...], aux[:, 7:8], aux[:, 8:9], rows
            )
            cums[i, :, 0:heads] = cum
            stacks[i] = jnp.concatenate(
                [jnp.concatenate(split2(v), axis=1) for v in (size, from_prev, to_end)], axis=0
            )
            for c in range(conv_tail // LANES):
                cols = slice(c * LANES, (c + 1) * LANES)
                act = conv(tail, start, cols, slice(inner + c * LANES, inner + (c + 1) * LANES), marks)
                bc[i, :, cols] = act.astype(BF16)
            causal = (iota((rows, rows), 0) >= iota((rows, rows), 1)) & (aux[:, 0:1] == seg_ref[i])
            scores[i] = jnp.where(causal, mm_nt(bc[i, :, n:], bc[i, :, 0:n]), 0.0)
            return carry

        tail[0:8, :] = jnp.zeros((8, tail_cols), F32)
        pbuf[0:8, :] = jnp.zeros((8, cols_g), F32)
        cums[...] = jnp.zeros_like(cums)
        tail_load.stage(2)
        blocks = length // 256
        turn_rows(range(blocks // 2))
        tail_load.stage(3)
        turn_rows(range(blocks // 2, blocks))
        leave(2).start()
        leave(3).start()
        tail_load.stage(4)
        loads[0].stage(2)
        tail_load.stage(5)
        leave(1).start()
        project(weight_tail.reshape(d_model, tail_cols), tail, slice(0, tail_cols))
        leave(4).start()
        loads[0].stage(3)
        lax.fori_loop(0, seq_chunks // 2, shared, 0)
        loads[0].stage(4)
        loads[1].stage(2)
        lax.fori_loop(seq_chunks // 2, seq_chunks, shared, 0)

    scan_steps = GROUPS * seq_chunks
    events = {}
    for k in range(1, 3 * GROUPS):
        begin = max(0, (k - 2) * 3 * seq_chunks // 8)
        times = [begin, *[begin + 1 + delay * seq_chunks // 8 for delay in LOAD_STEPS]]
        if k == 1:
            times = [None, None, seq_chunks // 4, 5 * seq_chunks // 8]
        need = min(k * seq_chunks, scan_steps)
        for number, when in enumerate(times):
            if when is not None:
                events.setdefault(min(when, need), []).append((k, number + 1))
        if k < 2 * GROUPS:
            events.setdefault(need, []).append((k, 5))
    late = sorted(events.pop(scan_steps), key=lambda pair: (pair[1] + pair[0], pair[0]))
    for at, happen in sorted(events.items()):

        @pl.when(step == at)
        def _(happen=sorted(happen, key=lambda pair: (pair[0], pair[1]))):
            for k, number in happen:
                loads[k].stage(number)

    @pl.when(step == scan_steps)
    def _():
        leave(0).start()
        rest = list(late)
        flat_gate = wg.reshape(d_model, inner)
        for k in range(GROUPS):
            while True:
                one = rest.pop(0)
                loads[one[0]].stage(one[1])
                if one == (GROUPS + k, 5):
                    break
            cols = slice(k * cols_g, (k + 1) * cols_g)
            gates[:, cols] = mm(normed[...], flat_gate[:, cols])

        def gate_norm(i, carry):
            at = pl.ds(pl.multiple_of(i * 64, 64), 64)
            squares = jnp.zeros((64, LANES), F32)
            for c in range(inner // LANES):
                cols = slice(c * LANES, (c + 1) * LANES)
                gate = gates[at, cols]
                gated = ssd_all[at, cols] * (gate * sigmoid(gate))
                squares = squares + gated * gated
            inverse = lax.rsqrt(jnp.sum(squares, axis=1, keepdims=True) / inner + EPS)
            inverses[at, :] = jnp.broadcast_to(inverse, (64, LANES))
            return carry

        parts = 4
        blocks = length // 64
        share = -(-len(rest) // parts)
        for i in range(parts):
            for k, number in rest[i * share : (i + 1) * share]:
                loads[k].stage(number)
            lax.fori_loop(i * blocks // parts, (i + 1) * blocks // parts, gate_norm, 0)
        for k in range(2 * GROUPS, 3 * GROUPS):
            loads[k].stage(5)

    for i in range(4):

        @pl.when(step == (1 + i) * seq_chunks // 2 + 1)
        def _(i=i):
            if i < 3:
                exchange(i).wait()
                counts[i + 1] = counts[i] + countr[i]
            if i < 2:
                exchange(i + 1).start()
            elif i == 2:
                for k in range(1, levels):
                    spread(k).start()
                countz[spot.level] = counts[3]
            else:
                for k in range(1, levels):
                    spread(k).wait()
                total = countz[0]
                for k in range(1, levels):
                    total = total + countz[k]
                counts[4] = total

    for g in range(GROUPS):

        @pl.when(step == g * seq_chunks)
        def _(g=g):
            if g == 0:
                loads[0].stage(5)
            project(wx.reshape(d_model, inner), pbuf, slice(g * cols_g, (g + 1) * cols_g))

    @pl.when(step < scan_steps)
    def _():
        @pl.when(chunk == 0)
        def _():
            state[...] = jnp.zeros_like(state)

        aux = aux_ref[here, :]
        marks = marks_of(aux)
        ex[...] = mm(stacks[chunk], e_ref[:, pl.ds(gcol, cols_g)])
        head0 = group * per_group
        pick = (iota((LANES, LANES), 0) == iota((LANES, LANES), 1) + head0).astype(BF16)
        moved = [mm(v, pick) for v in split3(cums[chunk])]
        cum = moved[0] + moved[1] + moved[2]
        cum_t = cum.T
        start = pl.multiple_of(chunk * rows, rows)
        px_ref[...] = pbuf[pl.ds(start + 8, rows), :]
        for c in range(tiles):
            cols = slice(c * LANES, (c + 1) * LANES)
            wcols = pl.ds(gcol + c * LANES, LANES)
            block = pbuf[pl.ds(start, rows + 8), cols]
            for at in range(0, rows, 64):
                part_rows = slice(at, at + 64)
                pre = cb_ref[:, wcols] + cw_ref[0:1, wcols] * block[8 + at : 72 + at]
                for k in range(1, taps):
                    shifted = block[8 + at - k : 72 + at - k]
                    pre = pre + (cw_ref[k : k + 1, wcols] * shifted) * marks[k][part_rows]
                act = pre * sigmoid(pre)
                xs[part_rows, cols] = act
                scaled = act * ex[part_rows, cols]
                xdt[part_rows, cols] = scaled.astype(BF16)
                xe[part_rows, cols] = (scaled * ex[2 * rows + at : 2 * rows + at + 64, cols]).astype(BF16)
        b, cc = bc[chunk, :, 0:n], bc[chunk, :, n:]
        state_low = state[...].astype(BF16)
        state_out_ref[...] = state_low
        yin[...] = mm(cc, state_low)
        state[...] = state[...] * ex[2 * rows - 1 : 2 * rows, :] + mm_tn(b, xe[...])
        score = scores[chunk]
        lane = iota((1, LANES), 1)
        masks = [(lane < width).astype(BF16), (lane >= width).astype(BF16)]
        for c in range(tiles):
            cols = slice(c * LANES, (c + 1) * LANES)
            mixing = []
            for h in (2 * c, 2 * c + 1):
                spread_h = jnp.minimum(cum[:, h : h + 1] - cum_t[h : h + 1, :], 0.0)
                mixing.append((score * jnp.exp(spread_h)).astype(BF16))
            x_low = xdt[:, cols]
            y = mm(
                jnp.concatenate(mixing, axis=1), jnp.concatenate([x_low * masks[0], x_low * masks[1]], axis=0)
            ) + ex[rows : 2 * rows, cols] * yin[:, cols]
            acols = pl.ds(gcol + c * LANES, LANES)
            ssd_ref[:, cols] = y
            ssd_all[here, acols] = y + skip_ref[:, acols] * xs[:, cols]

    @pl.when(step >= scan_steps)
    def _():
        turn = step - scan_steps
        block_rows = gms.shape[0]
        base = pl.multiple_of(turn * block_rows, block_rows)
        flat_gate = wg.reshape(d_model, inner)
        flat_out = wo.reshape(inner, d_model)
        sub = 64

        @pl.when(turn == 0)
        def _():
            dgain_ref[...] = jnp.zeros_like(dgain_ref)
            small_ref[...] = jnp.zeros_like(small_ref)

        def norm_of(i):
            at = pl.ds(pl.multiple_of(i * sub, sub), sub)
            return at, pl.ds(pl.multiple_of(base + i * sub, sub), sub)

        def forward_part(i, carry):
            at, full_at = norm_of(i)
            inverse = inverses[full_at, :]
            for c in range(inner // LANES):
                cols = slice(c * LANES, (c + 1) * LANES)
                gate = gates[full_at, cols]
                unit = ssd_all[full_at, cols] * (gate * sigmoid(gate)) * inverse
                mixed_ref[at, cols] = (unit * gain_ref[:, cols]).astype(BF16)
            return carry

        lax.fori_loop(0, block_rows // sub, forward_part, 0)
        results = gms.at[:, 0:d_model]
        results[...] = mm(mixed_ref[...], flat_out[...])
        scale = 2.0 * loss_weight / (counts[4, 0:1, :] * d_model)

        def loss_part(i, carry):
            at, full_at = norm_of(i)
            valid = jnp.broadcast_to(aux_ref[full_at, 9:10], (sub, LANES))
            squares = jnp.zeros((8, LANES), F32)
            for c in range(d_model // LANES):
                cols = slice(c * LANES, (c + 1) * LANES)
                result = tokens[full_at, cols].astype(F32) + results[at, cols]
                output_ref[at, cols] = result.astype(BF16)
                error = result - teacher_ref[at, cols].astype(F32)
                squares = squares + jnp.sum((valid * error * error).reshape(sub // 8, 8, LANES), axis=0)
                gb_ref[at, cols] = (valid * (cotan_ref[at, cols].astype(F32) + scale * error)).astype(BF16)
            small_ref[0:8, :] += squares
            return carry

        lax.fori_loop(0, block_rows // sub, loss_part, 0)
        small_ref[8:16, :] = counts[4]
        grads = gb_ref[...]
        for k in range(GROUPS):
            cols = slice(k * cols_g, (k + 1) * cols_g)
            gms[:, cols] = mm_nt(grads, flat_out[cols, :])

        def backward_part(i, carry):
            at, full_at = norm_of(i)
            cross = jnp.zeros((sub, LANES), F32)
            for c in range(inner // LANES):
                cols = slice(c * LANES, (c + 1) * LANES)
                cross = cross + gms[at, cols] * mixed_ref[at, cols].astype(F32)
            inverse = inverses[full_at, :]
            mean_cross = jnp.sum(cross, axis=1, keepdims=True) / inner
            for c in range(inner // LANES):
                cols = slice(c * LANES, (c + 1) * LANES)
                gate = gates[full_at, cols]
                sig = sigmoid(gate)
                silu = gate * sig
                ssd = ssd_all[full_at, cols]
                unit = ssd * silu * inverse
                grad_mixed = gms[at, cols]
                dgain_ref[:, cols] += jnp.sum((grad_mixed * unit).reshape(sub // 8, 8, LANES), axis=0)
                grad_gated = inverse * (grad_mixed * gain_ref[:, cols] - unit * mean_cross)
                dy_ref[at, cols] = (grad_gated * silu).astype(BF16)
                dz_ref[at, cols] = (
                    grad_gated * ssd * (sig + silu * (1.0 - sig))
                ).astype(BF16)
            return carry

        lax.fori_loop(0, block_rows // sub, backward_part, 0)
        gn_ref[...] = mm_nt(dz_ref[...], flat_gate[...])

        @pl.when(turn == length // block_rows - 1)
        def _():
            for k in range(len(leaves)):
                leave(k).wait()


def first(
    tokens, norm_gain, aux, seg_rows, count, conv_w, conv_b, bias, rate, skip_row, gain_row, e,
    cotangent, teacher, w_in, w_tail, w_out, levels, loss_weight,
):
    length, d = tokens.shape
    heads, inner = bias.shape[1], skip_row.shape[1]
    rows_f = w_in.shape[0]
    n = (conv_w.shape[1] - inner) // 2
    r = CHUNK
    chunks = length // r
    wide = inner // GROUPS
    tcols = w_tail.shape[1]
    units = 3 * GROUPS
    tall = 256
    scan_steps = GROUPS * chunks

    def scan_block(s):
        s = jnp.minimum(s, scan_steps - 1)
        return s % chunks, s // chunks

    block = lambda h: pl.BlockSpec((h, wide), scan_block)
    late = lambda w, deep=2: pl.BlockSpec(
        (tall, w), lambda s: (jnp.maximum(s - scan_steps, 0), 0), pipeline_mode=pl.Buffered(deep)
    )
    whole = lambda a: pl.BlockSpec(a.shape, lambda s: (0,) * a.ndim, pipeline_mode=pl.Buffered(1))
    fixed = lambda *dims: pl.BlockSpec(dims, lambda s: (0,) * len(dims))
    anywhere = pl.BlockSpec(memory_space=pl.ANY)
    vm = pltpu.VMEM
    shape = jax.ShapeDtypeStruct
    wide_shape = (levels, 2, 2, rows_f, inner)
    return pl.pallas_call(
        functools.partial(
            first_kernel, inner=inner, heads=heads, width=inner // heads, levels=levels, seq_chunks=chunks,
            loss_weight=loss_weight,
        ),
        grid=(scan_steps + length // tall,),
        in_specs=[
            late(d), late(d), anywhere,
            *[whole(a) for a in (norm_gain, aux, seg_rows, count, conv_w, conv_b, bias, rate, skip_row, gain_row, e)],
            anywhere, anywhere, anywhere,
        ],
        out_specs=[
            block(r), block(r), block(n), *[anywhere] * 5,
            late(d), late(d), late(inner), late(inner), late(inner), late(d), fixed(8, inner), fixed(16, LANES),
        ],
        out_shape=[
            shape((length, inner), F32), shape((length, inner), F32), shape((chunks * n, inner), BF16),
            shape((length, tcols), F32), shape((length, d), BF16), shape((d, length), BF16),
            shape(wide_shape, BF16), shape((levels, 2, 2, rows_f, tcols), BF16),
            shape((length, d), BF16), shape((length, d), BF16), shape((length, inner), BF16),
            shape((length, inner), BF16), shape((length, inner), BF16), shape((length, d), F32),
            shape((8, inner), F32), shape((16, LANES), F32),
        ],
        scratch_shapes=[
            vm((length, d), BF16), vm((length, d), BF16), vm((d, length), BF16),
            vm(wide_shape, BF16), vm(wide_shape, BF16), vm((levels, 2, 2, 2 * rows_f, d), BF16),
            vm((levels, 2, 2, rows_f, tcols), BF16),
            vm((length + 8, tcols), F32), vm((length + 8, wide), F32), vm((length, inner), F32),
            vm((length, inner), F32), vm((tall, inner), F32), vm((length, LANES), F32),
            vm((3 * r, wide), F32), vm((n, wide), F32), vm((r, wide), F32), vm((r, wide), BF16), vm((r, wide), BF16),
            vm((chunks, r, 2 * n), BF16), vm((r, wide), F32), vm((chunks, r, LANES), F32), vm((chunks, r, r), F32),
            vm((chunks, 3 * r, 2 * heads), BF16),
            vm((5, 8, LANES), F32), vm((3, 8, LANES), F32), vm((levels, 8, LANES), F32),
            pltpu.SemaphoreType.DMA((units + 1, 7 + 2 * levels)),
            pltpu.SemaphoreType.DMA((4 + 2 * levels,)),
            pltpu.SemaphoreType.DMA((1,)),
            pltpu.SemaphoreType.DMA((5,)),
        ],
        compiler_params=pltpu.CompilerParams(
            dimension_semantics=("arbitrary",), vmem_limit_bytes=60 * 2**20,
            collective_id=2, has_side_effects=True,
        ),
        name="scan_forward",
    )(
        cotangent, teacher, tokens, norm_gain, aux, seg_rows, count, conv_w, conv_b, bias, rate, skip_row, gain_row, e,
        w_in, w_tail, w_out,
    )


def on_device(
    tokens,
    norm_gain,
    in_weight,
    conv_weight,
    conv_bias,
    step_bias,
    decay_log,
    skip_gain,
    out_gain,
    out_weight,
    cotangent,
    teacher,
    segment,
    valid_mask,
):
    seqs, length, width = tokens.shape
    rows = seqs * length
    shards = lax.axis_size("fsdp")
    devices = lax.axis_size("rep") * shards
    levels = shards // 4
    loss_weight = float(rows * devices * width // 8)
    heads, inner = step_bias.shape[0], out_gain.shape[0]
    aux, seg_rows, count, bias, rate, rate_t, skip_row, conv_row, ngain_row, gain_row, e, in_tail = prepare(
        segment, valid_mask, step_bias, decay_log, skip_gain, conv_bias, norm_gain, out_gain, in_weight
    )
    params = (conv_weight, conv_row, bias, rate, skip_row)
    flat, cotan, target = (v.reshape(rows, width) for v in (tokens, cotangent, teacher))
    (
        px, y, states, tail, normed, normed_t, wx, wt, output, grad_branch, mixed, dy, dz, gn, dgain, sums
    ) = first(
        flat, ngain_row, aux, seg_rows, count, *params, gain_row, e, cotan, target,
        in_weight, in_tail, out_weight, levels, loss_weight,
    )
    wx, wt = (w.reshape(-1, w.shape[-1]) for w in (wx, wt))
    grad_out = mm_tn(mixed, grad_branch).astype(BF16)
    grad_gate = mm(normed_t, dz).astype(BF16)
    grad_in, grad_out, grad_tokens, small, norm_sum = back(
        px, 0, tail, y, dy, states, aux, seg_rows, *params, e, rate_t,
        ngain_row, dgain, sums[:8], normed_t, wx, wt, gn, flat, grad_branch,
        grad_gate.reshape(levels, 2, 2, width // shards, inner),
        grad_out.reshape(levels, 2, 2, inner // shards, width), in_weight.shape[1],
    )
    outs = finish(
        grad_in, grad_out, grad_tokens, output, small, norm_sum, sums, e, *conv_weight.shape, heads, inner
    )
    return (
        outs[0].reshape(tokens.shape), outs[1].reshape(()), outs[2].reshape(tokens.shape), *outs[3:]
    )


def solution(mesh):
    tokens = P(("rep", "fsdp"), None, None)
    marks = P(("rep", "fsdp"), None)
    shard = P("fsdp", None)
    return jax.shard_map(
        on_device,
        mesh=mesh,
        in_specs=(tokens, P(), shard, P(), P(), P(), P(), P(), P(), shard, tokens, tokens, marks, marks),
        out_specs=(tokens, P(), tokens, P(), shard, P(), P(), P(), P(), P(), P(), shard),
        check_vma=False,
    )
```
